32 devices in a mesh: grp: 4 (over x, core), blk: 8 (over z, y).
Axes of the slice: x: 2, y: 2, z: 4, core: 2. Of those that a mesh axis runs over, the one named last changes fastest.
Arguments:
- particles: bfloat16 [64, 2, 4000], P(('blk', 'grp')), may hold values from -6 to 6
- ctf_class: int32 [64], P(('blk', 'grp')), may hold values from 0 to 63
- orient_prior: bfloat16 [64, 192], P(('blk', 'grp')), may hold values from -6 to 6
- ctf_curves: float32 [64, 4000], replicated, may hold values from -1 to 1
- noise_weight: float32 [4000], replicated, may hold values from 0.005 to 0.05
- shift_phase: float32 [9, 4000], replicated, may hold values from -3.140625 to 3.140625
- trans_index: int32 [9], replicated, may hold values from 0 to 8, each once
- projections: bfloat16 [256, 2, 4000], P(('grp', 'blk')), may hold values from -1.75 to 1.75
- orient_subset: int32 [256], P(('grp', 'blk')), may hold values from 0 to 191
Outputs:
- scores: float32 [64, 9, 256], P('blk', None, 'grp')
The draws below stay inside these ranges and needn't reach their ends.
Inputs may be any that keep to these rules, and one draw needn't show every extreme that they name: `trans_index`: each row of shift_phase is named once.
All inputs are finite; a program needn't handle non-finite values.
Results may differ from the reference program's by a relative error of at most 0.00056.
Values may be sent and summed in bfloat16 or wider, within the bound.
No kernel may reach another device: no remote copies, remote signals or barrier semaphores. Data moves between devices by JAX's collectives and lax.ppermute only.
A program may use at most 128 MiB of HBM per device.

```python
import math
import jax
import jax.numpy as jnp
from jax import lax

K = 4000
NT = 9
NC = 64
SUBSETS = 192
PROJ_DEV = 8
NPART = 64
NPROJ = 256
N_BLK = 8


def plant(values, stream_key, smallest, high):
    longest = values.shape.index(max(values.shape))
    spots = []
    for shift in (0, 1):
        where = [jax.random.randint(jax.random.fold_in(stream_key, axis), (), 0, length) for axis, length in enumerate(values.shape)]
        where[longest] = (where[longest] + shift) % values.shape[longest]
        spots.append(tuple(where))
    return values.at[spots[0]].set(smallest).at[spots[1]].set(high)


def steps_of(own_key, dims, split, least, high):
    level = 1.0
    for dim, parts in split:
        draws = jax.random.uniform(jax.random.fold_in(jax.random.fold_in(own_key, 6), dim), (parts,), jnp.float32, least / len(split), high / len(split))
        level = level * jnp.repeat(jnp.exp(draws), dims[dim] // parts).reshape((-1,) + (1,) * (len(dims) - 1 - dim))
    return level


def noise(key, extent, spread, bound, pieces=(), held_as=jnp.bfloat16):
    values = jax.random.normal(key, extent, jnp.float32) * spread
    if len(pieces) > 0:
        values = steps_of(key, extent, pieces, -0.22, 0.18) * values
    return jnp.clip(values, min=-bound, max=bound).astype(held_as)


def setup_inputs(seed: int = 0) -> dict:
    arg_keys = jax.random.split(jax.random.key(seed), 10)
    particles = noise(arg_keys[0], (NPART, 2, K), 1.0, 6.0, ((0, 32),))
    ctf_class = plant(jax.random.randint(arg_keys[1], (NPART,), 0, NC), jax.random.fold_in(arg_keys[1], 1), 0, NC - 1).astype(jnp.int32)
    orient_prior = noise(arg_keys[2], (NPART, SUBSETS), 1.0, 6.0, ((0, 32),))
    ctf_curves = jnp.clip(jax.random.uniform(arg_keys[3], (NC, K), jnp.float32, -1.0, 1.0), -1.0, 1.0)
    noise_weight = jnp.clip(jnp.exp(jax.random.uniform(arg_keys[4], (K,), jnp.float32, math.log(0.005), math.log(0.05))), 0.005, 0.05)
    shift_phase = jnp.clip(jax.random.uniform(arg_keys[5], (NT, K), jnp.float32, -3.140625, 3.140625), -3.140625, 3.140625)
    trans_index = jax.random.permutation(arg_keys[6], NT).astype(jnp.int32)
    projections = noise(arg_keys[7], (NPROJ, 2, K), 0.3, 1.75, ((0, 32),))
    orient_subset = plant(jax.random.randint(arg_keys[8], (NPROJ,), 0, SUBSETS), jax.random.fold_in(arg_keys[8], 1), 0, SUBSETS - 1).astype(jnp.int32)
    return {"particles": particles, "ctf_class": ctf_class, "orient_prior": orient_prior, "ctf_curves": ctf_curves, "noise_weight": noise_weight, "shift_phase": shift_phase, "trans_index": trans_index, "projections": projections, "orient_subset": orient_subset}


def reference(particles, ctf_class, orient_prior, ctf_curves, noise_weight, shift_phase, trans_index, projections, orient_subset):
    highest = lax.Precision.HIGHEST
    weight_rows = ctf_curves * noise_weight[None, :]
    curve = weight_rows[ctf_class]
    weighted = (particles.astype(jnp.float32) * curve[:, None, :]).astype(jnp.bfloat16)
    weighted_wide = weighted.astype(jnp.float32)
    angle = shift_phase[trans_index]
    cos_part = jnp.cos(angle)
    sin_part = jnp.sin(angle)
    curve_sq = ctf_curves * ctf_curves * noise_weight[None, :]
    prior = orient_prior.astype(jnp.float32)
    block_len = PROJ_DEV * N_BLK
    blocks = NPROJ // block_len
    bank_blocks = projections.reshape(blocks, block_len, 2, K)
    id_blocks = orient_subset.reshape(blocks, block_len)

    def score_block(inputs):
        bank, subset_ids = inputs
        bank_real = bank[:, 0, :].astype(jnp.float32)
        bank_imag = bank[:, 1, :].astype(jnp.float32)
        real_shift = cos_part[:, None, :] * bank_real[None] + sin_part[:, None, :] * bank_imag[None]
        imag_shift = cos_part[:, None, :] * bank_imag[None] - sin_part[:, None, :] * bank_real[None]
        shifted = jnp.stack([real_shift, imag_shift], axis=2).astype(jnp.bfloat16)
        cross = jnp.einsum("nck,tmck->ntm", weighted_wide, shifted.astype(jnp.float32), precision=highest)
        power = bank_real * bank_real + bank_imag * bank_imag
        norm_table = jnp.dot(curve_sq, power.T, precision=highest)
        norm_sel = norm_table[ctf_class]
        prior_term = prior[:, subset_ids]
        return cross - 0.5 * norm_sel[:, None, :] + prior_term[:, None, :]

    result = lax.map(score_block, (bank_blocks, id_blocks))
    return jnp.transpose(result, (1, 2, 0, 3)).reshape(NPART, NT, NPROJ)
```

```python
import jax
import jax.numpy as jnp
from jax import lax
from jax.sharding import PartitionSpec as P


def per_device(
    particles,
    ctf_class,
    orient_prior,
    ctf_curves,
    noise_weight,
    shift_phase,
    trans_index,
    projections,
    orient_subset,
):
    highest = lax.Precision.HIGHEST
    nb, ng = lax.axis_size("blk"), lax.axis_size("grp")
    me = lax.axis_index("blk")
    n_part, n_proj = particles.shape[0], projections.shape[0]
    length = particles.shape[2]
    classes_count = ctf_curves.shape[0]
    subset_count = orient_prior.shape[1]
    chunk = 128 * -(-length // (128 * nb))
    pad = nb * chunk - length

    def chunk_of(rows):
        wide = jnp.pad(rows, ((0, 0), (0, pad)))
        return lax.dynamic_slice(wide, (0, me * chunk), (rows.shape[0], chunk))

    curve = jnp.concatenate(
        [lax.dynamic_slice(ctf_curves, (ctf_class[i], 0), (1, length)) for i in range(n_part)]
    )
    curve = curve * noise_weight[None, :]
    weighted = (particles.astype(jnp.float32) * curve[:, None, :]).astype(jnp.bfloat16)

    small = jnp.concatenate(
        [
            ctf_class.astype(jnp.bfloat16),
            orient_subset.astype(jnp.bfloat16),
            orient_prior.reshape(-1),
        ]
    )
    n_small = small.shape[0]
    n_ext = -(-n_small // (2 * chunk))
    ext = jnp.pad(small, (0, n_ext * 2 * chunk - n_small)).reshape(1, n_ext, 2, chunk)

    rows = jnp.concatenate([projections, weighted], axis=0)
    rows = jnp.pad(rows, ((0, 0), (0, 0), (0, pad)))
    rows = rows.reshape(n_proj + n_part, 2, nb, chunk).transpose(2, 0, 1, 3)
    message = jnp.concatenate([rows, jnp.broadcast_to(ext, (nb, n_ext, 2, chunk))], axis=1)
    recv = lax.all_to_all(message, "blk", 0, 0, tiled=True)
    gath = lax.all_gather(recv[:, n_proj:], "grp", axis=1)

    bank = recv[:, :n_proj].reshape(nb * n_proj, 2, chunk)
    weighted_all = gath[:, :, :n_part].reshape(nb * ng * n_part, 2, chunk)
    small_all = gath[:, :, n_part:].reshape(nb, ng, n_ext * 2 * chunk)[:, :, :n_small]
    classes = small_all[:, :, :n_part].reshape(-1).astype(jnp.int32)
    prior_all = small_all[:, :, n_part + n_proj :].reshape(nb, ng * n_part, subset_count)
    prior = lax.dynamic_index_in_dim(prior_all, me, 0, keepdims=False).astype(jnp.float32)
    own = recv[:, n_proj + n_part :].reshape(nb, n_ext * 2 * chunk)
    subset_ids = own[:, n_part : n_part + n_proj].reshape(-1).astype(jnp.int32)

    angle = chunk_of(shift_phase[trans_index])
    cos_part = jnp.cos(angle)
    sin_part = jnp.sin(angle)
    bank_real = bank[:, 0, :].astype(jnp.float32)
    bank_imag = bank[:, 1, :].astype(jnp.float32)
    real_shift = cos_part[:, None, :] * bank_real[None] + sin_part[:, None, :] * bank_imag[None]
    imag_shift = cos_part[:, None, :] * bank_imag[None] - sin_part[:, None, :] * bank_real[None]
    shifted = jnp.stack([real_shift, imag_shift], axis=2).astype(jnp.bfloat16)
    cross = jnp.einsum("nck,tmck->ntm", weighted_all, shifted, preferred_element_type=jnp.float32)

    curve_sq = chunk_of(ctf_curves)
    curve_sq = curve_sq * curve_sq * chunk_of(noise_weight[None, :])
    power = bank_real * bank_real + bank_imag * bank_imag
    norm_table = jnp.dot(curve_sq, power.T, precision=highest)
    onehot_rows = (
        classes[:, None] == jnp.arange(classes_count, dtype=jnp.int32)[None, :]
    ).astype(jnp.float32)
    norm_sel = jnp.dot(onehot_rows, norm_table, precision=highest)
    subset_onehot = (
        subset_ids[None, :] == jnp.arange(subset_count, dtype=jnp.int32)[:, None]
    ).astype(jnp.float32)
    prior_term = jnp.dot(prior, subset_onehot, precision=highest)
    partial = cross - 0.5 * norm_sel[:, None, :]
    total = lax.psum_scatter(partial, "blk", scatter_dimension=0, tiled=True)
    return total + prior_term[:, None, :]


def solution(mesh):
    placed = (
        P(("blk", "grp"), None, None),
        P(("blk", "grp")),
        P(("blk", "grp"), None),
        P(),
        P(),
        P(),
        P(),
        P(("grp", "blk"), None, None),
        P(("grp", "blk")),
    )
    return jax.shard_map(
        per_device, mesh=mesh, in_specs=placed, out_specs=P("blk", None, "grp"), check_vma=False
    )
```

```python
import functools

import jax
import jax.numpy as jnp
from jax import lax
from jax.experimental import pallas as pl
from jax.experimental.pallas import tpu as pltpu
from jax.sharding import PartitionSpec as P

F32 = jnp.float32
BF16 = jnp.bfloat16
HIGHEST = lax.Precision.HIGHEST
NT_DIMS = (((1,), (1,)), ((), ()))
MIB = 1 << 20
ROWS = 8


def _vmem():
    return pl.BlockSpec(memory_space=pltpu.VMEM)


def _smem():
    return pl.BlockSpec(memory_space=pltpu.SMEM)


def _params(mib):
    return pltpu.CompilerParams(vmem_limit_bytes=mib * MIB)


def pack_kernel(
    nz, ny, chunk, class_ref, subset_ref, particles_ref, prior_ref, curves_ref, noise_ref, proj_ref, *rest
):
    banks, parts, (held, sems) = rest[:nz], rest[nz : 2 * nz], rest[2 * nz :]
    n_part, n_proj = particles_ref.shape[0], proj_ref.shape[0]
    length = proj_ref.shape[2]
    z = lax.axis_index("blk") // ny
    copies = []
    for i in range(n_part):
        first = pl.multiple_of(class_ref[i] // ROWS * ROWS, ROWS)
        copy = pltpu.make_async_copy(curves_ref.at[pl.ds(first, ROWS)], held.at[i], sems.at[i])
        copy.start()
        copies.append(copy)

    def piece(values, c):
        width = min(chunk, length - c * chunk)
        values = values[:, c * chunk : c * chunk + width]
        if width < chunk:
            values = jnp.concatenate(
                [values, jnp.zeros((values.shape[0], chunk - width), values.dtype)], axis=1
            )
        return values

    row8 = lax.broadcasted_iota(jnp.int32, (ROWS, chunk), 0)
    lane8 = lax.broadcasted_iota(jnp.int32, (ROWS, chunk), 1)
    ids = jnp.zeros((ROWS, chunk), F32)
    for j in range(n_proj):
        ids = jnp.where(row8 == j, subset_ref[j].astype(F32), ids)

    for c in range(nz):
        real = jnp.zeros((ROWS, chunk), F32)
        imag = jnp.zeros((ROWS, chunk), F32)
        for j in range(n_proj):
            both = piece(proj_ref[j].astype(F32), c)
            real = jnp.where(row8 == j, both[0:1], real)
            imag = jnp.where(row8 == j, both[1:2], imag)
        if c == nz - 1:
            real = jnp.where(lane8 == length - c * chunk, ids, real)
        bank = jnp.concatenate([real, imag], axis=0).astype(BF16)
        for s in range(nz):

            @pl.when((z ^ s) == c)
            def _():
                banks[s][...] = bank

    for copy in copies:
        copy.wait()
    subsets = prior_ref.shape[1]
    prior = prior_ref[...].astype(F32)
    prior = jnp.concatenate([prior, jnp.zeros((n_part, chunk - subsets), F32)], axis=1)
    weighted = []
    for i in range(n_part):
        curve = held[i, pl.ds(class_ref[i] % ROWS, 1), :] * noise_ref[...]
        weighted.append(particles_ref[i].astype(F32) * curve)
    for c in range(nz):
        rows = jnp.zeros((ROWS, chunk), F32)
        for i in range(n_part):
            both = piece(weighted[i], c)
            rows = jnp.where(row8 == i, both[0:1], rows)
            rows = jnp.where(row8 == n_part + i, both[1:2], rows)
            extra = jnp.where(
                lane8 == subsets, class_ref[i].astype(F32), jnp.broadcast_to(prior[i : i + 1], rows.shape)
            )
            rows = jnp.where(row8 == 2 * n_part + i, extra, rows)
        part = rows.astype(BF16)
        for s in range(nz):

            @pl.when((z ^ s) == c)
            def _():
                parts[s][...] = part


def table_kernel(
    nz, ny, chunk, trans_ref, curves_ref, noise_ref, phase_ref, cos_ref, sin_ref, square_ref, angle
):
    z = lax.axis_index("blk") // ny
    length = curves_ref.shape[1]
    angle[...] = jnp.zeros_like(angle)
    square_ref[...] = jnp.zeros_like(square_ref)
    for c in range(nz):
        width = min(chunk, length - c * chunk)
        span = slice(c * chunk, c * chunk + width)

        @pl.when(z == c)
        def _():
            for t in range(phase_ref.shape[0]):
                angle[t : t + 1, :width] = phase_ref[pl.ds(trans_ref[t], 1), span]
            curve = curves_ref[:, span]
            square_ref[:, :width] = curve * curve * noise_ref[:, span]

    cos_ref[...] = jnp.cos(angle[...])
    sin_ref[...] = jnp.sin(angle[...])


def score_kernel(nz, ny, ng, n_part, tail, subsets, cos_ref, sin_ref, square_ref, *rest):
    n_bank = nz * ny
    banks, parts, outs = rest[:n_bank], rest[n_bank : n_bank + ng], rest[n_bank + ng : n_bank + ng + nz]
    real_ref, imag_ref, shifted_ref = rest[n_bank + ng + nz :]
    blk = lax.axis_index("blk")
    z, y, g = blk // ny, blk % ny, lax.axis_index("grp")
    n_proj = banks[0].shape[0] // 2
    chunk = banks[0].shape[1]
    total = n_bank * n_proj
    shifts = cos_ref.shape[0]
    classes_count = square_ref.shape[0]

    for s in range(nz):
        for r in range(ny):
            both = banks[s * ny + r][...].astype(F32)
            where = pl.multiple_of(((z ^ s) * ny + (y ^ r)) * n_proj, n_proj)
            real_ref[pl.ds(where, n_proj), :] = both[:n_proj]
            imag_ref[pl.ds(where, n_proj), :] = both[n_proj:]
    real, imag = real_ref[...], imag_ref[...]

    held = jnp.concatenate([part[...] for part in parts], axis=0)
    count = nz * ng * n_part
    out_row = lax.broadcasted_iota(jnp.int32, (3 * count, held.shape[0]), 0)
    in_row = lax.broadcasted_iota(jnp.int32, (3 * count, held.shape[0]), 1)
    kind, rest_row = out_row // count, out_row % count
    slot, rest_row = rest_row // (ng * n_part), rest_row % (ng * n_part)
    group, i = rest_row // n_part, rest_row % n_part
    source = (group ^ g) * (nz * ROWS) + slot * ROWS + kind * n_part + i
    pick = (in_row == source).astype(F32).astype(BF16)
    ordered = jnp.dot(pick, held, preferred_element_type=F32)
    weighted = jnp.concatenate([ordered[:count], ordered[count : 2 * count]], axis=1).astype(BF16)
    extra = ordered[2 * count :]

    for t in range(shifts):
        cos_part, sin_part = cos_ref[t : t + 1, :], sin_ref[t : t + 1, :]
        rows = slice(t * total, (t + 1) * total)
        shifted_ref[rows, :chunk] = (cos_part * real + sin_part * imag).astype(BF16)
        shifted_ref[rows, chunk:] = (cos_part * imag - sin_part * real).astype(BF16)
    cross = lax.dot_general(weighted, shifted_ref[...], NT_DIMS, preferred_element_type=F32)

    power = real * real + imag * imag
    norm_table = lax.dot_general(
        square_ref[...], power, NT_DIMS, precision=HIGHEST, preferred_element_type=F32
    )
    class_col = lax.broadcasted_iota(jnp.int32, (count, classes_count), 1).astype(F32)
    onehot = (class_col == extra[:, subsets : subsets + 1]).astype(F32)
    norm = jnp.dot(onehot, norm_table, precision=HIGHEST, preferred_element_type=F32)
    subset_col = lax.broadcasted_iota(jnp.int32, (total, subsets), 1).astype(F32)
    subset_hot = (subset_col == real[:, tail : tail + 1]).astype(F32).astype(BF16)
    prior = lax.dot_general(
        extra[:, :subsets].astype(BF16), subset_hot, NT_DIMS, preferred_element_type=F32
    )
    added = jnp.where(z == nz - 1, prior, jnp.zeros_like(prior)) - 0.5 * norm
    added = jnp.concatenate([added] * shifts, axis=1)
    result = cross + added
    dest = ng * n_part
    for s in range(nz):
        outs[s][...] = result[s * dest : (s + 1) * dest]


def sum_kernel(n_proj, *refs):
    *terms, out_ref = refs
    total = terms[0][...]
    for term in terms[1:]:
        total = total + term[...]
    for t in range(out_ref.shape[0]):
        out_ref[t] = total[:, t * n_proj : (t + 1) * n_proj]


def per_device(
    particles,
    ctf_class,
    orient_prior,
    ctf_curves,
    noise_weight,
    shift_phase,
    trans_index,
    projections,
    orient_subset,
):
    nb, ng = lax.axis_size("blk"), lax.axis_size("grp")
    nz = 4
    ny = nb // nz
    n_part, n_proj = particles.shape[0], projections.shape[0]
    length = particles.shape[2]
    shifts = shift_phase.shape[0]
    classes_count = ctf_curves.shape[0]
    subsets = orient_prior.shape[1]
    chunk = 128 * -(-length // (128 * nz))
    tail = length - (nz - 1) * chunk
    noise = noise_weight.reshape(1, length)
    shape = jax.ShapeDtypeStruct

    packed = pl.pallas_call(
        functools.partial(pack_kernel, nz, ny, chunk),
        out_shape=[shape((2 * n_proj, chunk), BF16)] * nz + [shape((ROWS, chunk), BF16)] * nz,
        in_specs=[_smem(), _smem(), _vmem(), _vmem(), pl.BlockSpec(memory_space=pl.ANY), _vmem(), _vmem()],
        out_specs=[_vmem()] * (2 * nz),
        scratch_shapes=[pltpu.VMEM((n_part, ROWS, length), F32), pltpu.SemaphoreType.DMA((n_part,))],
        compiler_params=_params(8),
        name="pack",
    )(ctf_class, orient_subset, particles, orient_prior, ctf_curves, noise, projections)
    banks, parts = packed[:nz], packed[nz:]

    def swap_plane(value, s):
        pairs = [(b, ((b // ny) ^ s) * ny + b % ny) for b in range(nb)]
        return lax.ppermute(value, "blk", pairs)

    def swap_inner(value, r):
        return lax.ppermute(value, "blk", [(b, b // ny * ny + ((b % ny) ^ r)) for b in range(nb)])

    def swap_group(value, r):
        return lax.ppermute(value, "grp", [(g, g ^ r) for g in range(ng)])

    parts = [parts[0]] + [swap_plane(parts[s], s) for s in range(1, nz)]
    banks = [banks[0]] + [swap_plane(banks[s], s) for s in range(1, nz)]
    part = jnp.concatenate(parts, axis=0)
    part_all = [part] + [swap_group(part, r) for r in range(1, ng)]
    bank_all = [
        banks[s] if r == 0 else swap_inner(banks[s], r) for s in range(nz) for r in range(ny)
    ]

    cos_part, sin_part, square = pl.pallas_call(
        functools.partial(table_kernel, nz, ny, chunk),
        out_shape=[shape((shifts, chunk), F32)] * 2 + [shape((classes_count, chunk), F32)],
        in_specs=[_smem(), _vmem(), _vmem(), _vmem()],
        out_specs=[_vmem()] * 3,
        scratch_shapes=[pltpu.VMEM((shifts, chunk), F32)],
        compiler_params=_params(8),
        cost_estimate=pl.CostEstimate(flops=4_000_000, bytes_accessed=2_000_000, transcendentals=0),
        name="tables",
    )(trans_index, ctf_curves, noise, shift_phase)

    count = nz * ng * n_part
    total = nb * n_proj
    outs = pl.pallas_call(
        functools.partial(score_kernel, nz, ny, ng, n_part, tail, subsets),
        out_shape=[shape((ng * n_part, shifts * total), F32)] * nz,
        in_specs=[_vmem()] * (3 + nb + ng),
        out_specs=[_vmem()] * nz,
        scratch_shapes=[
            pltpu.VMEM((total, chunk), F32),
            pltpu.VMEM((total, chunk), F32),
            pltpu.VMEM((shifts * total, 2 * chunk), BF16),
        ],
        compiler_params=_params(32),
        cost_estimate=pl.CostEstimate(
            flops=4 * count * total * shifts * chunk, bytes_accessed=4_000_000, transcendentals=0
        ),
        name="score",
    )(cos_part, sin_part, square, *bank_all, *part_all)
    terms = [outs[0]] + [swap_plane(outs[s], s) for s in range(1, nz)]
    scores = pl.pallas_call(
        functools.partial(sum_kernel, total),
        out_shape=shape((shifts, ng * n_part, total), F32),
        in_specs=[_vmem()] * nz,
        out_specs=_vmem(),
        compiler_params=_params(4),
        name="sum",
    )(*terms)
    return scores.transpose(1, 0, 2)


def solution(mesh):
    placed = (
        P(("blk", "grp"), None, None),
        P(("blk", "grp")),
        P(("blk", "grp"), None),
        P(),
        P(),
        P(),
        P(),
        P(("grp", "blk"), None, None),
        P(("grp", "blk")),
    )
    return jax.shard_map(
        per_device, mesh=mesh, in_specs=placed, out_specs=P("blk", None, "grp"), check_vma=False
    )
```

```python
import functools

import jax
import jax.numpy as jnp
from jax import lax
from jax.experimental import pallas as pl
from jax.experimental.pallas import tpu as pltpu
from jax.sharding import PartitionSpec as P

F32 = jnp.float32
BF16 = jnp.bfloat16
HIGHEST = lax.Precision.HIGHEST
NT_DIMS = (((1,), (1,)), ((), ()))
MIB = 1 << 20
ROWS = 8


def _vmem():
    return pl.BlockSpec(memory_space=pltpu.VMEM)


def _smem():
    return pl.BlockSpec(memory_space=pltpu.SMEM)


def _params(mib):
    return pltpu.CompilerParams(vmem_limit_bytes=mib * MIB)


def pack_kernel(
    half,
    chunk,
    class_hbm,
    subset_hbm,
    particles_hbm,
    prior_hbm,
    curves_hbm,
    noise_hbm,
    proj_hbm,
    bank_keep,
    part_keep,
    send,
    class_ref,
    subset_ref,
    particles_ref,
    prior_ref,
    curves_ref,
    noise_ref,
    proj_ref,
    sems,
):
    pairs = [
        (proj_hbm, proj_ref),
        (subset_hbm, subset_ref),
        (class_hbm, class_ref),
        (curves_hbm, curves_ref),
        (particles_hbm, particles_ref),
        (noise_hbm, noise_ref),
        (prior_hbm, prior_ref),
    ]
    copies = [pltpu.make_async_copy(a, b, sems.at[n]) for n, (a, b) in enumerate(pairs)]
    for copy in copies:
        copy.start()
    n_part, n_proj = particles_ref.shape[0], proj_ref.shape[0]
    length = proj_ref.shape[2]
    mine = lax.axis_index("blk") // half

    def piece(values, c):
        width = min(chunk, length - c * chunk)
        values = values[:, c * chunk : c * chunk + width]
        if width < chunk:
            values = jnp.concatenate(
                [values, jnp.zeros((values.shape[0], chunk - width), values.dtype)], axis=1
            )
        return values

    row8 = lax.broadcasted_iota(jnp.int32, (ROWS, chunk), 0)
    lane8 = lax.broadcasted_iota(jnp.int32, (ROWS, chunk), 1)
    for copy in copies[:2]:
        copy.wait()
    for c in range(2):
        real = jnp.zeros((ROWS, chunk), F32)
        imag = jnp.zeros((ROWS, chunk), F32)
        for j in range(n_proj):
            both = piece(proj_ref[j].astype(F32), c)
            real = jnp.where(row8 == j, both[0:1], real)
            imag = jnp.where(row8 == j, both[1:2], imag)
        if c == 1:
            for j in range(n_proj):
                place = (row8 == j) & (lane8 == length - chunk)
                real = jnp.where(place, subset_ref[j].astype(F32), real)
        bank = jnp.concatenate([real, imag], axis=0).astype(BF16)

        @pl.when(mine == c)
        def _():
            bank_keep[...] = bank

        @pl.when(mine != c)
        def _():
            send[: 2 * n_proj] = bank

    for copy in copies[2:]:
        copy.wait()
    subsets = prior_ref.shape[1]
    prior = prior_ref[...].astype(F32)
    prior = jnp.concatenate([prior, jnp.zeros((n_part, chunk - subsets), F32)], axis=1)
    weighted = []
    for i in range(n_part):
        curve = curves_ref[pl.ds(class_ref[i], 1), :] * noise_ref[...]
        weighted.append(particles_ref[i].astype(F32) * curve)
    for c in range(2):
        rows = jnp.zeros((ROWS, chunk), F32)
        for i in range(n_part):
            both = piece(weighted[i], c)
            rows = jnp.where(row8 == i, both[0:1], rows)
            rows = jnp.where(row8 == n_part + i, both[1:2], rows)
            extra = jnp.where(
                lane8 == subsets, class_ref[i].astype(F32), jnp.broadcast_to(prior[i : i + 1], rows.shape)
            )
            rows = jnp.where(row8 == 2 * n_part + i, extra, rows)
        part = rows.astype(BF16)

        @pl.when(mine == c)
        def _():
            part_keep[...] = part

        @pl.when(mine != c)
        def _():
            send[2 * n_proj :] = part


def table_kernel(
    half, chunk, trans_ref, curves_ref, noise_ref, phase_ref, cos_ref, sin_ref, square_ref, angle
):
    mine = lax.axis_index("blk") // half
    length = curves_ref.shape[1]
    angle[...] = jnp.zeros_like(angle)
    square_ref[...] = jnp.zeros_like(square_ref)
    for c in range(2):
        width = min(chunk, length - c * chunk)
        span = slice(c * chunk, c * chunk + width)

        @pl.when(mine == c)
        def _():
            for t in range(phase_ref.shape[0]):
                angle[t : t + 1, :width] = phase_ref[pl.ds(trans_ref[t], 1), span]
            curve = curves_ref[:, span]
            square_ref[:, :width] = curve * curve * noise_ref[:, span]

    cos_ref[...] = jnp.cos(angle[...])
    sin_ref[...] = jnp.sin(angle[...])


def score_kernel(half, offsets, groups, n_part, tail, subsets, cos_ref, sin_ref, square_ref, *rest):
    n_bank, n_held = len(offsets), len(groups)
    banks, parts, outs = rest[:n_bank], rest[n_bank : n_bank + n_held], rest[n_bank + n_held :][:2]
    real_ref, imag_ref, shifted_ref = rest[n_bank + n_held + 2 :]
    blk, g = lax.axis_index("blk"), lax.axis_index("grp")
    ng = sum(len(group) for group in groups)
    total, chunk = real_ref.shape
    n_proj = total // (2 * half)
    shifts = cos_ref.shape[0]
    classes_count = square_ref.shape[0]

    for bank, offs in zip(banks, offsets):
        for n, offset in enumerate(offs):
            both = bank[2 * n_proj * n : 2 * n_proj * (n + 1)].astype(F32)
            where = pl.multiple_of((blk ^ offset) * n_proj, n_proj)
            real_ref[pl.ds(where, n_proj), :] = both[:n_proj]
            imag_ref[pl.ds(where, n_proj), :] = both[n_proj:]
    real, imag = real_ref[...], imag_ref[...]

    held = jnp.concatenate([part[...] for part in parts], axis=0)
    count = 2 * ng * n_part
    out_row = lax.broadcasted_iota(jnp.int32, (3 * count, held.shape[0]), 0)
    in_row = lax.broadcasted_iota(jnp.int32, (3 * count, held.shape[0]), 1)
    kind, rest_row = out_row // count, out_row % count
    slot, rest_row = rest_row // (ng * n_part), rest_row % (ng * n_part)
    group, i = rest_row // n_part, rest_row % n_part
    source = (group ^ g) * (2 * ROWS) + slot * ROWS + kind * n_part + i
    pick = (in_row == source).astype(F32).astype(BF16)
    ordered = jnp.dot(pick, held, preferred_element_type=F32)
    weighted = jnp.concatenate([ordered[:count], ordered[count : 2 * count]], axis=1).astype(BF16)
    extra = ordered[2 * count :]

    for t in range(shifts):
        cos_part, sin_part = cos_ref[t : t + 1, :], sin_ref[t : t + 1, :]
        rows = slice(t * total, (t + 1) * total)
        shifted_ref[rows, :chunk] = (cos_part * real + sin_part * imag).astype(BF16)
        shifted_ref[rows, chunk:] = (cos_part * imag - sin_part * real).astype(BF16)
    cross = lax.dot_general(weighted, shifted_ref[...], NT_DIMS, preferred_element_type=F32)

    power = real * real + imag * imag
    norm_table = lax.dot_general(
        square_ref[...], power, NT_DIMS, precision=HIGHEST, preferred_element_type=F32
    )
    class_col = lax.broadcasted_iota(jnp.int32, (count, classes_count), 1).astype(F32)
    onehot = (class_col == extra[:, subsets : subsets + 1]).astype(F32)
    norm = jnp.dot(onehot, norm_table, precision=HIGHEST, preferred_element_type=F32)
    subset_col = lax.broadcasted_iota(jnp.int32, (total, subsets), 1).astype(F32)
    subset_hot = (subset_col == real[:, tail : tail + 1]).astype(F32).astype(BF16)
    prior = lax.dot_general(
        extra[:, :subsets].astype(BF16), subset_hot, NT_DIMS, preferred_element_type=F32
    )
    added = jnp.where(blk // half == 1, prior, jnp.zeros_like(prior)) - 0.5 * norm
    added = jnp.concatenate([added] * shifts, axis=1)
    result = cross + added
    dest = ng * n_part
    for s in range(2):
        outs[s][...] = result[s * dest : (s + 1) * dest]


def sum_kernel(n_proj, *refs):
    *terms, out_ref = refs
    total = terms[0][...]
    for term in terms[1:]:
        total = total + term[...]
    for t in range(out_ref.shape[0]):
        out_ref[t] = total[:, t * n_proj : (t + 1) * n_proj]


def per_device(
    particles,
    ctf_class,
    orient_prior,
    ctf_curves,
    noise_weight,
    shift_phase,
    trans_index,
    projections,
    orient_subset,
):
    nb, ng = lax.axis_size("blk"), lax.axis_size("grp")
    half = nb // 2
    n_part, n_proj = particles.shape[0], projections.shape[0]
    length = particles.shape[2]
    shifts = shift_phase.shape[0]
    classes_count = ctf_curves.shape[0]
    subsets = orient_prior.shape[1]
    chunk = 128 * -(-length // 256)
    tail = length - chunk
    noise = noise_weight.reshape(1, length)
    shape = jax.ShapeDtypeStruct

    bank_keep, part_keep, send = pl.pallas_call(
        functools.partial(pack_kernel, half, chunk),
        out_shape=[
            shape((2 * n_proj, chunk), BF16),
            shape((ROWS, chunk), BF16),
            shape((2 * n_proj + ROWS, chunk), BF16),
        ],
        in_specs=[pl.BlockSpec(memory_space=pl.ANY)] * 7,
        out_specs=[_vmem()] * 3,
        scratch_shapes=[
            pltpu.SMEM(ctf_class.shape, jnp.int32),
            pltpu.SMEM(orient_subset.shape, jnp.int32),
            pltpu.VMEM(particles.shape, BF16),
            pltpu.VMEM(orient_prior.shape, BF16),
            pltpu.VMEM(ctf_curves.shape, F32),
            pltpu.VMEM(noise.shape, F32),
            pltpu.VMEM(projections.shape, BF16),
            pltpu.SemaphoreType.DMA((7,)),
        ],
        compiler_params=_params(56),
        name="pack",
    )(ctf_class, orient_subset, particles, orient_prior, ctf_curves, noise, projections)

    def swap(value, axis, bit):
        size = lax.axis_size(axis)
        return lax.ppermute(value, axis, [(i, i ^ bit) for i in range(size)])

    def doubled(first, axis, bits, offsets):
        pieces, held = [first], [offsets]
        for bit in bits:
            whole = pieces[0] if len(pieces) == 1 else jnp.concatenate(pieces, axis=0)
            all_offsets = [offset for offs in held for offset in offs]
            pieces, held = [whole], [all_offsets]
            pieces.append(swap(whole, axis, bit))
            held.append([offset ^ bit for offset in all_offsets])
        return pieces, held

    recv = swap(send, "blk", half)
    bank = jnp.concatenate([bank_keep, recv[: 2 * n_proj]], axis=0)
    part = jnp.concatenate([part_keep, recv[2 * n_proj :]], axis=0)
    blk_bits = [1 << n for n in range(half.bit_length() - 2, -1, -1)]
    grp_bits = [1 << n for n in range(ng.bit_length() - 1)]
    banks, offsets = doubled(bank, "blk", blk_bits, [0, half])
    parts, groups = doubled(part, "grp", grp_bits, [0])

    cos_part, sin_part, square = pl.pallas_call(
        functools.partial(table_kernel, half, chunk),
        out_shape=[shape((shifts, chunk), F32)] * 2 + [shape((classes_count, chunk), F32)],
        in_specs=[_smem(), _vmem(), _vmem(), _vmem()],
        out_specs=[_vmem()] * 3,
        scratch_shapes=[pltpu.VMEM((shifts, chunk), F32)],
        compiler_params=_params(8),
        cost_estimate=pl.CostEstimate(flops=4_000_000, bytes_accessed=2_000_000, transcendentals=0),
        name="tables",
    )(trans_index, ctf_curves, noise, shift_phase)

    count = 2 * ng * n_part
    total = nb * n_proj
    keep, give = pl.pallas_call(
        functools.partial(score_kernel, half, offsets, groups, n_part, tail, subsets),
        out_shape=[shape((ng * n_part, shifts * total), F32)] * 2,
        in_specs=[_vmem()] * (3 + len(banks) + len(parts)),
        out_specs=[_vmem()] * 2,
        scratch_shapes=[
            pltpu.VMEM((total, chunk), F32),
            pltpu.VMEM((total, chunk), F32),
            pltpu.VMEM((shifts * total, 2 * chunk), BF16),
        ],
        compiler_params=_params(40),
        cost_estimate=pl.CostEstimate(
            flops=4 * count * total * shifts * chunk, bytes_accessed=4_000_000, transcendentals=0
        ),
        name="score",
    )(cos_part, sin_part, square, *banks, *parts)
    scores = pl.pallas_call(
        functools.partial(sum_kernel, total),
        out_shape=shape((shifts, ng * n_part, total), F32),
        in_specs=[_vmem()] * 2,
        out_specs=_vmem(),
        compiler_params=_params(4),
        name="sum",
    )(keep, swap(give, "blk", half))
    return scores.transpose(1, 0, 2)


def solution(mesh):
    placed = (
        P(("blk", "grp"), None, None),
        P(("blk", "grp")),
        P(("blk", "grp"), None),
        P(),
        P(),
        P(),
        P(),
        P(("grp", "blk"), None, None),
        P(("grp", "blk")),
    )
    return jax.shard_map(
        per_device, mesh=mesh, in_specs=placed, out_specs=P("blk", None, "grp"), check_vma=False
    )
```

```python
import functools

import jax
import jax.numpy as jnp
from jax import lax
from jax.experimental import pallas as pl
from jax.experimental.pallas import tpu as pltpu
from jax.sharding import PartitionSpec as P

F32 = jnp.float32
BF16 = jnp.bfloat16
HIGHEST = lax.Precision.HIGHEST
NT_DIMS = (((1,), (1,)), ((), ()))
MIB = 1 << 20


def _vmem():
    return pl.BlockSpec(memory_space=pltpu.VMEM)


def _smem():
    return pl.BlockSpec(memory_space=pltpu.SMEM)


def _params(mib):
    return pltpu.CompilerParams(vmem_limit_bytes=mib * MIB)


def pack_kernel(
    class_hbm,
    subset_hbm,
    particles_hbm,
    prior_hbm,
    curves_hbm,
    noise_hbm,
    proj_hbm,
    bank_ref,
    part_ref,
    class_ref,
    subset_ref,
    particles_ref,
    prior_ref,
    curves_ref,
    noise_ref,
    proj_ref,
    sems,
):
    pairs = [
        (proj_hbm, proj_ref),
        (subset_hbm, subset_ref),
        (class_hbm, class_ref),
        (curves_hbm, curves_ref),
        (particles_hbm, particles_ref),
        (noise_hbm, noise_ref),
        (prior_hbm, prior_ref),
    ]
    copies = [pltpu.make_async_copy(a, b, sems.at[n]) for n, (a, b) in enumerate(pairs)]
    for copy in copies:
        copy.start()
    n_part, n_proj = particles_ref.shape[0], proj_ref.shape[0]
    length = proj_ref.shape[2]
    wide = bank_ref.shape[1]

    def padded(values, width):
        zeros = jnp.zeros((values.shape[0], width - values.shape[1]), values.dtype)
        return jnp.concatenate([values, zeros], axis=1)

    row = lax.broadcasted_iota(jnp.int32, (n_proj, wide), 0)
    lane = lax.broadcasted_iota(jnp.int32, (n_proj, wide), 1)
    for copy in copies[:2]:
        copy.wait()
    real = jnp.zeros((n_proj, wide), F32)
    imag = jnp.zeros((n_proj, wide), F32)
    for j in range(n_proj):
        both = padded(proj_ref[j].astype(F32), wide)
        real = jnp.where(row == j, both[0:1], real)
        imag = jnp.where(row == j, both[1:2], imag)
    for j in range(n_proj):
        real = jnp.where((row == j) & (lane == length), subset_ref[j].astype(F32), real)
    bank_ref[...] = jnp.concatenate([real, imag], axis=0).astype(BF16)

    for copy in copies[2:]:
        copy.wait()
    subsets = prior_ref.shape[1]
    extra = part_ref.shape[1] - wide
    row = lax.broadcasted_iota(jnp.int32, (2 * n_part, wide), 0)
    row_extra = lax.broadcasted_iota(jnp.int32, (2 * n_part, extra), 0)
    lane_extra = lax.broadcasted_iota(jnp.int32, (2 * n_part, extra), 1)
    prior = padded(prior_ref[...].astype(F32), extra)
    rows = jnp.zeros((2 * n_part, wide), F32)
    rows_extra = jnp.zeros((2 * n_part, extra), F32)
    for i in range(n_part):
        curve = curves_ref[pl.ds(class_ref[i], 1), :] * noise_ref[...]
        both = padded(particles_ref[i].astype(F32) * curve, wide)
        rows = jnp.where(row == i, both[0:1], rows)
        rows = jnp.where(row == n_part + i, both[1:2], rows)
        small = jnp.where(
            lane_extra == subsets,
            class_ref[i].astype(F32),
            jnp.broadcast_to(prior[i : i + 1], rows_extra.shape),
        )
        rows_extra = jnp.where(row_extra == i, small, rows_extra)
    part_ref[:, :wide] = rows.astype(BF16)
    part_ref[:, wide:] = rows_extra.astype(BF16)


def sine_cosine(x):
    turns = jnp.floor(x * 0.6366197723675814 + 0.5)
    r = ((x - turns * 1.5703125) - turns * 4.837512969970703125e-4) - turns * 7.549789954891882e-8
    z = r * r
    sine = r + r * z * (-1.6666654611e-1 + z * (8.3321608736e-3 - z * 1.9515295891e-4))
    cosine = 1.0 - 0.5 * z + z * z * (
        4.166664568298827e-2 + z * (-1.388731625493765e-3 + z * 2.443315711809948e-5)
    )
    quarter = turns.astype(jnp.int32) & 3
    swapped = (quarter & 1) == 1
    first, second = jnp.where(swapped, cosine, sine), jnp.where(swapped, sine, cosine)
    first = jnp.where(quarter >= 2, -first, first)
    second = jnp.where((quarter == 1) | (quarter == 2), -second, second)
    return first, second


def split_terms(values):
    high = values.astype(BF16)
    low = (values - high.astype(F32)).astype(BF16)
    return jnp.concatenate([high, low], axis=0)


def table_kernel(trans_ref, curves_ref, noise_ref, phase_ref, cos_ref, sin_ref, square_ref, angle):
    length = curves_ref.shape[1]
    wide = cos_ref.shape[1]
    for t in range(phase_ref.shape[0]):
        angle[t : t + 1, :] = phase_ref[pl.ds(trans_ref[t], 1), :]
    zeros = jnp.zeros((cos_ref.shape[0], wide - length), F32)
    sine, cosine = sine_cosine(angle[...])
    cos_ref[...] = jnp.concatenate([cosine, zeros], axis=1)
    sin_ref[...] = jnp.concatenate([sine, zeros], axis=1)
    curve = curves_ref[...]
    square = split_terms(curve * curve * noise_ref[...])
    square_ref[...] = jnp.concatenate(
        [square, jnp.zeros((square.shape[0], wide - length), BF16)], axis=1
    )


def score_kernel(
    half, offsets, n_parts, bits, n_part, n_proj, length, subsets, cos_ref, sin_ref, square_ref, *rest
):
    n_bank = len(offsets)
    banks, parts, outs = rest[:n_bank], rest[n_bank : n_bank + n_parts], rest[n_bank + n_parts :][:2]
    real_ref, imag_ref, shifted_ref = rest[n_bank + n_parts + 2 :]
    blk, g = lax.axis_index("blk"), lax.axis_index("grp")
    ng = 1 << len(bits)
    total, wide = real_ref.shape
    shifts = cos_ref.shape[0]
    classes_count = square_ref.shape[0] // 2

    for bank, offs in zip(banks, offsets):
        for n, offset in enumerate(offs):
            both = bank[2 * n_proj * n : 2 * n_proj * (n + 1)].astype(F32)
            where = pl.multiple_of((blk % half ^ offset) * n_proj, n_proj)
            real_ref[pl.ds(where, n_proj), :] = both[:n_proj]
            imag_ref[pl.ds(where, n_proj), :] = both[n_proj:]
    real, imag = real_ref[...], imag_ref[...]

    held = jnp.concatenate([part[...] for part in parts], axis=0)
    count = 2 * ng * n_part
    out_row = lax.broadcasted_iota(jnp.int32, (2 * count, held.shape[0]), 0)
    in_row = lax.broadcasted_iota(jnp.int32, (2 * count, held.shape[0]), 1)
    kind, rest_row = out_row // count, out_row % count
    source, rest_row = rest_row // (ng * n_part), rest_row % (ng * n_part)
    away, i = rest_row // n_part ^ g, rest_row % n_part
    for n, bit in enumerate(bits):
        source += jnp.where(away & bit != 0, 2 << n, 0)
    pick = (in_row == source * (2 * n_part) + kind * n_part + i).astype(F32).astype(BF16)
    ordered = jnp.dot(pick, held, preferred_element_type=F32)
    weighted = jnp.concatenate([ordered[:count, :wide], ordered[count:, :wide]], axis=1).astype(BF16)
    prior_rows = ordered[:count, wide : wide + subsets].astype(BF16)
    class_rows = ordered[:count, wide + subsets : wide + subsets + 1]

    for t in range(shifts):
        cos_part, sin_part = cos_ref[t : t + 1, :], sin_ref[t : t + 1, :]
        rows = slice(t * total, (t + 1) * total)
        shifted_ref[rows, :wide] = (cos_part * real + sin_part * imag).astype(BF16)
        shifted_ref[rows, wide:] = (cos_part * imag - sin_part * real).astype(BF16)
    cross = lax.dot_general(weighted, shifted_ref[...], NT_DIMS, preferred_element_type=F32)

    power = split_terms(real * real + imag * imag)
    table = lax.dot_general(square_ref[...], power, NT_DIMS, preferred_element_type=F32)
    table = table[:classes_count, total:] + table[classes_count:, :total] + table[:classes_count, :total]
    class_col = lax.broadcasted_iota(jnp.int32, (count, classes_count), 1).astype(F32)
    onehot = (class_col == class_rows).astype(F32)
    norm = jnp.dot(onehot, table, precision=HIGHEST, preferred_element_type=F32)
    subset_col = lax.broadcasted_iota(jnp.int32, (total, subsets), 1).astype(F32)
    subset_hot = (subset_col == real[:, length : length + 1]).astype(F32).astype(BF16)
    prior = lax.dot_general(prior_rows, subset_hot, NT_DIMS, preferred_element_type=F32)
    result = cross + jnp.concatenate([prior - 0.5 * norm] * shifts, axis=1)
    dest = ng * n_part
    for s in range(2):
        outs[s][...] = result[s * dest : (s + 1) * dest]


def place_kernel(half, keep_ref, recv_ref, out_ref):
    first = lax.axis_index("blk") < half
    low = jnp.where(first, keep_ref[...], recv_ref[...])
    high = jnp.where(first, recv_ref[...], keep_ref[...])
    shifts, _, width = out_ref.shape
    width = width // 2
    for t in range(shifts):
        span = slice(t * width, (t + 1) * width)
        out_ref[t] = jnp.concatenate([low[:, span], high[:, span]], axis=1)


def per_device(
    particles,
    ctf_class,
    orient_prior,
    ctf_curves,
    noise_weight,
    shift_phase,
    trans_index,
    projections,
    orient_subset,
):
    nb, ng = lax.axis_size("blk"), lax.axis_size("grp")
    half = nb // 2
    n_part, n_proj = particles.shape[0], projections.shape[0]
    length = particles.shape[2]
    shifts = shift_phase.shape[0]
    classes_count = ctf_curves.shape[0]
    subsets = orient_prior.shape[1]
    wide = 128 * (length // 128 + 1)
    extra = 128 * (subsets // 128 + 1)
    noise = noise_weight.reshape(1, length)
    shape = jax.ShapeDtypeStruct

    bank, part = pl.pallas_call(
        pack_kernel,
        out_shape=[shape((2 * n_proj, wide), BF16), shape((2 * n_part, wide + extra), BF16)],
        in_specs=[pl.BlockSpec(memory_space=pl.ANY)] * 7,
        out_specs=[_vmem()] * 2,
        scratch_shapes=[
            pltpu.SMEM(ctf_class.shape, jnp.int32),
            pltpu.SMEM(orient_subset.shape, jnp.int32),
            pltpu.VMEM(particles.shape, BF16),
            pltpu.VMEM(orient_prior.shape, BF16),
            pltpu.VMEM(ctf_curves.shape, F32),
            pltpu.VMEM(noise.shape, F32),
            pltpu.VMEM(projections.shape, BF16),
            pltpu.SemaphoreType.DMA((7,)),
        ],
        compiler_params=_params(56),
        name="pack",
    )(ctf_class, orient_subset, particles, orient_prior, ctf_curves, noise, projections)

    def swap(value, axis, bit):
        size = lax.axis_size(axis)
        return lax.ppermute(value, axis, [(i, i ^ bit) for i in range(size)])

    def doubled(pieces, offsets, axis, bits):
        held = offsets
        for bit in bits:
            whole = pieces[0] if len(pieces) == 1 else jnp.concatenate(pieces, axis=0)
            all_offsets = [offset for offs in held for offset in offs]
            pieces = [whole, swap(whole, axis, bit)]
            held = [all_offsets, [offset ^ bit for offset in all_offsets]]
        return pieces, held

    blk_bits = [1 << n for n in range(half.bit_length() - 2, -1, -1)]
    grp_bits = [1 << n for n in range(ng.bit_length() - 2, -1, -1)]
    banks, offsets = doubled([bank], [[0]], "blk", blk_bits)
    parts, _ = doubled([part, swap(part, "blk", half)], [[0], [0]], "grp", grp_bits)

    cos_part, sin_part, square = pl.pallas_call(
        table_kernel,
        out_shape=[shape((shifts, wide), F32)] * 2 + [shape((2 * classes_count, wide), BF16)],
        in_specs=[_smem(), _vmem(), _vmem(), _vmem()],
        out_specs=[_vmem()] * 3,
        scratch_shapes=[pltpu.VMEM((shifts, length), F32)],
        compiler_params=_params(8),
        cost_estimate=pl.CostEstimate(flops=4_000_000, bytes_accessed=2_000_000, transcendentals=0),
        name="tables",
    )(trans_index, ctf_curves, noise, shift_phase)

    count = 2 * ng * n_part
    total = half * n_proj
    keep, give = pl.pallas_call(
        functools.partial(
            score_kernel, half, offsets, len(parts), grp_bits, n_part, n_proj, length, subsets
        ),
        out_shape=[shape((ng * n_part, shifts * total), F32)] * 2,
        in_specs=[_vmem()] * (3 + len(banks) + len(parts)),
        out_specs=[_vmem()] * 2,
        scratch_shapes=[
            pltpu.VMEM((total, wide), F32),
            pltpu.VMEM((total, wide), F32),
            pltpu.VMEM((shifts * total, 2 * wide), BF16),
        ],
        compiler_params=_params(44),
        cost_estimate=pl.CostEstimate(
            flops=4 * count * total * shifts * wide, bytes_accessed=4_000_000, transcendentals=0
        ),
        name="score",
    )(cos_part, sin_part, square, *banks, *parts)
    scores = pl.pallas_call(
        functools.partial(place_kernel, half),
        out_shape=shape((shifts, ng * n_part, 2 * total), F32),
        in_specs=[_vmem()] * 2,
        out_specs=_vmem(),
        compiler_params=_params(4),
        name="place",
    )(keep, swap(give, "blk", half))
    return scores.transpose(1, 0, 2)


def solution(mesh):
    placed = (
        P(("blk", "grp"), None, None),
        P(("blk", "grp")),
        P(("blk", "grp"), None),
        P(),
        P(),
        P(),
        P(),
        P(("grp", "blk"), None, None),
        P(("grp", "blk")),
    )
    return jax.shard_map(
        per_device, mesh=mesh, in_specs=placed, out_specs=P("blk", None, "grp"), check_vma=False
    )
```

```python
import functools

import jax
import jax.numpy as jnp
from jax import lax
from jax.experimental import pallas as pl
from jax.experimental.pallas import tpu as pltpu
from jax.sharding import PartitionSpec as P

F32 = jnp.float32
BF16 = jnp.bfloat16
HIGHEST = lax.Precision.HIGHEST
NT_DIMS = (((1,), (1,)), ((), ()))
MIB = 1 << 20


def _vmem():
    return pl.BlockSpec(memory_space=pltpu.VMEM)


def _smem():
    return pl.BlockSpec(memory_space=pltpu.SMEM)


def _params(mib):
    return pltpu.CompilerParams(vmem_limit_bytes=mib * MIB)


def pack_kernel(
    class_hbm,
    subset_hbm,
    particles_hbm,
    prior_hbm,
    curves_hbm,
    noise_hbm,
    proj_hbm,
    bank_ref,
    part_ref,
    class_ref,
    subset_ref,
    particles_ref,
    prior_ref,
    curves_ref,
    noise_ref,
    proj_ref,
    sems,
):
    pairs = [
        (proj_hbm, proj_ref),
        (subset_hbm, subset_ref),
        (class_hbm, class_ref),
        (curves_hbm, curves_ref),
        (particles_hbm, particles_ref),
        (noise_hbm, noise_ref),
        (prior_hbm, prior_ref),
    ]
    copies = [pltpu.make_async_copy(a, b, sems.at[n]) for n, (a, b) in enumerate(pairs)]
    for copy in copies:
        copy.start()
    n_part, n_proj = particles_ref.shape[0], proj_ref.shape[0]
    length = proj_ref.shape[2]
    wide = bank_ref.shape[1]

    def padded(values, width):
        zeros = jnp.zeros((values.shape[0], width - values.shape[1]), values.dtype)
        return jnp.concatenate([values, zeros], axis=1)

    row = lax.broadcasted_iota(jnp.int32, (n_proj, wide), 0)
    lane = lax.broadcasted_iota(jnp.int32, (n_proj, wide), 1)
    for copy in copies[:2]:
        copy.wait()
    real = jnp.zeros((n_proj, wide), F32)
    imag = jnp.zeros((n_proj, wide), F32)
    for j in range(n_proj):
        both = padded(proj_ref[j].astype(F32), wide)
        real = jnp.where(row == j, both[0:1], real)
        imag = jnp.where(row == j, both[1:2], imag)
    for j in range(n_proj):
        real = jnp.where((row == j) & (lane == length), subset_ref[j].astype(F32), real)
    bank_ref[...] = jnp.concatenate([real, imag], axis=0).astype(BF16)

    for copy in copies[2:]:
        copy.wait()
    subsets = prior_ref.shape[1]
    extra = part_ref.shape[1] - wide
    row = lax.broadcasted_iota(jnp.int32, (2 * n_part, wide), 0)
    row_extra = lax.broadcasted_iota(jnp.int32, (2 * n_part, extra), 0)
    lane_extra = lax.broadcasted_iota(jnp.int32, (2 * n_part, extra), 1)
    prior = padded(prior_ref[...].astype(F32), extra)
    rows = jnp.zeros((2 * n_part, wide), F32)
    rows_extra = jnp.zeros((2 * n_part, extra), F32)
    for i in range(n_part):
        curve = curves_ref[pl.ds(class_ref[i], 1), :] * noise_ref[...]
        both = padded(particles_ref[i].astype(F32) * curve, wide)
        rows = jnp.where(row == i, both[0:1], rows)
        rows = jnp.where(row == n_part + i, both[1:2], rows)
        small = jnp.where(
            lane_extra == subsets,
            class_ref[i].astype(F32),
            jnp.broadcast_to(prior[i : i + 1], rows_extra.shape),
        )
        rows_extra = jnp.where(row_extra == i, small, rows_extra)
    part_ref[:, :wide] = rows.astype(BF16)
    part_ref[:, wide:] = rows_extra.astype(BF16)


def sine_cosine(x):
    turns = jnp.floor(x * 0.6366197723675814 + 0.5)
    r = ((x - turns * 1.5703125) - turns * 4.837512969970703125e-4) - turns * 7.549789954891882e-8
    z = r * r
    sine = r + r * z * (-1.6666654611e-1 + z * (8.3321608736e-3 - z * 1.9515295891e-4))
    cosine = 1.0 - 0.5 * z + z * z * (
        4.166664568298827e-2 + z * (-1.388731625493765e-3 + z * 2.443315711809948e-5)
    )
    quarter = turns.astype(jnp.int32) & 3
    swapped = (quarter & 1) == 1
    first, second = jnp.where(swapped, cosine, sine), jnp.where(swapped, sine, cosine)
    first = jnp.where(quarter >= 2, -first, first)
    second = jnp.where((quarter == 1) | (quarter == 2), -second, second)
    return first, second


def split_terms(values):
    high = values.astype(BF16)
    low = (values - high.astype(F32)).astype(BF16)
    return jnp.concatenate([high, low], axis=0)


def table_kernel(trans_ref, curves_ref, noise_ref, phase_ref, cos_ref, sin_ref, square_ref, angle):
    length = curves_ref.shape[1]
    wide = cos_ref.shape[1]
    for t in range(phase_ref.shape[0]):
        angle[t : t + 1, :] = phase_ref[pl.ds(trans_ref[t], 1), :]
    zeros = jnp.zeros((cos_ref.shape[0], wide - length), F32)
    sine, cosine = sine_cosine(angle[...])
    cos_ref[...] = jnp.concatenate([cosine, zeros], axis=1)
    sin_ref[...] = jnp.concatenate([sine, zeros], axis=1)
    curve = curves_ref[...]
    square = split_terms(curve * curve * noise_ref[...])
    square_ref[...] = jnp.concatenate(
        [square, jnp.zeros((square.shape[0], wide - length), BF16)], axis=1
    )


def score_kernel(
    half, offsets, n_parts, ng, n_part, n_proj, length, subsets, cos_ref, sin_ref, square_ref, *rest
):
    n_bank = len(offsets)
    banks, parts, outs = rest[:n_bank], rest[n_bank : n_bank + n_parts], rest[n_bank + n_parts :][:2]
    real_ref, imag_ref, shifted_ref = rest[n_bank + n_parts + 2 :]
    blk = lax.axis_index("blk")
    total, wide = real_ref.shape
    shifts = cos_ref.shape[0]
    classes_count = square_ref.shape[0] // 2

    for bank, offs in zip(banks, offsets):
        for n, offset in enumerate(offs):
            both = bank[2 * n_proj * n : 2 * n_proj * (n + 1)].astype(F32)
            where = pl.multiple_of((blk % half ^ offset) * n_proj, n_proj)
            real_ref[pl.ds(where, n_proj), :] = both[:n_proj]
            imag_ref[pl.ds(where, n_proj), :] = both[n_proj:]
    real, imag = real_ref[...], imag_ref[...]

    held = jnp.concatenate([part[...] for part in parts], axis=0)
    count = 2 * ng * n_part
    out_row = lax.broadcasted_iota(jnp.int32, (2 * count, held.shape[0]), 0)
    in_row = lax.broadcasted_iota(jnp.int32, (2 * count, held.shape[0]), 1)
    kind, rest_row = out_row // count, out_row % count
    source, rest_row = rest_row // (ng * n_part) ^ blk // half, rest_row % (ng * n_part)
    source, i = source * ng + rest_row // n_part, rest_row % n_part
    pick = (in_row == source * (2 * n_part) + kind * n_part + i).astype(F32).astype(BF16)
    ordered = jnp.dot(pick, held, preferred_element_type=F32)
    weighted = jnp.concatenate([ordered[:count, :wide], ordered[count:, :wide]], axis=1).astype(BF16)
    prior_rows = ordered[:count, wide : wide + subsets].astype(BF16)
    class_rows = ordered[:count, wide + subsets : wide + subsets + 1]

    for t in range(shifts):
        cos_part, sin_part = cos_ref[t : t + 1, :], sin_ref[t : t + 1, :]
        rows = slice(t * total, (t + 1) * total)
        shifted_ref[rows, :wide] = (cos_part * real + sin_part * imag).astype(BF16)
        shifted_ref[rows, wide:] = (cos_part * imag - sin_part * real).astype(BF16)
    cross = lax.dot_general(weighted, shifted_ref[...], NT_DIMS, preferred_element_type=F32)

    power = split_terms(real * real + imag * imag)
    table = lax.dot_general(square_ref[...], power, NT_DIMS, preferred_element_type=F32)
    table = table[:classes_count, total:] + table[classes_count:, :total] + table[:classes_count, :total]
    class_col = lax.broadcasted_iota(jnp.int32, (count, classes_count), 1).astype(F32)
    onehot = (class_col == class_rows).astype(F32)
    norm = jnp.dot(onehot, table, precision=HIGHEST, preferred_element_type=F32)
    subset_col = lax.broadcasted_iota(jnp.int32, (total, subsets), 1).astype(F32)
    subset_hot = (subset_col == real[:, length : length + 1]).astype(F32).astype(BF16)
    prior = lax.dot_general(prior_rows, subset_hot, NT_DIMS, preferred_element_type=F32)
    result = cross + jnp.concatenate([prior - 0.5 * norm] * shifts, axis=1)
    dest = ng * n_part
    for s in range(2):
        outs[s][...] = result[s * dest : (s + 1) * dest]


def place_kernel(half, keep_ref, recv_ref, out_ref):
    first = lax.axis_index("blk") < half
    low = jnp.where(first, keep_ref[...], recv_ref[...])
    high = jnp.where(first, recv_ref[...], keep_ref[...])
    shifts, _, width = out_ref.shape
    width = width // 2
    for t in range(shifts):
        span = slice(t * width, (t + 1) * width)
        out_ref[t] = jnp.concatenate([low[:, span], high[:, span]], axis=1)


def per_device(
    particles,
    ctf_class,
    orient_prior,
    ctf_curves,
    noise_weight,
    shift_phase,
    trans_index,
    projections,
    orient_subset,
):
    nb, ng = lax.axis_size("blk"), lax.axis_size("grp")
    half = nb // 2
    n_part, n_proj = particles.shape[0], projections.shape[0]
    length = particles.shape[2]
    shifts = shift_phase.shape[0]
    classes_count = ctf_curves.shape[0]
    subsets = orient_prior.shape[1]
    wide = 128 * (length // 128 + 1)
    extra = 128 * (subsets // 128 + 1)
    noise = noise_weight.reshape(1, length)
    shape = jax.ShapeDtypeStruct

    bank, part = pl.pallas_call(
        pack_kernel,
        out_shape=[shape((2 * n_proj, wide), BF16), shape((2 * n_part, wide + extra), BF16)],
        in_specs=[pl.BlockSpec(memory_space=pltpu.HBM)] * 7,
        out_specs=[_vmem()] * 2,
        scratch_shapes=[
            pltpu.SMEM(ctf_class.shape, jnp.int32),
            pltpu.SMEM(orient_subset.shape, jnp.int32),
            pltpu.VMEM(particles.shape, BF16),
            pltpu.VMEM(orient_prior.shape, BF16),
            pltpu.VMEM(ctf_curves.shape, F32),
            pltpu.VMEM(noise.shape, F32),
            pltpu.VMEM(projections.shape, BF16),
            pltpu.SemaphoreType.DMA((7,)),
        ],
        compiler_params=_params(16),
        name="pack",
    )(ctf_class, orient_subset, particles, orient_prior, ctf_curves, noise, projections)

    def swap(value, axis, bit):
        size = lax.axis_size(axis)
        return lax.ppermute(value, axis, [(i, i ^ bit) for i in range(size)])

    def doubled(pieces, offsets, axis, bits):
        held = offsets
        for bit in bits:
            whole = pieces[0] if len(pieces) == 1 else jnp.concatenate(pieces, axis=0)
            all_offsets = [offset for offs in held for offset in offs]
            pieces = [whole, swap(whole, axis, bit)]
            held = [all_offsets, [offset ^ bit for offset in all_offsets]]
        return pieces, held

    blk_bits = [1 << n for n in range(half.bit_length() - 2, -1, -1)]
    banks, offsets = doubled([bank], [[0]], "blk", blk_bits)
    members = [
        [b * ng + g for b in (low, low + half) for g in range(ng)] for low in range(half)
    ]
    parts = [
        lax.all_gather(part, ("blk", "grp"), axis_index_groups=members, axis=0, tiled=True)
    ]

    cos_part, sin_part, square = pl.pallas_call(
        table_kernel,
        out_shape=[shape((shifts, wide), F32)] * 2 + [shape((2 * classes_count, wide), BF16)],
        in_specs=[_smem(), _vmem(), _vmem(), _vmem()],
        out_specs=[_vmem()] * 3,
        scratch_shapes=[pltpu.VMEM((shifts, length), F32)],
        compiler_params=_params(8),
        cost_estimate=pl.CostEstimate(flops=4_000_000, bytes_accessed=2_000_000, transcendentals=0),
        name="tables",
    )(trans_index, ctf_curves, noise, shift_phase)

    count = 2 * ng * n_part
    total = half * n_proj
    keep, give = pl.pallas_call(
        functools.partial(
            score_kernel, half, offsets, len(parts), ng, n_part, n_proj, length, subsets
        ),
        out_shape=[shape((ng * n_part, shifts * total), F32)] * 2,
        in_specs=[_vmem()] * (3 + len(banks) + len(parts)),
        out_specs=[_vmem()] * 2,
        scratch_shapes=[
            pltpu.VMEM((total, wide), F32),
            pltpu.VMEM((total, wide), F32),
            pltpu.VMEM((shifts * total, 2 * wide), BF16),
        ],
        compiler_params=_params(44),
        cost_estimate=pl.CostEstimate(
            flops=4 * count * total * shifts * wide, bytes_accessed=4_000_000, transcendentals=0
        ),
        name="score",
    )(cos_part, sin_part, square, *banks, *parts)
    scores = pl.pallas_call(
        functools.partial(place_kernel, half),
        out_shape=shape((shifts, ng * n_part, 2 * total), F32),
        in_specs=[_vmem()] * 2,
        out_specs=_vmem(),
        compiler_params=_params(4),
        name="place",
    )(keep, swap(give, "blk", half))
    return scores.transpose(1, 0, 2)


def solution(mesh):
    placed = (
        P(("blk", "grp"), None, None),
        P(("blk", "grp")),
        P(("blk", "grp"), None),
        P(),
        P(),
        P(),
        P(),
        P(("grp", "blk"), None, None),
        P(("grp", "blk")),
    )
    return jax.shard_map(
        per_device, mesh=mesh, in_specs=placed, out_specs=P("blk", None, "grp"), check_vma=False
    )
```

```python
import functools

import jax
import jax.numpy as jnp
from jax import lax
from jax.experimental import pallas as pl
from jax.experimental.pallas import tpu as pltpu
from jax.sharding import PartitionSpec as P

F32 = jnp.float32
BF16 = jnp.bfloat16
HIGHEST = lax.Precision.HIGHEST
NT_DIMS = (((1,), (1,)), ((), ()))
MIB = 1 << 20


def _vmem():
    return pl.BlockSpec(memory_space=pltpu.VMEM)


def _params(mib):
    return pltpu.CompilerParams(vmem_limit_bytes=mib * MIB)


def pack_kernel(
    class_hbm,
    subset_hbm,
    particles_hbm,
    prior_hbm,
    curves_hbm,
    noise_hbm,
    proj_hbm,
    phase_hbm,
    trans_hbm,
    bank_ref,
    part_ref,
    curves_ref,
    noise_ref,
    angle_ref,
    class_ref,
    subset_ref,
    trans_ref,
    particles_ref,
    prior_ref,
    phase_ref,
    proj_ref,
    sems,
):
    pairs = [
        (proj_hbm, proj_ref),
        (subset_hbm, subset_ref),
        (class_hbm, class_ref),
        (curves_hbm, curves_ref),
        (particles_hbm, particles_ref),
        (noise_hbm, noise_ref),
        (prior_hbm, prior_ref),
        (trans_hbm, trans_ref),
        (phase_hbm, phase_ref),
    ]
    copies = [pltpu.make_async_copy(a, b, sems.at[n]) for n, (a, b) in enumerate(pairs)]
    for copy in copies:
        copy.start()
    n_part, n_proj = particles_ref.shape[0], proj_ref.shape[0]
    length = proj_ref.shape[2]
    wide = bank_ref.shape[1]

    def padded(values, width):
        zeros = jnp.zeros((values.shape[0], width - values.shape[1]), values.dtype)
        return jnp.concatenate([values, zeros], axis=1)

    row = lax.broadcasted_iota(jnp.int32, (n_proj, wide), 0)
    lane = lax.broadcasted_iota(jnp.int32, (n_proj, wide), 1)
    for copy in copies[:2]:
        copy.wait()
    real = jnp.zeros((n_proj, wide), F32)
    imag = jnp.zeros((n_proj, wide), F32)
    for j in range(n_proj):
        both = padded(proj_ref[j].astype(F32), wide)
        real = jnp.where(row == j, both[0:1], real)
        imag = jnp.where(row == j, both[1:2], imag)
    last = slice(wide - 128, wide)
    ends = real[:, last]
    for j in range(n_proj):
        here = (row[:, last] == j) & (lane[:, last] == length)
        ends = jnp.where(here, subset_ref[j].astype(F32), ends)
    real = jnp.concatenate([real[:, : wide - 128], ends], axis=1)
    bank_ref[...] = jnp.concatenate([real, imag], axis=0).astype(BF16)

    for copy in copies[2:]:
        copy.wait()
    subsets = prior_ref.shape[1]
    extra = part_ref.shape[1] - wide
    row = lax.broadcasted_iota(jnp.int32, (2 * n_part, wide), 0)
    row_extra = lax.broadcasted_iota(jnp.int32, (2 * n_part, extra), 0)
    lane_extra = lax.broadcasted_iota(jnp.int32, (2 * n_part, extra), 1)
    prior = padded(prior_ref[...].astype(F32), extra)
    rows = jnp.zeros((2 * n_part, wide), F32)
    rows_extra = jnp.zeros((2 * n_part, extra), F32)
    for i in range(n_part):
        curve = curves_ref[pl.ds(class_ref[i], 1), :] * noise_ref[...]
        both = padded(particles_ref[i].astype(F32) * curve, wide)
        rows = jnp.where(row == i, both[0:1], rows)
        rows = jnp.where(row == n_part + i, both[1:2], rows)
        small = jnp.where(
            lane_extra == subsets,
            class_ref[i].astype(F32),
            jnp.broadcast_to(prior[i : i + 1], rows_extra.shape),
        )
        rows_extra = jnp.where(row_extra == i, small, rows_extra)
    part_ref[:, :wide] = rows.astype(BF16)
    part_ref[:, wide:] = rows_extra.astype(BF16)
    for t in range(phase_ref.shape[0]):
        angle_ref[t : t + 1, :] = phase_ref[pl.ds(trans_ref[t], 1), :]


def sine_cosine(x):
    turns = jnp.floor(x * 0.6366197723675814 + 0.5)
    r = ((x - turns * 1.5703125) - turns * 4.837512969970703125e-4) - turns * 7.549789954891882e-8
    z = r * r
    sine = r + r * z * (-1.6666654611e-1 + z * (8.3321608736e-3 - z * 1.9515295891e-4))
    cosine = 1.0 - 0.5 * z + z * z * (
        4.166664568298827e-2 + z * (-1.388731625493765e-3 + z * 2.443315711809948e-5)
    )
    quarter = turns.astype(jnp.int32) & 3
    swapped = (quarter & 1) == 1
    first, second = jnp.where(swapped, cosine, sine), jnp.where(swapped, sine, cosine)
    first = jnp.where(quarter >= 2, -first, first)
    second = jnp.where((quarter == 1) | (quarter == 2), -second, second)
    return first, second


def split_terms(values):
    high = values.astype(BF16)
    low = (values - high.astype(F32)).astype(BF16)
    return jnp.concatenate([high, low], axis=0)


def table_kernel(curves_ref, noise_ref, angle_ref, cos_ref, sin_ref, square_ref):
    length = curves_ref.shape[1]
    wide = cos_ref.shape[1]
    zeros = jnp.zeros((cos_ref.shape[0], wide - length), F32)
    sine, cosine = sine_cosine(angle_ref[...])
    cos_ref[...] = jnp.concatenate([cosine, zeros], axis=1)
    sin_ref[...] = jnp.concatenate([sine, zeros], axis=1)
    curve = curves_ref[...]
    square = split_terms(curve * curve * noise_ref[...])
    square_ref[...] = jnp.concatenate(
        [square, jnp.zeros((square.shape[0], wide - length), BF16)], axis=1
    )


def shift_rows(shifted_ref, cos_ref, sin_ref, real, imag, offset, total):
    n_proj, wide = real.shape
    for t in range(cos_ref.shape[0]):
        cos_part, sin_part = cos_ref[t : t + 1, :], sin_ref[t : t + 1, :]
        rows = slice(t * total + offset * n_proj, t * total + (offset + 1) * n_proj)
        shifted_ref[rows, :wide] = (cos_part * real + sin_part * imag).astype(BF16)
        shifted_ref[rows, wide:] = (cos_part * imag - sin_part * real).astype(BF16)


def norm_of(square_ref, powers):
    power = jnp.concatenate(powers, axis=0)
    count, classes_count = power.shape[0], square_ref.shape[0] // 2
    table = lax.dot_general(
        square_ref[...], split_terms(power), NT_DIMS, preferred_element_type=F32
    )
    return (
        table[:classes_count, count:] + table[classes_count:, :count] + table[:classes_count, :count]
    )


def shift_kernel(offsets, total, cos_ref, sin_ref, square_ref, *rest):
    banks, (shifted_ref, norm_ref) = rest[: len(offsets)], rest[len(offsets) :]
    powers = []
    for bank, offs in zip(banks, offsets):
        n_proj = bank.shape[0] // (2 * len(offs))
        for n, offset in enumerate(offs):
            both = bank[2 * n_proj * n : 2 * n_proj * (n + 1)].astype(F32)
            real, imag = both[:n_proj], both[n_proj:]
            shift_rows(shifted_ref, cos_ref, sin_ref, real, imag, offset, total)
            powers.append(real * real + imag * imag)
    norm_ref[...] = norm_of(square_ref, powers)


def score_kernel(
    half, offsets, n_parts, bits, n_part, n_proj, length, subsets, shifted_in, cos_ref, sin_ref, square_ref, norm_ref, *rest
):
    n_bank = len(offsets)
    banks, parts, outs = rest[:n_bank], rest[n_bank : n_bank + n_parts], rest[n_bank + n_parts :][:2]
    shifted_ref = rest[n_bank + n_parts + 2]
    g = lax.axis_index("grp")
    ng = 1 << len(bits)
    total, wide = half * n_proj, cos_ref.shape[1]
    shifts = cos_ref.shape[0]
    classes_count = square_ref.shape[0] // 2

    powers = []
    for n, offset in enumerate(offsets[-1]):
        both = banks[-1][2 * n_proj * n : 2 * n_proj * (n + 1)].astype(F32)
        real, imag = both[:n_proj], both[n_proj:]
        shift_rows(shifted_ref, cos_ref, sin_ref, real, imag, offset, total)
        powers.append(real * real + imag * imag)
    norm_last = norm_of(square_ref, powers)

    held = jnp.concatenate([part[...] for part in parts], axis=0)
    count = 2 * ng * n_part
    out_row = lax.broadcasted_iota(jnp.int32, (2 * count, held.shape[0]), 0)
    in_row = lax.broadcasted_iota(jnp.int32, (2 * count, held.shape[0]), 1)
    kind, rest_row = out_row // count, out_row % count
    source, rest_row = rest_row // (ng * n_part), rest_row % (ng * n_part)
    away, i = rest_row // n_part ^ g, rest_row % n_part
    for n, bit in enumerate(bits):
        source += jnp.where(away & bit != 0, 2 << n, 0)
    pick = (in_row == source * (2 * n_part) + kind * n_part + i).astype(F32).astype(BF16)
    ordered = jnp.dot(pick, held, preferred_element_type=F32)
    weighted = jnp.concatenate([ordered[:count, :wide], ordered[count:, :wide]], axis=1).astype(BF16)
    prior_rows = ordered[:count, wide : wide + subsets].astype(BF16)
    class_rows = ordered[:count, wide + subsets : wide + subsets + 1]
    cross = lax.dot_general(weighted, shifted_ref[...], NT_DIMS, preferred_element_type=F32)

    order = [offset for offs in offsets for offset in offs]
    first = len(order) - len(offsets[-1])
    norms, ids = {}, {}
    ids_at = length // 128 * 128
    for n, offset in enumerate(order):
        table, m = (norm_ref, n) if n < first else (norm_last, n - first)
        norms[offset] = table[:, m * n_proj : (m + 1) * n_proj]
    for bank, offs in zip(banks, offsets):
        for n, offset in enumerate(offs):
            rows = bank[2 * n_proj * n : 2 * n_proj * (n + 1), ids_at : ids_at + 128].astype(F32)
            ids[offset] = rows[:n_proj]
    table = jnp.concatenate([norms[offset] for offset in range(half)], axis=1)
    id_rows = jnp.concatenate([ids[offset] for offset in range(half)], axis=0)
    id_rows = id_rows[:, length - ids_at : length - ids_at + 1]
    class_col = lax.broadcasted_iota(jnp.int32, (count, classes_count), 1).astype(F32)
    onehot = (class_col == class_rows).astype(F32)
    norm = jnp.dot(onehot, table, precision=HIGHEST, preferred_element_type=F32)
    subset_col = lax.broadcasted_iota(jnp.int32, (total, subsets), 1).astype(F32)
    subset_hot = (subset_col == id_rows).astype(F32).astype(BF16)
    prior = lax.dot_general(prior_rows, subset_hot, NT_DIMS, preferred_element_type=F32)
    result = cross + jnp.concatenate([prior - 0.5 * norm] * shifts, axis=1)
    dest = ng * n_part
    lanes = outs[0].shape[1]
    for s in range(2):
        rows = result[s * dest : (s + 1) * dest]
        if rows.shape[1] < lanes:
            zeros = jnp.zeros((dest, lanes - rows.shape[1]), F32)
            rows = jnp.concatenate([rows, zeros], axis=1)
        outs[s][...] = rows


def place_kernel(half, n_proj, keep_ref, recv_ref, out_ref):
    blk = lax.axis_index("blk")
    first = blk < half
    low = jnp.where(first, keep_ref[...], recv_ref[...])
    high = jnp.where(first, recv_ref[...], keep_ref[...])
    lanes = low.shape[1]
    lane = lax.broadcasted_iota(jnp.int32, low.shape, 1)

    def exchanged(values):
        bit = 1
        while bit < half:
            step = bit * n_proj
            upper = (lane & step) != 0
            other = jnp.where(
                upper, pltpu.roll(values, step, 1), pltpu.roll(values, lanes - step, 1)
            )
            values = jnp.where((blk & bit) != 0, other, values)
            bit *= 2
        return values

    low, high = exchanged(low), exchanged(high)
    shifts, _, width = out_ref.shape
    width = width // 2
    for t in range(shifts):
        span = slice(t * width, (t + 1) * width)
        out_ref[t] = jnp.concatenate([low[:, span], high[:, span]], axis=1)


def per_device(
    particles,
    ctf_class,
    orient_prior,
    ctf_curves,
    noise_weight,
    shift_phase,
    trans_index,
    projections,
    orient_subset,
):
    nb, ng = lax.axis_size("blk"), lax.axis_size("grp")
    half = nb // 2
    n_part, n_proj = particles.shape[0], projections.shape[0]
    length = particles.shape[2]
    shifts = shift_phase.shape[0]
    classes_count = ctf_curves.shape[0]
    subsets = orient_prior.shape[1]
    wide = 128 * (length // 128 + 1)
    extra = 128 * (subsets // 128 + 1)
    noise = noise_weight.reshape(1, length)
    shape = jax.ShapeDtypeStruct

    def vmem_out(dims, dtype):
        return pltpu.VMEM(dims, dtype)

    operands = (
        ctf_class,
        orient_subset,
        particles,
        orient_prior,
        ctf_curves,
        noise,
        projections,
        shift_phase,
        trans_index,
    )
    bank, part, curves, noise, angle = pl.pallas_call(
        pack_kernel,
        out_shape=[
            vmem_out((2 * n_proj, wide), BF16),
            vmem_out((2 * n_part, wide + extra), BF16),
            vmem_out(ctf_curves.shape, F32),
            vmem_out(noise.shape, F32),
            vmem_out(shift_phase.shape, F32),
        ],
        in_specs=[pl.BlockSpec(memory_space=pltpu.HBM)] * len(operands),
        out_specs=[_vmem()] * 5,
        scratch_shapes=[
            pltpu.SMEM(ctf_class.shape, jnp.int32),
            pltpu.SMEM(orient_subset.shape, jnp.int32),
            pltpu.SMEM(trans_index.shape, jnp.int32),
            pltpu.VMEM(particles.shape, BF16),
            pltpu.VMEM(orient_prior.shape, BF16),
            pltpu.VMEM(shift_phase.shape, F32),
            pltpu.VMEM(projections.shape, BF16),
            pltpu.SemaphoreType.DMA((len(operands),)),
        ],
        compiler_params=_params(16),
        name="pack",
    )(*[pltpu.with_memory_space_constraint(operand, pltpu.HBM) for operand in operands])

    def swap(value, axis, bit):
        size = lax.axis_size(axis)
        return lax.ppermute(value, axis, [(i, i ^ bit) for i in range(size)])

    def joined(pieces):
        return pieces[0] if len(pieces) == 1 else jnp.concatenate(pieces, axis=0)

    def doubled(pieces, axis, bits):
        for bit in bits:
            whole = joined(pieces)
            pieces = [whole, swap(whole, axis, bit)]
        return pieces

    grp_bits = [1 << n for n in range(ng.bit_length() - 2, -1, -1)]
    parts = doubled([part, swap(part, "blk", half)], "grp", grp_bits)

    near = swap(bank, "blk", 1)
    planes, far_offsets = [bank], [0]
    for n in range(half.bit_length() - 2, 0, -1):
        planes.append(swap(joined(planes), "blk", 1 << n))
        far_offsets += [offset ^ (1 << n) for offset in far_offsets]
    far, far_offsets = joined(planes[1:]), far_offsets[1:]
    last = swap(far, "blk", 1)
    banks = [bank, near, far, last]
    offsets = [[0], [1], far_offsets, [offset ^ 1 for offset in far_offsets]]

    cos_part, sin_part, square = pl.pallas_call(
        table_kernel,
        out_shape=[
            vmem_out((shifts, wide), F32),
            vmem_out((shifts, wide), F32),
            vmem_out((2 * classes_count, wide), BF16),
        ],
        in_specs=[_vmem()] * 3,
        out_specs=[_vmem()] * 3,
        compiler_params=_params(8),
        cost_estimate=pl.CostEstimate(flops=4_000_000, bytes_accessed=2_000_000, transcendentals=0),
        name="tables",
    )(curves, noise, angle)

    count = 2 * ng * n_part
    total = half * n_proj
    early = total - len(far_offsets) * n_proj
    shifted, norm = pl.pallas_call(
        functools.partial(shift_kernel, offsets[:3], total),
        out_shape=[
            vmem_out((shifts * total, 2 * wide), BF16),
            vmem_out((classes_count, early), F32),
        ],
        in_specs=[_vmem()] * 6,
        out_specs=[_vmem()] * 2,
        compiler_params=_params(8),
        cost_estimate=pl.CostEstimate(
            flops=6 * early * shifts * wide, bytes_accessed=4_000_000, transcendentals=0
        ),
        name="shift",
    )(cos_part, sin_part, square, *banks[:3])
    lanes = 128 * -(-shifts * total // 128)
    keep, give, _ = pl.pallas_call(
        functools.partial(
            score_kernel, half, offsets, len(parts), grp_bits, n_part, n_proj, length, subsets
        ),
        out_shape=[vmem_out((ng * n_part, lanes), F32)] * 2
        + [vmem_out((shifts * total, 2 * wide), BF16)],
        in_specs=[_vmem()] * (5 + len(banks) + len(parts)),
        out_specs=[_vmem()] * 3,
        input_output_aliases={0: 2},
        compiler_params=_params(8),
        cost_estimate=pl.CostEstimate(
            flops=4 * count * total * shifts * wide, bytes_accessed=4_000_000, transcendentals=0
        ),
        name="score",
    )(shifted, cos_part, sin_part, square, norm, *banks, *parts)
    scores = pl.pallas_call(
        functools.partial(place_kernel, half, n_proj),
        out_shape=shape((shifts, ng * n_part, 2 * total), F32),
        in_specs=[_vmem()] * 2,
        out_specs=_vmem(),
        compiler_params=_params(4),
        name="place",
    )(keep, swap(give, "blk", half))
    return scores.transpose(1, 0, 2)


def solution(mesh):
    placed = (
        P(("blk", "grp"), None, None),
        P(("blk", "grp")),
        P(("blk", "grp"), None),
        P(),
        P(),
        P(),
        P(),
        P(("grp", "blk"), None, None),
        P(("grp", "blk")),
    )
    return jax.shard_map(
        per_device, mesh=mesh, in_specs=placed, out_specs=P("blk", None, "grp"), check_vma=False
    )
```

```python
import functools

import jax
import jax.numpy as jnp
from jax import lax
from jax.experimental import pallas as pl
from jax.experimental.pallas import tpu as pltpu
from jax.sharding import PartitionSpec as P

F32 = jnp.float32
BF16 = jnp.bfloat16
HIGHEST = lax.Precision.HIGHEST
NT_DIMS = (((1,), (1,)), ((), ()))
MIB = 1 << 20


def _vmem():
    return pl.BlockSpec(memory_space=pltpu.VMEM)


def _params(mib):
    return pltpu.CompilerParams(vmem_limit_bytes=mib * MIB)


def pack_kernel(
    class_hbm,
    subset_hbm,
    particles_hbm,
    prior_hbm,
    curves_hbm,
    noise_hbm,
    proj_hbm,
    phase_hbm,
    trans_hbm,
    bank_ref,
    part_ref,
    curves_ref,
    noise_ref,
    angle_ref,
    class_ref,
    subset_ref,
    trans_ref,
    particles_ref,
    prior_ref,
    phase_ref,
    proj_ref,
    sems,
):
    pairs = [
        (proj_hbm, proj_ref),
        (subset_hbm, subset_ref),
        (class_hbm, class_ref),
        (curves_hbm, curves_ref),
        (particles_hbm, particles_ref),
        (noise_hbm, noise_ref),
        (prior_hbm, prior_ref),
        (trans_hbm, trans_ref),
        (phase_hbm, phase_ref),
    ]
    copies = [pltpu.make_async_copy(a, b, sems.at[n]) for n, (a, b) in enumerate(pairs)]
    for copy in copies:
        copy.start()
    n_part, n_proj = particles_ref.shape[0], proj_ref.shape[0]
    length = proj_ref.shape[2]
    wide = bank_ref.shape[1]

    def padded(values, width):
        zeros = jnp.zeros((values.shape[0], width - values.shape[1]), values.dtype)
        return jnp.concatenate([values, zeros], axis=1)

    row = lax.broadcasted_iota(jnp.int32, (n_proj, wide), 0)
    lane = lax.broadcasted_iota(jnp.int32, (n_proj, wide), 1)
    for copy in copies[:2]:
        copy.wait()
    real = jnp.zeros((n_proj, wide), F32)
    imag = jnp.zeros((n_proj, wide), F32)
    for j in range(n_proj):
        both = padded(proj_ref[j].astype(F32), wide)
        real = jnp.where(row == j, both[0:1], real)
        imag = jnp.where(row == j, both[1:2], imag)
    last = slice(wide - 128, wide)
    ends = real[:, last]
    for j in range(n_proj):
        here = (row[:, last] == j) & (lane[:, last] == length)
        ends = jnp.where(here, subset_ref[j].astype(F32), ends)
    real = jnp.concatenate([real[:, : wide - 128], ends], axis=1)
    bank_ref[...] = jnp.concatenate([real, imag], axis=0).astype(BF16)

    for copy in copies[2:]:
        copy.wait()
    subsets = prior_ref.shape[1]
    extra = part_ref.shape[1] - wide
    row = lax.broadcasted_iota(jnp.int32, (2 * n_part, wide), 0)
    row_extra = lax.broadcasted_iota(jnp.int32, (2 * n_part, extra), 0)
    lane_extra = lax.broadcasted_iota(jnp.int32, (2 * n_part, extra), 1)
    prior = padded(prior_ref[...].astype(F32), extra)
    rows = jnp.zeros((2 * n_part, wide), F32)
    rows_extra = jnp.zeros((2 * n_part, extra), F32)
    for i in range(n_part):
        curve = curves_ref[pl.ds(class_ref[i], 1), :] * noise_ref[...]
        both = padded(particles_ref[i].astype(F32) * curve, wide)
        rows = jnp.where(row == i, both[0:1], rows)
        rows = jnp.where(row == n_part + i, both[1:2], rows)
        small = jnp.where(
            lane_extra == subsets,
            class_ref[i].astype(F32),
            jnp.broadcast_to(prior[i : i + 1], rows_extra.shape),
        )
        rows_extra = jnp.where(row_extra == i, small, rows_extra)
    part_ref[:, :wide] = rows.astype(BF16)
    part_ref[:, wide:] = rows_extra.astype(BF16)
    for t in range(phase_ref.shape[0]):
        angle_ref[t : t + 1, :] = phase_ref[pl.ds(trans_ref[t], 1), :]


def sine_cosine(x):
    turns = jnp.floor(x * 0.6366197723675814 + 0.5)
    r = ((x - turns * 1.5703125) - turns * 4.837512969970703125e-4) - turns * 7.549789954891882e-8
    z = r * r
    sine = r + r * z * (-1.6666654611e-1 + z * (8.3321608736e-3 - z * 1.9515295891e-4))
    cosine = 1.0 - 0.5 * z + z * z * (
        4.166664568298827e-2 + z * (-1.388731625493765e-3 + z * 2.443315711809948e-5)
    )
    quarter = turns.astype(jnp.int32) & 3
    swapped = (quarter & 1) == 1
    first, second = jnp.where(swapped, cosine, sine), jnp.where(swapped, sine, cosine)
    first = jnp.where(quarter >= 2, -first, first)
    second = jnp.where((quarter == 1) | (quarter == 2), -second, second)
    return first, second


def split_terms(values):
    high = values.astype(BF16)
    low = (values - high.astype(F32)).astype(BF16)
    return jnp.concatenate([high, low], axis=0)


def table_kernel(curves_ref, noise_ref, angle_ref, cos_ref, sin_ref, square_ref):
    length = curves_ref.shape[1]
    wide = cos_ref.shape[1]
    zeros = jnp.zeros((cos_ref.shape[0], wide - length), F32)
    sine, cosine = sine_cosine(angle_ref[...])
    cos_ref[...] = jnp.concatenate([cosine, zeros], axis=1)
    sin_ref[...] = jnp.concatenate([sine, zeros], axis=1)
    curve = curves_ref[...]
    square = split_terms(curve * curve * noise_ref[...])
    square_ref[...] = jnp.concatenate(
        [square, jnp.zeros((square.shape[0], wide - length), BF16)], axis=1
    )


def shift_rows(shifted_ref, cos_ref, sin_ref, real, imag, at):
    n_proj, wide = real.shape
    shifts = cos_ref.shape[0]
    for t in range(shifts):
        cos_part, sin_part = cos_ref[t : t + 1, :], sin_ref[t : t + 1, :]
        rows = slice((at * shifts + t) * n_proj, (at * shifts + t + 1) * n_proj)
        shifted_ref[rows, :wide] = (cos_part * real + sin_part * imag).astype(BF16)
        shifted_ref[rows, wide:] = (cos_part * imag - sin_part * real).astype(BF16)


def norm_of(square_ref, powers):
    power = jnp.concatenate(powers, axis=0)
    count, classes_count = power.shape[0], square_ref.shape[0] // 2
    table = lax.dot_general(
        square_ref[...], split_terms(power), NT_DIMS, preferred_element_type=F32
    )
    return (
        table[:classes_count, count:] + table[classes_count:, :count] + table[:classes_count, :count]
    )


def shift_bank(banks, shifted_ref, cos_ref, sin_ref, square_ref, n_proj):
    powers = []
    for bank in banks:
        for n in range(bank.shape[0] // (2 * n_proj)):
            both = bank[2 * n_proj * n : 2 * n_proj * (n + 1)].astype(F32)
            real, imag = both[:n_proj], both[n_proj:]
            shift_rows(shifted_ref, cos_ref, sin_ref, real, imag, len(powers))
            powers.append(real * real + imag * imag)
    return norm_of(square_ref, powers)


def shift_kernel(n_proj, cos_ref, sin_ref, square_ref, *rest):
    *banks, shifted_ref, norm_ref = rest
    norm_ref[...] = shift_bank(banks, shifted_ref, cos_ref, sin_ref, square_ref, n_proj)


def join_kernel(n_parts, *refs):
    parts, out_ref = refs[:n_parts], refs[-1]
    at = 0
    for part in parts:
        out_ref[at : at + part.shape[0], :] = part[...]
        at += part.shape[0]


def added_rows(extra, table, banks, n_proj, length, subsets):
    ids_at = length // 128 * 128
    ids = []
    for bank in banks:
        for n in range(bank.shape[0] // (2 * n_proj)):
            rows = bank[2 * n_proj * n : 2 * n_proj * (n + 1), ids_at : ids_at + 128].astype(F32)
            ids.append(rows[:n_proj])
    ids = jnp.concatenate(ids, axis=0)[:, length - ids_at : length - ids_at + 1]
    count, classes_count = extra.shape[0], table.shape[0]
    class_col = lax.broadcasted_iota(jnp.int32, (count, classes_count), 1).astype(F32)
    onehot = (class_col == extra[:, subsets : subsets + 1]).astype(F32)
    norm = jnp.dot(onehot, table, precision=HIGHEST, preferred_element_type=F32)
    subset_col = lax.broadcasted_iota(jnp.int32, (ids.shape[0], subsets), 1).astype(F32)
    subset_hot = (subset_col == ids).astype(F32).astype(BF16)
    prior = lax.dot_general(
        extra[:, :subsets].astype(BF16), subset_hot, NT_DIMS, preferred_element_type=F32
    )
    return prior - 0.5 * norm


def score_rows(weighted, shifted, added, n_proj):
    cross = lax.dot_general(weighted, shifted, NT_DIMS, preferred_element_type=F32)
    pieces = added.shape[1] // n_proj
    width = cross.shape[1] // pieces
    rows = []
    for n in range(pieces):
        rows += [cross[:, n * width : (n + 1) * width], added[:, n * n_proj : (n + 1) * n_proj]]
    return jnp.concatenate(rows, axis=1)


def early_kernel(
    n_parts, ng, half_weight, weights, n_part, n_proj, length, subsets, shifted_ref, norm_ref, *rest
):
    parts, (*banks, weighted_ref, extra_ref, rows_ref) = rest[:n_parts], rest[n_parts:]
    g = lax.axis_index("grp")
    wide = weighted_ref.shape[1] // 2

    held = jnp.concatenate([part[...] for part in parts], axis=0)
    count = 2 * ng * n_part
    out_row = lax.broadcasted_iota(jnp.int32, (2 * count, held.shape[0]), 0)
    in_row = lax.broadcasted_iota(jnp.int32, (2 * count, held.shape[0]), 1)
    kind, rest_row = out_row // count, out_row % count
    source, rest_row = rest_row // (ng * n_part) * half_weight, rest_row % (ng * n_part)
    away, i = rest_row // n_part ^ g, rest_row % n_part
    for bit, weight in weights:
        source += jnp.where(away & bit != 0, weight, 0)
    pick = (in_row == source * (2 * n_part) + kind * n_part + i).astype(F32).astype(BF16)
    ordered = jnp.dot(pick, held, preferred_element_type=F32)
    weighted_ref[:, :wide] = ordered[:count, :wide].astype(BF16)
    weighted_ref[:, wide:] = ordered[count:, :wide].astype(BF16)
    extra = ordered[:count, wide:]
    extra_ref[...] = extra
    added = added_rows(extra, norm_ref[...], banks, n_proj, length, subsets)
    rows_ref[...] = score_rows(weighted_ref[...], shifted_ref[...], added, n_proj)


def final_kernel(
    n_proj, length, subsets, weighted_ref, extra_ref, rows_ref, cos_ref, sin_ref, square_ref, last_ref, *rest
):
    *outs, shifted_ref = rest
    table = shift_bank([last_ref], shifted_ref, cos_ref, sin_ref, square_ref, n_proj)
    added = added_rows(extra_ref[...], table, [last_ref], n_proj, length, subsets)
    rows = score_rows(weighted_ref[...], shifted_ref[...], added, n_proj)
    rows = jnp.concatenate([rows_ref[...], rows], axis=1)
    dest, lanes = outs[0].shape
    if rows.shape[1] < lanes:
        zeros = jnp.zeros((rows.shape[0], lanes - rows.shape[1]), F32)
        rows = jnp.concatenate([rows, zeros], axis=1)
    for s, out in enumerate(outs):
        out[...] = rows[s * dest : (s + 1) * dest]


def place_kernel(half, n_proj, order, keep_ref, recv_ref, out_ref):
    blk = lax.axis_index("blk")
    first = blk < half
    low = jnp.where(first, keep_ref[...], recv_ref[...])
    high = jnp.where(first, recv_ref[...], keep_ref[...])
    shifts = out_ref.shape[0]
    width = (shifts + 1) * n_proj

    def by_shift(values):
        found = {offset: values[:, n * width : (n + 1) * width] for n, offset in enumerate(order)}
        lined = []
        for t in range(shifts + 1):
            span = slice(t * n_proj, (t + 1) * n_proj)
            lined += [found[offset][:, span] for offset in range(half)]
        return jnp.concatenate(lined, axis=1)

    def exchanged(values):
        total = (shifts + 1) * half * n_proj
        lanes = 128 * -(-total // 128)
        if lanes > total:
            zeros = jnp.zeros((values.shape[0], lanes - total), F32)
            values = jnp.concatenate([values, zeros], axis=1)
        lane = lax.broadcasted_iota(jnp.int32, values.shape, 1)
        bit = 1
        while bit < half:
            step = bit * n_proj
            other = jnp.where(
                (lane & step) != 0, pltpu.roll(values, step, 1), pltpu.roll(values, lanes - step, 1)
            )
            values = jnp.where((blk & bit) != 0, other, values)
            bit *= 2
        return values

    low, high = exchanged(by_shift(low)), exchanged(by_shift(high))
    span = half * n_proj
    lined = [
        jnp.concatenate([low[:, t * span : (t + 1) * span], high[:, t * span : (t + 1) * span]], axis=1)
        for t in range(shifts + 1)
    ]
    for t in range(shifts):
        out_ref[t] = lined[t] + lined[shifts]


def per_device(
    particles,
    ctf_class,
    orient_prior,
    ctf_curves,
    noise_weight,
    shift_phase,
    trans_index,
    projections,
    orient_subset,
):
    nb, ng = lax.axis_size("blk"), lax.axis_size("grp")
    half = nb // 2
    n_part, n_proj = particles.shape[0], projections.shape[0]
    length = particles.shape[2]
    shifts = shift_phase.shape[0]
    classes_count = ctf_curves.shape[0]
    subsets = orient_prior.shape[1]
    wide = 128 * (length // 128 + 1)
    extra = 128 * (subsets // 128 + 1)
    noise = noise_weight.reshape(1, length)
    shape = jax.ShapeDtypeStruct

    def vmem_out(dims, dtype):
        return pltpu.VMEM(dims, dtype)

    operands = (
        ctf_class,
        orient_subset,
        particles,
        orient_prior,
        ctf_curves,
        noise,
        projections,
        shift_phase,
        trans_index,
    )
    bank, part, curves, noise, angle = pl.pallas_call(
        pack_kernel,
        out_shape=[
            vmem_out((2 * n_proj, wide), BF16),
            vmem_out((2 * n_part, wide + extra), BF16),
            vmem_out(ctf_curves.shape, F32),
            vmem_out(noise.shape, F32),
            vmem_out(shift_phase.shape, F32),
        ],
        in_specs=[pl.BlockSpec(memory_space=pltpu.HBM)] * len(operands),
        out_specs=[_vmem()] * 5,
        scratch_shapes=[
            pltpu.SMEM(ctf_class.shape, jnp.int32),
            pltpu.SMEM(orient_subset.shape, jnp.int32),
            pltpu.SMEM(trans_index.shape, jnp.int32),
            pltpu.VMEM(particles.shape, BF16),
            pltpu.VMEM(orient_prior.shape, BF16),
            pltpu.VMEM(shift_phase.shape, F32),
            pltpu.VMEM(projections.shape, BF16),
            pltpu.SemaphoreType.DMA((len(operands),)),
        ],
        compiler_params=_params(16),
        name="pack",
    )(*[pltpu.with_memory_space_constraint(operand, pltpu.HBM) for operand in operands])

    def swap(value, axis, bit):
        size = lax.axis_size(axis)
        return lax.ppermute(value, axis, [(i, i ^ bit) for i in range(size)])

    def swap_both(value, blk_bit, grp_bit):
        pairs = [
            (g * nb + b, (g ^ grp_bit) * nb + (b ^ blk_bit)) for g in range(ng) for b in range(nb)
        ]
        return lax.ppermute(value, ("grp", "blk"), pairs)

    def joined(pieces):
        return pieces[0] if len(pieces) == 1 else jnp.concatenate(pieces, axis=0)

    planes, far_offsets = [bank], [0]
    for n in range(half.bit_length() - 2, 0, -1):
        planes.append(swap(joined(planes), "blk", 1 << n))
        far_offsets += [offset ^ (1 << n) for offset in far_offsets]
    far, far_offsets = joined(planes[1:]), far_offsets[1:]
    near = swap(bank, "blk", 1)

    weights, weight = [], 1
    for n in range(ng.bit_length() - 2, 1, -1):
        part = joined([part, swap(part, "grp", 1 << n)])
        weights.append((1 << n, weight))
        weight *= 2
    half_weight = weight
    weights += [(2, 2 * weight), (1, 4 * weight)]
    parts = [part, swap(part, "blk", half), swap(part, "grp", 2), swap_both(part, half, 2)]

    cos_part, sin_part, square = pl.pallas_call(
        table_kernel,
        out_shape=[
            vmem_out((shifts, wide), F32),
            vmem_out((shifts, wide), F32),
            vmem_out((2 * classes_count, wide), BF16),
        ],
        in_specs=[_vmem()] * 3,
        out_specs=[_vmem()] * 3,
        compiler_params=_params(8),
        cost_estimate=pl.CostEstimate(flops=4_000_000, bytes_accessed=2_000_000, transcendentals=0),
        name="tables",
    )(curves, noise, angle)

    any_space = pl.BlockSpec(memory_space=pl.ANY)
    part = pl.pallas_call(
        functools.partial(join_kernel, len(parts)),
        out_shape=vmem_out((sum(piece.shape[0] for piece in parts), part.shape[1]), BF16),
        in_specs=[_vmem()] * len(parts) + [any_space] * 3,
        out_specs=_vmem(),
        compiler_params=_params(4),
        name="join",
    )(*parts, near, far, cos_part)
    parts = [part, swap(part, "grp", 1)]
    last = swap(far, "blk", 1)
    order = [0, 1] + far_offsets + [offset ^ 1 for offset in far_offsets]

    count = 2 * ng * n_part
    early = (2 + len(far_offsets)) * n_proj
    late = len(far_offsets) * n_proj
    shifted, norm = pl.pallas_call(
        functools.partial(shift_kernel, n_proj),
        out_shape=[
            vmem_out((shifts * early, 2 * wide), BF16),
            vmem_out((classes_count, early), F32),
        ],
        in_specs=[_vmem()] * 6,
        out_specs=[_vmem()] * 2,
        compiler_params=_params(8),
        cost_estimate=pl.CostEstimate(
            flops=6 * early * shifts * wide, bytes_accessed=4_000_000, transcendentals=0
        ),
        name="shift",
    )(cos_part, sin_part, square, bank, near, far)
    weighted, extra_rows, rows = pl.pallas_call(
        functools.partial(
            early_kernel, len(parts), ng, half_weight, weights, n_part, n_proj, length, subsets
        ),
        out_shape=[
            vmem_out((count, 2 * wide), BF16),
            vmem_out((count, extra), F32),
            vmem_out((count, (shifts + 1) * early), F32),
        ],
        in_specs=[_vmem()] * (5 + len(parts)),
        out_specs=[_vmem()] * 3,
        compiler_params=_params(8),
        cost_estimate=pl.CostEstimate(
            flops=4 * count * early * shifts * wide, bytes_accessed=4_000_000, transcendentals=0
        ),
        name="early",
    )(shifted, norm, *parts, bank, near, far)
    lanes = 128 * -(-(shifts + 1) * half * n_proj // 128)
    keep, give = pl.pallas_call(
        functools.partial(final_kernel, n_proj, length, subsets),
        out_shape=[vmem_out((ng * n_part, lanes), F32)] * 2,
        in_specs=[_vmem()] * 7,
        out_specs=[_vmem()] * 2,
        scratch_shapes=[pltpu.VMEM((shifts * late, 2 * wide), BF16)],
        compiler_params=_params(24),
        cost_estimate=pl.CostEstimate(
            flops=4 * count * late * shifts * wide, bytes_accessed=4_000_000, transcendentals=0
        ),
        name="final",
    )(weighted, extra_rows, rows, cos_part, sin_part, square, last)
    scores = pl.pallas_call(
        functools.partial(place_kernel, half, n_proj, order),
        out_shape=shape((shifts, ng * n_part, nb * n_proj), F32),
        in_specs=[_vmem()] * 2,
        out_specs=_vmem(),
        compiler_params=_params(4),
        name="place",
    )(keep, swap(give, "blk", half))
    return scores.transpose(1, 0, 2)


def solution(mesh):
    placed = (
        P(("blk", "grp"), None, None),
        P(("blk", "grp")),
        P(("blk", "grp"), None),
        P(),
        P(),
        P(),
        P(),
        P(("grp", "blk"), None, None),
        P(("grp", "blk")),
    )
    return jax.shard_map(
        per_device, mesh=mesh, in_specs=placed, out_specs=P("blk", None, "grp"), check_vma=False
    )
```

```python
import functools

import jax
import jax.numpy as jnp
from jax import lax
from jax.experimental import pallas as pl
from jax.experimental.pallas import tpu as pltpu
from jax.sharding import PartitionSpec as P

F32 = jnp.float32
BF16 = jnp.bfloat16
HIGHEST = lax.Precision.HIGHEST
NT_DIMS = (((1,), (1,)), ((), ()))
MIB = 1 << 20


def _vmem():
    return pl.BlockSpec(memory_space=pltpu.VMEM)


def _params(mib):
    return pltpu.CompilerParams(vmem_limit_bytes=mib * MIB)


def pack_kernel(
    class_hbm,
    subset_hbm,
    particles_hbm,
    prior_hbm,
    curves_hbm,
    noise_hbm,
    proj_hbm,
    phase_hbm,
    trans_hbm,
    bank_ref,
    part_ref,
    curves_ref,
    noise_ref,
    angle_ref,
    class_ref,
    subset_ref,
    trans_ref,
    particles_ref,
    prior_ref,
    phase_ref,
    proj_ref,
    sems,
):
    pairs = [
        (proj_hbm, proj_ref),
        (subset_hbm, subset_ref),
        (class_hbm, class_ref),
        (curves_hbm, curves_ref),
        (particles_hbm, particles_ref),
        (noise_hbm, noise_ref),
        (prior_hbm, prior_ref),
        (trans_hbm, trans_ref),
        (phase_hbm, phase_ref),
    ]
    copies = [pltpu.make_async_copy(a, b, sems.at[n]) for n, (a, b) in enumerate(pairs)]
    for copy in copies:
        copy.start()
    n_part, n_proj = particles_ref.shape[0], proj_ref.shape[0]
    length = proj_ref.shape[2]
    wide = bank_ref.shape[1]

    def padded(values, width):
        zeros = jnp.zeros((values.shape[0], width - values.shape[1]), values.dtype)
        return jnp.concatenate([values, zeros], axis=1)

    row = lax.broadcasted_iota(jnp.int32, (n_proj, wide), 0)
    lane = lax.broadcasted_iota(jnp.int32, (n_proj, wide), 1)
    for copy in copies[:2]:
        copy.wait()
    real = jnp.zeros((n_proj, wide), F32)
    imag = jnp.zeros((n_proj, wide), F32)
    for j in range(n_proj):
        both = padded(proj_ref[j].astype(F32), wide)
        real = jnp.where(row == j, both[0:1], real)
        imag = jnp.where(row == j, both[1:2], imag)
    last = slice(wide - 128, wide)
    ends = real[:, last]
    for j in range(n_proj):
        here = (row[:, last] == j) & (lane[:, last] == length)
        ends = jnp.where(here, subset_ref[j].astype(F32), ends)
    real = jnp.concatenate([real[:, : wide - 128], ends], axis=1)
    bank_ref[...] = jnp.concatenate([real, imag], axis=0).astype(BF16)

    for copy in copies[2:]:
        copy.wait()
    subsets = prior_ref.shape[1]
    extra = part_ref.shape[1] - wide
    row = lax.broadcasted_iota(jnp.int32, (2 * n_part, wide), 0)
    row_extra = lax.broadcasted_iota(jnp.int32, (2 * n_part, extra), 0)
    lane_extra = lax.broadcasted_iota(jnp.int32, (2 * n_part, extra), 1)
    prior = padded(prior_ref[...].astype(F32), extra)
    rows = jnp.zeros((2 * n_part, wide), F32)
    rows_extra = jnp.zeros((2 * n_part, extra), F32)
    for i in range(n_part):
        curve = curves_ref[pl.ds(class_ref[i], 1), :] * noise_ref[...]
        both = padded(particles_ref[i].astype(F32) * curve, wide)
        rows = jnp.where(row == i, both[0:1], rows)
        rows = jnp.where(row == n_part + i, both[1:2], rows)
        small = jnp.where(
            lane_extra == subsets,
            class_ref[i].astype(F32),
            jnp.broadcast_to(prior[i : i + 1], rows_extra.shape),
        )
        rows_extra = jnp.where(row_extra == i, small, rows_extra)
    part_ref[:, :wide] = rows.astype(BF16)
    part_ref[:, wide:] = rows_extra.astype(BF16)
    for t in range(phase_ref.shape[0]):
        angle_ref[t : t + 1, :] = phase_ref[pl.ds(trans_ref[t], 1), :]


def sine_cosine(x):
    turns = jnp.floor(x * 0.6366197723675814 + 0.5)
    r = ((x - turns * 1.5703125) - turns * 4.837512969970703125e-4) - turns * 7.549789954891882e-8
    z = r * r
    sine = r + r * z * (-1.6666654611e-1 + z * (8.3321608736e-3 - z * 1.9515295891e-4))
    cosine = 1.0 - 0.5 * z + z * z * (
        4.166664568298827e-2 + z * (-1.388731625493765e-3 + z * 2.443315711809948e-5)
    )
    quarter = turns.astype(jnp.int32) & 3
    swapped = (quarter & 1) == 1
    first, second = jnp.where(swapped, cosine, sine), jnp.where(swapped, sine, cosine)
    first = jnp.where(quarter >= 2, -first, first)
    second = jnp.where((quarter == 1) | (quarter == 2), -second, second)
    return first, second


def split_terms(values):
    high = values.astype(BF16)
    low = (values - high.astype(F32)).astype(BF16)
    return jnp.concatenate([high, low], axis=0)


def table_kernel(curves_ref, noise_ref, angle_ref, cos_ref, sin_ref, square_ref):
    length = curves_ref.shape[1]
    wide = cos_ref.shape[1]
    zeros = jnp.zeros((cos_ref.shape[0], wide - length), F32)
    sine, cosine = sine_cosine(angle_ref[...])
    cos_ref[...] = jnp.concatenate([cosine, zeros], axis=1)
    sin_ref[...] = jnp.concatenate([sine, zeros], axis=1)
    curve = curves_ref[...]
    square = split_terms(curve * curve * noise_ref[...])
    square_ref[...] = jnp.concatenate(
        [square, jnp.zeros((square.shape[0], wide - length), BF16)], axis=1
    )


def shift_rows(shifted_ref, cos_ref, sin_ref, real, imag, at):
    n_proj, wide = real.shape
    shifts = cos_ref.shape[0]
    for t in range(shifts):
        cos_part, sin_part = cos_ref[t : t + 1, :], sin_ref[t : t + 1, :]
        rows = slice((at * shifts + t) * n_proj, (at * shifts + t + 1) * n_proj)
        shifted_ref[rows, :wide] = (cos_part * real + sin_part * imag).astype(BF16)
        shifted_ref[rows, wide:] = (cos_part * imag - sin_part * real).astype(BF16)


def norm_of(square_ref, powers):
    power = jnp.concatenate(powers, axis=0)
    count, classes_count = power.shape[0], square_ref.shape[0] // 2
    table = lax.dot_general(
        square_ref[...], split_terms(power), NT_DIMS, preferred_element_type=F32
    )
    return (
        table[:classes_count, count:] + table[classes_count:, :count] + table[:classes_count, :count]
    )


def shift_bank(banks, shifted_ref, cos_ref, sin_ref, square_ref, n_proj):
    powers = []
    for bank in banks:
        for n in range(bank.shape[0] // (2 * n_proj)):
            both = bank[2 * n_proj * n : 2 * n_proj * (n + 1)].astype(F32)
            real, imag = both[:n_proj], both[n_proj:]
            shift_rows(shifted_ref, cos_ref, sin_ref, real, imag, len(powers))
            powers.append(real * real + imag * imag)
    return norm_of(square_ref, powers)


def shift_kernel(n_proj, cos_ref, sin_ref, square_ref, *rest):
    *banks, shifted_ref, norm_ref = rest
    norm_ref[...] = shift_bank(banks, shifted_ref, cos_ref, sin_ref, square_ref, n_proj)


def added_rows(extra, table, banks, n_proj, length, subsets):
    ids_at = length // 128 * 128
    ids = []
    for bank in banks:
        for n in range(bank.shape[0] // (2 * n_proj)):
            rows = bank[2 * n_proj * n : 2 * n_proj * (n + 1), ids_at : ids_at + 128].astype(F32)
            ids.append(rows[:n_proj])
    ids = jnp.concatenate(ids, axis=0)[:, length - ids_at : length - ids_at + 1]
    count, classes_count = extra.shape[0], table.shape[0]
    class_col = lax.broadcasted_iota(jnp.int32, (count, classes_count), 1).astype(F32)
    onehot = (class_col == extra[:, subsets : subsets + 1]).astype(F32)
    norm = jnp.dot(onehot, table, precision=HIGHEST, preferred_element_type=F32)
    subset_col = lax.broadcasted_iota(jnp.int32, (ids.shape[0], subsets), 1).astype(F32)
    subset_hot = (subset_col == ids).astype(F32).astype(BF16)
    prior = lax.dot_general(
        extra[:, :subsets].astype(BF16), subset_hot, NT_DIMS, preferred_element_type=F32
    )
    return prior - 0.5 * norm


def score_rows(weighted, shifted, added, n_proj):
    cross = lax.dot_general(weighted, shifted, NT_DIMS, preferred_element_type=F32)
    pieces = added.shape[1] // n_proj
    width = cross.shape[1] // pieces
    rows = []
    for n in range(pieces):
        rows += [cross[:, n * width : (n + 1) * width], added[:, n * n_proj : (n + 1) * n_proj]]
    return jnp.concatenate(rows, axis=1)


def early_kernel(
    n_parts, ng, weights, n_part, n_proj, length, subsets, shifted_ref, norm_ref, *rest
):
    parts, (*banks, weighted_ref, extra_ref, rows_ref) = rest[:n_parts], rest[n_parts:]
    g = lax.axis_index("grp")
    wide = weighted_ref.shape[1] // 2

    held = jnp.concatenate([part[...] for part in parts], axis=0)
    count = 2 * ng * n_part
    out_row = lax.broadcasted_iota(jnp.int32, (2 * count, held.shape[0]), 0)
    in_row = lax.broadcasted_iota(jnp.int32, (2 * count, held.shape[0]), 1)
    kind, rest_row = out_row // count, out_row % count
    source, rest_row = rest_row // (ng * n_part), rest_row % (ng * n_part)
    away, i = rest_row // n_part ^ g, rest_row % n_part
    for bit, weight in weights:
        source += jnp.where(away & bit != 0, weight, 0)
    pick = (in_row == source * (2 * n_part) + kind * n_part + i).astype(F32).astype(BF16)
    ordered = jnp.dot(pick, held, preferred_element_type=F32)
    weighted_ref[:, :wide] = ordered[:count, :wide].astype(BF16)
    weighted_ref[:, wide:] = ordered[count:, :wide].astype(BF16)
    extra = ordered[:count, wide:]
    extra_ref[...] = extra
    added = added_rows(extra, norm_ref[...], banks, n_proj, length, subsets)
    rows_ref[...] = score_rows(weighted_ref[...], shifted_ref[...], added, n_proj)


def final_kernel(
    n_proj, length, subsets, weighted_ref, extra_ref, rows_ref, cos_ref, sin_ref, square_ref, last_ref, *rest
):
    *outs, shifted_ref = rest
    table = shift_bank([last_ref], shifted_ref, cos_ref, sin_ref, square_ref, n_proj)
    added = added_rows(extra_ref[...], table, [last_ref], n_proj, length, subsets)
    rows = score_rows(weighted_ref[...], shifted_ref[...], added, n_proj)
    rows = jnp.concatenate([rows_ref[...], rows], axis=1)
    dest, lanes = outs[0].shape
    if rows.shape[1] < lanes:
        zeros = jnp.zeros((rows.shape[0], lanes - rows.shape[1]), F32)
        rows = jnp.concatenate([rows, zeros], axis=1)
    for s, out in enumerate(outs):
        out[...] = rows[s * dest : (s + 1) * dest]


def place_kernel(half, n_proj, order, keep_ref, recv_ref, out_ref):
    blk = lax.axis_index("blk")
    first = blk < half
    low = jnp.where(first, keep_ref[...], recv_ref[...])
    high = jnp.where(first, recv_ref[...], keep_ref[...])
    shifts = out_ref.shape[0]
    width = (shifts + 1) * n_proj

    def by_shift(values):
        found = {offset: values[:, n * width : (n + 1) * width] for n, offset in enumerate(order)}
        lined = []
        for t in range(shifts + 1):
            span = slice(t * n_proj, (t + 1) * n_proj)
            lined += [found[offset][:, span] for offset in range(half)]
        return jnp.concatenate(lined, axis=1)

    def exchanged(values):
        total = (shifts + 1) * half * n_proj
        lanes = 128 * -(-total // 128)
        if lanes > total:
            zeros = jnp.zeros((values.shape[0], lanes - total), F32)
            values = jnp.concatenate([values, zeros], axis=1)
        lane = lax.broadcasted_iota(jnp.int32, values.shape, 1)
        bit = 1
        while bit < half:
            step = bit * n_proj
            other = jnp.where(
                (lane & step) != 0, pltpu.roll(values, step, 1), pltpu.roll(values, lanes - step, 1)
            )
            values = jnp.where((blk & bit) != 0, other, values)
            bit *= 2
        return values

    low, high = exchanged(by_shift(low)), exchanged(by_shift(high))
    span = half * n_proj
    lined = [
        jnp.concatenate([low[:, t * span : (t + 1) * span], high[:, t * span : (t + 1) * span]], axis=1)
        for t in range(shifts + 1)
    ]
    for t in range(shifts):
        out_ref[t] = lined[t] + lined[shifts]


def per_device(
    particles,
    ctf_class,
    orient_prior,
    ctf_curves,
    noise_weight,
    shift_phase,
    trans_index,
    projections,
    orient_subset,
):
    nb, ng = lax.axis_size("blk"), lax.axis_size("grp")
    half = nb // 2
    n_part, n_proj = particles.shape[0], projections.shape[0]
    length = particles.shape[2]
    shifts = shift_phase.shape[0]
    classes_count = ctf_curves.shape[0]
    subsets = orient_prior.shape[1]
    wide = 128 * (length // 128 + 1)
    extra = 128 * (subsets // 128 + 1)
    noise = noise_weight.reshape(1, length)
    shape = jax.ShapeDtypeStruct

    def vmem_out(dims, dtype):
        return pltpu.VMEM(dims, dtype)

    operands = (
        ctf_class,
        orient_subset,
        particles,
        orient_prior,
        ctf_curves,
        noise,
        projections,
        shift_phase,
        trans_index,
    )
    bank, part, curves, noise, angle = pl.pallas_call(
        pack_kernel,
        out_shape=[
            vmem_out((2 * n_proj, wide), BF16),
            vmem_out((2 * n_part, wide + extra), BF16),
            vmem_out(ctf_curves.shape, F32),
            vmem_out(noise.shape, F32),
            vmem_out(shift_phase.shape, F32),
        ],
        in_specs=[pl.BlockSpec(memory_space=pltpu.HBM)] * len(operands),
        out_specs=[_vmem()] * 5,
        scratch_shapes=[
            pltpu.SMEM(ctf_class.shape, jnp.int32),
            pltpu.SMEM(orient_subset.shape, jnp.int32),
            pltpu.SMEM(trans_index.shape, jnp.int32),
            pltpu.VMEM(particles.shape, BF16),
            pltpu.VMEM(orient_prior.shape, BF16),
            pltpu.VMEM(shift_phase.shape, F32),
            pltpu.VMEM(projections.shape, BF16),
            pltpu.SemaphoreType.DMA((len(operands),)),
        ],
        compiler_params=_params(16),
        name="pack",
    )(*[pltpu.with_memory_space_constraint(operand, pltpu.HBM) for operand in operands])

    def swap(value, axis, bit):
        size = lax.axis_size(axis)
        return lax.ppermute(value, axis, [(i, i ^ bit) for i in range(size)])

    def joined(pieces):
        return pieces[0] if len(pieces) == 1 else jnp.concatenate(pieces, axis=0)

    parts, weights = [part, swap(part, "blk", half)], []
    for n in range(ng.bit_length() - 2, -1, -1):
        part = joined(parts)
        parts = [part, swap(part, "grp", 1 << n)]
        weights.append((1 << n, 2 << len(weights)))

    planes, early_order = [bank], [0]
    for n in range(half.bit_length() - 2, 0, -1):
        planes.append(swap(joined(planes), "blk", 1 << n))
        early_order += [offset ^ (1 << n) for offset in early_order]
    last = swap(joined(planes), "blk", 1)
    order = early_order + [offset ^ 1 for offset in early_order]

    cos_part, sin_part, square = pl.pallas_call(
        table_kernel,
        out_shape=[
            vmem_out((shifts, wide), F32),
            vmem_out((shifts, wide), F32),
            vmem_out((2 * classes_count, wide), BF16),
        ],
        in_specs=[_vmem()] * 3,
        out_specs=[_vmem()] * 3,
        compiler_params=_params(8),
        cost_estimate=pl.CostEstimate(flops=4_000_000, bytes_accessed=2_000_000, transcendentals=0),
        name="tables",
    )(curves, noise, angle)

    count = 2 * ng * n_part
    early = late = len(early_order) * n_proj
    shifted, norm = pl.pallas_call(
        functools.partial(shift_kernel, n_proj),
        out_shape=[
            vmem_out((shifts * early, 2 * wide), BF16),
            vmem_out((classes_count, early), F32),
        ],
        in_specs=[_vmem()] * (3 + len(planes)),
        out_specs=[_vmem()] * 2,
        compiler_params=_params(8),
        cost_estimate=pl.CostEstimate(
            flops=6 * early * shifts * wide, bytes_accessed=4_000_000, transcendentals=0
        ),
        name="shift",
    )(cos_part, sin_part, square, *planes)
    weighted, extra_rows, rows = pl.pallas_call(
        functools.partial(
            early_kernel, len(parts), ng, weights, n_part, n_proj, length, subsets
        ),
        out_shape=[
            vmem_out((count, 2 * wide), BF16),
            vmem_out((count, extra), F32),
            vmem_out((count, (shifts + 1) * early), F32),
        ],
        in_specs=[_vmem()] * (2 + len(parts) + len(planes)),
        out_specs=[_vmem()] * 3,
        compiler_params=_params(8),
        cost_estimate=pl.CostEstimate(
            flops=4 * count * early * shifts * wide, bytes_accessed=4_000_000, transcendentals=0
        ),
        name="early",
    )(shifted, norm, *parts, *planes)
    lanes = 128 * -(-(shifts + 1) * half * n_proj // 128)
    keep, give = pl.pallas_call(
        functools.partial(final_kernel, n_proj, length, subsets),
        out_shape=[vmem_out((ng * n_part, lanes), F32)] * 2,
        in_specs=[_vmem()] * 7,
        out_specs=[_vmem()] * 2,
        scratch_shapes=[pltpu.VMEM((shifts * late, 2 * wide), BF16)],
        compiler_params=_params(24),
        cost_estimate=pl.CostEstimate(
            flops=4 * count * late * shifts * wide, bytes_accessed=4_000_000, transcendentals=0
        ),
        name="final",
    )(weighted, extra_rows, rows, cos_part, sin_part, square, last)
    scores = pl.pallas_call(
        functools.partial(place_kernel, half, n_proj, order),
        out_shape=shape((shifts, ng * n_part, nb * n_proj), F32),
        in_specs=[_vmem()] * 2,
        out_specs=_vmem(),
        compiler_params=_params(4),
        name="place",
    )(keep, swap(give, "blk", half))
    return scores.transpose(1, 0, 2)


def solution(mesh):
    placed = (
        P(("blk", "grp"), None, None),
        P(("blk", "grp")),
        P(("blk", "grp"), None),
        P(),
        P(),
        P(),
        P(),
        P(("grp", "blk"), None, None),
        P(("grp", "blk")),
    )
    return jax.shard_map(
        per_device, mesh=mesh, in_specs=placed, out_specs=P("blk", None, "grp"), check_vma=False
    )
```

```python
import functools

import jax
import jax.numpy as jnp
from jax import lax
from jax.experimental import pallas as pl
from jax.experimental.pallas import tpu as pltpu
from jax.sharding import PartitionSpec as P

F32 = jnp.float32
BF16 = jnp.bfloat16
HIGHEST = lax.Precision.HIGHEST
NT_DIMS = (((1,), (1,)), ((), ()))
MIB = 1 << 20


def _vmem():
    return pl.BlockSpec(memory_space=pltpu.VMEM)


def _params(mib):
    return pltpu.CompilerParams(vmem_limit_bytes=mib * MIB)


def pack_kernel(
    class_hbm,
    subset_hbm,
    particles_hbm,
    prior_hbm,
    curves_hbm,
    noise_hbm,
    proj_hbm,
    phase_hbm,
    trans_hbm,
    bank_ref,
    part_ref,
    curves_ref,
    noise_ref,
    angle_ref,
    class_ref,
    subset_ref,
    trans_ref,
    particles_ref,
    prior_ref,
    phase_ref,
    proj_ref,
    sems,
):
    pairs = [
        (proj_hbm, proj_ref),
        (subset_hbm, subset_ref),
        (class_hbm, class_ref),
        (curves_hbm, curves_ref),
        (particles_hbm, particles_ref),
        (noise_hbm, noise_ref),
        (prior_hbm, prior_ref),
        (trans_hbm, trans_ref),
        (phase_hbm, phase_ref),
    ]
    copies = [pltpu.make_async_copy(a, b, sems.at[n]) for n, (a, b) in enumerate(pairs)]
    for copy in copies:
        copy.start()
    n_part, n_proj = particles_ref.shape[0], proj_ref.shape[0]
    length = proj_ref.shape[2]
    wide = bank_ref.shape[1]

    def padded(values, width):
        zeros = jnp.zeros((values.shape[0], width - values.shape[1]), values.dtype)
        return jnp.concatenate([values, zeros], axis=1)

    row = lax.broadcasted_iota(jnp.int32, (n_proj, wide), 0)
    lane = lax.broadcasted_iota(jnp.int32, (n_proj, wide), 1)
    for copy in copies[:2]:
        copy.wait()
    real = jnp.zeros((n_proj, wide), F32)
    imag = jnp.zeros((n_proj, wide), F32)
    for j in range(n_proj):
        both = padded(proj_ref[j].astype(F32), wide)
        real = jnp.where(row == j, both[0:1], real)
        imag = jnp.where(row == j, both[1:2], imag)
    last = slice(wide - 128, wide)
    ends = real[:, last]
    for j in range(n_proj):
        here = (row[:, last] == j) & (lane[:, last] == length)
        ends = jnp.where(here, subset_ref[j].astype(F32), ends)
    real = jnp.concatenate([real[:, : wide - 128], ends], axis=1)
    bank_ref[...] = jnp.concatenate([real, imag], axis=0).astype(BF16)

    for copy in copies[2:]:
        copy.wait()
    subsets = prior_ref.shape[1]
    extra = part_ref.shape[1] - wide
    row = lax.broadcasted_iota(jnp.int32, (2 * n_part, wide), 0)
    row_extra = lax.broadcasted_iota(jnp.int32, (2 * n_part, extra), 0)
    lane_extra = lax.broadcasted_iota(jnp.int32, (2 * n_part, extra), 1)
    prior = padded(prior_ref[...].astype(F32), extra)
    rows = jnp.zeros((2 * n_part, wide), F32)
    rows_extra = jnp.zeros((2 * n_part, extra), F32)
    for i in range(n_part):
        curve = curves_ref[pl.ds(class_ref[i], 1), :] * noise_ref[...]
        both = padded(particles_ref[i].astype(F32) * curve, wide)
        rows = jnp.where(row == i, both[0:1], rows)
        rows = jnp.where(row == n_part + i, both[1:2], rows)
        small = jnp.where(
            lane_extra == subsets,
            class_ref[i].astype(F32),
            jnp.broadcast_to(prior[i : i + 1], rows_extra.shape),
        )
        rows_extra = jnp.where(row_extra == i, small, rows_extra)
    part_ref[:, :wide] = rows.astype(BF16)
    part_ref[:, wide:] = rows_extra.astype(BF16)
    for t in range(phase_ref.shape[0]):
        angle_ref[t : t + 1, :] = phase_ref[pl.ds(trans_ref[t], 1), :]


def sine_cosine(x):
    turns = jnp.floor(x * 0.6366197723675814 + 0.5)
    r = ((x - turns * 1.5703125) - turns * 4.837512969970703125e-4) - turns * 7.549789954891882e-8
    z = r * r
    sine = r + r * z * (-1.6666654611e-1 + z * (8.3321608736e-3 - z * 1.9515295891e-4))
    cosine = 1.0 - 0.5 * z + z * z * (
        4.166664568298827e-2 + z * (-1.388731625493765e-3 + z * 2.443315711809948e-5)
    )
    quarter = turns.astype(jnp.int32) & 3
    swapped = (quarter & 1) == 1
    first, second = jnp.where(swapped, cosine, sine), jnp.where(swapped, sine, cosine)
    first = jnp.where(quarter >= 2, -first, first)
    second = jnp.where((quarter == 1) | (quarter == 2), -second, second)
    return first, second


def split_terms(values):
    high = values.astype(BF16)
    low = (values - high.astype(F32)).astype(BF16)
    return jnp.concatenate([high, low], axis=0)


def table_kernel(curves_ref, noise_ref, angle_ref, cos_ref, sin_ref, square_ref):
    length = curves_ref.shape[1]
    wide = cos_ref.shape[1]
    zeros = jnp.zeros((cos_ref.shape[0], wide - length), F32)
    sine, cosine = sine_cosine(angle_ref[...])
    cos_ref[...] = jnp.concatenate([cosine, zeros], axis=1)
    sin_ref[...] = jnp.concatenate([sine, zeros], axis=1)
    curve = curves_ref[...]
    square = split_terms(curve * curve * noise_ref[...])
    square_ref[...] = jnp.concatenate(
        [square, jnp.zeros((square.shape[0], wide - length), BF16)], axis=1
    )


def shift_rows(shifted_ref, cos_ref, sin_ref, real, imag, at):
    n_proj, wide = real.shape
    shifts = cos_ref.shape[0]
    for t in range(shifts):
        cos_part, sin_part = cos_ref[t : t + 1, :], sin_ref[t : t + 1, :]
        rows = slice((at * shifts + t) * n_proj, (at * shifts + t + 1) * n_proj)
        shifted_ref[rows, :wide] = (cos_part * real + sin_part * imag).astype(BF16)
        shifted_ref[rows, wide:] = (cos_part * imag - sin_part * real).astype(BF16)


def norm_of(square_ref, powers):
    power = jnp.concatenate(powers, axis=0)
    count, classes_count = power.shape[0], square_ref.shape[0] // 2
    table = lax.dot_general(
        square_ref[...], split_terms(power), NT_DIMS, preferred_element_type=F32
    )
    return (
        table[:classes_count, count:] + table[classes_count:, :count] + table[:classes_count, :count]
    )


def shift_bank(banks, shifted_ref, cos_ref, sin_ref, square_ref, n_proj):
    powers = []
    for bank in banks:
        for n in range(bank.shape[0] // (2 * n_proj)):
            both = bank[2 * n_proj * n : 2 * n_proj * (n + 1)].astype(F32)
            real, imag = both[:n_proj], both[n_proj:]
            shift_rows(shifted_ref, cos_ref, sin_ref, real, imag, len(powers))
            powers.append(real * real + imag * imag)
    return norm_of(square_ref, powers)


def shift_kernel(n_proj, cos_ref, sin_ref, square_ref, *rest):
    *banks, shifted_ref, norm_ref = rest
    norm_ref[...] = shift_bank(banks, shifted_ref, cos_ref, sin_ref, square_ref, n_proj)


def added_rows(extra, table, banks, n_proj, length, subsets):
    ids_at = length // 128 * 128
    ids = []
    for bank in banks:
        for n in range(bank.shape[0] // (2 * n_proj)):
            rows = bank[2 * n_proj * n : 2 * n_proj * (n + 1), ids_at : ids_at + 128].astype(F32)
            ids.append(rows[:n_proj])
    ids = jnp.concatenate(ids, axis=0)[:, length - ids_at : length - ids_at + 1]
    count, classes_count = extra.shape[0], table.shape[0]
    class_col = lax.broadcasted_iota(jnp.int32, (count, classes_count), 1).astype(F32)
    onehot = (class_col == extra[:, subsets : subsets + 1]).astype(F32)
    norm = jnp.dot(onehot, table, precision=HIGHEST, preferred_element_type=F32)
    subset_col = lax.broadcasted_iota(jnp.int32, (ids.shape[0], subsets), 1).astype(F32)
    subset_hot = (subset_col == ids).astype(F32).astype(BF16)
    prior = lax.dot_general(
        extra[:, :subsets].astype(BF16), subset_hot, NT_DIMS, preferred_element_type=F32
    )
    return prior - 0.5 * norm


def score_rows(weighted, shifted, added, n_proj):
    cross = lax.dot_general(weighted, shifted, NT_DIMS, preferred_element_type=F32)
    pieces = added.shape[1] // n_proj
    width = cross.shape[1] // pieces
    rows = []
    for n in range(pieces):
        rows += [cross[:, n * width : (n + 1) * width], added[:, n * n_proj : (n + 1) * n_proj]]
    return jnp.concatenate(rows, axis=1)


def early_kernel(
    n_parts, ng, weights, n_part, n_proj, length, subsets, shifted_ref, norm_ref, *rest
):
    parts, (*banks, weighted_ref, extra_ref, rows_ref) = rest[:n_parts], rest[n_parts:]
    g = lax.axis_index("grp")
    wide = weighted_ref.shape[1] // 2

    held = jnp.concatenate([part[...] for part in parts], axis=0)
    count = 2 * ng * n_part
    out_row = lax.broadcasted_iota(jnp.int32, (2 * count, held.shape[0]), 0)
    in_row = lax.broadcasted_iota(jnp.int32, (2 * count, held.shape[0]), 1)
    kind, rest_row = out_row // count, out_row % count
    source, rest_row = rest_row // (ng * n_part), rest_row % (ng * n_part)
    away, i = rest_row // n_part ^ g, rest_row % n_part
    for bit, weight in weights:
        source += jnp.where(away & bit != 0, weight, 0)
    pick = (in_row == source * (2 * n_part) + kind * n_part + i).astype(F32).astype(BF16)
    ordered = jnp.dot(pick, held, preferred_element_type=F32)
    weighted_ref[:, :wide] = ordered[:count, :wide].astype(BF16)
    weighted_ref[:, wide:] = ordered[count:, :wide].astype(BF16)
    extra = ordered[:count, wide:]
    extra_ref[...] = extra
    added = added_rows(extra, norm_ref[...], banks, n_proj, length, subsets)
    rows_ref[...] = score_rows(weighted_ref[...], shifted_ref[...], added, n_proj)


def final_kernel(
    n_proj, length, subsets, weighted_ref, extra_ref, rows_ref, cos_ref, sin_ref, square_ref, last_ref, *rest
):
    *outs, shifted_ref = rest
    table = shift_bank([last_ref], shifted_ref, cos_ref, sin_ref, square_ref, n_proj)
    added = added_rows(extra_ref[...], table, [last_ref], n_proj, length, subsets)
    rows = score_rows(weighted_ref[...], shifted_ref[...], added, n_proj)
    rows = jnp.concatenate([rows_ref[...], rows], axis=1)
    dest, lanes = outs[0].shape
    if rows.shape[1] < lanes:
        zeros = jnp.zeros((rows.shape[0], lanes - rows.shape[1]), F32)
        rows = jnp.concatenate([rows, zeros], axis=1)
    for s, out in enumerate(outs):
        out[...] = rows[s * dest : (s + 1) * dest]


def place_kernel(half, n_proj, order, keep_ref, recv_ref, out_ref):
    blk = lax.axis_index("blk")
    first = blk < half
    low = jnp.where(first, keep_ref[...], recv_ref[...])
    high = jnp.where(first, recv_ref[...], keep_ref[...])
    shifts = out_ref.shape[0]
    width = (shifts + 1) * n_proj

    def by_shift(values):
        found = {offset: values[:, n * width : (n + 1) * width] for n, offset in enumerate(order)}
        lined = []
        for t in range(shifts + 1):
            span = slice(t * n_proj, (t + 1) * n_proj)
            lined += [found[offset][:, span] for offset in range(half)]
        return jnp.concatenate(lined, axis=1)

    def exchanged(values):
        total = (shifts + 1) * half * n_proj
        lanes = 128 * -(-total // 128)
        if lanes > total:
            zeros = jnp.zeros((values.shape[0], lanes - total), F32)
            values = jnp.concatenate([values, zeros], axis=1)
        lane = lax.broadcasted_iota(jnp.int32, values.shape, 1)
        bit = 1
        while bit < half:
            step = bit * n_proj
            other = jnp.where(
                (lane & step) != 0, pltpu.roll(values, step, 1), pltpu.roll(values, lanes - step, 1)
            )
            values = jnp.where((blk & bit) != 0, other, values)
            bit *= 2
        return values

    low, high = exchanged(by_shift(low)), exchanged(by_shift(high))
    span = half * n_proj
    lined = [
        jnp.concatenate([low[:, t * span : (t + 1) * span], high[:, t * span : (t + 1) * span]], axis=1)
        for t in range(shifts + 1)
    ]
    for t in range(shifts):
        out_ref[t] = lined[t] + lined[shifts]


def per_device(
    particles,
    ctf_class,
    orient_prior,
    ctf_curves,
    noise_weight,
    shift_phase,
    trans_index,
    projections,
    orient_subset,
):
    nb, ng = lax.axis_size("blk"), lax.axis_size("grp")
    half = nb // 2
    n_part, n_proj = particles.shape[0], projections.shape[0]
    length = particles.shape[2]
    shifts = shift_phase.shape[0]
    classes_count = ctf_curves.shape[0]
    subsets = orient_prior.shape[1]
    wide = 128 * (length // 128 + 1)
    extra = 128 * (subsets // 128 + 1)
    noise = noise_weight.reshape(1, length)
    shape = jax.ShapeDtypeStruct

    def vmem_out(dims, dtype):
        return pltpu.VMEM(dims, dtype)

    operands = (
        ctf_class,
        orient_subset,
        particles,
        orient_prior,
        ctf_curves,
        noise,
        projections,
        shift_phase,
        trans_index,
    )
    bank, part, curves, noise, angle = pl.pallas_call(
        pack_kernel,
        out_shape=[
            vmem_out((2 * n_proj, wide), BF16),
            vmem_out((2 * n_part, wide + extra), BF16),
            vmem_out(ctf_curves.shape, F32),
            vmem_out(noise.shape, F32),
            vmem_out(shift_phase.shape, F32),
        ],
        in_specs=[pl.BlockSpec(memory_space=pltpu.HBM)] * len(operands),
        out_specs=[_vmem()] * 5,
        scratch_shapes=[
            pltpu.SMEM(ctf_class.shape, jnp.int32),
            pltpu.SMEM(orient_subset.shape, jnp.int32),
            pltpu.SMEM(trans_index.shape, jnp.int32),
            pltpu.VMEM(particles.shape, BF16),
            pltpu.VMEM(orient_prior.shape, BF16),
            pltpu.VMEM(shift_phase.shape, F32),
            pltpu.VMEM(projections.shape, BF16),
            pltpu.SemaphoreType.DMA((len(operands),)),
        ],
        compiler_params=_params(16),
        name="pack",
    )(*[pltpu.with_memory_space_constraint(operand, pltpu.HBM) for operand in operands])

    def swap(value, axis, bit):
        size = lax.axis_size(axis)
        return lax.ppermute(value, axis, [(i, i ^ bit) for i in range(size)])

    def joined(pieces):
        return pieces[0] if len(pieces) == 1 else jnp.concatenate(pieces, axis=0)

    parts, weights = [part, swap(part, "blk", half)], []
    for n in range(ng.bit_length() - 2, -1, -1):
        part = joined(parts)
        parts = [part, swap(part, "grp", 1 << n)]
        weights.append((1 << n, 2 << len(weights)))

    planes, early_order, bit = [bank], [0], 1
    while 2 * bit < half:
        planes.append(swap(joined(planes), "blk", bit))
        early_order += [offset ^ bit for offset in early_order]
        bit *= 2
    last = swap(joined(planes), "blk", bit)
    order = early_order + [offset ^ bit for offset in early_order]

    cos_part, sin_part, square = pl.pallas_call(
        table_kernel,
        out_shape=[
            vmem_out((shifts, wide), F32),
            vmem_out((shifts, wide), F32),
            vmem_out((2 * classes_count, wide), BF16),
        ],
        in_specs=[_vmem()] * 3,
        out_specs=[_vmem()] * 3,
        compiler_params=_params(8),
        cost_estimate=pl.CostEstimate(flops=4_000_000, bytes_accessed=2_000_000, transcendentals=0),
        name="tables",
    )(curves, noise, angle)

    count = 2 * ng * n_part
    early = late = len(early_order) * n_proj
    shifted, norm = pl.pallas_call(
        functools.partial(shift_kernel, n_proj),
        out_shape=[
            vmem_out((shifts * early, 2 * wide), BF16),
            vmem_out((classes_count, early), F32),
        ],
        in_specs=[_vmem()] * (3 + len(planes)),
        out_specs=[_vmem()] * 2,
        compiler_params=_params(8),
        cost_estimate=pl.CostEstimate(
            flops=6 * early * shifts * wide, bytes_accessed=4_000_000, transcendentals=0
        ),
        name="shift",
    )(cos_part, sin_part, square, *planes)
    weighted, extra_rows, rows = pl.pallas_call(
        functools.partial(
            early_kernel, len(parts), ng, weights, n_part, n_proj, length, subsets
        ),
        out_shape=[
            vmem_out((count, 2 * wide), BF16),
            vmem_out((count, extra), F32),
            vmem_out((count, (shifts + 1) * early), F32),
        ],
        in_specs=[_vmem()] * (2 + len(parts) + len(planes)),
        out_specs=[_vmem()] * 3,
        compiler_params=_params(8),
        cost_estimate=pl.CostEstimate(
            flops=4 * count * early * shifts * wide, bytes_accessed=4_000_000, transcendentals=0
        ),
        name="early",
    )(shifted, norm, *parts, *planes)
    lanes = 128 * -(-(shifts + 1) * half * n_proj // 128)
    keep, give = pl.pallas_call(
        functools.partial(final_kernel, n_proj, length, subsets),
        out_shape=[vmem_out((ng * n_part, lanes), F32)] * 2,
        in_specs=[_vmem()] * 7,
        out_specs=[_vmem()] * 2,
        scratch_shapes=[pltpu.VMEM((shifts * late, 2 * wide), BF16)],
        compiler_params=_params(24),
        cost_estimate=pl.CostEstimate(
            flops=4 * count * late * shifts * wide, bytes_accessed=4_000_000, transcendentals=0
        ),
        name="final",
    )(weighted, extra_rows, rows, cos_part, sin_part, square, last)
    scores = pl.pallas_call(
        functools.partial(place_kernel, half, n_proj, order),
        out_shape=shape((shifts, ng * n_part, nb * n_proj), F32),
        in_specs=[_vmem()] * 2,
        out_specs=_vmem(),
        compiler_params=_params(4),
        name="place",
    )(keep, swap(give, "blk", half))
    return scores.transpose(1, 0, 2)


def solution(mesh):
    placed = (
        P(("blk", "grp"), None, None),
        P(("blk", "grp")),
        P(("blk", "grp"), None),
        P(),
        P(),
        P(),
        P(),
        P(("grp", "blk"), None, None),
        P(("grp", "blk")),
    )
    return jax.shard_map(
        per_device, mesh=mesh, in_specs=placed, out_specs=P("blk", None, "grp"), check_vma=False
    )
```

```python
import functools

import jax
import jax.numpy as jnp
from jax import lax
from jax.experimental import pallas as pl
from jax.experimental.pallas import tpu as pltpu
from jax.sharding import PartitionSpec as P

F32 = jnp.float32
BF16 = jnp.bfloat16
HIGHEST = lax.Precision.HIGHEST
NT_DIMS = (((1,), (1,)), ((), ()))
MIB = 1 << 20


def _vmem():
    return pl.BlockSpec(memory_space=pltpu.VMEM)


def _params(mib):
    return pltpu.CompilerParams(vmem_limit_bytes=mib * MIB)


def pack_kernel(
    class_hbm,
    subset_hbm,
    particles_hbm,
    prior_hbm,
    curves_hbm,
    noise_hbm,
    proj_hbm,
    phase_hbm,
    trans_hbm,
    bank_ref,
    part_ref,
    curves_ref,
    noise_ref,
    angle_ref,
    class_ref,
    subset_ref,
    trans_ref,
    particles_ref,
    prior_ref,
    phase_ref,
    proj_ref,
    sems,
):
    pairs = [
        (proj_hbm, proj_ref),
        (subset_hbm, subset_ref),
        (class_hbm, class_ref),
        (curves_hbm, curves_ref),
        (particles_hbm, particles_ref),
        (noise_hbm, noise_ref),
        (prior_hbm, prior_ref),
        (trans_hbm, trans_ref),
        (phase_hbm, phase_ref),
    ]
    copies = [pltpu.make_async_copy(a, b, sems.at[n]) for n, (a, b) in enumerate(pairs)]
    for copy in copies:
        copy.start()
    n_part, n_proj = particles_ref.shape[0], proj_ref.shape[0]
    length = proj_ref.shape[2]
    wide = bank_ref.shape[1]

    def padded(values, width):
        zeros = jnp.zeros((values.shape[0], width - values.shape[1]), values.dtype)
        return jnp.concatenate([values, zeros], axis=1)

    row = lax.broadcasted_iota(jnp.int32, (n_proj, wide), 0)
    lane = lax.broadcasted_iota(jnp.int32, (n_proj, wide), 1)
    for copy in copies[:2]:
        copy.wait()
    real = jnp.zeros((n_proj, wide), F32)
    imag = jnp.zeros((n_proj, wide), F32)
    for j in range(n_proj):
        both = padded(proj_ref[j].astype(F32), wide)
        real = jnp.where(row == j, both[0:1], real)
        imag = jnp.where(row == j, both[1:2], imag)
    last = slice(wide - 128, wide)
    ends = real[:, last]
    for j in range(n_proj):
        here = (row[:, last] == j) & (lane[:, last] == length)
        ends = jnp.where(here, subset_ref[j].astype(F32), ends)
    real = jnp.concatenate([real[:, : wide - 128], ends], axis=1)
    bank_ref[...] = jnp.concatenate([real, imag], axis=0).astype(BF16)

    for copy in copies[2:]:
        copy.wait()
    subsets = prior_ref.shape[1]
    extra = part_ref.shape[1] - wide
    row = lax.broadcasted_iota(jnp.int32, (2 * n_part, wide), 0)
    row_extra = lax.broadcasted_iota(jnp.int32, (2 * n_part, extra), 0)
    lane_extra = lax.broadcasted_iota(jnp.int32, (2 * n_part, extra), 1)
    prior = padded(prior_ref[...].astype(F32), extra)
    rows = jnp.zeros((2 * n_part, wide), F32)
    rows_extra = jnp.zeros((2 * n_part, extra), F32)
    for i in range(n_part):
        curve = curves_ref[pl.ds(class_ref[i], 1), :] * noise_ref[...]
        both = padded(particles_ref[i].astype(F32) * curve, wide)
        rows = jnp.where(row == i, both[0:1], rows)
        rows = jnp.where(row == n_part + i, both[1:2], rows)
        small = jnp.where(
            lane_extra == subsets,
            class_ref[i].astype(F32),
            jnp.broadcast_to(prior[i : i + 1], rows_extra.shape),
        )
        rows_extra = jnp.where(row_extra == i, small, rows_extra)
    part_ref[:, :wide] = rows.astype(BF16)
    part_ref[:, wide:] = rows_extra.astype(BF16)
    for t in range(phase_ref.shape[0]):
        angle_ref[t : t + 1, :] = phase_ref[pl.ds(trans_ref[t], 1), :]


def sine_cosine(x):
    turns = jnp.floor(x * 0.6366197723675814 + 0.5)
    r = ((x - turns * 1.5703125) - turns * 4.837512969970703125e-4) - turns * 7.549789954891882e-8
    z = r * r
    sine = r + r * z * (-1.6666654611e-1 + z * (8.3321608736e-3 - z * 1.9515295891e-4))
    cosine = 1.0 - 0.5 * z + z * z * (
        4.166664568298827e-2 + z * (-1.388731625493765e-3 + z * 2.443315711809948e-5)
    )
    quarter = turns.astype(jnp.int32) & 3
    swapped = (quarter & 1) == 1
    first, second = jnp.where(swapped, cosine, sine), jnp.where(swapped, sine, cosine)
    first = jnp.where(quarter >= 2, -first, first)
    second = jnp.where((quarter == 1) | (quarter == 2), -second, second)
    return first, second


def split_terms(values):
    high = values.astype(BF16)
    low = (values - high.astype(F32)).astype(BF16)
    return jnp.concatenate([high, low], axis=0)


def table_kernel(curves_ref, noise_ref, angle_ref, cos_ref, sin_ref, square_ref):
    length = curves_ref.shape[1]
    wide = cos_ref.shape[1]
    zeros = jnp.zeros((cos_ref.shape[0], wide - length), F32)
    sine, cosine = sine_cosine(angle_ref[...])
    cos_ref[...] = jnp.concatenate([cosine, zeros], axis=1)
    sin_ref[...] = jnp.concatenate([sine, zeros], axis=1)
    curve = curves_ref[...]
    square = split_terms(curve * curve * noise_ref[...])
    square_ref[...] = jnp.concatenate(
        [square, jnp.zeros((square.shape[0], wide - length), BF16)], axis=1
    )


def score_pieces(weighted_ref, banks, cos_ref, sin_ref, square_ref, n_proj):
    shifts, wide = cos_ref.shape
    classes_count = square_ref.shape[0] // 2
    step = 256 if wide % 256 == 0 else 128
    cross, table = None, None
    for at in range(0, wide, step):
        span = slice(at, at + step)
        reals, imags = [], []
        for bank in banks:
            for first in range(0, bank.shape[0], 2 * n_proj):
                both = bank[first : first + 2 * n_proj, span].astype(F32)
                reals.append(both[:n_proj])
                imags.append(both[n_proj:])
        real, imag = jnp.concatenate(reals, axis=0), jnp.concatenate(imags, axis=0)
        real_rows, imag_rows = [], []
        for t in range(shifts):
            cos_part, sin_part = cos_ref[t : t + 1, span], sin_ref[t : t + 1, span]
            real_rows.append((cos_part * real + sin_part * imag).astype(BF16))
            imag_rows.append((cos_part * imag - sin_part * real).astype(BF16))
        terms = lax.dot_general(
            weighted_ref[:, span],
            jnp.concatenate(real_rows, axis=0),
            NT_DIMS,
            preferred_element_type=F32,
        ) + lax.dot_general(
            weighted_ref[:, wide + at : wide + at + step],
            jnp.concatenate(imag_rows, axis=0),
            NT_DIMS,
            preferred_element_type=F32,
        )
        power = split_terms(real * real + imag * imag)
        norms = lax.dot_general(
            square_ref[:, span], power, NT_DIMS, preferred_element_type=F32
        )
        cross = terms if cross is None else cross + terms
        table = norms if table is None else table + norms
    count = table.shape[1] // 2
    table = (
        table[:classes_count, count:] + table[classes_count:, :count] + table[:classes_count, :count]
    )
    return cross, table


def in_lanes(values, blk, bits, n_proj, lanes):
    if values.shape[1] < lanes:
        zeros = jnp.zeros((values.shape[0], lanes - values.shape[1]), F32)
        values = jnp.concatenate([values, zeros], axis=1)
    lane = lax.broadcasted_iota(jnp.int32, values.shape, 1)
    for bit in bits:
        step = bit * n_proj
        other = jnp.where(
            (lane & step) != 0, pltpu.roll(values, step, 1), pltpu.roll(values, lanes - step, 1)
        )
        values = jnp.where((blk & bit) != 0, other, values)
    return values


def added_rows(extra, table, banks, n_proj, length, subsets):
    ids_at = length // 128 * 128
    ids = []
    for bank in banks:
        for n in range(bank.shape[0] // (2 * n_proj)):
            rows = bank[2 * n_proj * n : 2 * n_proj * (n + 1), ids_at : ids_at + 128].astype(F32)
            ids.append(rows[:n_proj])
    ids = jnp.concatenate(ids, axis=0)[:, length - ids_at : length - ids_at + 1]
    count, classes_count = extra.shape[0], table.shape[0]
    class_col = lax.broadcasted_iota(jnp.int32, (count, classes_count), 1).astype(F32)
    onehot = (class_col == extra[:, subsets : subsets + 1]).astype(F32)
    norm = jnp.dot(onehot, table, precision=HIGHEST, preferred_element_type=F32)
    subset_col = lax.broadcasted_iota(jnp.int32, (ids.shape[0], subsets), 1).astype(F32)
    subset_hot = (subset_col == ids).astype(F32).astype(BF16)
    prior = lax.dot_general(
        extra[:, :subsets].astype(BF16), subset_hot, NT_DIMS, preferred_element_type=F32
    )
    return prior - 0.5 * norm


def early_kernel(
    n_parts, ng, weights, bits, n_part, n_proj, length, subsets, cos_ref, sin_ref, square_ref, *rest
):
    parts, (*banks, weighted_ref, extra_ref, rows_ref) = rest[:n_parts], rest[n_parts:]
    blk, g = lax.axis_index("blk"), lax.axis_index("grp")
    wide = weighted_ref.shape[1] // 2

    held = jnp.concatenate([part[...] for part in parts], axis=0)
    count = 2 * ng * n_part
    out_row = lax.broadcasted_iota(jnp.int32, (2 * count, held.shape[0]), 0)
    in_row = lax.broadcasted_iota(jnp.int32, (2 * count, held.shape[0]), 1)
    kind, rest_row = out_row // count, out_row % count
    source, rest_row = rest_row // (ng * n_part), rest_row % (ng * n_part)
    away, i = rest_row // n_part ^ g, rest_row % n_part
    for bit, weight in weights:
        source += jnp.where(away & bit != 0, weight, 0)
    pick = (in_row == source * (2 * n_part) + kind * n_part + i).astype(F32).astype(BF16)
    ordered = jnp.dot(pick, held, preferred_element_type=F32)
    weighted_ref[:, :wide] = ordered[:count, :wide].astype(BF16)
    weighted_ref[:, wide:] = ordered[count:, :wide].astype(BF16)
    extra = ordered[:count, wide:]
    extra_ref[...] = extra
    cross, table = score_pieces(weighted_ref, banks, cos_ref, sin_ref, square_ref, n_proj)
    added = added_rows(extra, table, banks, n_proj, length, subsets)
    rows = jnp.concatenate([cross, added], axis=1)
    rows_ref[...] = in_lanes(rows, blk, bits, n_proj, rows_ref.shape[1])


def final_kernel(
    bits, n_proj, length, subsets, weighted_ref, extra_ref, rows_ref, cos_ref, sin_ref, square_ref, last_ref, *outs
):
    blk = lax.axis_index("blk")
    cross, table = score_pieces(weighted_ref, [last_ref], cos_ref, sin_ref, square_ref, n_proj)
    added = added_rows(extra_ref[...], table, [last_ref], n_proj, length, subsets)
    rows = jnp.concatenate([cross, added], axis=1)
    dest, lanes = outs[0].shape[0], rows_ref.shape[1]
    rows = in_lanes(rows, blk, bits, n_proj, lanes)
    for s, out in enumerate(outs):
        out[:, :lanes] = rows_ref[s * dest : (s + 1) * dest, :]
        out[:, lanes:] = rows[s * dest : (s + 1) * dest]


def place_kernel(half, keep_ref, recv_ref, out_ref):
    blk = lax.axis_index("blk")
    own_first, early_first = blk < half, (blk & (half // 2)) == 0
    keep, recv = keep_ref[...], recv_ref[...]
    lanes = keep.shape[1] // 2
    parts = []
    for values in (jnp.where(own_first, keep, recv), jnp.where(own_first, recv, keep)):
        early, late = values[:, :lanes], values[:, lanes:]
        parts += [jnp.where(early_first, early, late), jnp.where(early_first, late, early)]
    shifts, _, width = out_ref.shape
    width = width // 4

    def line(t):
        return jnp.concatenate([part[:, t * width : (t + 1) * width] for part in parts], axis=1)

    added = line(shifts)
    for t in range(shifts):
        out_ref[t] = line(t) + added


def per_device(
    particles,
    ctf_class,
    orient_prior,
    ctf_curves,
    noise_weight,
    shift_phase,
    trans_index,
    projections,
    orient_subset,
):
    nb, ng = lax.axis_size("blk"), lax.axis_size("grp")
    half = nb // 2
    n_part, n_proj = particles.shape[0], projections.shape[0]
    length = particles.shape[2]
    shifts = shift_phase.shape[0]
    classes_count = ctf_curves.shape[0]
    subsets = orient_prior.shape[1]
    wide = 128 * (length // 128 + 1)
    extra = 128 * (subsets // 128 + 1)
    noise = noise_weight.reshape(1, length)
    shape = jax.ShapeDtypeStruct

    def vmem_out(dims, dtype):
        return pltpu.VMEM(dims, dtype)

    operands = (
        ctf_class,
        orient_subset,
        particles,
        orient_prior,
        ctf_curves,
        noise,
        projections,
        shift_phase,
        trans_index,
    )
    bank, part, curves, noise, angle = pl.pallas_call(
        pack_kernel,
        out_shape=[
            vmem_out((2 * n_proj, wide), BF16),
            vmem_out((2 * n_part, wide + extra), BF16),
            vmem_out(ctf_curves.shape, F32),
            vmem_out(noise.shape, F32),
            vmem_out(shift_phase.shape, F32),
        ],
        in_specs=[pl.BlockSpec(memory_space=pltpu.HBM)] * len(operands),
        out_specs=[_vmem()] * 5,
        scratch_shapes=[
            pltpu.SMEM(ctf_class.shape, jnp.int32),
            pltpu.SMEM(orient_subset.shape, jnp.int32),
            pltpu.SMEM(trans_index.shape, jnp.int32),
            pltpu.VMEM(particles.shape, BF16),
            pltpu.VMEM(orient_prior.shape, BF16),
            pltpu.VMEM(shift_phase.shape, F32),
            pltpu.VMEM(projections.shape, BF16),
            pltpu.SemaphoreType.DMA((len(operands),)),
        ],
        compiler_params=_params(16),
        name="pack",
    )(*[pltpu.with_memory_space_constraint(operand, pltpu.HBM) for operand in operands])

    def swap(value, axis, bit):
        size = lax.axis_size(axis)
        return lax.ppermute(value, axis, [(i, i ^ bit) for i in range(size)])

    def joined(pieces):
        return pieces[0] if len(pieces) == 1 else jnp.concatenate(pieces, axis=0)

    across = swap(part, "blk", half)
    planes, bit = [bank], 1
    while 2 * bit < half:
        planes.append(swap(joined(planes), "blk", bit))
        bit *= 2
    last = swap(joined(planes), "blk", bit)

    cos_part, sin_part, square = pl.pallas_call(
        table_kernel,
        out_shape=[
            vmem_out((shifts, wide), F32),
            vmem_out((shifts, wide), F32),
            vmem_out((2 * classes_count, wide), BF16),
        ],
        in_specs=[_vmem()] * 3,
        out_specs=[_vmem()] * 3,
        compiler_params=_params(8),
        cost_estimate=pl.CostEstimate(flops=4_000_000, bytes_accessed=2_000_000, transcendentals=0),
        name="tables",
    )(curves, noise, angle)

    across, planes[-1], cos_part = lax.optimization_barrier((across, planes[-1], cos_part))
    parts, weights = [part, across], []
    for n in range(ng.bit_length() - 2, -1, -1):
        part = joined(parts)
        parts = [part, swap(part, "grp", 1 << n)]
        weights.append((1 << n, 2 << len(weights)))

    count = 2 * ng * n_part
    early = half // 2 * n_proj
    lanes = 128 * -(-(shifts + 1) * early // 128)
    bits = [1 << n for n in range(half.bit_length() - 2)]
    weighted, extra_rows, rows = pl.pallas_call(
        functools.partial(
            early_kernel, len(parts), ng, weights, bits, n_part, n_proj, length, subsets
        ),
        out_shape=[
            vmem_out((count, 2 * wide), BF16),
            vmem_out((count, extra), F32),
            vmem_out((count, lanes), F32),
        ],
        in_specs=[_vmem()] * (3 + len(parts) + len(planes)),
        out_specs=[_vmem()] * 3,
        compiler_params=_params(16),
        cost_estimate=pl.CostEstimate(
            flops=4 * count * early * shifts * wide, bytes_accessed=4_000_000, transcendentals=0
        ),
        name="early",
    )(cos_part, sin_part, square, *parts, *planes)
    keep, give = pl.pallas_call(
        functools.partial(final_kernel, bits, n_proj, length, subsets),
        out_shape=[vmem_out((ng * n_part, 2 * lanes), F32)] * 2,
        in_specs=[_vmem()] * 7,
        out_specs=[_vmem()] * 2,
        compiler_params=_params(16),
        cost_estimate=pl.CostEstimate(
            flops=4 * count * early * shifts * wide, bytes_accessed=4_000_000, transcendentals=0
        ),
        name="final",
    )(weighted, extra_rows, rows, cos_part, sin_part, square, last)
    scores = pl.pallas_call(
        functools.partial(place_kernel, half),
        out_shape=shape((shifts, ng * n_part, nb * n_proj), F32),
        in_specs=[_vmem()] * 2,
        out_specs=_vmem(),
        compiler_params=_params(4),
        name="place",
    )(keep, swap(give, "blk", half))
    return scores.transpose(1, 0, 2)


def solution(mesh):
    placed = (
        P(("blk", "grp"), None, None),
        P(("blk", "grp")),
        P(("blk", "grp"), None),
        P(),
        P(),
        P(),
        P(),
        P(("grp", "blk"), None, None),
        P(("grp", "blk")),
    )
    return jax.shard_map(
        per_device, mesh=mesh, in_specs=placed, out_specs=P("blk", None, "grp"), check_vma=False
    )
```

```python
import functools

import jax
import jax.numpy as jnp
from jax import lax
from jax.experimental import pallas as pl
from jax.experimental.pallas import tpu as pltpu
from jax.sharding import PartitionSpec as P

F32 = jnp.float32
BF16 = jnp.bfloat16
HIGHEST = lax.Precision.HIGHEST
NT_DIMS = (((1,), (1,)), ((), ()))
MIB = 1 << 20


def _vmem():
    return pl.BlockSpec(memory_space=pltpu.VMEM)


def _params(mib):
    return pltpu.CompilerParams(vmem_limit_bytes=mib * MIB)


def pack_kernel(
    class_hbm,
    subset_hbm,
    particles_hbm,
    prior_hbm,
    curves_hbm,
    noise_hbm,
    proj_hbm,
    phase_hbm,
    trans_hbm,
    bank_ref,
    part_ref,
    curves_ref,
    noise_ref,
    angle_ref,
    class_ref,
    subset_ref,
    trans_ref,
    particles_ref,
    prior_ref,
    phase_ref,
    proj_ref,
    sems,
):
    pairs = [
        (proj_hbm, proj_ref),
        (subset_hbm, subset_ref),
        (class_hbm, class_ref),
        (curves_hbm, curves_ref),
        (particles_hbm, particles_ref),
        (noise_hbm, noise_ref),
        (prior_hbm, prior_ref),
        (trans_hbm, trans_ref),
        (phase_hbm, phase_ref),
    ]
    copies = [pltpu.make_async_copy(a, b, sems.at[n]) for n, (a, b) in enumerate(pairs)]
    for copy in copies:
        copy.start()
    n_part, n_proj = particles_ref.shape[0], proj_ref.shape[0]
    length = proj_ref.shape[2]
    wide = bank_ref.shape[1]

    def padded(values, width):
        zeros = jnp.zeros((values.shape[0], width - values.shape[1]), values.dtype)
        return jnp.concatenate([values, zeros], axis=1)

    row = lax.broadcasted_iota(jnp.int32, (n_proj, wide), 0)
    lane = lax.broadcasted_iota(jnp.int32, (n_proj, wide), 1)
    for copy in copies[:2]:
        copy.wait()
    real = jnp.zeros((n_proj, wide), F32)
    imag = jnp.zeros((n_proj, wide), F32)
    for j in range(n_proj):
        both = padded(proj_ref[j].astype(F32), wide)
        real = jnp.where(row == j, both[0:1], real)
        imag = jnp.where(row == j, both[1:2], imag)
    last = slice(wide - 128, wide)
    ends = real[:, last]
    for j in range(n_proj):
        here = (row[:, last] == j) & (lane[:, last] == length)
        ends = jnp.where(here, subset_ref[j].astype(F32), ends)
    real = jnp.concatenate([real[:, : wide - 128], ends], axis=1)
    bank_ref[...] = jnp.concatenate([real, imag], axis=0).astype(BF16)

    for copy in copies[2:]:
        copy.wait()
    subsets = prior_ref.shape[1]
    extra = part_ref.shape[1] - wide
    row = lax.broadcasted_iota(jnp.int32, (2 * n_part, wide), 0)
    row_extra = lax.broadcasted_iota(jnp.int32, (2 * n_part, extra), 0)
    lane_extra = lax.broadcasted_iota(jnp.int32, (2 * n_part, extra), 1)
    prior = padded(prior_ref[...].astype(F32), extra)
    rows = jnp.zeros((2 * n_part, wide), F32)
    rows_extra = jnp.zeros((2 * n_part, extra), F32)
    for i in range(n_part):
        curve = curves_ref[pl.ds(class_ref[i], 1), :] * noise_ref[...]
        both = padded(particles_ref[i].astype(F32) * curve, wide)
        rows = jnp.where(row == i, both[0:1], rows)
        rows = jnp.where(row == n_part + i, both[1:2], rows)
        small = jnp.where(
            lane_extra == subsets,
            class_ref[i].astype(F32),
            jnp.broadcast_to(prior[i : i + 1], rows_extra.shape),
        )
        rows_extra = jnp.where(row_extra == i, small, rows_extra)
    part_ref[:, :wide] = rows.astype(BF16)
    part_ref[:, wide:] = rows_extra.astype(BF16)
    for t in range(phase_ref.shape[0]):
        angle_ref[t : t + 1, :] = phase_ref[pl.ds(trans_ref[t], 1), :]


def sine_cosine(x):
    turns = jnp.floor(x * 0.6366197723675814 + 0.5)
    r = ((x - turns * 1.5703125) - turns * 4.837512969970703125e-4) - turns * 7.549789954891882e-8
    z = r * r
    sine = r + r * z * (-1.6666654611e-1 + z * (8.3321608736e-3 - z * 1.9515295891e-4))
    cosine = 1.0 - 0.5 * z + z * z * (
        4.166664568298827e-2 + z * (-1.388731625493765e-3 + z * 2.443315711809948e-5)
    )
    quarter = turns.astype(jnp.int32) & 3
    swapped = (quarter & 1) == 1
    first, second = jnp.where(swapped, cosine, sine), jnp.where(swapped, sine, cosine)
    first = jnp.where(quarter >= 2, -first, first)
    second = jnp.where((quarter == 1) | (quarter == 2), -second, second)
    return first, second


def split_terms(values):
    high = values.astype(BF16)
    low = (values - high.astype(F32)).astype(BF16)
    return jnp.concatenate([high, low], axis=0)


def table_kernel(curves_ref, noise_ref, angle_ref, cos_ref, sin_ref, square_ref):
    length = curves_ref.shape[1]
    wide = cos_ref.shape[1]
    zeros = jnp.zeros((cos_ref.shape[0], wide - length), F32)
    sine, cosine = sine_cosine(angle_ref[...])
    cos_ref[...] = jnp.concatenate([cosine, zeros], axis=1)
    sin_ref[...] = jnp.concatenate([sine, zeros], axis=1)
    curve = curves_ref[...]
    square = split_terms(curve * curve * noise_ref[...])
    square_ref[...] = jnp.concatenate(
        [square, jnp.zeros((square.shape[0], wide - length), BF16)], axis=1
    )


def score_pieces(weighted_ref, banks, cos_ref, sin_ref, square_ref, n_proj):
    shifts, wide = cos_ref.shape
    classes_count = square_ref.shape[0] // 2
    step = 256 if wide % 256 == 0 else 128
    cross, table = None, None
    for at in range(0, wide, step):
        span = slice(at, at + step)
        reals, imags = [], []
        for bank in banks:
            for first in range(0, bank.shape[0], 2 * n_proj):
                both = bank[first : first + 2 * n_proj, span].astype(F32)
                reals.append(both[:n_proj])
                imags.append(both[n_proj:])
        real, imag = jnp.concatenate(reals, axis=0), jnp.concatenate(imags, axis=0)
        real_rows, imag_rows = [], []
        for t in range(shifts):
            cos_part, sin_part = cos_ref[t : t + 1, span], sin_ref[t : t + 1, span]
            real_rows.append((cos_part * real + sin_part * imag).astype(BF16))
            imag_rows.append((cos_part * imag - sin_part * real).astype(BF16))
        terms = lax.dot_general(
            weighted_ref[:, span],
            jnp.concatenate(real_rows, axis=0),
            NT_DIMS,
            preferred_element_type=F32,
        ) + lax.dot_general(
            weighted_ref[:, wide + at : wide + at + step],
            jnp.concatenate(imag_rows, axis=0),
            NT_DIMS,
            preferred_element_type=F32,
        )
        power = split_terms(real * real + imag * imag)
        norms = lax.dot_general(
            square_ref[:, span], power, NT_DIMS, preferred_element_type=F32
        )
        cross = terms if cross is None else cross + terms
        table = norms if table is None else table + norms
    count = table.shape[1] // 2
    table = (
        table[:classes_count, count:] + table[classes_count:, :count] + table[:classes_count, :count]
    )
    return cross, table


def in_lanes(values, blk, bits, n_proj, lanes):
    if values.shape[1] < lanes:
        zeros = jnp.zeros((values.shape[0], lanes - values.shape[1]), F32)
        values = jnp.concatenate([values, zeros], axis=1)
    lane = lax.broadcasted_iota(jnp.int32, values.shape, 1)
    for bit in bits:
        step = bit * n_proj
        other = jnp.where(
            (lane & step) != 0, pltpu.roll(values, step, 1), pltpu.roll(values, lanes - step, 1)
        )
        values = jnp.where((blk & bit) != 0, other, values)
    return values


def added_rows(extra, table, banks, n_proj, length, subsets):
    ids_at = length // 128 * 128
    ids = []
    for bank in banks:
        for n in range(bank.shape[0] // (2 * n_proj)):
            rows = bank[2 * n_proj * n : 2 * n_proj * (n + 1), ids_at : ids_at + 128].astype(F32)
            ids.append(rows[:n_proj])
    ids = jnp.concatenate(ids, axis=0)[:, length - ids_at : length - ids_at + 1]
    count, classes_count = extra.shape[0], table.shape[0]
    class_col = lax.broadcasted_iota(jnp.int32, (count, classes_count), 1).astype(F32)
    onehot = (class_col == extra[:, subsets : subsets + 1]).astype(F32)
    norm = jnp.dot(onehot, table, precision=HIGHEST, preferred_element_type=F32)
    subset_col = lax.broadcasted_iota(jnp.int32, (ids.shape[0], subsets), 1).astype(F32)
    subset_hot = (subset_col == ids).astype(F32).astype(BF16)
    prior = lax.dot_general(
        extra[:, :subsets].astype(BF16), subset_hot, NT_DIMS, preferred_element_type=F32
    )
    return prior - 0.5 * norm


def early_kernel(
    n_parts, ng, weights, bits, n_part, n_proj, length, subsets, cos_ref, sin_ref, square_ref, *rest
):
    parts, (*banks, weighted_ref, extra_ref, rows_ref) = rest[:n_parts], rest[n_parts:]
    blk, g = lax.axis_index("blk"), lax.axis_index("grp")
    wide = weighted_ref.shape[1] // 2

    held = jnp.concatenate([part[...] for part in parts], axis=0)
    count = 2 * ng * n_part
    out_row = lax.broadcasted_iota(jnp.int32, (2 * count, held.shape[0]), 0)
    in_row = lax.broadcasted_iota(jnp.int32, (2 * count, held.shape[0]), 1)
    kind, rest_row = out_row // count, out_row % count
    source, rest_row = rest_row // (ng * n_part), rest_row % (ng * n_part)
    away, i = rest_row // n_part ^ g, rest_row % n_part
    for bit, weight in weights:
        source += jnp.where(away & bit != 0, weight, 0)
    pick = (in_row == source * (2 * n_part) + kind * n_part + i).astype(F32).astype(BF16)
    ordered = jnp.dot(pick, held, preferred_element_type=F32)
    weighted_ref[:, :wide] = ordered[:count, :wide].astype(BF16)
    weighted_ref[:, wide:] = ordered[count:, :wide].astype(BF16)
    extra = ordered[:count, wide:]
    extra_ref[...] = extra
    cross, table = score_pieces(weighted_ref, banks, cos_ref, sin_ref, square_ref, n_proj)
    added = added_rows(extra, table, banks, n_proj, length, subsets)
    rows = jnp.concatenate([cross, added], axis=1)
    rows_ref[...] = in_lanes(rows, blk, bits, n_proj, rows_ref.shape[1])


def final_kernel(
    bits, n_proj, length, subsets, weighted_ref, extra_ref, rows_ref, cos_ref, sin_ref, square_ref, last_ref, *outs
):
    blk = lax.axis_index("blk")
    cross, table = score_pieces(weighted_ref, [last_ref], cos_ref, sin_ref, square_ref, n_proj)
    added = added_rows(extra_ref[...], table, [last_ref], n_proj, length, subsets)
    rows = jnp.concatenate([cross, added], axis=1)
    dest, lanes = outs[0].shape[0], rows_ref.shape[1]
    rows = in_lanes(rows, blk, bits, n_proj, lanes)
    for s, out in enumerate(outs):
        out[:, :lanes] = rows_ref[s * dest : (s + 1) * dest, :]
        out[:, lanes:] = rows[s * dest : (s + 1) * dest]


def place_kernel(half, keep_ref, recv_ref, out_ref):
    blk = lax.axis_index("blk")
    own_first, early_first = blk < half, (blk & (half // 2)) == 0
    keep, recv = keep_ref[...], recv_ref[...]
    lanes = keep.shape[1] // 2
    parts = []
    for values in (jnp.where(own_first, keep, recv), jnp.where(own_first, recv, keep)):
        early, late = values[:, :lanes], values[:, lanes:]
        parts += [jnp.where(early_first, early, late), jnp.where(early_first, late, early)]
    shifts, _, width = out_ref.shape
    width = width // 4

    def line(t):
        return jnp.concatenate([part[:, t * width : (t + 1) * width] for part in parts], axis=1)

    added = line(shifts)
    for t in range(shifts):
        out_ref[t] = line(t) + added


def per_device(
    particles,
    ctf_class,
    orient_prior,
    ctf_curves,
    noise_weight,
    shift_phase,
    trans_index,
    projections,
    orient_subset,
):
    nb, ng = lax.axis_size("blk"), lax.axis_size("grp")
    half = nb // 2
    n_part, n_proj = particles.shape[0], projections.shape[0]
    length = particles.shape[2]
    shifts = shift_phase.shape[0]
    classes_count = ctf_curves.shape[0]
    subsets = orient_prior.shape[1]
    wide = 128 * (length // 128 + 1)
    extra = 128 * (subsets // 128 + 1)
    noise = noise_weight.reshape(1, length)
    shape = jax.ShapeDtypeStruct

    def vmem_out(dims, dtype):
        return pltpu.VMEM(dims, dtype)

    operands = (
        ctf_class,
        orient_subset,
        particles,
        orient_prior,
        ctf_curves,
        noise,
        projections,
        shift_phase,
        trans_index,
    )
    bank, part, curves, noise, angle = pl.pallas_call(
        pack_kernel,
        out_shape=[
            vmem_out((2 * n_proj, wide), BF16),
            vmem_out((2 * n_part, wide + extra), BF16),
            vmem_out(ctf_curves.shape, F32),
            vmem_out(noise.shape, F32),
            vmem_out(shift_phase.shape, F32),
        ],
        in_specs=[pl.BlockSpec(memory_space=pltpu.HBM)] * len(operands),
        out_specs=[_vmem()] * 5,
        scratch_shapes=[
            pltpu.SMEM(ctf_class.shape, jnp.int32),
            pltpu.SMEM(orient_subset.shape, jnp.int32),
            pltpu.SMEM(trans_index.shape, jnp.int32),
            pltpu.VMEM(particles.shape, BF16),
            pltpu.VMEM(orient_prior.shape, BF16),
            pltpu.VMEM(shift_phase.shape, F32),
            pltpu.VMEM(projections.shape, BF16),
            pltpu.SemaphoreType.DMA((len(operands),)),
        ],
        compiler_params=_params(16),
        name="pack",
    )(*[pltpu.with_memory_space_constraint(operand, pltpu.HBM) for operand in operands])

    def swap(value, axis, bit):
        size = lax.axis_size(axis)
        return lax.ppermute(value, axis, [(i, i ^ bit) for i in range(size)])

    def joined(pieces):
        return pieces[0] if len(pieces) == 1 else jnp.concatenate(pieces, axis=0)

    across = swap(part, "blk", half)
    planes, bit = [bank], 1
    while 2 * bit < half:
        planes.append(swap(joined(planes), "blk", bit))
        bit *= 2
    last = swap(joined(planes), "blk", bit)

    parts, weights = [part, across], []
    for n in range(ng.bit_length() - 2, -1, -1):
        part = joined(parts)
        parts = [part, swap(part, "grp", 1 << n)]
        weights.append((1 << n, 2 << len(weights)))

    cos_part, sin_part, square = pl.pallas_call(
        table_kernel,
        out_shape=[
            vmem_out((shifts, wide), F32),
            vmem_out((shifts, wide), F32),
            vmem_out((2 * classes_count, wide), BF16),
        ],
        in_specs=[_vmem()] * 3,
        out_specs=[_vmem()] * 3,
        compiler_params=_params(8),
        cost_estimate=pl.CostEstimate(flops=4_000_000, bytes_accessed=2_000_000, transcendentals=0),
        name="tables",
    )(curves, noise, angle)

    count = 2 * ng * n_part
    early = half // 2 * n_proj
    lanes = 128 * -(-(shifts + 1) * early // 128)
    bits = [1 << n for n in range(half.bit_length() - 2)]
    weighted, extra_rows, rows = pl.pallas_call(
        functools.partial(
            early_kernel, len(parts), ng, weights, bits, n_part, n_proj, length, subsets
        ),
        out_shape=[
            vmem_out((count, 2 * wide), BF16),
            vmem_out((count, extra), F32),
            vmem_out((count, lanes), F32),
        ],
        in_specs=[_vmem()] * (3 + len(parts) + len(planes)),
        out_specs=[_vmem()] * 3,
        compiler_params=_params(16),
        cost_estimate=pl.CostEstimate(
            flops=4 * count * early * shifts * wide, bytes_accessed=4_000_000, transcendentals=0
        ),
        name="early",
    )(cos_part, sin_part, square, *parts, *planes)
    keep, give = pl.pallas_call(
        functools.partial(final_kernel, bits, n_proj, length, subsets),
        out_shape=[vmem_out((ng * n_part, 2 * lanes), F32)] * 2,
        in_specs=[_vmem()] * 7,
        out_specs=[_vmem()] * 2,
        compiler_params=_params(16),
        cost_estimate=pl.CostEstimate(
            flops=4 * count * early * shifts * wide, bytes_accessed=4_000_000, transcendentals=0
        ),
        name="final",
    )(weighted, extra_rows, rows, cos_part, sin_part, square, last)
    scores = pl.pallas_call(
        functools.partial(place_kernel, half),
        out_shape=shape((shifts, ng * n_part, nb * n_proj), F32),
        in_specs=[_vmem()] * 2,
        out_specs=_vmem(),
        compiler_params=_params(4),
        name="place",
    )(keep, swap(give, "blk", half))
    return scores.transpose(1, 0, 2)


def solution(mesh):
    placed = (
        P(("blk", "grp"), None, None),
        P(("blk", "grp")),
        P(("blk", "grp"), None),
        P(),
        P(),
        P(),
        P(),
        P(("grp", "blk"), None, None),
        P(("grp", "blk")),
    )
    return jax.shard_map(
        per_device, mesh=mesh, in_specs=placed, out_specs=P("blk", None, "grp"), check_vma=False
    )
```

```python
import functools

import jax
import jax.numpy as jnp
from jax import lax
from jax.experimental import pallas as pl
from jax.experimental.pallas import tpu as pltpu
from jax.sharding import PartitionSpec as P

F32 = jnp.float32
BF16 = jnp.bfloat16
HIGHEST = lax.Precision.HIGHEST
NT_DIMS = (((1,), (1,)), ((), ()))
MIB = 1 << 20


def _vmem():
    return pl.BlockSpec(memory_space=pltpu.VMEM)


def _params(mib):
    return pltpu.CompilerParams(vmem_limit_bytes=mib * MIB)


def pack_kernel(
    class_hbm,
    subset_hbm,
    particles_hbm,
    prior_hbm,
    curves_hbm,
    noise_hbm,
    proj_hbm,
    phase_hbm,
    trans_hbm,
    bank_ref,
    part_ref,
    curves_ref,
    noise_ref,
    angle_ref,
    class_ref,
    subset_ref,
    trans_ref,
    particles_ref,
    prior_ref,
    phase_ref,
    proj_ref,
    sems,
):
    pairs = [
        (proj_hbm, proj_ref),
        (subset_hbm, subset_ref),
        (class_hbm, class_ref),
        (curves_hbm, curves_ref),
        (particles_hbm, particles_ref),
        (noise_hbm, noise_ref),
        (prior_hbm, prior_ref),
        (trans_hbm, trans_ref),
        (phase_hbm, phase_ref),
    ]
    copies = [pltpu.make_async_copy(a, b, sems.at[n]) for n, (a, b) in enumerate(pairs)]
    for copy in copies:
        copy.start()
    n_part, n_proj = particles_ref.shape[0], proj_ref.shape[0]
    length = proj_ref.shape[2]
    wide = bank_ref.shape[1]

    def padded(values, width):
        zeros = jnp.zeros((values.shape[0], width - values.shape[1]), values.dtype)
        return jnp.concatenate([values, zeros], axis=1)

    row = lax.broadcasted_iota(jnp.int32, (n_proj, wide), 0)
    lane = lax.broadcasted_iota(jnp.int32, (n_proj, wide), 1)
    for copy in copies[:2]:
        copy.wait()
    real = jnp.zeros((n_proj, wide), F32)
    imag = jnp.zeros((n_proj, wide), F32)
    for j in range(n_proj):
        both = padded(proj_ref[j].astype(F32), wide)
        real = jnp.where(row == j, both[0:1], real)
        imag = jnp.where(row == j, both[1:2], imag)
    last = slice(wide - 128, wide)
    ends = real[:, last]
    for j in range(n_proj):
        here = (row[:, last] == j) & (lane[:, last] == length)
        ends = jnp.where(here, subset_ref[j].astype(F32), ends)
    real = jnp.concatenate([real[:, : wide - 128], ends], axis=1)
    bank_ref[...] = jnp.concatenate([real, imag], axis=0).astype(BF16)

    for copy in copies[2:]:
        copy.wait()
    subsets = prior_ref.shape[1]
    extra = part_ref.shape[1] - wide
    row = lax.broadcasted_iota(jnp.int32, (2 * n_part, wide), 0)
    row_extra = lax.broadcasted_iota(jnp.int32, (2 * n_part, extra), 0)
    lane_extra = lax.broadcasted_iota(jnp.int32, (2 * n_part, extra), 1)
    prior = padded(prior_ref[...].astype(F32), 2 * extra)
    rows = jnp.zeros((2 * n_part, wide), F32)
    rows_extra = jnp.zeros((2 * n_part, extra), F32)
    for i in range(n_part):
        curve = curves_ref[pl.ds(class_ref[i], 1), :] * noise_ref[...]
        both = padded(particles_ref[i].astype(F32) * curve, wide)
        rows = jnp.where(row == i, both[0:1], rows)
        rows = jnp.where(row == n_part + i, both[1:2], rows)
        rest = jnp.where(
            lane_extra == subsets - extra,
            class_ref[i].astype(F32),
            jnp.broadcast_to(prior[i : i + 1, extra:], rows_extra.shape),
        )
        rows_extra = jnp.where(row_extra == i, prior[i : i + 1, :extra], rows_extra)
        rows_extra = jnp.where(row_extra == n_part + i, rest, rows_extra)
    part_ref[:, :wide] = rows.astype(BF16)
    part_ref[:, wide:] = rows_extra.astype(BF16)
    for t in range(phase_ref.shape[0]):
        angle_ref[t : t + 1, :] = phase_ref[pl.ds(trans_ref[t], 1), :]


def sine_cosine(x):
    turns = jnp.floor(x * 0.6366197723675814 + 0.5)
    r = ((x - turns * 1.5703125) - turns * 4.837512969970703125e-4) - turns * 7.549789954891882e-8
    z = r * r
    sine = r + r * z * (-1.6666654611e-1 + z * (8.3321608736e-3 - z * 1.9515295891e-4))
    cosine = 1.0 - 0.5 * z + z * z * (
        4.166664568298827e-2 + z * (-1.388731625493765e-3 + z * 2.443315711809948e-5)
    )
    quarter = turns.astype(jnp.int32) & 3
    swapped = (quarter & 1) == 1
    first, second = jnp.where(swapped, cosine, sine), jnp.where(swapped, sine, cosine)
    first = jnp.where(quarter >= 2, -first, first)
    second = jnp.where((quarter == 1) | (quarter == 2), -second, second)
    return first, second


def split_terms(values):
    high = values.astype(BF16)
    low = (values - high.astype(F32)).astype(BF16)
    return jnp.concatenate([high, low], axis=0)


def table_kernel(curves_ref, noise_ref, angle_ref, cos_ref, sin_ref, square_ref):
    length = curves_ref.shape[1]
    wide = cos_ref.shape[1]
    zeros = jnp.zeros((cos_ref.shape[0], wide - length), F32)
    sine, cosine = sine_cosine(angle_ref[...])
    cos_ref[...] = jnp.concatenate([cosine, zeros], axis=1)
    sin_ref[...] = jnp.concatenate([sine, zeros], axis=1)
    curve = curves_ref[...]
    square = split_terms(curve * curve * noise_ref[...])
    square_ref[...] = jnp.concatenate(
        [square, jnp.zeros((square.shape[0], wide - length), BF16)], axis=1
    )


def added_rows(extra, norm, banks, n_proj, length, subsets):
    ids_at = length // 128 * 128
    ids = []
    for bank in banks:
        for first in range(0, bank.shape[0], 2 * n_proj):
            rows = bank[first : first + 2 * n_proj, ids_at : ids_at + 128].astype(F32)
            ids.append(rows[:n_proj])
    ids = jnp.concatenate(ids, axis=0)[:, length - ids_at : length - ids_at + 1]
    subset_col = lax.broadcasted_iota(jnp.int32, (ids.shape[0], subsets), 1).astype(F32)
    subset_hot = (subset_col == ids).astype(F32).astype(BF16)
    prior = lax.dot_general(
        extra[:, :subsets].astype(BF16), subset_hot, NT_DIMS, preferred_element_type=F32
    )
    return prior - 0.5 * norm


def score_pieces(weighted_ref, extra, banks, cos_ref, sin_ref, squares_of, length, subsets, n_proj):
    shifts, wide = cos_ref.shape
    step = 256 if wide % 256 == 0 else 128
    cross, norm = None, None
    for at in range(0, wide, step):
        span = slice(at, at + step)
        reals, imags = [], []
        for bank in banks:
            for first in range(0, bank.shape[0], 2 * n_proj):
                both = bank[first : first + 2 * n_proj, span].astype(F32)
                reals.append(both[:n_proj])
                imags.append(both[n_proj:])
        real_rows, imag_rows = [], []
        for real, imag in zip(reals, imags):
            for t in range(shifts):
                cos_part, sin_part = cos_ref[t : t + 1, span], sin_ref[t : t + 1, span]
                real_rows.append(cos_part * real + sin_part * imag)
                imag_rows.append(cos_part * imag - sin_part * real)
        terms = lax.dot_general(
            weighted_ref[:, span],
            jnp.concatenate(real_rows, axis=0).astype(BF16),
            NT_DIMS,
            preferred_element_type=F32,
        ) + lax.dot_general(
            weighted_ref[:, wide + at : wide + at + step],
            jnp.concatenate(imag_rows, axis=0).astype(BF16),
            NT_DIMS,
            preferred_element_type=F32,
        )
        real, imag = jnp.concatenate(reals, axis=0), jnp.concatenate(imags, axis=0)
        power = split_terms(real * real + imag * imag)
        norms = lax.dot_general(squares_of(span), power, NT_DIMS, preferred_element_type=F32)
        cross = terms if cross is None else cross + terms
        norm = norms if norm is None else norm + norms
    count, total = cross.shape[0], norm.shape[1] // 2
    norm = norm[:count, total:] + norm[count:, :total] + norm[:count, :total]
    added = added_rows(extra, norm, banks, n_proj, length, subsets)
    width = shifts * n_proj
    pieces = []
    for n in range(total // n_proj):
        pieces.append(
            jnp.concatenate(
                [cross[:, n * width : (n + 1) * width], added[:, n * n_proj : (n + 1) * n_proj]], axis=1
            )
        )
    return pieces


def store_pieces(out, pieces, first, slot, rows):
    for n, piece in enumerate(pieces):
        at = (first + n) * slot
        out[:, at : at + piece.shape[1]] = piece[rows]


def early_kernel(
    n_parts, ng, weights, n_part, n_proj, length, subsets, cos_ref, sin_ref, square_ref, *rest
):
    parts, rest = rest[:n_parts], rest[n_parts:]
    *banks, weighted_ref, extra_ref, select_ref, rows_ref = rest
    g = lax.axis_index("grp")
    wide = weighted_ref.shape[1] // 2
    classes_count = square_ref.shape[0] // 2

    held = jnp.concatenate([part[...] for part in parts], axis=0)
    count = 2 * ng * n_part
    out_row = lax.broadcasted_iota(jnp.int32, (2 * count, held.shape[0]), 0)
    in_row = lax.broadcasted_iota(jnp.int32, (2 * count, held.shape[0]), 1)
    kind, rest_row = out_row // count, out_row % count
    source, rest_row = rest_row // (ng * n_part), rest_row % (ng * n_part)
    away, i = rest_row // n_part ^ g, rest_row % n_part
    for bit, weight in weights:
        source += jnp.where(away & bit != 0, weight, 0)
    pick = (in_row == source * (2 * n_part) + kind * n_part + i).astype(F32).astype(BF16)
    ordered = jnp.dot(pick, held, preferred_element_type=F32)
    weighted_ref[:, :wide] = ordered[:count, :wide].astype(BF16)
    weighted_ref[:, wide:] = ordered[count:, :wide].astype(BF16)
    extra = jnp.concatenate([ordered[:count, wide:], ordered[count:, wide:]], axis=1)
    extra_ref[...] = extra
    class_col = lax.broadcasted_iota(jnp.int32, (count, classes_count), 1).astype(F32)
    onehot = (class_col == extra[:, subsets : subsets + 1]).astype(F32).astype(BF16)

    def squares_of(span):
        high = jnp.dot(onehot, square_ref[:classes_count, span], preferred_element_type=F32)
        low = jnp.dot(onehot, square_ref[classes_count:, span], preferred_element_type=F32)
        both = jnp.concatenate([high, low], axis=0).astype(BF16)
        select_ref[:, span] = both
        return both

    pieces = score_pieces(
        weighted_ref, extra, banks, cos_ref, sin_ref, squares_of, length, subsets, n_proj
    )
    store_pieces(rows_ref, pieces, 0, rows_ref.shape[1] // len(pieces), slice(None))


def final_kernel(
    half, n_proj, length, subsets, weighted_ref, extra_ref, select_ref, rows_ref, cos_ref, sin_ref, last_ref, *outs
):
    pieces = score_pieces(
        weighted_ref,
        extra_ref[...],
        [last_ref],
        cos_ref,
        sin_ref,
        lambda span: select_ref[:, span],
        length,
        subsets,
        n_proj,
    )
    dest, lanes = outs[0].shape
    held = rows_ref.shape[1]
    for s, out in enumerate(outs):
        rows = slice(s * dest, (s + 1) * dest)
        out[:, :held] = rows_ref[rows, :]
        store_pieces(out, pieces, half - len(pieces), lanes // half, rows)


def place_kernel(half, n_proj, order, keep_ref, recv_ref, out_ref):
    blk = lax.axis_index("blk")
    own_first = blk < half
    keep, recv = keep_ref[...], recv_ref[...]
    slot = keep.shape[1] // half
    shifts = out_ref.shape[0]
    parts = []
    for values in (jnp.where(own_first, keep, recv), jnp.where(own_first, recv, keep)):
        found = [values[:, order.index(n) * slot : (order.index(n) + 1) * slot] for n in range(half)]
        bit = 1
        while bit < half:
            swapped = (blk & bit) != 0
            found = [jnp.where(swapped, found[n ^ bit], found[n]) for n in range(half)]
            bit *= 2
        parts += found

    def line(t):
        return jnp.concatenate([part[:, t * n_proj : (t + 1) * n_proj] for part in parts], axis=1)

    added = line(shifts)
    for t in range(shifts):
        out_ref[t] = line(t) + added


def per_device(
    particles,
    ctf_class,
    orient_prior,
    ctf_curves,
    noise_weight,
    shift_phase,
    trans_index,
    projections,
    orient_subset,
):
    nb, ng = lax.axis_size("blk"), lax.axis_size("grp")
    half = nb // 2
    n_part, n_proj = particles.shape[0], projections.shape[0]
    length = particles.shape[2]
    shifts = shift_phase.shape[0]
    classes_count = ctf_curves.shape[0]
    subsets = orient_prior.shape[1]
    wide = 128 * (length // 128 + 1)
    extra = 128 * -(-(subsets + 1) // 256)
    noise = noise_weight.reshape(1, length)
    shape = jax.ShapeDtypeStruct

    def vmem_out(dims, dtype):
        return pltpu.VMEM(dims, dtype)

    operands = (
        ctf_class,
        orient_subset,
        particles,
        orient_prior,
        ctf_curves,
        noise,
        projections,
        shift_phase,
        trans_index,
    )
    bank, part, curves, noise, angle = pl.pallas_call(
        pack_kernel,
        out_shape=[
            vmem_out((2 * n_proj, wide), BF16),
            vmem_out((2 * n_part, wide + extra), BF16),
            vmem_out(ctf_curves.shape, F32),
            vmem_out(noise.shape, F32),
            vmem_out(shift_phase.shape, F32),
        ],
        in_specs=[pl.BlockSpec(memory_space=pltpu.HBM)] * len(operands),
        out_specs=[_vmem()] * 5,
        scratch_shapes=[
            pltpu.SMEM(ctf_class.shape, jnp.int32),
            pltpu.SMEM(orient_subset.shape, jnp.int32),
            pltpu.SMEM(trans_index.shape, jnp.int32),
            pltpu.VMEM(particles.shape, BF16),
            pltpu.VMEM(orient_prior.shape, BF16),
            pltpu.VMEM(shift_phase.shape, F32),
            pltpu.VMEM(projections.shape, BF16),
            pltpu.SemaphoreType.DMA((len(operands),)),
        ],
        compiler_params=_params(16),
        name="pack",
    )(*[pltpu.with_memory_space_constraint(operand, pltpu.HBM) for operand in operands])

    def swap(value, axis, bit):
        size = lax.axis_size(axis)
        return lax.ppermute(value, axis, [(i, i ^ bit) for i in range(size)])

    def joined(pieces):
        return pieces[0] if len(pieces) == 1 else jnp.concatenate(pieces, axis=0)

    across = swap(part, "blk", half)
    near = swap(bank, "blk", 1)
    planes, order = [bank], [0]
    for n in range(half.bit_length() - 2, 0, -1):
        planes.append(swap(joined(planes), "blk", 1 << n))
        order += [offset ^ (1 << n) for offset in order]
    far, near = lax.optimization_barrier((joined(planes[1:]), near))
    last = swap(jnp.pad(far, ((0, 0), (0, 3 * 128))), "blk", 1)
    planes = [bank, near, far]
    order = [0, 1] + order[1:] + [offset ^ 1 for offset in order[1:]]

    cos_part, sin_part, square = pl.pallas_call(
        table_kernel,
        out_shape=[
            vmem_out((shifts, wide), F32),
            vmem_out((shifts, wide), F32),
            vmem_out((2 * classes_count, wide), BF16),
        ],
        in_specs=[_vmem()] * 3,
        out_specs=[_vmem()] * 3,
        compiler_params=_params(8),
        cost_estimate=pl.CostEstimate(flops=4_000_000, bytes_accessed=2_000_000, transcendentals=0),
        name="tables",
    )(curves, noise, angle)

    across, cos_part = lax.optimization_barrier((across, cos_part))
    parts, weights = [part, across], []
    for n in range(ng.bit_length() - 2, -1, -1):
        part = joined(parts)
        parts = [part, swap(part, "grp", 1 << n)]
        weights.append((1 << n, 2 << len(weights)))

    count = 2 * ng * n_part
    late = half // 2 - 1
    slot = 128 * -(-(shifts + 1) * n_proj // 128)
    weighted, extra_rows, select, rows = pl.pallas_call(
        functools.partial(early_kernel, len(parts), ng, weights, n_part, n_proj, length, subsets),
        out_shape=[
            vmem_out((count, 2 * wide), BF16),
            vmem_out((count, 2 * extra), F32),
            vmem_out((2 * count, wide), BF16),
            vmem_out((count, (half - late) * slot), F32),
        ],
        in_specs=[_vmem()] * (3 + len(parts) + len(planes)),
        out_specs=[_vmem()] * 4,
        compiler_params=_params(16),
        cost_estimate=pl.CostEstimate(
            flops=4 * count * (half - late) * n_proj * shifts * wide,
            bytes_accessed=4_000_000,
            transcendentals=0,
        ),
        name="early",
    )(cos_part, sin_part, square, *parts, *planes)
    keep, give = pl.pallas_call(
        functools.partial(final_kernel, half, n_proj, length, subsets),
        out_shape=[vmem_out((ng * n_part, half * slot), F32)] * 2,
        in_specs=[_vmem()] * 7,
        out_specs=[_vmem()] * 2,
        compiler_params=_params(16),
        cost_estimate=pl.CostEstimate(
            flops=4 * count * late * n_proj * shifts * wide, bytes_accessed=4_000_000, transcendentals=0
        ),
        name="final",
    )(weighted, extra_rows, select, rows, cos_part, sin_part, last)
    scores = pl.pallas_call(
        functools.partial(place_kernel, half, n_proj, order),
        out_shape=shape((shifts, ng * n_part, nb * n_proj), F32),
        in_specs=[_vmem()] * 2,
        out_specs=_vmem(),
        compiler_params=_params(4),
        name="place",
    )(keep, swap(give, "blk", half))
    return scores.transpose(1, 0, 2)


def solution(mesh):
    placed = (
        P(("blk", "grp"), None, None),
        P(("blk", "grp")),
        P(("blk", "grp"), None),
        P(),
        P(),
        P(),
        P(),
        P(("grp", "blk"), None, None),
        P(("grp", "blk")),
    )
    return jax.shard_map(
        per_device, mesh=mesh, in_specs=placed, out_specs=P("blk", None, "grp"), check_vma=False
    )
```

```python
import functools

import jax
import jax.numpy as jnp
from jax import lax
from jax.experimental import pallas as pl
from jax.experimental.pallas import tpu as pltpu
from jax.sharding import PartitionSpec as P

F32 = jnp.float32
BF16 = jnp.bfloat16
HIGHEST = lax.Precision.HIGHEST
NT_DIMS = (((1,), (1,)), ((), ()))
MIB = 1 << 20


def _vmem():
    return pl.BlockSpec(memory_space=pltpu.VMEM)


def _params(mib):
    return pltpu.CompilerParams(vmem_limit_bytes=mib * MIB)


def pack_kernel(
    class_hbm,
    subset_hbm,
    particles_hbm,
    prior_hbm,
    curves_hbm,
    noise_hbm,
    proj_hbm,
    phase_hbm,
    trans_hbm,
    bank_ref,
    part_ref,
    curves_ref,
    noise_ref,
    angle_ref,
    class_ref,
    subset_ref,
    trans_ref,
    particles_ref,
    prior_ref,
    phase_ref,
    proj_ref,
    sems,
):
    pairs = [
        (proj_hbm, proj_ref),
        (subset_hbm, subset_ref),
        (class_hbm, class_ref),
        (curves_hbm, curves_ref),
        (particles_hbm, particles_ref),
        (noise_hbm, noise_ref),
        (prior_hbm, prior_ref),
        (trans_hbm, trans_ref),
        (phase_hbm, phase_ref),
    ]
    copies = [pltpu.make_async_copy(a, b, sems.at[n]) for n, (a, b) in enumerate(pairs)]
    for copy in copies:
        copy.start()
    n_part, n_proj = particles_ref.shape[0], proj_ref.shape[0]
    length = proj_ref.shape[2]
    wide = bank_ref.shape[1]

    def padded(values, width):
        zeros = jnp.zeros((values.shape[0], width - values.shape[1]), values.dtype)
        return jnp.concatenate([values, zeros], axis=1)

    row = lax.broadcasted_iota(jnp.int32, (n_proj, wide), 0)
    lane = lax.broadcasted_iota(jnp.int32, (n_proj, wide), 1)
    for copy in copies[:2]:
        copy.wait()
    real = jnp.zeros((n_proj, wide), F32)
    imag = jnp.zeros((n_proj, wide), F32)
    for j in range(n_proj):
        both = padded(proj_ref[j].astype(F32), wide)
        real = jnp.where(row == j, both[0:1], real)
        imag = jnp.where(row == j, both[1:2], imag)
    last = slice(wide - 128, wide)
    ends = real[:, last]
    for j in range(n_proj):
        here = (row[:, last] == j) & (lane[:, last] == length)
        ends = jnp.where(here, subset_ref[j].astype(F32), ends)
    real = jnp.concatenate([real[:, : wide - 128], ends], axis=1)
    bank_ref[...] = jnp.concatenate([real, imag], axis=0).astype(BF16)

    for copy in copies[2:]:
        copy.wait()
    subsets = prior_ref.shape[1]
    extra = part_ref.shape[1] - wide
    row = lax.broadcasted_iota(jnp.int32, (2 * n_part, wide), 0)
    row_extra = lax.broadcasted_iota(jnp.int32, (2 * n_part, extra), 0)
    lane_extra = lax.broadcasted_iota(jnp.int32, (2 * n_part, extra), 1)
    prior = padded(prior_ref[...].astype(F32), 2 * extra)
    rows = jnp.zeros((2 * n_part, wide), F32)
    rows_extra = jnp.zeros((2 * n_part, extra), F32)
    for i in range(n_part):
        curve = curves_ref[pl.ds(class_ref[i], 1), :] * noise_ref[...]
        both = padded(particles_ref[i].astype(F32) * curve, wide)
        rows = jnp.where(row == i, both[0:1], rows)
        rows = jnp.where(row == n_part + i, both[1:2], rows)
        rest = jnp.where(
            lane_extra == subsets - extra,
            class_ref[i].astype(F32),
            jnp.broadcast_to(prior[i : i + 1, extra:], rows_extra.shape),
        )
        rows_extra = jnp.where(row_extra == i, prior[i : i + 1, :extra], rows_extra)
        rows_extra = jnp.where(row_extra == n_part + i, rest, rows_extra)
    part_ref[:, :wide] = rows.astype(BF16)
    part_ref[:, wide:] = rows_extra.astype(BF16)
    for t in range(phase_ref.shape[0]):
        angle_ref[t : t + 1, :] = phase_ref[pl.ds(trans_ref[t], 1), :]


def sine_cosine(x):
    turns = jnp.floor(x * 0.6366197723675814 + 0.5)
    r = ((x - turns * 1.5703125) - turns * 4.837512969970703125e-4) - turns * 7.549789954891882e-8
    z = r * r
    sine = r + r * z * (-1.6666654611e-1 + z * (8.3321608736e-3 - z * 1.9515295891e-4))
    cosine = 1.0 - 0.5 * z + z * z * (
        4.166664568298827e-2 + z * (-1.388731625493765e-3 + z * 2.443315711809948e-5)
    )
    quarter = turns.astype(jnp.int32) & 3
    swapped = (quarter & 1) == 1
    first, second = jnp.where(swapped, cosine, sine), jnp.where(swapped, sine, cosine)
    first = jnp.where(quarter >= 2, -first, first)
    second = jnp.where((quarter == 1) | (quarter == 2), -second, second)
    return first, second


def split_terms(values):
    high = values.astype(BF16)
    low = (values - high.astype(F32)).astype(BF16)
    return jnp.concatenate([high, low], axis=0)


def table_kernel(curves_ref, noise_ref, angle_ref, cos_ref, sin_ref, square_ref):
    length = curves_ref.shape[1]
    wide = cos_ref.shape[1]
    zeros = jnp.zeros((cos_ref.shape[0], wide - length), F32)
    sine, cosine = sine_cosine(angle_ref[...])
    cos_ref[...] = jnp.concatenate([cosine, zeros], axis=1)
    sin_ref[...] = jnp.concatenate([sine, zeros], axis=1)
    curve = curves_ref[...]
    square = split_terms(curve * curve * noise_ref[...])
    square_ref[...] = jnp.concatenate(
        [square, jnp.zeros((square.shape[0], wide - length), BF16)], axis=1
    )


def added_rows(extra, norm, banks, n_proj, length, subsets):
    ids_at = length // 128 * 128
    ids = []
    for bank in banks:
        for first in range(0, bank.shape[0], 2 * n_proj):
            rows = bank[first : first + 2 * n_proj, ids_at : ids_at + 128].astype(F32)
            ids.append(rows[:n_proj])
    ids = jnp.concatenate(ids, axis=0)[:, length - ids_at : length - ids_at + 1]
    subset_col = lax.broadcasted_iota(jnp.int32, (ids.shape[0], subsets), 1).astype(F32)
    subset_hot = (subset_col == ids).astype(F32).astype(BF16)
    prior = lax.dot_general(
        extra[:, :subsets].astype(BF16), subset_hot, NT_DIMS, preferred_element_type=F32
    )
    return prior - 0.5 * norm


def bank_pieces(bank, span, n_proj):
    for first in range(0, bank.shape[0], 2 * n_proj):
        both = bank[first : first + 2 * n_proj, span].astype(F32)
        yield both[:n_proj], both[n_proj:]


def shifted_rows(real, imag, cos_ref, sin_ref, span):
    real_rows, imag_rows = [], []
    for t in range(cos_ref.shape[0]):
        cos_part, sin_part = cos_ref[t : t + 1, span], sin_ref[t : t + 1, span]
        real_rows.append(cos_part * real + sin_part * imag)
        imag_rows.append(cos_part * imag - sin_part * real)
    return (
        jnp.concatenate(real_rows, axis=0).astype(BF16),
        jnp.concatenate(imag_rows, axis=0).astype(BF16),
    )


def spans_of(wide):
    step = 256 if wide % 256 == 0 else 128
    return [slice(at, at + step) for at in range(0, wide, step)]


def shift_kernel(n_proj, cos_ref, sin_ref, *rest):
    *banks, shifted_ref, power_ref = rest
    shifts, wide = cos_ref.shape
    width = shifts * n_proj
    for span in spans_of(wide):
        powers, at = [], 0
        for bank in banks:
            for real, imag in bank_pieces(bank, span, n_proj):
                real_rows, imag_rows = shifted_rows(real, imag, cos_ref, sin_ref, span)
                shifted_ref[at : at + width, span] = real_rows
                shifted_ref[at : at + width, wide + span.start : wide + span.stop] = imag_rows
                powers.append(real * real + imag * imag)
                at += width
        power_ref[:, span] = split_terms(jnp.concatenate(powers, axis=0))


def multiply(left, right):
    return lax.dot_general(left, right, NT_DIMS, preferred_element_type=F32)


def pieces_of(cross, norm, extra, banks, length, subsets, n_proj):
    count, total = cross.shape[0], norm.shape[1] // 2
    width = cross.shape[1] * n_proj // total
    norm = norm[:count, total:] + norm[count:, :total] + norm[:count, :total]
    added = added_rows(extra, norm, banks, n_proj, length, subsets)
    pieces = []
    for n in range(total // n_proj):
        scores = cross[:, n * width : (n + 1) * width]
        pieces.append(jnp.concatenate([scores, added[:, n * n_proj : (n + 1) * n_proj]], axis=1))
    return pieces


def store_pieces(out, pieces, first, slot, rows):
    for n, piece in enumerate(pieces):
        at = (first + n) * slot
        out[:, at : at + piece.shape[1]] = piece[rows]


def early_kernel(n_parts, n_banks, ng, weights, n_part, n_proj, length, subsets, square_ref, *rest):
    parts, rest = rest[:n_parts], rest[n_parts:]
    groups, (weighted_ref, extra_ref, select_ref, rows_ref) = [], rest[-4:]
    for n in n_banks:
        groups.append((rest[0], rest[1], rest[2 : 2 + n]))
        rest = rest[2 + n :]
    g = lax.axis_index("grp")
    wide = weighted_ref.shape[1] // 2
    classes_count = square_ref.shape[0] // 2

    held = jnp.concatenate([part[...] for part in parts], axis=0)
    count = 2 * ng * n_part
    out_row = lax.broadcasted_iota(jnp.int32, (2 * count, held.shape[0]), 0)
    in_row = lax.broadcasted_iota(jnp.int32, (2 * count, held.shape[0]), 1)
    kind, rest_row = out_row // count, out_row % count
    source, rest_row = rest_row // (ng * n_part), rest_row % (ng * n_part)
    away, i = rest_row // n_part ^ g, rest_row % n_part
    for bit, weight in weights:
        source += jnp.where(away & bit != 0, weight, 0)
    pick = (in_row == source * (2 * n_part) + kind * n_part + i).astype(F32).astype(BF16)
    ordered = jnp.dot(pick, held, preferred_element_type=F32)
    weighted_ref[:, :wide] = ordered[:count, :wide].astype(BF16)
    weighted_ref[:, wide:] = ordered[count:, :wide].astype(BF16)
    extra = jnp.concatenate([ordered[:count, wide:], ordered[count:, wide:]], axis=1)
    extra_ref[...] = extra
    class_col = lax.broadcasted_iota(jnp.int32, (count, classes_count), 1).astype(F32)
    onehot = (class_col == extra[:, subsets : subsets + 1]).astype(F32).astype(BF16)
    for n in range(2):
        squares = square_ref[n * classes_count : (n + 1) * classes_count, :]
        chosen = jnp.dot(onehot, squares, preferred_element_type=F32)
        select_ref[n * count : (n + 1) * count, :] = chosen.astype(BF16)

    pieces = []
    for shifted_ref, power_ref, banks in groups:
        cross = multiply(weighted_ref[...], shifted_ref[...])
        norm = multiply(select_ref[...], power_ref[...])
        pieces += pieces_of(cross, norm, extra, banks, length, subsets, n_proj)
    store_pieces(rows_ref, pieces, 0, rows_ref.shape[1] // len(pieces), slice(None))


def final_kernel(
    half, n_proj, length, subsets, weighted_ref, extra_ref, select_ref, rows_ref, cos_ref, sin_ref, last_ref, *outs
):
    shifts, wide = cos_ref.shape
    cross, norm = None, None
    for span in spans_of(wide):
        terms, powers = [], []
        for real, imag in bank_pieces(last_ref, span, n_proj):
            real_rows, imag_rows = shifted_rows(real, imag, cos_ref, sin_ref, span)
            terms.append(
                multiply(weighted_ref[:, span], real_rows)
                + multiply(weighted_ref[:, wide + span.start : wide + span.stop], imag_rows)
            )
            powers.append(real * real + imag * imag)
        terms = jnp.concatenate(terms, axis=1)
        norms = multiply(select_ref[:, span], split_terms(jnp.concatenate(powers, axis=0)))
        cross = terms if cross is None else cross + terms
        norm = norms if norm is None else norm + norms
    pieces = pieces_of(cross, norm, extra_ref[...], [last_ref], length, subsets, n_proj)
    dest, lanes = outs[0].shape
    held = rows_ref.shape[1]
    for s, out in enumerate(outs):
        rows = slice(s * dest, (s + 1) * dest)
        out[:, :held] = rows_ref[rows, :]
        store_pieces(out, pieces, half - len(pieces), lanes // half, rows)


def place_kernel(half, n_proj, order, keep_ref, recv_ref, out_ref):
    blk = lax.axis_index("blk")
    own_first = blk < half
    keep, recv = keep_ref[...], recv_ref[...]
    slot = keep.shape[1] // half
    shifts = out_ref.shape[0]
    parts = []
    for values in (jnp.where(own_first, keep, recv), jnp.where(own_first, recv, keep)):
        found = [values[:, order.index(n) * slot : (order.index(n) + 1) * slot] for n in range(half)]
        bit = 1
        while bit < half:
            swapped = (blk & bit) != 0
            found = [jnp.where(swapped, found[n ^ bit], found[n]) for n in range(half)]
            bit *= 2
        parts += found

    def line(t):
        return jnp.concatenate([part[:, t * n_proj : (t + 1) * n_proj] for part in parts], axis=1)

    added = line(shifts)
    for t in range(shifts):
        out_ref[t] = line(t) + added


def per_device(
    particles,
    ctf_class,
    orient_prior,
    ctf_curves,
    noise_weight,
    shift_phase,
    trans_index,
    projections,
    orient_subset,
):
    nb, ng = lax.axis_size("blk"), lax.axis_size("grp")
    half = nb // 2
    n_part, n_proj = particles.shape[0], projections.shape[0]
    length = particles.shape[2]
    shifts = shift_phase.shape[0]
    classes_count = ctf_curves.shape[0]
    subsets = orient_prior.shape[1]
    wide = 128 * (length // 128 + 1)
    extra = 128 * -(-(subsets + 1) // 256)
    noise = noise_weight.reshape(1, length)
    shape = jax.ShapeDtypeStruct

    def vmem_out(dims, dtype):
        return pltpu.VMEM(dims, dtype)

    operands = (
        ctf_class,
        orient_subset,
        particles,
        orient_prior,
        ctf_curves,
        noise,
        projections,
        shift_phase,
        trans_index,
    )
    bank, part, curves, noise, angle = pl.pallas_call(
        pack_kernel,
        out_shape=[
            vmem_out((2 * n_proj, wide), BF16),
            vmem_out((2 * n_part, wide + extra), BF16),
            vmem_out(ctf_curves.shape, F32),
            vmem_out(noise.shape, F32),
            vmem_out(shift_phase.shape, F32),
        ],
        in_specs=[pl.BlockSpec(memory_space=pltpu.HBM)] * len(operands),
        out_specs=[_vmem()] * 5,
        scratch_shapes=[
            pltpu.SMEM(ctf_class.shape, jnp.int32),
            pltpu.SMEM(orient_subset.shape, jnp.int32),
            pltpu.SMEM(trans_index.shape, jnp.int32),
            pltpu.VMEM(particles.shape, BF16),
            pltpu.VMEM(orient_prior.shape, BF16),
            pltpu.VMEM(shift_phase.shape, F32),
            pltpu.VMEM(projections.shape, BF16),
            pltpu.SemaphoreType.DMA((len(operands),)),
        ],
        compiler_params=_params(16),
        name="pack",
    )(*[pltpu.with_memory_space_constraint(operand, pltpu.HBM) for operand in operands])

    def swap(value, axis, bit):
        size = lax.axis_size(axis)
        return lax.ppermute(value, axis, [(i, i ^ bit) for i in range(size)])

    def joined(pieces):
        return pieces[0] if len(pieces) == 1 else jnp.concatenate(pieces, axis=0)

    across = swap(part, "blk", half)
    near = swap(bank, "blk", 1)
    planes, order = [bank], [0]
    for n in range(half.bit_length() - 2, 0, -1):
        planes.append(swap(joined(planes), "blk", 1 << n))
        order += [offset ^ (1 << n) for offset in order]
    far, near = lax.optimization_barrier((joined(planes[1:]), near))
    last = swap(jnp.pad(far, ((0, 0), (0, 3 * 128))), "blk", 1)
    order = [0, 1] + order[1:] + [offset ^ 1 for offset in order[1:]]

    cos_part, sin_part, square = pl.pallas_call(
        table_kernel,
        out_shape=[
            vmem_out((shifts, wide), F32),
            vmem_out((shifts, wide), F32),
            vmem_out((2 * classes_count, wide), BF16),
        ],
        in_specs=[_vmem()] * 3,
        out_specs=[_vmem()] * 3,
        compiler_params=_params(8),
        cost_estimate=pl.CostEstimate(flops=4_000_000, bytes_accessed=2_000_000, transcendentals=0),
        name="tables",
    )(curves, noise, angle)

    def shifted_call(banks, name):
        total = sum(piece.shape[0] for piece in banks) // 2
        return pl.pallas_call(
            functools.partial(shift_kernel, n_proj),
            out_shape=[vmem_out((shifts * total, 2 * wide), BF16), vmem_out((2 * total, wide), BF16)],
            in_specs=[_vmem()] * (2 + len(banks)),
            out_specs=[_vmem()] * 2,
            compiler_params=_params(16),
            cost_estimate=pl.CostEstimate(
                flops=6 * total * shifts * wide, bytes_accessed=4_000_000, transcendentals=0
            ),
            name=name,
        )(cos_part, sin_part, *banks)

    own_rows, own_power = shifted_call([bank], "shift_own")

    across, own_power = lax.optimization_barrier((across, own_power))
    parts, weights = [part, across], []
    for n in range(ng.bit_length() - 2, -1, -1):
        part = joined(parts)
        parts = [part, swap(part, "grp", 1 << n)]
        weights.append((1 << n, 2 << len(weights)))

    rest_rows, rest_power = shifted_call([near, far], "shift_rest")
    count = 2 * ng * n_part
    late = half // 2 - 1
    slot = 128 * -(-(shifts + 1) * n_proj // 128)
    weighted, extra_rows, select, rows = pl.pallas_call(
        functools.partial(
            early_kernel, len(parts), (1, 2), ng, weights, n_part, n_proj, length, subsets
        ),
        out_shape=[
            vmem_out((count, 2 * wide), BF16),
            vmem_out((count, 2 * extra), F32),
            vmem_out((2 * count, wide), BF16),
            vmem_out((count, (half - late) * slot), F32),
        ],
        in_specs=[_vmem()] * (8 + len(parts)),
        out_specs=[_vmem()] * 4,
        compiler_params=_params(16),
        cost_estimate=pl.CostEstimate(
            flops=4 * count * (half - late) * n_proj * shifts * wide,
            bytes_accessed=4_000_000,
            transcendentals=0,
        ),
        name="early",
    )(square, *parts, own_rows, own_power, bank, rest_rows, rest_power, near, far)
    keep, give = pl.pallas_call(
        functools.partial(final_kernel, half, n_proj, length, subsets),
        out_shape=[vmem_out((ng * n_part, half * slot), F32)] * 2,
        in_specs=[_vmem()] * 7,
        out_specs=[_vmem()] * 2,
        compiler_params=_params(16),
        cost_estimate=pl.CostEstimate(
            flops=4 * count * late * n_proj * shifts * wide, bytes_accessed=4_000_000, transcendentals=0
        ),
        name="final",
    )(weighted, extra_rows, select, rows, cos_part, sin_part, last)
    scores = pl.pallas_call(
        functools.partial(place_kernel, half, n_proj, order),
        out_shape=shape((shifts, ng * n_part, nb * n_proj), F32),
        in_specs=[_vmem()] * 2,
        out_specs=_vmem(),
        compiler_params=_params(4),
        name="place",
    )(keep, swap(give, "blk", half))
    return scores.transpose(1, 0, 2)


def solution(mesh):
    placed = (
        P(("blk", "grp"), None, None),
        P(("blk", "grp")),
        P(("blk", "grp"), None),
        P(),
        P(),
        P(),
        P(),
        P(("grp", "blk"), None, None),
        P(("grp", "blk")),
    )
    return jax.shard_map(
        per_device, mesh=mesh, in_specs=placed, out_specs=P("blk", None, "grp"), check_vma=False
    )
```

```python
import functools

import jax
import jax.numpy as jnp
from jax import lax
from jax.experimental import pallas as pl
from jax.experimental.pallas import tpu as pltpu
from jax.sharding import PartitionSpec as P

F32 = jnp.float32
BF16 = jnp.bfloat16
HIGHEST = lax.Precision.HIGHEST
NT_DIMS = (((1,), (1,)), ((), ()))
MIB = 1 << 20


def _vmem():
    return pl.BlockSpec(memory_space=pltpu.VMEM)


def _params(mib):
    return pltpu.CompilerParams(vmem_limit_bytes=mib * MIB)


def pack_kernel(
    class_hbm,
    subset_hbm,
    particles_hbm,
    prior_hbm,
    curves_hbm,
    noise_hbm,
    proj_hbm,
    phase_hbm,
    trans_hbm,
    bank_ref,
    part_ref,
    curves_ref,
    noise_ref,
    angle_ref,
    class_ref,
    subset_ref,
    trans_ref,
    particles_ref,
    prior_ref,
    phase_ref,
    proj_ref,
    sems,
):
    pairs = [
        (proj_hbm, proj_ref),
        (subset_hbm, subset_ref),
        (class_hbm, class_ref),
        (curves_hbm, curves_ref),
        (particles_hbm, particles_ref),
        (noise_hbm, noise_ref),
        (prior_hbm, prior_ref),
        (trans_hbm, trans_ref),
        (phase_hbm, phase_ref),
    ]
    copies = [pltpu.make_async_copy(a, b, sems.at[n]) for n, (a, b) in enumerate(pairs)]
    for copy in copies:
        copy.start()
    n_part, n_proj = particles_ref.shape[0], proj_ref.shape[0]
    length = proj_ref.shape[2]
    wide = bank_ref.shape[1]

    def padded(values, width):
        zeros = jnp.zeros((values.shape[0], width - values.shape[1]), values.dtype)
        return jnp.concatenate([values, zeros], axis=1)

    row = lax.broadcasted_iota(jnp.int32, (n_proj, wide), 0)
    lane = lax.broadcasted_iota(jnp.int32, (n_proj, wide), 1)
    for copy in copies[:2]:
        copy.wait()
    real = jnp.zeros((n_proj, wide), F32)
    imag = jnp.zeros((n_proj, wide), F32)
    for j in range(n_proj):
        both = padded(proj_ref[j].astype(F32), wide)
        real = jnp.where(row == j, both[0:1], real)
        imag = jnp.where(row == j, both[1:2], imag)
    last = slice(wide - 128, wide)
    ends = real[:, last]
    for j in range(n_proj):
        here = (row[:, last] == j) & (lane[:, last] == length)
        ends = jnp.where(here, subset_ref[j].astype(F32), ends)
    real = jnp.concatenate([real[:, : wide - 128], ends], axis=1)
    bank_ref[...] = jnp.concatenate([real, imag], axis=0).astype(BF16)

    for copy in copies[2:]:
        copy.wait()
    subsets = prior_ref.shape[1]
    extra = part_ref.shape[1] - wide
    row = lax.broadcasted_iota(jnp.int32, (2 * n_part, wide), 0)
    row_extra = lax.broadcasted_iota(jnp.int32, (2 * n_part, extra), 0)
    lane_extra = lax.broadcasted_iota(jnp.int32, (2 * n_part, extra), 1)
    prior = padded(prior_ref[...].astype(F32), 2 * extra)
    rows = jnp.zeros((2 * n_part, wide), F32)
    rows_extra = jnp.zeros((2 * n_part, extra), F32)
    for i in range(n_part):
        curve = curves_ref[pl.ds(class_ref[i], 1), :] * noise_ref[...]
        both = padded(particles_ref[i].astype(F32) * curve, wide)
        rows = jnp.where(row == i, both[0:1], rows)
        rows = jnp.where(row == n_part + i, both[1:2], rows)
        rest = jnp.where(
            lane_extra == subsets - extra,
            class_ref[i].astype(F32),
            jnp.broadcast_to(prior[i : i + 1, extra:], rows_extra.shape),
        )
        rows_extra = jnp.where(row_extra == i, prior[i : i + 1, :extra], rows_extra)
        rows_extra = jnp.where(row_extra == n_part + i, rest, rows_extra)
    part_ref[:, :wide] = rows.astype(BF16)
    part_ref[:, wide:] = rows_extra.astype(BF16)
    for t in range(phase_ref.shape[0]):
        angle_ref[t : t + 1, :] = phase_ref[pl.ds(trans_ref[t], 1), :]


def sine_cosine(x):
    turns = jnp.floor(x * 0.6366197723675814 + 0.5)
    r = ((x - turns * 1.5703125) - turns * 4.837512969970703125e-4) - turns * 7.549789954891882e-8
    z = r * r
    sine = r + r * z * (-1.6666654611e-1 + z * (8.3321608736e-3 - z * 1.9515295891e-4))
    cosine = 1.0 - 0.5 * z + z * z * (
        4.166664568298827e-2 + z * (-1.388731625493765e-3 + z * 2.443315711809948e-5)
    )
    quarter = turns.astype(jnp.int32) & 3
    swapped = (quarter & 1) == 1
    first, second = jnp.where(swapped, cosine, sine), jnp.where(swapped, sine, cosine)
    first = jnp.where(quarter >= 2, -first, first)
    second = jnp.where((quarter == 1) | (quarter == 2), -second, second)
    return first, second


def split_terms(values):
    high = values.astype(BF16)
    low = (values - high.astype(F32)).astype(BF16)
    return jnp.concatenate([high, low], axis=0)


def table_kernel(curves_ref, noise_ref, angle_ref, cos_ref, sin_ref, square_ref):
    length = curves_ref.shape[1]
    wide = cos_ref.shape[1]
    zeros = jnp.zeros((cos_ref.shape[0], wide - length), F32)
    sine, cosine = sine_cosine(angle_ref[...])
    cos_ref[...] = jnp.concatenate([cosine, zeros], axis=1)
    sin_ref[...] = jnp.concatenate([sine, zeros], axis=1)
    curve = curves_ref[...]
    square = split_terms(curve * curve * noise_ref[...])
    square_ref[...] = jnp.concatenate(
        [square, jnp.zeros((square.shape[0], wide - length), BF16)], axis=1
    )


def added_rows(extra, norm, banks, n_proj, length, subsets):
    ids_at = length // 128 * 128
    ids = []
    for bank in banks:
        for first in range(0, bank.shape[0], 2 * n_proj):
            rows = bank[first : first + 2 * n_proj, ids_at : ids_at + 128].astype(F32)
            ids.append(rows[:n_proj])
    ids = jnp.concatenate(ids, axis=0)[:, length - ids_at : length - ids_at + 1]
    subset_col = lax.broadcasted_iota(jnp.int32, (ids.shape[0], subsets), 1).astype(F32)
    subset_hot = (subset_col == ids).astype(F32).astype(BF16)
    prior = lax.dot_general(
        extra[:, :subsets].astype(BF16), subset_hot, NT_DIMS, preferred_element_type=F32
    )
    return prior - 0.5 * norm


def bank_pieces(bank, span, n_proj):
    for first in range(0, bank.shape[0], 2 * n_proj):
        both = bank[first : first + 2 * n_proj, span].astype(F32)
        yield both[:n_proj], both[n_proj:]


def shifted_rows(real, imag, cos_ref, sin_ref, span):
    real_rows, imag_rows = [], []
    for t in range(cos_ref.shape[0]):
        cos_part, sin_part = cos_ref[t : t + 1, span], sin_ref[t : t + 1, span]
        real_rows.append(cos_part * real + sin_part * imag)
        imag_rows.append(cos_part * imag - sin_part * real)
    return (
        jnp.concatenate(real_rows, axis=0).astype(BF16),
        jnp.concatenate(imag_rows, axis=0).astype(BF16),
    )


def spans_of(wide):
    step = 256 if wide % 256 == 0 else 128
    return [slice(at, at + step) for at in range(0, wide, step)]


def shift_kernel(n_proj, cos_ref, sin_ref, *rest):
    *banks, shifted_ref, power_ref = rest
    shifts, wide = cos_ref.shape
    width = shifts * n_proj
    for span in spans_of(wide):
        powers, at = [], 0
        for bank in banks:
            for real, imag in bank_pieces(bank, span, n_proj):
                real_rows, imag_rows = shifted_rows(real, imag, cos_ref, sin_ref, span)
                shifted_ref[at : at + width, span] = real_rows
                shifted_ref[at : at + width, wide + span.start : wide + span.stop] = imag_rows
                powers.append(real * real + imag * imag)
                at += width
        power_ref[:, span] = split_terms(jnp.concatenate(powers, axis=0))


def multiply(left, right):
    return lax.dot_general(left, right, NT_DIMS, preferred_element_type=F32)


def pieces_of(cross, norm, extra, banks, length, subsets, n_proj):
    count, total = cross.shape[0], norm.shape[1] // 2
    width = cross.shape[1] * n_proj // total
    norm = norm[:count, total:] + norm[count:, :total] + norm[:count, :total]
    added = added_rows(extra, norm, banks, n_proj, length, subsets)
    pieces = []
    for n in range(total // n_proj):
        scores = cross[:, n * width : (n + 1) * width]
        pieces.append(jnp.concatenate([scores, added[:, n * n_proj : (n + 1) * n_proj]], axis=1))
    return pieces


def store_pieces(out, pieces, first, slot, rows):
    for n, piece in enumerate(pieces):
        at = (first + n) * slot
        out[:, at : at + piece.shape[1]] = piece[rows]


def early_kernel(n_parts, n_banks, ng, weights, n_part, n_proj, length, subsets, square_ref, *rest):
    parts, rest = rest[:n_parts], rest[n_parts:]
    groups, (weighted_ref, extra_ref, select_ref, rows_ref) = [], rest[-4:]
    for n in n_banks:
        groups.append((rest[0], rest[1], rest[2 : 2 + n]))
        rest = rest[2 + n :]
    g = lax.axis_index("grp")
    wide = weighted_ref.shape[1] // 2
    classes_count = square_ref.shape[0] // 2

    held = jnp.concatenate([part[...] for part in parts], axis=0)
    count = 2 * ng * n_part
    out_row = lax.broadcasted_iota(jnp.int32, (2 * count, held.shape[0]), 0)
    in_row = lax.broadcasted_iota(jnp.int32, (2 * count, held.shape[0]), 1)
    kind, rest_row = out_row // count, out_row % count
    source, rest_row = rest_row // (ng * n_part), rest_row % (ng * n_part)
    away, i = rest_row // n_part ^ g, rest_row % n_part
    for bit, weight in weights:
        source += jnp.where(away & bit != 0, weight, 0)
    pick = (in_row == source * (2 * n_part) + kind * n_part + i).astype(F32).astype(BF16)
    ordered = jnp.dot(pick, held, preferred_element_type=F32)
    weighted_ref[:, :wide] = ordered[:count, :wide].astype(BF16)
    weighted_ref[:, wide:] = ordered[count:, :wide].astype(BF16)
    extra = jnp.concatenate([ordered[:count, wide:], ordered[count:, wide:]], axis=1)
    extra_ref[...] = extra
    class_col = lax.broadcasted_iota(jnp.int32, (count, classes_count), 1).astype(F32)
    onehot = (class_col == extra[:, subsets : subsets + 1]).astype(F32).astype(BF16)
    for n in range(2):
        squares = square_ref[n * classes_count : (n + 1) * classes_count, :]
        chosen = jnp.dot(onehot, squares, preferred_element_type=F32)
        select_ref[n * count : (n + 1) * count, :] = chosen.astype(BF16)

    pieces = []
    for shifted_ref, power_ref, banks in groups:
        cross = multiply(shifted_ref[...], weighted_ref[...]).T
        norm = multiply(select_ref[...], power_ref[...])
        pieces += pieces_of(cross, norm, extra, banks, length, subsets, n_proj)
    store_pieces(rows_ref, pieces, 0, rows_ref.shape[1] // len(pieces), slice(None))


def final_kernel(
    half, n_proj, length, subsets, weighted_ref, extra_ref, select_ref, rows_ref, cos_ref, sin_ref, last_ref, *outs
):
    shifts, wide = cos_ref.shape
    cross, norm = None, None
    for span in spans_of(wide):
        terms, powers = [], []
        for real, imag in bank_pieces(last_ref, span, n_proj):
            real_rows, imag_rows = shifted_rows(real, imag, cos_ref, sin_ref, span)
            terms.append(
                multiply(real_rows, weighted_ref[:, span])
                + multiply(imag_rows, weighted_ref[:, wide + span.start : wide + span.stop])
            )
            powers.append(real * real + imag * imag)
        terms = jnp.concatenate(terms, axis=0)
        norms = multiply(select_ref[:, span], split_terms(jnp.concatenate(powers, axis=0)))
        cross = terms if cross is None else cross + terms
        norm = norms if norm is None else norm + norms
    pieces = pieces_of(cross.T, norm, extra_ref[...], [last_ref], length, subsets, n_proj)
    dest, lanes = outs[0].shape
    held = rows_ref.shape[1]
    for s, out in enumerate(outs):
        rows = slice(s * dest, (s + 1) * dest)
        out[:, :held] = rows_ref[rows, :]
        store_pieces(out, pieces, half - len(pieces), lanes // half, rows)


def place_kernel(half, n_proj, order, keep_ref, recv_ref, out_ref):
    blk = lax.axis_index("blk")
    own_first = blk < half
    keep, recv = keep_ref[...], recv_ref[...]
    slot = keep.shape[1] // half
    shifts = out_ref.shape[0]
    parts = []
    for values in (jnp.where(own_first, keep, recv), jnp.where(own_first, recv, keep)):
        found = [values[:, order.index(n) * slot : (order.index(n) + 1) * slot] for n in range(half)]
        bit = 1
        while bit < half:
            swapped = (blk & bit) != 0
            found = [jnp.where(swapped, found[n ^ bit], found[n]) for n in range(half)]
            bit *= 2
        parts += found

    def line(t):
        return jnp.concatenate([part[:, t * n_proj : (t + 1) * n_proj] for part in parts], axis=1)

    added = line(shifts)
    for t in range(shifts):
        out_ref[t] = line(t) + added


def per_device(
    particles,
    ctf_class,
    orient_prior,
    ctf_curves,
    noise_weight,
    shift_phase,
    trans_index,
    projections,
    orient_subset,
):
    nb, ng = lax.axis_size("blk"), lax.axis_size("grp")
    half = nb // 2
    n_part, n_proj = particles.shape[0], projections.shape[0]
    length = particles.shape[2]
    shifts = shift_phase.shape[0]
    classes_count = ctf_curves.shape[0]
    subsets = orient_prior.shape[1]
    wide = 128 * (length // 128 + 1)
    extra = 128 * -(-(subsets + 1) // 256)
    noise = noise_weight.reshape(1, length)
    shape = jax.ShapeDtypeStruct

    def vmem_out(dims, dtype):
        return pltpu.VMEM(dims, dtype)

    operands = (
        ctf_class,
        orient_subset,
        particles,
        orient_prior,
        ctf_curves,
        noise,
        projections,
        shift_phase,
        trans_index,
    )
    bank, part, curves, noise, angle = pl.pallas_call(
        pack_kernel,
        out_shape=[
            vmem_out((2 * n_proj, wide), BF16),
            vmem_out((2 * n_part, wide + extra), BF16),
            vmem_out(ctf_curves.shape, F32),
            vmem_out(noise.shape, F32),
            vmem_out(shift_phase.shape, F32),
        ],
        in_specs=[pl.BlockSpec(memory_space=pltpu.HBM)] * len(operands),
        out_specs=[_vmem()] * 5,
        scratch_shapes=[
            pltpu.SMEM(ctf_class.shape, jnp.int32),
            pltpu.SMEM(orient_subset.shape, jnp.int32),
            pltpu.SMEM(trans_index.shape, jnp.int32),
            pltpu.VMEM(particles.shape, BF16),
            pltpu.VMEM(orient_prior.shape, BF16),
            pltpu.VMEM(shift_phase.shape, F32),
            pltpu.VMEM(projections.shape, BF16),
            pltpu.SemaphoreType.DMA((len(operands),)),
        ],
        compiler_params=_params(16),
        name="pack",
    )(*[pltpu.with_memory_space_constraint(operand, pltpu.HBM) for operand in operands])

    def swap(value, axis, bit):
        size = lax.axis_size(axis)
        return lax.ppermute(value, axis, [(i, i ^ bit) for i in range(size)])

    def joined(pieces):
        return pieces[0] if len(pieces) == 1 else jnp.concatenate(pieces, axis=0)

    across = swap(part, "blk", half)
    near = swap(bank, "blk", 1)
    planes, order = [bank], [0]
    for n in range(half.bit_length() - 2, 0, -1):
        planes.append(swap(joined(planes), "blk", 1 << n))
        order += [offset ^ (1 << n) for offset in order]
    far, near = lax.optimization_barrier((joined(planes[1:]), near))
    last = swap(jnp.pad(far, ((0, 0), (0, 3 * 128))), "blk", 1)
    order = [0, 1] + order[1:] + [offset ^ 1 for offset in order[1:]]

    cos_part, sin_part, square = pl.pallas_call(
        table_kernel,
        out_shape=[
            vmem_out((shifts, wide), F32),
            vmem_out((shifts, wide), F32),
            vmem_out((2 * classes_count, wide), BF16),
        ],
        in_specs=[_vmem()] * 3,
        out_specs=[_vmem()] * 3,
        compiler_params=_params(8),
        cost_estimate=pl.CostEstimate(flops=4_000_000, bytes_accessed=2_000_000, transcendentals=0),
        name="tables",
    )(curves, noise, angle)

    def shifted_call(banks, name):
        total = sum(piece.shape[0] for piece in banks) // 2
        return pl.pallas_call(
            functools.partial(shift_kernel, n_proj),
            out_shape=[vmem_out((shifts * total, 2 * wide), BF16), vmem_out((2 * total, wide), BF16)],
            in_specs=[_vmem()] * (2 + len(banks)),
            out_specs=[_vmem()] * 2,
            compiler_params=_params(16),
            cost_estimate=pl.CostEstimate(
                flops=6 * total * shifts * wide, bytes_accessed=4_000_000, transcendentals=0
            ),
            name=name,
        )(cos_part, sin_part, *banks)

    own_rows, own_power = shifted_call([bank], "shift_own")

    across, own_power = lax.optimization_barrier((across, own_power))
    parts, weights = [part, across], []
    for n in range(ng.bit_length() - 2, -1, -1):
        part = joined(parts)
        parts = [part, swap(part, "grp", 1 << n)]
        weights.append((1 << n, 2 << len(weights)))

    rest_rows, rest_power = shifted_call([near, far], "shift_rest")
    count = 2 * ng * n_part
    late = half // 2 - 1
    slot = 128 * -(-(shifts + 1) * n_proj // 128)
    weighted, extra_rows, select, rows = pl.pallas_call(
        functools.partial(
            early_kernel, len(parts), (1, 2), ng, weights, n_part, n_proj, length, subsets
        ),
        out_shape=[
            vmem_out((count, 2 * wide), BF16),
            vmem_out((count, 2 * extra), F32),
            vmem_out((2 * count, wide), BF16),
            vmem_out((count, (half - late) * slot), F32),
        ],
        in_specs=[_vmem()] * (8 + len(parts)),
        out_specs=[_vmem()] * 4,
        compiler_params=_params(16),
        cost_estimate=pl.CostEstimate(
            flops=4 * count * (half - late) * n_proj * shifts * wide,
            bytes_accessed=4_000_000,
            transcendentals=0,
        ),
        name="early",
    )(square, *parts, own_rows, own_power, bank, rest_rows, rest_power, near, far)
    keep, give = pl.pallas_call(
        functools.partial(final_kernel, half, n_proj, length, subsets),
        out_shape=[vmem_out((ng * n_part, half * slot), F32)] * 2,
        in_specs=[_vmem()] * 7,
        out_specs=[_vmem()] * 2,
        compiler_params=_params(16),
        cost_estimate=pl.CostEstimate(
            flops=4 * count * late * n_proj * shifts * wide, bytes_accessed=4_000_000, transcendentals=0
        ),
        name="final",
    )(weighted, extra_rows, select, rows, cos_part, sin_part, last)
    scores = pl.pallas_call(
        functools.partial(place_kernel, half, n_proj, order),
        out_shape=shape((shifts, ng * n_part, nb * n_proj), F32),
        in_specs=[_vmem()] * 2,
        out_specs=_vmem(),
        compiler_params=_params(4),
        name="place",
    )(keep, swap(give, "blk", half))
    return scores.transpose(1, 0, 2)


def solution(mesh):
    placed = (
        P(("blk", "grp"), None, None),
        P(("blk", "grp")),
        P(("blk", "grp"), None),
        P(),
        P(),
        P(),
        P(),
        P(("grp", "blk"), None, None),
        P(("grp", "blk")),
    )
    return jax.shard_map(
        per_device, mesh=mesh, in_specs=placed, out_specs=P("blk", None, "grp"), check_vma=False
    )
```

```python
import functools

import jax
import jax.numpy as jnp
from jax import lax
from jax.experimental import pallas as pl
from jax.experimental.pallas import tpu as pltpu
from jax.sharding import PartitionSpec as P

F32 = jnp.float32
BF16 = jnp.bfloat16
HIGHEST = lax.Precision.HIGHEST
NT_DIMS = (((1,), (1,)), ((), ()))
MIB = 1 << 20


def _vmem():
    return pl.BlockSpec(memory_space=pltpu.VMEM)


def _params(mib):
    return pltpu.CompilerParams(vmem_limit_bytes=mib * MIB)


def pack_kernel(
    class_hbm,
    subset_hbm,
    particles_hbm,
    prior_hbm,
    curves_hbm,
    noise_hbm,
    proj_hbm,
    phase_hbm,
    trans_hbm,
    bank_ref,
    part_ref,
    curves_ref,
    noise_ref,
    angle_ref,
    class_ref,
    subset_ref,
    trans_ref,
    particles_ref,
    prior_ref,
    phase_ref,
    proj_ref,
    sems,
):
    pairs = [
        (proj_hbm, proj_ref),
        (subset_hbm, subset_ref),
        (class_hbm, class_ref),
        (curves_hbm, curves_ref),
        (particles_hbm, particles_ref),
        (noise_hbm, noise_ref),
        (prior_hbm, prior_ref),
        (trans_hbm, trans_ref),
        (phase_hbm, phase_ref),
    ]
    copies = [pltpu.make_async_copy(a, b, sems.at[n]) for n, (a, b) in enumerate(pairs)]
    for copy in copies:
        copy.start()
    n_part, n_proj = particles_ref.shape[0], proj_ref.shape[0]
    length = proj_ref.shape[2]
    wide = bank_ref.shape[1]

    def padded(values, width):
        zeros = jnp.zeros((values.shape[0], width - values.shape[1]), values.dtype)
        return jnp.concatenate([values, zeros], axis=1)

    row = lax.broadcasted_iota(jnp.int32, (n_proj, wide), 0)
    lane = lax.broadcasted_iota(jnp.int32, (n_proj, wide), 1)
    for copy in copies[:2]:
        copy.wait()
    real = jnp.zeros((n_proj, wide), F32)
    imag = jnp.zeros((n_proj, wide), F32)
    for j in range(n_proj):
        both = padded(proj_ref[j].astype(F32), wide)
        real = jnp.where(row == j, both[0:1], real)
        imag = jnp.where(row == j, both[1:2], imag)
    last = slice(wide - 128, wide)
    ends = real[:, last]
    for j in range(n_proj):
        here = (row[:, last] == j) & (lane[:, last] == length)
        ends = jnp.where(here, subset_ref[j].astype(F32), ends)
    real = jnp.concatenate([real[:, : wide - 128], ends], axis=1)
    bank_ref[...] = jnp.concatenate([real, imag], axis=0).astype(BF16)

    for copy in copies[2:]:
        copy.wait()
    subsets = prior_ref.shape[1]
    extra = part_ref.shape[1] - wide
    row = lax.broadcasted_iota(jnp.int32, (2 * n_part, wide), 0)
    row_extra = lax.broadcasted_iota(jnp.int32, (2 * n_part, extra), 0)
    lane_extra = lax.broadcasted_iota(jnp.int32, (2 * n_part, extra), 1)
    prior = padded(prior_ref[...].astype(F32), 2 * extra)
    rows = jnp.zeros((2 * n_part, wide), F32)
    rows_extra = jnp.zeros((2 * n_part, extra), F32)
    for i in range(n_part):
        curve = curves_ref[pl.ds(class_ref[i], 1), :] * noise_ref[...]
        both = padded(particles_ref[i].astype(F32) * curve, wide)
        rows = jnp.where(row == i, both[0:1], rows)
        rows = jnp.where(row == n_part + i, both[1:2], rows)
        rest = jnp.where(
            lane_extra == subsets - extra,
            class_ref[i].astype(F32),
            jnp.broadcast_to(prior[i : i + 1, extra:], rows_extra.shape),
        )
        rows_extra = jnp.where(row_extra == i, prior[i : i + 1, :extra], rows_extra)
        rows_extra = jnp.where(row_extra == n_part + i, rest, rows_extra)
    part_ref[:, :wide] = rows.astype(BF16)
    part_ref[:, wide:] = rows_extra.astype(BF16)
    for t in range(phase_ref.shape[0]):
        angle_ref[t : t + 1, :] = phase_ref[pl.ds(trans_ref[t], 1), :]


def sine_cosine(x):
    turns = jnp.floor(x * 0.6366197723675814 + 0.5)
    r = ((x - turns * 1.5703125) - turns * 4.837512969970703125e-4) - turns * 7.549789954891882e-8
    z = r * r
    sine = r + r * z * (-1.6666654611e-1 + z * (8.3321608736e-3 - z * 1.9515295891e-4))
    cosine = 1.0 - 0.5 * z + z * z * (
        4.166664568298827e-2 + z * (-1.388731625493765e-3 + z * 2.443315711809948e-5)
    )
    quarter = turns.astype(jnp.int32) & 3
    swapped = (quarter & 1) == 1
    first, second = jnp.where(swapped, cosine, sine), jnp.where(swapped, sine, cosine)
    first = jnp.where(quarter >= 2, -first, first)
    second = jnp.where((quarter == 1) | (quarter == 2), -second, second)
    return first, second


def split_terms(values):
    high = values.astype(BF16)
    low = (values - high.astype(F32)).astype(BF16)
    return jnp.concatenate([high, low], axis=0)


def table_kernel(curves_ref, noise_ref, angle_ref, cos_ref, sin_ref, square_ref):
    length = curves_ref.shape[1]
    wide = cos_ref.shape[1]
    zeros = jnp.zeros((cos_ref.shape[0], wide - length), F32)
    sine, cosine = sine_cosine(angle_ref[...])
    cos_ref[...] = jnp.concatenate([cosine, zeros], axis=1)
    sin_ref[...] = jnp.concatenate([sine, zeros], axis=1)
    curve = curves_ref[...]
    square = split_terms(curve * curve * noise_ref[...])
    square_ref[...] = jnp.concatenate(
        [square, jnp.zeros((square.shape[0], wide - length), BF16)], axis=1
    )


def added_rows(extra, norm, banks, n_proj, length, subsets):
    ids_at = length // 128 * 128
    ids = []
    for bank in banks:
        for first in range(0, bank.shape[0], 2 * n_proj):
            rows = bank[first : first + 2 * n_proj, ids_at : ids_at + 128].astype(F32)
            ids.append(rows[:n_proj])
    ids = jnp.concatenate(ids, axis=0)[:, length - ids_at : length - ids_at + 1]
    subset_col = lax.broadcasted_iota(jnp.int32, (ids.shape[0], subsets), 1).astype(F32)
    subset_hot = (subset_col == ids).astype(F32).astype(BF16)
    prior = lax.dot_general(
        extra[:, :subsets].astype(BF16), subset_hot, NT_DIMS, preferred_element_type=F32
    )
    return prior - 0.5 * norm


def bank_pieces(bank, span, n_proj):
    for first in range(0, bank.shape[0], 2 * n_proj):
        both = bank[first : first + 2 * n_proj, span].astype(F32)
        yield both[:n_proj], both[n_proj:]


def shifted_rows(real, imag, cos_ref, sin_ref, span):
    real_rows, imag_rows = [], []
    for t in range(cos_ref.shape[0]):
        cos_part, sin_part = cos_ref[t : t + 1, span], sin_ref[t : t + 1, span]
        real_rows.append(cos_part * real + sin_part * imag)
        imag_rows.append(cos_part * imag - sin_part * real)
    return (
        jnp.concatenate(real_rows, axis=0).astype(BF16),
        jnp.concatenate(imag_rows, axis=0).astype(BF16),
    )


def spans_of(wide):
    step = 256 if wide % 256 == 0 else 128
    return [slice(at, at + step) for at in range(0, wide, step)]


def table_of(norms):
    classes_count, total = norms.shape[0] // 2, norms.shape[1] // 2
    return (
        norms[:classes_count, total:] + norms[classes_count:, :total] + norms[:classes_count, :total]
    )


def shift_kernel(n_proj, cos_ref, sin_ref, square_ref, *rest):
    *banks, shifted_ref, table_ref = rest
    shifts, wide = cos_ref.shape
    width = shifts * n_proj
    norms = None
    for span in spans_of(wide):
        powers, at = [], 0
        for bank in banks:
            for real, imag in bank_pieces(bank, span, n_proj):
                real_rows, imag_rows = shifted_rows(real, imag, cos_ref, sin_ref, span)
                shifted_ref[at : at + width, span] = real_rows
                shifted_ref[at : at + width, wide + span.start : wide + span.stop] = imag_rows
                powers.append(real * real + imag * imag)
                at += width
        terms = multiply(square_ref[:, span], split_terms(jnp.concatenate(powers, axis=0)))
        norms = terms if norms is None else norms + terms
    table_ref[...] = table_of(norms)


def multiply(left, right):
    return lax.dot_general(left, right, NT_DIMS, preferred_element_type=F32)


def pieces_of(cross, table, extra, banks, length, subsets, n_proj):
    classes_count, total = table.shape
    width = cross.shape[1] * n_proj // total
    class_col = lax.broadcasted_iota(jnp.int32, (cross.shape[0], classes_count), 1).astype(F32)
    onehot = (class_col == extra[:, subsets : subsets + 1]).astype(F32)
    norm = jnp.dot(onehot, table, precision=HIGHEST, preferred_element_type=F32)
    added = added_rows(extra, norm, banks, n_proj, length, subsets)
    pieces = []
    for n in range(total // n_proj):
        scores = cross[:, n * width : (n + 1) * width]
        pieces.append(jnp.concatenate([scores, added[:, n * n_proj : (n + 1) * n_proj]], axis=1))
    return pieces


def store_pieces(out, pieces, first, slot, rows):
    for n, piece in enumerate(pieces):
        at = (first + n) * slot
        out[:, at : at + piece.shape[1]] = piece[rows]


def early_kernel(n_parts, n_banks, ng, weights, n_part, n_proj, length, subsets, *rest):
    parts, rest = rest[:n_parts], rest[n_parts:]
    groups, (weighted_ref, extra_ref, rows_ref) = [], rest[-3:]
    for n in n_banks:
        groups.append((rest[0], rest[1], rest[2 : 2 + n]))
        rest = rest[2 + n :]
    g = lax.axis_index("grp")
    wide = weighted_ref.shape[1] // 2

    held = jnp.concatenate([part[...] for part in parts], axis=0)
    count = 2 * ng * n_part
    out_row = lax.broadcasted_iota(jnp.int32, (2 * count, held.shape[0]), 0)
    in_row = lax.broadcasted_iota(jnp.int32, (2 * count, held.shape[0]), 1)
    kind, rest_row = out_row // count, out_row % count
    source, rest_row = rest_row // (ng * n_part), rest_row % (ng * n_part)
    away, i = rest_row // n_part ^ g, rest_row % n_part
    for bit, weight in weights:
        source += jnp.where(away & bit != 0, weight, 0)
    pick = (in_row == source * (2 * n_part) + kind * n_part + i).astype(F32).astype(BF16)
    ordered = jnp.dot(pick, held, preferred_element_type=F32)
    weighted_ref[:, :wide] = ordered[:count, :wide].astype(BF16)
    weighted_ref[:, wide:] = ordered[count:, :wide].astype(BF16)
    extra = jnp.concatenate([ordered[:count, wide:], ordered[count:, wide:]], axis=1)
    extra_ref[...] = extra
    pieces = []
    for shifted_ref, table_ref, banks in groups:
        cross = multiply(weighted_ref[...], shifted_ref[...])
        pieces += pieces_of(cross, table_ref[...], extra, banks, length, subsets, n_proj)
    store_pieces(rows_ref, pieces, 0, rows_ref.shape[1] // len(pieces), slice(None))


def final_kernel(
    half, n_proj, length, subsets, weighted_ref, extra_ref, rows_ref, cos_ref, sin_ref, square_ref, last_ref, *outs
):
    shifts, wide = cos_ref.shape
    cross, norm = None, None
    for span in spans_of(wide):
        terms, powers = [], []
        for real, imag in bank_pieces(last_ref, span, n_proj):
            real_rows, imag_rows = shifted_rows(real, imag, cos_ref, sin_ref, span)
            terms.append(
                multiply(weighted_ref[:, span], real_rows)
                + multiply(weighted_ref[:, wide + span.start : wide + span.stop], imag_rows)
            )
            powers.append(real * real + imag * imag)
        terms = jnp.concatenate(terms, axis=1)
        norms = multiply(square_ref[:, span], split_terms(jnp.concatenate(powers, axis=0)))
        cross = terms if cross is None else cross + terms
        norm = norms if norm is None else norm + norms
    pieces = pieces_of(cross, table_of(norm), extra_ref[...], [last_ref], length, subsets, n_proj)
    dest, lanes = outs[0].shape
    held = rows_ref.shape[1]
    for s, out in enumerate(outs):
        rows = slice(s * dest, (s + 1) * dest)
        out[:, :held] = rows_ref[rows, :]
        store_pieces(out, pieces, half - len(pieces), lanes // half, rows)


def place_kernel(half, n_proj, order, keep_ref, recv_ref, out_ref):
    blk = lax.axis_index("blk")
    own_first = blk < half
    keep, recv = keep_ref[...], recv_ref[...]
    slot = keep.shape[1] // half
    shifts = out_ref.shape[0]
    parts = []
    for values in (jnp.where(own_first, keep, recv), jnp.where(own_first, recv, keep)):
        found = [values[:, order.index(n) * slot : (order.index(n) + 1) * slot] for n in range(half)]
        bit = 1
        while bit < half:
            swapped = (blk & bit) != 0
            found = [jnp.where(swapped, found[n ^ bit], found[n]) for n in range(half)]
            bit *= 2
        parts += found

    def line(t):
        return jnp.concatenate([part[:, t * n_proj : (t + 1) * n_proj] for part in parts], axis=1)

    added = line(shifts)
    for t in range(shifts):
        out_ref[t] = line(t) + added


def per_device(
    particles,
    ctf_class,
    orient_prior,
    ctf_curves,
    noise_weight,
    shift_phase,
    trans_index,
    projections,
    orient_subset,
):
    nb, ng = lax.axis_size("blk"), lax.axis_size("grp")
    half = nb // 2
    n_part, n_proj = particles.shape[0], projections.shape[0]
    length = particles.shape[2]
    shifts = shift_phase.shape[0]
    classes_count = ctf_curves.shape[0]
    subsets = orient_prior.shape[1]
    wide = 128 * (length // 128 + 1)
    extra = 128 * -(-(subsets + 1) // 256)
    noise = noise_weight.reshape(1, length)
    shape = jax.ShapeDtypeStruct

    def vmem_out(dims, dtype):
        return pltpu.VMEM(dims, dtype)

    operands = (
        ctf_class,
        orient_subset,
        particles,
        orient_prior,
        ctf_curves,
        noise,
        projections,
        shift_phase,
        trans_index,
    )
    bank, part, curves, noise, angle = pl.pallas_call(
        pack_kernel,
        out_shape=[
            vmem_out((2 * n_proj, wide), BF16),
            vmem_out((2 * n_part, wide + extra), BF16),
            vmem_out(ctf_curves.shape, F32),
            vmem_out(noise.shape, F32),
            vmem_out(shift_phase.shape, F32),
        ],
        in_specs=[pl.BlockSpec(memory_space=pltpu.HBM)] * len(operands),
        out_specs=[_vmem()] * 5,
        scratch_shapes=[
            pltpu.SMEM(ctf_class.shape, jnp.int32),
            pltpu.SMEM(orient_subset.shape, jnp.int32),
            pltpu.SMEM(trans_index.shape, jnp.int32),
            pltpu.VMEM(particles.shape, BF16),
            pltpu.VMEM(orient_prior.shape, BF16),
            pltpu.VMEM(shift_phase.shape, F32),
            pltpu.VMEM(projections.shape, BF16),
            pltpu.SemaphoreType.DMA((len(operands),)),
        ],
        compiler_params=_params(16),
        name="pack",
    )(*[pltpu.with_memory_space_constraint(operand, pltpu.HBM) for operand in operands])

    def swap(value, axis, bit):
        size = lax.axis_size(axis)
        return lax.ppermute(value, axis, [(i, i ^ bit) for i in range(size)])

    def joined(pieces):
        return pieces[0] if len(pieces) == 1 else jnp.concatenate(pieces, axis=0)

    across = swap(part, "blk", half)
    near = swap(bank, "blk", 1)
    planes, order = [bank], [0]
    for n in range(half.bit_length() - 2, 0, -1):
        planes.append(swap(joined(planes), "blk", 1 << n))
        order += [offset ^ (1 << n) for offset in order]
    far, near = lax.optimization_barrier((joined(planes[1:]), near))
    last = swap(jnp.pad(far, ((0, 0), (0, 3 * 128))), "blk", 1)
    order = [0, 1] + order[1:] + [offset ^ 1 for offset in order[1:]]

    cos_part, sin_part, square = pl.pallas_call(
        table_kernel,
        out_shape=[
            vmem_out((shifts, wide), F32),
            vmem_out((shifts, wide), F32),
            vmem_out((2 * classes_count, wide), BF16),
        ],
        in_specs=[_vmem()] * 3,
        out_specs=[_vmem()] * 3,
        compiler_params=_params(8),
        cost_estimate=pl.CostEstimate(flops=4_000_000, bytes_accessed=2_000_000, transcendentals=0),
        name="tables",
    )(curves, noise, angle)

    def shifted_call(banks, name):
        total = sum(piece.shape[0] for piece in banks) // 2
        return pl.pallas_call(
            functools.partial(shift_kernel, n_proj),
            out_shape=[vmem_out((shifts * total, 2 * wide), BF16), vmem_out((classes_count, total), F32)],
            in_specs=[_vmem()] * (3 + len(banks)),
            out_specs=[_vmem()] * 2,
            compiler_params=_params(16),
            cost_estimate=pl.CostEstimate(
                flops=6 * total * shifts * wide, bytes_accessed=4_000_000, transcendentals=0
            ),
            name=name,
        )(cos_part, sin_part, square, *banks)

    own_rows, own_norms = shifted_call([bank], "shift_own")

    across, own_norms = lax.optimization_barrier((across, own_norms))
    parts, weights = [part, across], []
    for n in range(ng.bit_length() - 2, -1, -1):
        part = joined(parts)
        parts = [part, swap(part, "grp", 1 << n)]
        weights.append((1 << n, 2 << len(weights)))

    rest_rows, rest_norms = shifted_call([near, far], "shift_rest")
    count = 2 * ng * n_part
    late = half // 2 - 1
    slot = 128 * -(-(shifts + 1) * n_proj // 128)
    weighted, extra_rows, rows = pl.pallas_call(
        functools.partial(
            early_kernel, len(parts), (1, 2), ng, weights, n_part, n_proj, length, subsets
        ),
        out_shape=[
            vmem_out((count, 2 * wide), BF16),
            vmem_out((count, 2 * extra), F32),
            vmem_out((count, (half - late) * slot), F32),
        ],
        in_specs=[_vmem()] * (7 + len(parts)),
        out_specs=[_vmem()] * 3,
        compiler_params=_params(16),
        cost_estimate=pl.CostEstimate(
            flops=4 * count * (half - late) * n_proj * shifts * wide,
            bytes_accessed=4_000_000,
            transcendentals=0,
        ),
        name="early",
    )(*parts, own_rows, own_norms, bank, rest_rows, rest_norms, near, far)
    keep, give = pl.pallas_call(
        functools.partial(final_kernel, half, n_proj, length, subsets),
        out_shape=[vmem_out((ng * n_part, half * slot), F32)] * 2,
        in_specs=[_vmem()] * 7,
        out_specs=[_vmem()] * 2,
        compiler_params=_params(16),
        cost_estimate=pl.CostEstimate(
            flops=4 * count * late * n_proj * shifts * wide, bytes_accessed=4_000_000, transcendentals=0
        ),
        name="final",
    )(weighted, extra_rows, rows, cos_part, sin_part, square, last)
    scores = pl.pallas_call(
        functools.partial(place_kernel, half, n_proj, order),
        out_shape=shape((shifts, ng * n_part, nb * n_proj), F32),
        in_specs=[_vmem()] * 2,
        out_specs=_vmem(),
        compiler_params=_params(4),
        name="place",
    )(keep, swap(give, "blk", half))
    return scores.transpose(1, 0, 2)


def solution(mesh):
    placed = (
        P(("blk", "grp"), None, None),
        P(("blk", "grp")),
        P(("blk", "grp"), None),
        P(),
        P(),
        P(),
        P(),
        P(("grp", "blk"), None, None),
        P(("grp", "blk")),
    )
    return jax.shard_map(
        per_device, mesh=mesh, in_specs=placed, out_specs=P("blk", None, "grp"), check_vma=False
    )
```

```python
import functools

import jax
import jax.numpy as jnp
from jax import lax
from jax.experimental import pallas as pl
from jax.experimental.pallas import tpu as pltpu
from jax.sharding import PartitionSpec as P

F32 = jnp.float32
BF16 = jnp.bfloat16
HIGHEST = lax.Precision.HIGHEST
NT_DIMS = (((1,), (1,)), ((), ()))
MIB = 1 << 20


def _vmem():
    return pl.BlockSpec(memory_space=pltpu.VMEM)


def _params(mib):
    return pltpu.CompilerParams(vmem_limit_bytes=mib * MIB)


def pack_kernel(
    class_hbm,
    subset_hbm,
    particles_hbm,
    prior_hbm,
    curves_hbm,
    noise_hbm,
    proj_hbm,
    phase_hbm,
    trans_hbm,
    bank_ref,
    part_ref,
    curves_ref,
    noise_ref,
    angle_ref,
    class_ref,
    subset_ref,
    trans_ref,
    particles_ref,
    prior_ref,
    phase_ref,
    proj_ref,
    sems,
):
    n_proj, n_class = proj_hbm.shape[0], curves_hbm.shape[0]
    pairs = [
        (proj_hbm.at[: n_proj // 2], proj_ref.at[: n_proj // 2]),
        (proj_hbm.at[n_proj // 2 :], proj_ref.at[n_proj // 2 :]),
        (subset_hbm, subset_ref),
        (class_hbm, class_ref),
        (curves_hbm.at[: n_class // 4], curves_ref.at[: n_class // 4]),
        (curves_hbm.at[n_class // 4 : n_class // 2], curves_ref.at[n_class // 4 : n_class // 2]),
        (curves_hbm.at[n_class // 2 : 3 * n_class // 4], curves_ref.at[n_class // 2 : 3 * n_class // 4]),
        (curves_hbm.at[3 * n_class // 4 :], curves_ref.at[3 * n_class // 4 :]),
        (particles_hbm, particles_ref),
        (noise_hbm, noise_ref),
        (prior_hbm, prior_ref),
        (trans_hbm, trans_ref),
        (phase_hbm, phase_ref),
    ]
    copies = [pltpu.make_async_copy(a, b, sems.at[n]) for n, (a, b) in enumerate(pairs)]
    for copy in copies:
        copy.start()
    n_part = particles_ref.shape[0]
    length = proj_ref.shape[2]
    wide = bank_ref.shape[1]

    def padded(values, width):
        zeros = jnp.zeros((values.shape[0], width - values.shape[1]), values.dtype)
        return jnp.concatenate([values, zeros], axis=1)

    row = lax.broadcasted_iota(jnp.int32, (n_proj, wide), 0)
    lane = lax.broadcasted_iota(jnp.int32, (n_proj, wide), 1)
    for copy in copies[:3]:
        copy.wait()
    real = jnp.zeros((n_proj, wide), F32)
    imag = jnp.zeros((n_proj, wide), F32)
    for j in range(n_proj):
        both = padded(proj_ref[j].astype(F32), wide)
        real = jnp.where(row == j, both[0:1], real)
        imag = jnp.where(row == j, both[1:2], imag)
    last = slice(wide - 128, wide)
    ends = real[:, last]
    for j in range(n_proj):
        here = (row[:, last] == j) & (lane[:, last] == length)
        ends = jnp.where(here, subset_ref[j].astype(F32), ends)
    real = jnp.concatenate([real[:, : wide - 128], ends], axis=1)
    bank_ref[...] = jnp.concatenate([real, imag], axis=0).astype(BF16)

    for copy in copies[3:]:
        copy.wait()
    subsets = prior_ref.shape[1]
    extra = part_ref.shape[1] - 2 * wide
    row = lax.broadcasted_iota(jnp.int32, (n_part, wide), 0)
    row_extra = lax.broadcasted_iota(jnp.int32, (n_part, extra), 0)
    lane_extra = lax.broadcasted_iota(jnp.int32, (n_part, extra), 1)
    real = jnp.zeros((n_part, wide), F32)
    imag = jnp.zeros((n_part, wide), F32)
    small = padded(prior_ref[...].astype(F32), extra)
    for i in range(n_part):
        curve = curves_ref[pl.ds(class_ref[i], 1), :] * noise_ref[...]
        both = padded(particles_ref[i].astype(F32) * curve, wide)
        real = jnp.where(row == i, both[0:1], real)
        imag = jnp.where(row == i, both[1:2], imag)
        place = (row_extra == i) & (lane_extra == subsets)
        small = jnp.where(place, class_ref[i].astype(F32), small)
    part_ref[:, :wide] = real.astype(BF16)
    part_ref[:, wide : 2 * wide] = imag.astype(BF16)
    part_ref[:, 2 * wide :] = small.astype(BF16)
    for t in range(phase_ref.shape[0]):
        angle_ref[t : t + 1, :] = phase_ref[pl.ds(trans_ref[t], 1), :]


def sine_cosine(x):
    turns = jnp.floor(x * 0.6366197723675814 + 0.5)
    r = ((x - turns * 1.5703125) - turns * 4.837512969970703125e-4) - turns * 7.549789954891882e-8
    z = r * r
    sine = r + r * z * (-1.6666654611e-1 + z * (8.3321608736e-3 - z * 1.9515295891e-4))
    cosine = 1.0 - 0.5 * z + z * z * (
        4.166664568298827e-2 + z * (-1.388731625493765e-3 + z * 2.443315711809948e-5)
    )
    quarter = turns.astype(jnp.int32) & 3
    swapped = (quarter & 1) == 1
    first, second = jnp.where(swapped, cosine, sine), jnp.where(swapped, sine, cosine)
    first = jnp.where(quarter >= 2, -first, first)
    second = jnp.where((quarter == 1) | (quarter == 2), -second, second)
    return first, second


def split_terms(values):
    high = values.astype(BF16)
    low = (values - high.astype(F32)).astype(BF16)
    return jnp.concatenate([high, low], axis=0)


def table_kernel(curves_ref, noise_ref, angle_ref, cos_ref, sin_ref, square_ref):
    length = curves_ref.shape[1]
    wide = cos_ref.shape[1]
    zeros = jnp.zeros((cos_ref.shape[0], wide - length), F32)
    sine, cosine = sine_cosine(angle_ref[...])
    cos_ref[...] = jnp.concatenate([cosine, zeros], axis=1)
    sin_ref[...] = jnp.concatenate([sine, zeros], axis=1)
    curve = curves_ref[...]
    square = split_terms(curve * curve * noise_ref[...])
    square_ref[...] = jnp.concatenate(
        [square, jnp.zeros((square.shape[0], wide - length), BF16)], axis=1
    )


def added_rows(extra, norm, banks, n_proj, length, subsets):
    ids_at = length // 128 * 128
    ids = []
    for bank in banks:
        for first in range(0, bank.shape[0], 2 * n_proj):
            rows = bank[first : first + 2 * n_proj, ids_at : ids_at + 128].astype(F32)
            ids.append(rows[:n_proj])
    ids = jnp.concatenate(ids, axis=0)[:, length - ids_at : length - ids_at + 1]
    subset_col = lax.broadcasted_iota(jnp.int32, (ids.shape[0], subsets), 1).astype(F32)
    subset_hot = (subset_col == ids).astype(F32).astype(BF16)
    prior = lax.dot_general(
        extra[:, :subsets].astype(BF16), subset_hot, NT_DIMS, preferred_element_type=F32
    )
    return prior - 0.5 * norm


def bank_pieces(bank, span, n_proj):
    for first in range(0, bank.shape[0], 2 * n_proj):
        both = bank[first : first + 2 * n_proj, span].astype(F32)
        yield both[:n_proj], both[n_proj:]


def shifted_rows(real, imag, cos_ref, sin_ref, span):
    real_rows, imag_rows = [], []
    for t in range(cos_ref.shape[0]):
        cos_part, sin_part = cos_ref[t : t + 1, span], sin_ref[t : t + 1, span]
        real_rows.append(cos_part * real + sin_part * imag)
        imag_rows.append(cos_part * imag - sin_part * real)
    return (
        jnp.concatenate(real_rows, axis=0).astype(BF16),
        jnp.concatenate(imag_rows, axis=0).astype(BF16),
    )


def spans_of(wide):
    step = 256 if wide % 256 == 0 else 128
    return [slice(at, at + step) for at in range(0, wide, step)]


def shift_kernel(n_proj, cos_ref, sin_ref, *rest):
    *banks, shifted_ref, power_ref = rest
    shifts, wide = cos_ref.shape
    width = shifts * n_proj
    for span in spans_of(wide):
        powers, at = [], 0
        for bank in banks:
            for real, imag in bank_pieces(bank, span, n_proj):
                real_rows, imag_rows = shifted_rows(real, imag, cos_ref, sin_ref, span)
                shifted_ref[at : at + width, span] = real_rows
                shifted_ref[at : at + width, wide + span.start : wide + span.stop] = imag_rows
                powers.append(real * real + imag * imag)
                at += width
        power_ref[:, span] = split_terms(jnp.concatenate(powers, axis=0))


def multiply(left, right):
    return lax.dot_general(left, right, NT_DIMS, preferred_element_type=F32)


def pieces_of(cross, norm, extra, banks, length, subsets, n_proj):
    count, total = cross.shape[0], norm.shape[1] // 2
    width = cross.shape[1] * n_proj // total
    norm = norm[:count, total:] + norm[count:, :total] + norm[:count, :total]
    added = added_rows(extra, norm, banks, n_proj, length, subsets)
    pieces = []
    for n in range(total // n_proj):
        scores = cross[:, n * width : (n + 1) * width]
        pieces.append(jnp.concatenate([scores, added[:, n * n_proj : (n + 1) * n_proj]], axis=1))
    return pieces


def store_pieces(out, pieces, first, slot, rows):
    for n, piece in enumerate(pieces):
        at = (first + n) * slot
        out[:, at : at + piece.shape[1]] = piece[rows]


def rows_of(parts, span):
    return jnp.concatenate([part[:, span] for part in parts], axis=0)


def early_kernel(n_parts, n_banks, n_proj, length, subsets, square_ref, *rest):
    parts, rest = rest[:n_parts], rest[n_parts:]
    groups, (select_ref, rows_ref) = [], rest[-2:]
    for n in n_banks:
        groups.append((rest[0], rest[1], rest[2 : 2 + n]))
        rest = rest[2 + n :]
    wide = select_ref.shape[1]
    classes_count = square_ref.shape[0] // 2
    weighted = rows_of(parts, slice(2 * wide))
    extra = rows_of(parts, slice(2 * wide, None)).astype(F32)
    count = extra.shape[0]
    class_col = lax.broadcasted_iota(jnp.int32, (count, classes_count), 1).astype(F32)
    onehot = (class_col == extra[:, subsets : subsets + 1]).astype(F32).astype(BF16)
    for n in range(2):
        squares = square_ref[n * classes_count : (n + 1) * classes_count, :]
        chosen = jnp.dot(onehot, squares, preferred_element_type=F32)
        select_ref[n * count : (n + 1) * count, :] = chosen.astype(BF16)

    pieces = []
    for shifted_ref, power_ref, banks in groups:
        cross = multiply(weighted, shifted_ref[...])
        norm = multiply(select_ref[...], power_ref[...])
        pieces += pieces_of(cross, norm, extra, banks, length, subsets, n_proj)
    store_pieces(rows_ref, pieces, 0, rows_ref.shape[1] // len(pieces), slice(None))


def final_kernel(
    half, n_parts, bits, n_proj, length, subsets, select_ref, rows_ref, cos_ref, sin_ref, last_ref, *rest
):
    parts, outs = rest[:n_parts], rest[n_parts:]
    shifts, wide = cos_ref.shape
    cross, norm = None, None
    for span in spans_of(wide):
        terms, powers = [], []
        for real, imag in bank_pieces(last_ref, span, n_proj):
            real_rows, imag_rows = shifted_rows(real, imag, cos_ref, sin_ref, span)
            terms.append(
                multiply(rows_of(parts, span), real_rows)
                + multiply(rows_of(parts, slice(wide + span.start, wide + span.stop)), imag_rows)
            )
            powers.append(real * real + imag * imag)
        terms = jnp.concatenate(terms, axis=1)
        norms = multiply(select_ref[:, span], split_terms(jnp.concatenate(powers, axis=0)))
        cross = terms if cross is None else cross + terms
        norm = norms if norm is None else norm + norms
    extra = rows_of(parts, slice(2 * wide, None)).astype(F32)
    pieces = pieces_of(cross, norm, extra, [last_ref], length, subsets, n_proj)
    dest, lanes = outs[0].shape
    slot = lanes // half
    ng = 1 << len(bits)
    n_part = dest // ng
    g = lax.axis_index("grp")
    row = lax.broadcasted_iota(jnp.int32, (dest, slot), 0)

    def in_rows(values, d):
        found = []
        for away in range(ng):
            source = d
            for n, bit in enumerate(bits):
                source += (2 << n) if away & bit else 0
            found.append(values[source * n_part : (source + 1) * n_part])
        values = jnp.concatenate(found, axis=0)
        for bit in bits:
            step = bit * n_part
            other = jnp.where(
                (row & step) != 0, pltpu.roll(values, step, 0), pltpu.roll(values, dest - step, 0)
            )
            values = jnp.where((g & bit) != 0, other, values)
        return values

    zeros = jnp.zeros((2 * dest, slot - pieces[0].shape[1]), F32)
    held = [rows_ref[:, at : at + slot] for at in range(0, rows_ref.shape[1], slot)]
    held += [jnp.concatenate([piece, zeros], axis=1) for piece in pieces]
    for d, out in enumerate(outs):
        for n, values in enumerate(held):
            out[:, n * slot : (n + 1) * slot] = in_rows(values, d)


def place_kernel(half, n_proj, order, keep_ref, recv_ref, out_ref):
    blk = lax.axis_index("blk")
    own_first = blk < half
    keep, recv = keep_ref[...], recv_ref[...]
    slot = keep.shape[1] // half
    shifts = out_ref.shape[0]
    parts = []
    for values in (jnp.where(own_first, keep, recv), jnp.where(own_first, recv, keep)):
        found = [values[:, order.index(n) * slot : (order.index(n) + 1) * slot] for n in range(half)]
        bit = 1
        while bit < half:
            swapped = (blk & bit) != 0
            found = [jnp.where(swapped, found[n ^ bit], found[n]) for n in range(half)]
            bit *= 2
        parts += found

    def line(t):
        return jnp.concatenate([part[:, t * n_proj : (t + 1) * n_proj] for part in parts], axis=1)

    added = line(shifts)
    for t in range(shifts):
        out_ref[t] = line(t) + added


def per_device(
    particles,
    ctf_class,
    orient_prior,
    ctf_curves,
    noise_weight,
    shift_phase,
    trans_index,
    projections,
    orient_subset,
):
    nb, ng = lax.axis_size("blk"), lax.axis_size("grp")
    half = nb // 2
    n_part, n_proj = particles.shape[0], projections.shape[0]
    length = particles.shape[2]
    shifts = shift_phase.shape[0]
    classes_count = ctf_curves.shape[0]
    subsets = orient_prior.shape[1]
    wide = 128 * (length // 128 + 1)
    extra = 128 * (subsets // 128 + 1)
    noise = noise_weight.reshape(1, length)
    shape = jax.ShapeDtypeStruct

    def vmem_out(dims, dtype):
        return pltpu.VMEM(dims, dtype)

    operands = (
        ctf_class,
        orient_subset,
        particles,
        orient_prior,
        ctf_curves,
        noise,
        projections,
        shift_phase,
        trans_index,
    )
    bank, part, curves, noise, angle = pl.pallas_call(
        pack_kernel,
        out_shape=[
            vmem_out((2 * n_proj, wide), BF16),
            vmem_out((n_part, 2 * wide + extra), BF16),
            vmem_out(ctf_curves.shape, F32),
            vmem_out(noise.shape, F32),
            vmem_out(shift_phase.shape, F32),
        ],
        in_specs=[pl.BlockSpec(memory_space=pltpu.HBM)] * len(operands),
        out_specs=[_vmem()] * 5,
        scratch_shapes=[
            pltpu.SMEM(ctf_class.shape, jnp.int32),
            pltpu.SMEM(orient_subset.shape, jnp.int32),
            pltpu.SMEM(trans_index.shape, jnp.int32),
            pltpu.VMEM(particles.shape, BF16),
            pltpu.VMEM(orient_prior.shape, BF16),
            pltpu.VMEM(shift_phase.shape, F32),
            pltpu.VMEM(projections.shape, BF16),
            pltpu.SemaphoreType.DMA((len(operands) + 4,)),
        ],
        compiler_params=_params(16),
        name="pack",
    )(*[pltpu.with_memory_space_constraint(operand, pltpu.HBM) for operand in operands])

    def swap(value, axis, bit):
        size = lax.axis_size(axis)
        return lax.ppermute(value, axis, [(i, i ^ bit) for i in range(size)])

    def joined(pieces):
        return pieces[0] if len(pieces) == 1 else jnp.concatenate(pieces, axis=0)

    across = swap(part, "blk", half)
    near = swap(bank, "blk", 1)
    planes, order = [bank], [0]
    for n in range(half.bit_length() - 2, 0, -1):
        planes.append(swap(joined(planes), "blk", 1 << n))
        order += [offset ^ (1 << n) for offset in order]
    far, near = lax.optimization_barrier((joined(planes[1:]), near))
    last = swap(jnp.pad(far, ((0, 0), (0, 3 * 128))), "blk", 1)
    order = [0, 1] + order[1:] + [offset ^ 1 for offset in order[1:]]

    cos_part, sin_part, square = pl.pallas_call(
        table_kernel,
        out_shape=[
            vmem_out((shifts, wide), F32),
            vmem_out((shifts, wide), F32),
            vmem_out((2 * classes_count, wide), BF16),
        ],
        in_specs=[_vmem()] * 3,
        out_specs=[_vmem()] * 3,
        compiler_params=_params(8),
        cost_estimate=pl.CostEstimate(flops=4_000_000, bytes_accessed=2_000_000, transcendentals=0),
        name="tables",
    )(curves, noise, angle)

    def shifted_call(banks, name):
        total = sum(piece.shape[0] for piece in banks) // 2
        return pl.pallas_call(
            functools.partial(shift_kernel, n_proj),
            out_shape=[vmem_out((shifts * total, 2 * wide), BF16), vmem_out((2 * total, wide), BF16)],
            in_specs=[_vmem()] * (2 + len(banks)),
            out_specs=[_vmem()] * 2,
            compiler_params=_params(16),
            cost_estimate=pl.CostEstimate(
                flops=6 * total * shifts * wide, bytes_accessed=4_000_000, transcendentals=0
            ),
            name=name,
        )(cos_part, sin_part, *banks)

    own_rows, own_power = shifted_call([bank], "shift_own")

    across, own_power = lax.optimization_barrier((across, own_power))
    parts = [part, across]
    bits = [1 << n for n in range(ng.bit_length() - 2, -1, -1)]
    for bit in bits:
        part = joined(parts)
        parts = [part, swap(part, "grp", bit)]

    rest_rows, rest_power = shifted_call([near, far], "shift_rest")
    count = 2 * ng * n_part
    late = half // 2 - 1
    slot = 128 * -(-(shifts + 1) * n_proj // 128)
    select, rows = pl.pallas_call(
        functools.partial(early_kernel, len(parts), (1, 2), n_proj, length, subsets),
        out_shape=[
            vmem_out((2 * count, wide), BF16),
            vmem_out((count, (half - late) * slot), F32),
        ],
        in_specs=[_vmem()] * (8 + len(parts)),
        out_specs=[_vmem()] * 2,
        compiler_params=_params(16),
        cost_estimate=pl.CostEstimate(
            flops=4 * count * (half - late) * n_proj * shifts * wide,
            bytes_accessed=4_000_000,
            transcendentals=0,
        ),
        name="early",
    )(square, *parts, own_rows, own_power, bank, rest_rows, rest_power, near, far)
    keep, give = pl.pallas_call(
        functools.partial(final_kernel, half, len(parts), bits, n_proj, length, subsets),
        out_shape=[vmem_out((ng * n_part, half * slot), F32)] * 2,
        in_specs=[_vmem()] * (5 + len(parts)),
        out_specs=[_vmem()] * 2,
        compiler_params=_params(16),
        cost_estimate=pl.CostEstimate(
            flops=4 * count * late * n_proj * shifts * wide, bytes_accessed=4_000_000, transcendentals=0
        ),
        name="final",
    )(select, rows, cos_part, sin_part, last, *parts)
    scores = pl.pallas_call(
        functools.partial(place_kernel, half, n_proj, order),
        out_shape=shape((shifts, ng * n_part, nb * n_proj), F32),
        in_specs=[_vmem()] * 2,
        out_specs=_vmem(),
        compiler_params=_params(4),
        name="place",
    )(keep, swap(give, "blk", half))
    return scores.transpose(1, 0, 2)


def solution(mesh):
    placed = (
        P(("blk", "grp"), None, None),
        P(("blk", "grp")),
        P(("blk", "grp"), None),
        P(),
        P(),
        P(),
        P(),
        P(("grp", "blk"), None, None),
        P(("grp", "blk")),
    )
    return jax.shard_map(
        per_device, mesh=mesh, in_specs=placed, out_specs=P("blk", None, "grp"), check_vma=False
    )
```

```python
import functools

import jax
import jax.numpy as jnp
from jax import lax
from jax.experimental import pallas as pl
from jax.experimental.pallas import tpu as pltpu
from jax.sharding import PartitionSpec as P

F32 = jnp.float32
BF16 = jnp.bfloat16
HIGHEST = lax.Precision.HIGHEST
NT_DIMS = (((1,), (1,)), ((), ()))
MIB = 1 << 20


def _vmem():
    return pl.BlockSpec(memory_space=pltpu.VMEM)


def _params(mib):
    return pltpu.CompilerParams(vmem_limit_bytes=mib * MIB)


def pack_kernel(
    class_hbm,
    subset_hbm,
    particles_hbm,
    prior_hbm,
    curves_hbm,
    noise_hbm,
    proj_hbm,
    phase_hbm,
    trans_hbm,
    bank_ref,
    part_ref,
    curves_ref,
    noise_ref,
    angle_ref,
    class_ref,
    subset_ref,
    trans_ref,
    particles_ref,
    prior_ref,
    phase_ref,
    proj_ref,
    sems,
):
    n_proj, n_class = proj_hbm.shape[0], curves_hbm.shape[0]
    pairs = [
        (proj_hbm.at[: n_proj // 2], proj_ref.at[: n_proj // 2]),
        (proj_hbm.at[n_proj // 2 :], proj_ref.at[n_proj // 2 :]),
        (subset_hbm, subset_ref),
        (class_hbm, class_ref),
        (curves_hbm.at[: n_class // 4], curves_ref.at[: n_class // 4]),
        (curves_hbm.at[n_class // 4 : n_class // 2], curves_ref.at[n_class // 4 : n_class // 2]),
        (curves_hbm.at[n_class // 2 : 3 * n_class // 4], curves_ref.at[n_class // 2 : 3 * n_class // 4]),
        (curves_hbm.at[3 * n_class // 4 :], curves_ref.at[3 * n_class // 4 :]),
        (particles_hbm, particles_ref),
        (noise_hbm, noise_ref),
        (prior_hbm, prior_ref),
        (trans_hbm, trans_ref),
        (phase_hbm, phase_ref),
    ]
    copies = [pltpu.make_async_copy(a, b, sems.at[n]) for n, (a, b) in enumerate(pairs)]
    for copy in copies:
        copy.start()
    n_part = particles_ref.shape[0]
    length = proj_ref.shape[2]
    wide = bank_ref.shape[1]

    def padded(values, width):
        zeros = jnp.zeros((values.shape[0], width - values.shape[1]), values.dtype)
        return jnp.concatenate([values, zeros], axis=1)

    row = lax.broadcasted_iota(jnp.int32, (n_proj, wide), 0)
    lane = lax.broadcasted_iota(jnp.int32, (n_proj, wide), 1)
    for copy in copies[:3]:
        copy.wait()
    real = jnp.zeros((n_proj, wide), F32)
    imag = jnp.zeros((n_proj, wide), F32)
    for j in range(n_proj):
        both = padded(proj_ref[j].astype(F32), wide)
        real = jnp.where(row == j, both[0:1], real)
        imag = jnp.where(row == j, both[1:2], imag)
    last = slice(wide - 128, wide)
    ends = real[:, last]
    for j in range(n_proj):
        here = (row[:, last] == j) & (lane[:, last] == length)
        ends = jnp.where(here, subset_ref[j].astype(F32), ends)
    real = jnp.concatenate([real[:, : wide - 128], ends], axis=1)
    bank_ref[...] = jnp.concatenate([real, imag], axis=0).astype(BF16)

    for copy in copies[3:]:
        copy.wait()
    subsets = prior_ref.shape[1]
    extra = part_ref.shape[1] - 2 * wide
    row = lax.broadcasted_iota(jnp.int32, (n_part, wide), 0)
    row_extra = lax.broadcasted_iota(jnp.int32, (n_part, extra), 0)
    lane_extra = lax.broadcasted_iota(jnp.int32, (n_part, extra), 1)
    real = jnp.zeros((n_part, wide), F32)
    imag = jnp.zeros((n_part, wide), F32)
    small = padded(prior_ref[...].astype(F32), extra)
    for i in range(n_part):
        curve = curves_ref[pl.ds(class_ref[i], 1), :] * noise_ref[...]
        both = padded(particles_ref[i].astype(F32) * curve, wide)
        real = jnp.where(row == i, both[0:1], real)
        imag = jnp.where(row == i, both[1:2], imag)
        place = (row_extra == i) & (lane_extra == subsets)
        small = jnp.where(place, class_ref[i].astype(F32), small)
    part_ref[:, :wide] = real.astype(BF16)
    part_ref[:, wide : 2 * wide] = imag.astype(BF16)
    part_ref[:, 2 * wide :] = small.astype(BF16)
    for t in range(phase_ref.shape[0]):
        angle_ref[t : t + 1, :] = phase_ref[pl.ds(trans_ref[t], 1), :]


def sine_cosine(x):
    turns = jnp.floor(x * 0.6366197723675814 + 0.5)
    r = ((x - turns * 1.5703125) - turns * 4.837512969970703125e-4) - turns * 7.549789954891882e-8
    z = r * r
    sine = r + r * z * (-1.6666654611e-1 + z * (8.3321608736e-3 - z * 1.9515295891e-4))
    cosine = 1.0 - 0.5 * z + z * z * (
        4.166664568298827e-2 + z * (-1.388731625493765e-3 + z * 2.443315711809948e-5)
    )
    quarter = turns.astype(jnp.int32) & 3
    swapped = (quarter & 1) == 1
    first, second = jnp.where(swapped, cosine, sine), jnp.where(swapped, sine, cosine)
    first = jnp.where(quarter >= 2, -first, first)
    second = jnp.where((quarter == 1) | (quarter == 2), -second, second)
    return first, second


def split_terms(values):
    high = values.astype(BF16)
    low = (values - high.astype(F32)).astype(BF16)
    return jnp.concatenate([high, low], axis=0)


def table_kernel(curves_ref, noise_ref, angle_ref, cos_ref, sin_ref, square_ref):
    length = curves_ref.shape[1]
    wide = cos_ref.shape[1]
    zeros = jnp.zeros((cos_ref.shape[0], wide - length), F32)
    sine, cosine = sine_cosine(angle_ref[...])
    cos_ref[...] = jnp.concatenate([cosine, zeros], axis=1)
    sin_ref[...] = jnp.concatenate([sine, zeros], axis=1)
    curve = curves_ref[...]
    square = split_terms(curve * curve * noise_ref[...])
    square_ref[...] = jnp.concatenate(
        [square, jnp.zeros((square.shape[0], wide - length), BF16)], axis=1
    )


def added_rows(extra, norm, banks, n_proj, length, subsets):
    ids_at = length // 128 * 128
    ids = []
    for bank in banks:
        for first in range(0, bank.shape[0], 2 * n_proj):
            rows = bank[first : first + 2 * n_proj, ids_at : ids_at + 128].astype(F32)
            ids.append(rows[:n_proj])
    ids = jnp.concatenate(ids, axis=0)[:, length - ids_at : length - ids_at + 1]
    subset_col = lax.broadcasted_iota(jnp.int32, (ids.shape[0], subsets), 1).astype(F32)
    subset_hot = (subset_col == ids).astype(F32).astype(BF16)
    prior = lax.dot_general(
        extra[:, :subsets].astype(BF16), subset_hot, NT_DIMS, preferred_element_type=F32
    )
    return prior - 0.5 * norm


def bank_pieces(bank, span, n_proj):
    for first in range(0, bank.shape[0], 2 * n_proj):
        both = bank[first : first + 2 * n_proj, span].astype(F32)
        yield both[:n_proj], both[n_proj:]


def shifted_rows(real, imag, cos_ref, sin_ref, span):
    real_rows, imag_rows = [], []
    for t in range(cos_ref.shape[0]):
        cos_part, sin_part = cos_ref[t : t + 1, span], sin_ref[t : t + 1, span]
        real_rows.append(cos_part * real + sin_part * imag)
        imag_rows.append(cos_part * imag - sin_part * real)
    return (
        jnp.concatenate(real_rows, axis=0).astype(BF16),
        jnp.concatenate(imag_rows, axis=0).astype(BF16),
    )


def spans_of(wide):
    step = 256 if wide % 256 == 0 else 128
    return [slice(at, at + step) for at in range(0, wide, step)]


def shift_kernel(n_proj, cos_ref, sin_ref, *rest):
    *banks, shifted_ref, power_ref = rest
    shifts, wide = cos_ref.shape
    width = shifts * n_proj
    for span in spans_of(wide):
        powers, at = [], 0
        for bank in banks:
            for real, imag in bank_pieces(bank, span, n_proj):
                real_rows, imag_rows = shifted_rows(real, imag, cos_ref, sin_ref, span)
                shifted_ref[at : at + width, span] = real_rows
                shifted_ref[at : at + width, wide + span.start : wide + span.stop] = imag_rows
                powers.append(real * real + imag * imag)
                at += width
        power_ref[:, span] = split_terms(jnp.concatenate(powers, axis=0))


def multiply(left, right):
    return lax.dot_general(left, right, NT_DIMS, preferred_element_type=F32)


def added(total, terms):
    return terms if total is None else total + terms


def pieces_of(cross, norm, extra, banks, length, subsets, n_proj):
    count, total = cross.shape[0], norm.shape[1] // 2
    width = cross.shape[1] * n_proj // total
    norm = norm[:count, total:] + norm[count:, :total] + norm[:count, :total]
    offset = added_rows(extra, norm, banks, n_proj, length, subsets)
    pieces = []
    for n in range(total // n_proj):
        scores = cross[:, n * width : (n + 1) * width]
        pieces.append(jnp.concatenate([scores, offset[:, n * n_proj : (n + 1) * n_proj]], axis=1))
    return pieces


def store_pieces(out, pieces, first, slot, rows):
    for n, piece in enumerate(pieces):
        at = (first + n) * slot
        out[:, at : at + piece.shape[1]] = piece[rows]


def rows_of(parts, span):
    return jnp.concatenate([part[:, span] for part in parts], axis=0)


def early_kernel(n_parts, n_banks, n_proj, length, subsets, square_ref, *rest):
    parts, rest = rest[:n_parts], rest[n_parts:]
    groups, (select_ref, rows_ref) = [], rest[-2:]
    for n in n_banks:
        groups.append((rest[0], rest[1], rest[2 : 2 + n]))
        rest = rest[2 + n :]
    wide = select_ref.shape[1]
    classes_count = square_ref.shape[0] // 2
    extra = rows_of(parts, slice(2 * wide, None)).astype(F32)
    count = extra.shape[0]
    class_col = lax.broadcasted_iota(jnp.int32, (count, classes_count), 1).astype(F32)
    onehot = (class_col == extra[:, subsets : subsets + 1]).astype(F32).astype(BF16)
    for n in range(2):
        squares = square_ref[n * classes_count : (n + 1) * classes_count, :]
        chosen = jnp.dot(onehot, squares, preferred_element_type=F32)
        select_ref[n * count : (n + 1) * count, :] = chosen.astype(BF16)

    pieces = []
    for shifted_ref, power_ref, banks in groups:
        cross, turned = None, None
        for at in range(0, wide, 512):
            span = slice(at, min(at + 512, wide))
            other = slice(wide + span.start, wide + span.stop)
            cross = added(cross, multiply(rows_of(parts, span), shifted_ref[:, span]))
            turned = added(turned, multiply(shifted_ref[:, other], rows_of(parts, other)))
        norm = multiply(select_ref[...], power_ref[...])
        pieces += pieces_of(cross + turned.T, norm, extra, banks, length, subsets, n_proj)
    store_pieces(rows_ref, pieces, 0, rows_ref.shape[1] // len(pieces), slice(None))


def final_kernel(
    half, n_parts, bits, n_proj, length, subsets, select_ref, rows_ref, cos_ref, sin_ref, last_ref, *rest
):
    parts, outs = rest[:n_parts], rest[n_parts:]
    shifts, wide = cos_ref.shape
    cross, turned, norm = None, None, None
    for span in spans_of(wide):
        terms, others, powers = [], [], []
        for real, imag in bank_pieces(last_ref, span, n_proj):
            real_rows, imag_rows = shifted_rows(real, imag, cos_ref, sin_ref, span)
            terms.append(multiply(rows_of(parts, span), real_rows))
            other = slice(wide + span.start, wide + span.stop)
            others.append(multiply(imag_rows, rows_of(parts, other)))
            powers.append(real * real + imag * imag)
        cross = added(cross, jnp.concatenate(terms, axis=1))
        turned = added(turned, jnp.concatenate(others, axis=0))
        power = split_terms(jnp.concatenate(powers, axis=0))
        norm = added(norm, multiply(select_ref[:, span], power))
    cross = cross + turned.T
    extra = rows_of(parts, slice(2 * wide, None)).astype(F32)
    pieces = pieces_of(cross, norm, extra, [last_ref], length, subsets, n_proj)
    dest, lanes = outs[0].shape
    slot = rows_ref.shape[1] // (half - len(pieces))
    width = pieces[0].shape[1]
    ng = 1 << len(bits)
    n_part = dest // ng
    g = lax.axis_index("grp")
    row = lax.broadcasted_iota(jnp.int32, (dest, slot), 0)

    def in_rows(values, d):
        found = []
        for away in range(ng):
            source = d
            for n, bit in enumerate(bits):
                source += (2 << n) if away & bit else 0
            found.append(values[source * n_part : (source + 1) * n_part])
        values = jnp.concatenate(found, axis=0)
        for bit in bits:
            step = bit * n_part
            other = jnp.where(
                (row & step) != 0, pltpu.roll(values, step, 0), pltpu.roll(values, dest - step, 0)
            )
            values = jnp.where((g & bit) != 0, other, values)
        return values

    zeros = jnp.zeros((2 * dest, slot - pieces[0].shape[1]), F32)
    held = [rows_ref[:, at : at + slot] for at in range(0, rows_ref.shape[1], slot)]
    held += [jnp.concatenate([piece, zeros], axis=1) for piece in pieces]
    padding = [jnp.zeros((dest, lanes - half * width), F32)] if lanes > half * width else []
    for d, out in enumerate(outs):
        rows = [in_rows(values, d)[:, :width] for values in held]
        out[...] = jnp.concatenate(rows + padding, axis=1)


def place_kernel(half, n_proj, order, keep_ref, recv_ref, out_ref):
    blk = lax.axis_index("blk")
    own_first = blk < half
    keep, recv = keep_ref[...], recv_ref[...]
    shifts = out_ref.shape[0]
    slot = (shifts + 1) * n_proj
    parts = []
    for values in (jnp.where(own_first, keep, recv), jnp.where(own_first, recv, keep)):
        found = [values[:, order.index(n) * slot : (order.index(n) + 1) * slot] for n in range(half)]
        bit = 1
        while bit < half:
            swapped = (blk & bit) != 0
            found = [jnp.where(swapped, found[n ^ bit], found[n]) for n in range(half)]
            bit *= 2
        parts += found

    def line(t):
        return jnp.concatenate([part[:, t * n_proj : (t + 1) * n_proj] for part in parts], axis=1)

    added = line(shifts)
    for t in range(shifts):
        out_ref[t] = line(t) + added


def per_device(
    particles,
    ctf_class,
    orient_prior,
    ctf_curves,
    noise_weight,
    shift_phase,
    trans_index,
    projections,
    orient_subset,
):
    nb, ng = lax.axis_size("blk"), lax.axis_size("grp")
    half = nb // 2
    n_part, n_proj = particles.shape[0], projections.shape[0]
    length = particles.shape[2]
    shifts = shift_phase.shape[0]
    classes_count = ctf_curves.shape[0]
    subsets = orient_prior.shape[1]
    wide = 128 * (length // 128 + 1)
    extra = 128 * (subsets // 128 + 1)
    noise = noise_weight.reshape(1, length)
    shape = jax.ShapeDtypeStruct

    def vmem_out(dims, dtype):
        return pltpu.VMEM(dims, dtype)

    operands = (
        ctf_class,
        orient_subset,
        particles,
        orient_prior,
        ctf_curves,
        noise,
        projections,
        shift_phase,
        trans_index,
    )
    bank, part, curves, noise, angle = pl.pallas_call(
        pack_kernel,
        out_shape=[
            vmem_out((2 * n_proj, wide), BF16),
            vmem_out((n_part, 2 * wide + extra), BF16),
            vmem_out(ctf_curves.shape, F32),
            vmem_out(noise.shape, F32),
            vmem_out(shift_phase.shape, F32),
        ],
        in_specs=[pl.BlockSpec(memory_space=pltpu.HBM)] * len(operands),
        out_specs=[_vmem()] * 5,
        scratch_shapes=[
            pltpu.SMEM(ctf_class.shape, jnp.int32),
            pltpu.SMEM(orient_subset.shape, jnp.int32),
            pltpu.SMEM(trans_index.shape, jnp.int32),
            pltpu.VMEM(particles.shape, BF16),
            pltpu.VMEM(orient_prior.shape, BF16),
            pltpu.VMEM(shift_phase.shape, F32),
            pltpu.VMEM(projections.shape, BF16),
            pltpu.SemaphoreType.DMA((len(operands) + 4,)),
        ],
        compiler_params=_params(16),
        name="pack",
    )(*[pltpu.with_memory_space_constraint(operand, pltpu.HBM) for operand in operands])

    def swap(value, axis, bit):
        size = lax.axis_size(axis)
        return lax.ppermute(value, axis, [(i, i ^ bit) for i in range(size)])

    def joined(pieces):
        return pieces[0] if len(pieces) == 1 else jnp.concatenate(pieces, axis=0)

    across = swap(part, "blk", half)
    near = swap(bank, "blk", 1)
    planes, order = [bank], [0]
    for n in range(half.bit_length() - 2, 0, -1):
        planes.append(swap(joined(planes), "blk", 1 << n))
        order += [offset ^ (1 << n) for offset in order]
    far, near = lax.optimization_barrier((joined(planes[1:]), near))
    last = swap(jnp.pad(far, ((0, 0), (0, 3 * 128))), "blk", 1)
    order = [0, 1] + order[1:] + [offset ^ 1 for offset in order[1:]]

    cos_part, sin_part, square = pl.pallas_call(
        table_kernel,
        out_shape=[
            vmem_out((shifts, wide), F32),
            vmem_out((shifts, wide), F32),
            vmem_out((2 * classes_count, wide), BF16),
        ],
        in_specs=[_vmem()] * 3,
        out_specs=[_vmem()] * 3,
        compiler_params=_params(8),
        cost_estimate=pl.CostEstimate(flops=4_000_000, bytes_accessed=2_000_000, transcendentals=0),
        name="tables",
    )(curves, noise, angle)

    def shifted_call(banks, name):
        total = sum(piece.shape[0] for piece in banks) // 2
        return pl.pallas_call(
            functools.partial(shift_kernel, n_proj),
            out_shape=[vmem_out((shifts * total, 2 * wide), BF16), vmem_out((2 * total, wide), BF16)],
            in_specs=[_vmem()] * (2 + len(banks)),
            out_specs=[_vmem()] * 2,
            compiler_params=_params(16),
            cost_estimate=pl.CostEstimate(
                flops=6 * total * shifts * wide, bytes_accessed=4_000_000, transcendentals=0
            ),
            name=name,
        )(cos_part, sin_part, *banks)

    own_rows, own_power = shifted_call([bank], "shift_own")

    across, own_power = lax.optimization_barrier((across, own_power))
    parts = [part, across]
    bits = [1 << n for n in range(ng.bit_length() - 2, -1, -1)]
    for bit in bits:
        part = joined(parts)
        parts = [part, swap(part, "grp", bit)]

    rest_rows, rest_power = shifted_call([near, far], "shift_rest")
    count = 2 * ng * n_part
    late = half // 2 - 1
    slot = 128 * -(-(shifts + 1) * n_proj // 128)
    lanes = 128 * -(-(shifts + 1) * n_proj * half // 128)
    select, rows = pl.pallas_call(
        functools.partial(early_kernel, len(parts), (1, 2), n_proj, length, subsets),
        out_shape=[
            vmem_out((2 * count, wide), BF16),
            vmem_out((count, (half - late) * slot), F32),
        ],
        in_specs=[_vmem()] * (8 + len(parts)),
        out_specs=[_vmem()] * 2,
        compiler_params=_params(16),
        cost_estimate=pl.CostEstimate(
            flops=4 * count * (half - late) * n_proj * shifts * wide,
            bytes_accessed=4_000_000,
            transcendentals=0,
        ),
        name="early",
    )(square, *parts, own_rows, own_power, bank, rest_rows, rest_power, near, far)
    keep, give = pl.pallas_call(
        functools.partial(final_kernel, half, len(parts), bits, n_proj, length, subsets),
        out_shape=[vmem_out((ng * n_part, lanes), F32)] * 2,
        in_specs=[_vmem()] * (5 + len(parts)),
        out_specs=[_vmem()] * 2,
        compiler_params=_params(16),
        cost_estimate=pl.CostEstimate(
            flops=4 * count * late * n_proj * shifts * wide, bytes_accessed=4_000_000, transcendentals=0
        ),
        name="final",
    )(select, rows, cos_part, sin_part, last, *parts)
    scores = pl.pallas_call(
        functools.partial(place_kernel, half, n_proj, order),
        out_shape=shape((shifts, ng * n_part, nb * n_proj), F32),
        in_specs=[_vmem()] * 2,
        out_specs=_vmem(),
        compiler_params=_params(4),
        name="place",
    )(keep, swap(give, "blk", half))
    return scores.transpose(1, 0, 2)


def solution(mesh):
    placed = (
        P(("blk", "grp"), None, None),
        P(("blk", "grp")),
        P(("blk", "grp"), None),
        P(),
        P(),
        P(),
        P(),
        P(("grp", "blk"), None, None),
        P(("grp", "blk")),
    )
    return jax.shard_map(
        per_device, mesh=mesh, in_specs=placed, out_specs=P("blk", None, "grp"), check_vma=False
    )
```

```python
import functools

import jax
import jax.numpy as jnp
from jax import lax
from jax.experimental import pallas as pl
from jax.experimental.pallas import tpu as pltpu
from jax.sharding import PartitionSpec as P

F32 = jnp.float32
BF16 = jnp.bfloat16
HIGHEST = lax.Precision.HIGHEST
NT_DIMS = (((1,), (1,)), ((), ()))
MIB = 1 << 20


def _vmem():
    return pl.BlockSpec(memory_space=pltpu.VMEM)


def _params(mib):
    return pltpu.CompilerParams(vmem_limit_bytes=mib * MIB)


def pack_kernel(
    class_hbm,
    subset_hbm,
    particles_hbm,
    prior_hbm,
    curves_hbm,
    noise_hbm,
    proj_hbm,
    phase_hbm,
    trans_hbm,
    bank_ref,
    part_ref,
    curves_ref,
    noise_ref,
    angle_ref,
    class_ref,
    subset_ref,
    trans_ref,
    particles_ref,
    prior_ref,
    phase_ref,
    proj_ref,
    sems,
):
    n_proj, n_class = proj_hbm.shape[0], curves_hbm.shape[0]
    pairs = [
        (proj_hbm.at[: n_proj // 2], proj_ref.at[: n_proj // 2]),
        (proj_hbm.at[n_proj // 2 :], proj_ref.at[n_proj // 2 :]),
        (subset_hbm, subset_ref),
        (class_hbm, class_ref),
        (curves_hbm.at[: n_class // 4], curves_ref.at[: n_class // 4]),
        (curves_hbm.at[n_class // 4 : n_class // 2], curves_ref.at[n_class // 4 : n_class // 2]),
        (curves_hbm.at[n_class // 2 : 3 * n_class // 4], curves_ref.at[n_class // 2 : 3 * n_class // 4]),
        (curves_hbm.at[3 * n_class // 4 :], curves_ref.at[3 * n_class // 4 :]),
        (particles_hbm, particles_ref),
        (noise_hbm, noise_ref),
        (prior_hbm, prior_ref),
        (trans_hbm, trans_ref),
        (phase_hbm, phase_ref),
    ]
    copies = [pltpu.make_async_copy(a, b, sems.at[n]) for n, (a, b) in enumerate(pairs)]
    for copy in copies:
        copy.start()
    n_part = particles_ref.shape[0]
    length = proj_ref.shape[2]
    wide = bank_ref.shape[1]

    def padded(values, width):
        zeros = jnp.zeros((values.shape[0], width - values.shape[1]), values.dtype)
        return jnp.concatenate([values, zeros], axis=1)

    row = lax.broadcasted_iota(jnp.int32, (n_proj, wide), 0)
    lane = lax.broadcasted_iota(jnp.int32, (n_proj, wide), 1)
    for copy in copies[:3]:
        copy.wait()
    real = jnp.zeros((n_proj, wide), F32)
    imag = jnp.zeros((n_proj, wide), F32)
    for j in range(n_proj):
        both = padded(proj_ref[j].astype(F32), wide)
        real = jnp.where(row == j, both[0:1], real)
        imag = jnp.where(row == j, both[1:2], imag)
    last = slice(wide - 128, wide)
    ends = real[:, last]
    for j in range(n_proj):
        here = (row[:, last] == j) & (lane[:, last] == length)
        ends = jnp.where(here, subset_ref[j].astype(F32), ends)
    real = jnp.concatenate([real[:, : wide - 128], ends], axis=1)
    bank_ref[...] = jnp.concatenate([real, imag], axis=0).astype(BF16)

    for copy in copies[3:]:
        copy.wait()
    subsets = prior_ref.shape[1]
    extra = part_ref.shape[1] - 2 * wide
    row = lax.broadcasted_iota(jnp.int32, (n_part, wide), 0)
    row_extra = lax.broadcasted_iota(jnp.int32, (n_part, extra), 0)
    lane_extra = lax.broadcasted_iota(jnp.int32, (n_part, extra), 1)
    real = jnp.zeros((n_part, wide), F32)
    imag = jnp.zeros((n_part, wide), F32)
    small = padded(prior_ref[...].astype(F32), extra)
    for i in range(n_part):
        curve = curves_ref[pl.ds(class_ref[i], 1), :] * noise_ref[...]
        both = padded(particles_ref[i].astype(F32) * curve, wide)
        real = jnp.where(row == i, both[0:1], real)
        imag = jnp.where(row == i, both[1:2], imag)
        place = (row_extra == i) & (lane_extra == subsets)
        small = jnp.where(place, class_ref[i].astype(F32), small)
    part_ref[:, :wide] = real.astype(BF16)
    part_ref[:, wide : 2 * wide] = imag.astype(BF16)
    part_ref[:, 2 * wide :] = small.astype(BF16)
    for t in range(phase_ref.shape[0]):
        angle_ref[t : t + 1, :] = phase_ref[pl.ds(trans_ref[t], 1), :]


def sine_cosine(x):
    turns = jnp.floor(x * 0.6366197723675814 + 0.5)
    r = ((x - turns * 1.5703125) - turns * 4.837512969970703125e-4) - turns * 7.549789954891882e-8
    z = r * r
    sine = r + r * z * (-1.6666654611e-1 + z * (8.3321608736e-3 - z * 1.9515295891e-4))
    cosine = 1.0 - 0.5 * z + z * z * (
        4.166664568298827e-2 + z * (-1.388731625493765e-3 + z * 2.443315711809948e-5)
    )
    quarter = turns.astype(jnp.int32) & 3
    swapped = (quarter & 1) == 1
    first, second = jnp.where(swapped, cosine, sine), jnp.where(swapped, sine, cosine)
    first = jnp.where(quarter >= 2, -first, first)
    second = jnp.where((quarter == 1) | (quarter == 2), -second, second)
    return first, second


def split_terms(values):
    high = values.astype(BF16)
    low = (values - high.astype(F32)).astype(BF16)
    return jnp.concatenate([high, low], axis=0)


def table_kernel(curves_ref, noise_ref, angle_ref, cos_ref, sin_ref, square_ref):
    length = curves_ref.shape[1]
    wide = cos_ref.shape[1]
    zeros = jnp.zeros((cos_ref.shape[0], wide - length), F32)
    sine, cosine = sine_cosine(angle_ref[...])
    cos_ref[...] = jnp.concatenate([cosine, zeros], axis=1)
    sin_ref[...] = jnp.concatenate([sine, zeros], axis=1)
    curve = curves_ref[...]
    square = split_terms(curve * curve * noise_ref[...])
    square_ref[...] = jnp.concatenate(
        [square, jnp.zeros((square.shape[0], wide - length), BF16)], axis=1
    )


def added_rows(extra, norm, banks, n_proj, length, subsets):
    ids_at = length // 128 * 128
    ids = []
    for bank in banks:
        for first in range(0, bank.shape[0], 2 * n_proj):
            rows = bank[first : first + 2 * n_proj, ids_at : ids_at + 128].astype(F32)
            ids.append(rows[:n_proj])
    ids = jnp.concatenate(ids, axis=0)[:, length - ids_at : length - ids_at + 1]
    subset_col = lax.broadcasted_iota(jnp.int32, (ids.shape[0], subsets), 1).astype(F32)
    subset_hot = (subset_col == ids).astype(F32).astype(BF16)
    prior = lax.dot_general(
        extra[:, :subsets].astype(BF16), subset_hot, NT_DIMS, preferred_element_type=F32
    )
    return prior - 0.5 * norm


def bank_pieces(bank, span, n_proj):
    for first in range(0, bank.shape[0], 2 * n_proj):
        both = bank[first : first + 2 * n_proj, span].astype(F32)
        yield both[:n_proj], both[n_proj:]


def shifted_rows(real, imag, cos_ref, sin_ref, span):
    real_rows, imag_rows = [], []
    for t in range(cos_ref.shape[0]):
        cos_part, sin_part = cos_ref[t : t + 1, span], sin_ref[t : t + 1, span]
        real_rows.append(cos_part * real + sin_part * imag)
        imag_rows.append(cos_part * imag - sin_part * real)
    return (
        jnp.concatenate(real_rows, axis=0).astype(BF16),
        jnp.concatenate(imag_rows, axis=0).astype(BF16),
    )


def spans_of(wide):
    step = 256 if wide % 256 == 0 else 128
    return [slice(at, at + step) for at in range(0, wide, step)]


def shift_kernel(n_proj, cos_ref, sin_ref, *rest):
    *banks, shifted_ref, power_ref = rest
    shifts, wide = cos_ref.shape
    width = shifts * n_proj
    for span in spans_of(wide):
        powers, at = [], 0
        for bank in banks:
            for real, imag in bank_pieces(bank, span, n_proj):
                real_rows, imag_rows = shifted_rows(real, imag, cos_ref, sin_ref, span)
                shifted_ref[at : at + width, span] = real_rows
                shifted_ref[at : at + width, wide + span.start : wide + span.stop] = imag_rows
                powers.append(real * real + imag * imag)
                at += width
        power_ref[:, span] = split_terms(jnp.concatenate(powers, axis=0))


def multiply(left, right):
    return lax.dot_general(left, right, NT_DIMS, preferred_element_type=F32)


def added(total, terms):
    return terms if total is None else total + terms


def pieces_of(cross, norm, extra, banks, length, subsets, n_proj):
    count, total = cross.shape[0], norm.shape[1] // 2
    width = cross.shape[1] * n_proj // total
    norm = norm[:count, total:] + norm[count:, :total] + norm[:count, :total]
    offset = added_rows(extra, norm, banks, n_proj, length, subsets)
    pieces = []
    for n in range(total // n_proj):
        scores = cross[:, n * width : (n + 1) * width]
        pieces.append(jnp.concatenate([scores, offset[:, n * n_proj : (n + 1) * n_proj]], axis=1))
    return pieces


def store_pieces(out, pieces, first, slot, rows):
    for n, piece in enumerate(pieces):
        at = (first + n) * slot
        out[:, at : at + piece.shape[1]] = piece[rows]


def rows_of(parts, span):
    return jnp.concatenate([part[:, span] for part in parts], axis=0)


def early_kernel(n_parts, n_banks, n_proj, length, subsets, square_ref, *rest):
    parts, rest = rest[:n_parts], rest[n_parts:]
    groups, (select_ref, rows_ref) = [], rest[-2:]
    for n in n_banks:
        groups.append((rest[0], rest[1], rest[2 : 2 + n]))
        rest = rest[2 + n :]
    wide = select_ref.shape[1]
    classes_count = square_ref.shape[0] // 2
    extra = rows_of(parts, slice(2 * wide, None)).astype(F32)
    count = extra.shape[0]
    class_col = lax.broadcasted_iota(jnp.int32, (count, classes_count), 1).astype(F32)
    onehot = (class_col == extra[:, subsets : subsets + 1]).astype(F32).astype(BF16)
    for n in range(2):
        squares = square_ref[n * classes_count : (n + 1) * classes_count, :]
        chosen = jnp.dot(onehot, squares, preferred_element_type=F32)
        select_ref[n * count : (n + 1) * count, :] = chosen.astype(BF16)

    pieces = []
    for shifted_ref, power_ref, banks in groups:
        cross, turned = None, None
        for at in range(0, wide, 512):
            span = slice(at, min(at + 512, wide))
            other = slice(wide + span.start, wide + span.stop)
            cross = added(cross, multiply(rows_of(parts, span), shifted_ref[:, span]))
            turned = added(turned, multiply(shifted_ref[:, other], rows_of(parts, other)))
        norm = multiply(select_ref[...], power_ref[...])
        pieces += pieces_of(cross + turned.T, norm, extra, banks, length, subsets, n_proj)
    store_pieces(rows_ref, pieces, 0, rows_ref.shape[1] // len(pieces), slice(None))


def final_kernel(
    half, n_parts, bits, n_proj, length, subsets, select_ref, rows_ref, cos_ref, sin_ref, last_ref, *rest
):
    parts, outs = rest[:n_parts], rest[n_parts:]
    shifts, wide = cos_ref.shape
    cross, turned, norm = None, None, None
    for span in spans_of(wide):
        terms, others, powers = [], [], []
        for real, imag in bank_pieces(last_ref, span, n_proj):
            real_rows, imag_rows = shifted_rows(real, imag, cos_ref, sin_ref, span)
            terms.append(multiply(rows_of(parts, span), real_rows))
            other = slice(wide + span.start, wide + span.stop)
            others.append(multiply(imag_rows, rows_of(parts, other)))
            powers.append(real * real + imag * imag)
        cross = added(cross, jnp.concatenate(terms, axis=1))
        turned = added(turned, jnp.concatenate(others, axis=0))
        power = split_terms(jnp.concatenate(powers, axis=0))
        norm = added(norm, multiply(select_ref[:, span], power))
    cross = cross + turned.T
    extra = rows_of(parts, slice(2 * wide, None)).astype(F32)
    pieces = pieces_of(cross, norm, extra, [last_ref], length, subsets, n_proj)
    dest, lanes = outs[0].shape
    slot = rows_ref.shape[1] // (half - len(pieces))
    width = pieces[0].shape[1]
    ng = 1 << len(bits)
    n_part = dest // ng
    g = lax.axis_index("grp")
    row = lax.broadcasted_iota(jnp.int32, (dest, slot), 0)

    def in_rows(values, d):
        found = []
        for away in range(ng):
            source = d
            for n, bit in enumerate(bits):
                source += (2 << n) if away & bit else 0
            found.append(values[source * n_part : (source + 1) * n_part])
        values = jnp.concatenate(found, axis=0)
        for bit in bits:
            step = bit * n_part
            other = jnp.where(
                (row & step) != 0, pltpu.roll(values, step, 0), pltpu.roll(values, dest - step, 0)
            )
            values = jnp.where((g & bit) != 0, other, values)
        return values

    zeros = jnp.zeros((2 * dest, slot - pieces[0].shape[1]), F32)
    held = [rows_ref[:, at : at + slot] for at in range(0, rows_ref.shape[1], slot)]
    held += [jnp.concatenate([piece, zeros], axis=1) for piece in pieces]
    padding = [jnp.zeros((dest, lanes - half * width), F32)] if lanes > half * width else []
    for d, out in enumerate(outs):
        rows = [in_rows(values, d)[:, :width] for values in held]
        out[...] = jnp.concatenate(rows + padding, axis=1)


def place_kernel(half, n_proj, order, keep_ref, recv_ref, out_ref):
    blk = lax.axis_index("blk")
    own_first = blk < half
    dest = keep_ref.shape[0]
    keep = keep_ref[...]
    recv = jnp.where(own_first, recv_ref[dest:], recv_ref[:dest])
    shifts = out_ref.shape[0]
    slot = (shifts + 1) * n_proj
    parts = []
    for values in (jnp.where(own_first, keep, recv), jnp.where(own_first, recv, keep)):
        found = [values[:, order.index(n) * slot : (order.index(n) + 1) * slot] for n in range(half)]
        bit = 1
        while bit < half:
            swapped = (blk & bit) != 0
            found = [jnp.where(swapped, found[n ^ bit], found[n]) for n in range(half)]
            bit *= 2
        parts += found

    def line(t):
        return jnp.concatenate([part[:, t * n_proj : (t + 1) * n_proj] for part in parts], axis=1)

    added = line(shifts)
    for t in range(shifts):
        out_ref[t] = line(t) + added


def per_device(
    particles,
    ctf_class,
    orient_prior,
    ctf_curves,
    noise_weight,
    shift_phase,
    trans_index,
    projections,
    orient_subset,
):
    nb, ng = lax.axis_size("blk"), lax.axis_size("grp")
    half = nb // 2
    n_part, n_proj = particles.shape[0], projections.shape[0]
    length = particles.shape[2]
    shifts = shift_phase.shape[0]
    classes_count = ctf_curves.shape[0]
    subsets = orient_prior.shape[1]
    wide = 128 * (length // 128 + 1)
    extra = 128 * (subsets // 128 + 1)
    noise = noise_weight.reshape(1, length)
    shape = jax.ShapeDtypeStruct

    def vmem_out(dims, dtype):
        return pltpu.VMEM(dims, dtype)

    operands = (
        ctf_class,
        orient_subset,
        particles,
        orient_prior,
        ctf_curves,
        noise,
        projections,
        shift_phase,
        trans_index,
    )
    bank, part, curves, noise, angle = pl.pallas_call(
        pack_kernel,
        out_shape=[
            vmem_out((2 * n_proj, wide), BF16),
            vmem_out((n_part, 2 * wide + extra), BF16),
            vmem_out(ctf_curves.shape, F32),
            vmem_out(noise.shape, F32),
            vmem_out(shift_phase.shape, F32),
        ],
        in_specs=[pl.BlockSpec(memory_space=pltpu.HBM)] * len(operands),
        out_specs=[_vmem()] * 5,
        scratch_shapes=[
            pltpu.SMEM(ctf_class.shape, jnp.int32),
            pltpu.SMEM(orient_subset.shape, jnp.int32),
            pltpu.SMEM(trans_index.shape, jnp.int32),
            pltpu.VMEM(particles.shape, BF16),
            pltpu.VMEM(orient_prior.shape, BF16),
            pltpu.VMEM(shift_phase.shape, F32),
            pltpu.VMEM(projections.shape, BF16),
            pltpu.SemaphoreType.DMA((len(operands) + 4,)),
        ],
        compiler_params=_params(16),
        name="pack",
    )(*[pltpu.with_memory_space_constraint(operand, pltpu.HBM) for operand in operands])

    def swap(value, axis, bit):
        size = lax.axis_size(axis)
        return lax.ppermute(value, axis, [(i, i ^ bit) for i in range(size)])

    def joined(pieces):
        return pieces[0] if len(pieces) == 1 else jnp.concatenate(pieces, axis=0)

    across = swap(part, "blk", half)
    near = swap(bank, "blk", 1)
    planes, order = [bank], [0]
    for n in range(half.bit_length() - 2, 0, -1):
        planes.append(swap(joined(planes), "blk", 1 << n))
        order += [offset ^ (1 << n) for offset in order]
    far, near = lax.optimization_barrier((joined(planes[1:]), near))
    last = swap(jnp.pad(far, ((0, 0), (0, 3 * 128))), "blk", 1)
    order = [0, 1] + order[1:] + [offset ^ 1 for offset in order[1:]]

    cos_part, sin_part, square = pl.pallas_call(
        table_kernel,
        out_shape=[
            vmem_out((shifts, wide), F32),
            vmem_out((shifts, wide), F32),
            vmem_out((2 * classes_count, wide), BF16),
        ],
        in_specs=[_vmem()] * 3,
        out_specs=[_vmem()] * 3,
        compiler_params=_params(8),
        cost_estimate=pl.CostEstimate(flops=4_000_000, bytes_accessed=2_000_000, transcendentals=0),
        name="tables",
    )(curves, noise, angle)

    def shifted_call(banks, name):
        total = sum(piece.shape[0] for piece in banks) // 2
        return pl.pallas_call(
            functools.partial(shift_kernel, n_proj),
            out_shape=[vmem_out((shifts * total, 2 * wide), BF16), vmem_out((2 * total, wide), BF16)],
            in_specs=[_vmem()] * (2 + len(banks)),
            out_specs=[_vmem()] * 2,
            compiler_params=_params(16),
            cost_estimate=pl.CostEstimate(
                flops=6 * total * shifts * wide, bytes_accessed=4_000_000, transcendentals=0
            ),
            name=name,
        )(cos_part, sin_part, *banks)

    own_rows, own_power = shifted_call([bank], "shift_own")

    across, own_power = lax.optimization_barrier((across, own_power))
    parts = [part, across]
    bits = [1 << n for n in range(ng.bit_length() - 2, -1, -1)]
    for bit in bits:
        part = joined(parts)
        parts = [part, swap(part, "grp", bit)]

    rest_rows, rest_power = shifted_call([near, far], "shift_rest")
    count = 2 * ng * n_part
    late = half // 2 - 1
    slot = 128 * -(-(shifts + 1) * n_proj // 128)
    lanes = 128 * -(-(shifts + 1) * n_proj * half // 128)
    select, rows = pl.pallas_call(
        functools.partial(early_kernel, len(parts), (1, 2), n_proj, length, subsets),
        out_shape=[
            vmem_out((2 * count, wide), BF16),
            vmem_out((count, (half - late) * slot), F32),
        ],
        in_specs=[_vmem()] * (8 + len(parts)),
        out_specs=[_vmem()] * 2,
        compiler_params=_params(16),
        cost_estimate=pl.CostEstimate(
            flops=4 * count * (half - late) * n_proj * shifts * wide,
            bytes_accessed=4_000_000,
            transcendentals=0,
        ),
        name="early",
    )(square, *parts, own_rows, own_power, bank, rest_rows, rest_power, near, far)
    keep, give = pl.pallas_call(
        functools.partial(final_kernel, half, len(parts), bits, n_proj, length, subsets),
        out_shape=[vmem_out((ng * n_part, lanes), F32)] * 2,
        in_specs=[_vmem()] * (5 + len(parts)),
        out_specs=[_vmem()] * 2,
        compiler_params=_params(16),
        cost_estimate=pl.CostEstimate(
            flops=4 * count * late * n_proj * shifts * wide, bytes_accessed=4_000_000, transcendentals=0
        ),
        name="final",
    )(select, rows, cos_part, sin_part, last, *parts)
    couples = [[b, b + half] for b in range(half)]
    recv = lax.all_gather(give, "blk", axis_index_groups=couples, axis=0, tiled=True)
    scores = pl.pallas_call(
        functools.partial(place_kernel, half, n_proj, order),
        out_shape=shape((shifts, ng * n_part, nb * n_proj), F32),
        in_specs=[_vmem()] * 2,
        out_specs=_vmem(),
        compiler_params=_params(4),
        name="place",
    )(keep, recv)
    return scores.transpose(1, 0, 2)


def solution(mesh):
    placed = (
        P(("blk", "grp"), None, None),
        P(("blk", "grp")),
        P(("blk", "grp"), None),
        P(),
        P(),
        P(),
        P(),
        P(("grp", "blk"), None, None),
        P(("grp", "blk")),
    )
    return jax.shard_map(
        per_device, mesh=mesh, in_specs=placed, out_specs=P("blk", None, "grp"), check_vma=False
    )
```

```python
import functools

import jax
import jax.numpy as jnp
from jax import lax
from jax.experimental import pallas as pl
from jax.experimental.pallas import tpu as pltpu
from jax.sharding import PartitionSpec as P

F32 = jnp.float32
BF16 = jnp.bfloat16
HIGHEST = lax.Precision.HIGHEST
NT_DIMS = (((1,), (1,)), ((), ()))
MIB = 1 << 20


def _vmem():
    return pl.BlockSpec(memory_space=pltpu.VMEM)


def _params(mib):
    return pltpu.CompilerParams(vmem_limit_bytes=mib * MIB)


def pack_kernel(
    class_hbm,
    subset_hbm,
    particles_hbm,
    prior_hbm,
    curves_hbm,
    noise_hbm,
    proj_hbm,
    phase_hbm,
    trans_hbm,
    bank_ref,
    part_ref,
    curves_ref,
    noise_ref,
    angle_ref,
    class_ref,
    subset_ref,
    trans_ref,
    particles_ref,
    prior_ref,
    phase_ref,
    proj_ref,
    sems,
):
    n_proj, n_class = proj_hbm.shape[0], curves_hbm.shape[0]
    pairs = [
        (proj_hbm.at[: n_proj // 2], proj_ref.at[: n_proj // 2]),
        (proj_hbm.at[n_proj // 2 :], proj_ref.at[n_proj // 2 :]),
        (subset_hbm, subset_ref),
        (class_hbm, class_ref),
        (curves_hbm.at[: n_class // 4], curves_ref.at[: n_class // 4]),
        (curves_hbm.at[n_class // 4 : n_class // 2], curves_ref.at[n_class // 4 : n_class // 2]),
        (curves_hbm.at[n_class // 2 : 3 * n_class // 4], curves_ref.at[n_class // 2 : 3 * n_class // 4]),
        (curves_hbm.at[3 * n_class // 4 :], curves_ref.at[3 * n_class // 4 :]),
        (particles_hbm, particles_ref),
        (noise_hbm, noise_ref),
        (prior_hbm, prior_ref),
        (trans_hbm, trans_ref),
        (phase_hbm, phase_ref),
    ]
    copies = [pltpu.make_async_copy(a, b, sems.at[n]) for n, (a, b) in enumerate(pairs)]
    for copy in copies:
        copy.start()
    n_part = particles_ref.shape[0]
    length = proj_ref.shape[2]
    wide = bank_ref.shape[1]

    def padded(values, width):
        zeros = jnp.zeros((values.shape[0], width - values.shape[1]), values.dtype)
        return jnp.concatenate([values, zeros], axis=1)

    row = lax.broadcasted_iota(jnp.int32, (n_proj, wide), 0)
    lane = lax.broadcasted_iota(jnp.int32, (n_proj, wide), 1)
    for copy in copies[:3]:
        copy.wait()
    real = jnp.zeros((n_proj, wide), F32)
    imag = jnp.zeros((n_proj, wide), F32)
    for j in range(n_proj):
        both = padded(proj_ref[j].astype(F32), wide)
        real = jnp.where(row == j, both[0:1], real)
        imag = jnp.where(row == j, both[1:2], imag)
    last = slice(wide - 128, wide)
    ends = real[:, last]
    for j in range(n_proj):
        here = (row[:, last] == j) & (lane[:, last] == length)
        ends = jnp.where(here, subset_ref[j].astype(F32), ends)
    real = jnp.concatenate([real[:, : wide - 128], ends], axis=1)
    bank_ref[...] = jnp.concatenate([real, imag], axis=0).astype(BF16)

    for copy in copies[-2:]:
        copy.wait()
    for t in range(phase_ref.shape[0]):
        angle_ref[t : t + 1, :] = phase_ref[pl.ds(trans_ref[t], 1), :]
    for copy in copies[3:-2]:
        copy.wait()
    subsets = prior_ref.shape[1]
    extra = part_ref.shape[1] - 2 * wide
    row = lax.broadcasted_iota(jnp.int32, (n_part, wide), 0)
    row_extra = lax.broadcasted_iota(jnp.int32, (n_part, extra), 0)
    lane_extra = lax.broadcasted_iota(jnp.int32, (n_part, extra), 1)
    real = jnp.zeros((n_part, wide), F32)
    imag = jnp.zeros((n_part, wide), F32)
    small = padded(prior_ref[...].astype(F32), extra)
    for i in range(n_part):
        curve = curves_ref[pl.ds(class_ref[i], 1), :] * noise_ref[...]
        both = padded(particles_ref[i].astype(F32) * curve, wide)
        real = jnp.where(row == i, both[0:1], real)
        imag = jnp.where(row == i, both[1:2], imag)
        place = (row_extra == i) & (lane_extra == subsets)
        small = jnp.where(place, class_ref[i].astype(F32), small)
    part_ref[:, :wide] = real.astype(BF16)
    part_ref[:, wide : 2 * wide] = imag.astype(BF16)
    part_ref[:, 2 * wide :] = small.astype(BF16)


def sine_cosine(x):
    turns = jnp.floor(x * 0.6366197723675814 + 0.5)
    r = ((x - turns * 1.5703125) - turns * 4.837512969970703125e-4) - turns * 7.549789954891882e-8
    z = r * r
    sine = r + r * z * (-1.6666654611e-1 + z * (8.3321608736e-3 - z * 1.9515295891e-4))
    cosine = 1.0 - 0.5 * z + z * z * (
        4.166664568298827e-2 + z * (-1.388731625493765e-3 + z * 2.443315711809948e-5)
    )
    quarter = turns.astype(jnp.int32) & 3
    swapped = (quarter & 1) == 1
    first, second = jnp.where(swapped, cosine, sine), jnp.where(swapped, sine, cosine)
    first = jnp.where(quarter >= 2, -first, first)
    second = jnp.where((quarter == 1) | (quarter == 2), -second, second)
    return first, second


def split_terms(values):
    high = values.astype(BF16)
    low = (values - high.astype(F32)).astype(BF16)
    return jnp.concatenate([high, low], axis=0)


def table_kernel(curves_ref, noise_ref, angle_ref, cos_ref, sin_ref, square_ref):
    length = curves_ref.shape[1]
    wide = cos_ref.shape[1]
    zeros = jnp.zeros((cos_ref.shape[0], wide - length), F32)
    sine, cosine = sine_cosine(angle_ref[...])
    cos_ref[...] = jnp.concatenate([cosine, zeros], axis=1)
    sin_ref[...] = jnp.concatenate([sine, zeros], axis=1)
    curve = curves_ref[...]
    square = split_terms(curve * curve * noise_ref[...])
    square_ref[...] = jnp.concatenate(
        [square, jnp.zeros((square.shape[0], wide - length), BF16)], axis=1
    )


def added_rows(extra, norm, banks, n_proj, length, subsets):
    ids_at = length // 128 * 128
    ids = []
    for bank in banks:
        for first in range(0, bank.shape[0], 2 * n_proj):
            rows = bank[first : first + 2 * n_proj, ids_at : ids_at + 128].astype(F32)
            ids.append(rows[:n_proj])
    ids = jnp.concatenate(ids, axis=0)[:, length - ids_at : length - ids_at + 1]
    subset_col = lax.broadcasted_iota(jnp.int32, (ids.shape[0], subsets), 1).astype(F32)
    subset_hot = (subset_col == ids).astype(F32).astype(BF16)
    prior = lax.dot_general(
        extra[:, :subsets].astype(BF16), subset_hot, NT_DIMS, preferred_element_type=F32
    )
    return prior - 0.5 * norm


def bank_pieces(bank, span, n_proj):
    for first in range(0, bank.shape[0], 2 * n_proj):
        both = bank[first : first + 2 * n_proj, span].astype(F32)
        yield both[:n_proj], both[n_proj:]


def shifted_rows(real, imag, cos_ref, sin_ref, span):
    real_rows, imag_rows = [], []
    for t in range(cos_ref.shape[0]):
        cos_part, sin_part = cos_ref[t : t + 1, span], sin_ref[t : t + 1, span]
        real_rows.append(cos_part * real + sin_part * imag)
        imag_rows.append(cos_part * imag - sin_part * real)
    return (
        jnp.concatenate(real_rows, axis=0).astype(BF16),
        jnp.concatenate(imag_rows, axis=0).astype(BF16),
    )


def spans_of(wide):
    step = 256 if wide % 256 == 0 else 128
    return [slice(at, at + step) for at in range(0, wide, step)]


def shift_kernel(n_proj, cos_ref, sin_ref, *rest):
    *banks, shifted_ref, power_ref = rest
    shifts, wide = cos_ref.shape
    width = shifts * n_proj
    for span in spans_of(wide):
        powers, at = [], 0
        for bank in banks:
            for real, imag in bank_pieces(bank, span, n_proj):
                real_rows, imag_rows = shifted_rows(real, imag, cos_ref, sin_ref, span)
                shifted_ref[at : at + width, span] = real_rows
                shifted_ref[at : at + width, wide + span.start : wide + span.stop] = imag_rows
                powers.append(real * real + imag * imag)
                at += width
        power_ref[:, span] = split_terms(jnp.concatenate(powers, axis=0))


def multiply(left, right):
    return lax.dot_general(left, right, NT_DIMS, preferred_element_type=F32)


def added(total, terms):
    return terms if total is None else total + terms


def pieces_of(cross, norm, extra, banks, length, subsets, n_proj):
    count, total = cross.shape[0], norm.shape[1] // 2
    width = cross.shape[1] * n_proj // total
    norm = norm[:count, total:] + norm[count:, :total] + norm[:count, :total]
    offset = added_rows(extra, norm, banks, n_proj, length, subsets)
    pieces = []
    for n in range(total // n_proj):
        scores = cross[:, n * width : (n + 1) * width]
        pieces.append(jnp.concatenate([scores, offset[:, n * n_proj : (n + 1) * n_proj]], axis=1))
    return pieces


def store_pieces(out, pieces, first, slot, rows):
    for n, piece in enumerate(pieces):
        at = (first + n) * slot
        out[:, at : at + piece.shape[1]] = piece[rows]


def rows_of(parts, span):
    return jnp.concatenate([part[:, span] for part in parts], axis=0)


def early_kernel(n_parts, n_banks, n_proj, length, subsets, square_ref, *rest):
    parts, rest = rest[:n_parts], rest[n_parts:]
    groups, (select_ref, rows_ref) = [], rest[-2:]
    for n in n_banks:
        groups.append((rest[0], rest[1], rest[2 : 2 + n]))
        rest = rest[2 + n :]
    wide = select_ref.shape[1]
    classes_count = square_ref.shape[0] // 2
    extra = rows_of(parts, slice(2 * wide, None)).astype(F32)
    count = extra.shape[0]
    class_col = lax.broadcasted_iota(jnp.int32, (count, classes_count), 1).astype(F32)
    onehot = (class_col == extra[:, subsets : subsets + 1]).astype(F32)
    nothing = jnp.zeros_like(onehot)
    pick = jnp.concatenate(
        [jnp.concatenate([onehot, nothing], axis=1), jnp.concatenate([nothing, onehot], axis=1)], axis=0
    ).astype(BF16)
    chosen = jnp.dot(pick, square_ref[...], preferred_element_type=F32)
    select_ref[...] = chosen.astype(BF16)

    pieces = []
    for shifted_ref, power_ref, banks in groups:
        cross, turned = None, None
        for at in range(0, wide, 512):
            span = slice(at, min(at + 512, wide))
            other = slice(wide + span.start, wide + span.stop)
            cross = added(cross, multiply(rows_of(parts, span), shifted_ref[:, span]))
            turned = added(turned, multiply(shifted_ref[:, other], rows_of(parts, other)))
        norm = multiply(select_ref[...], power_ref[...])
        pieces += pieces_of(cross + turned.T, norm, extra, banks, length, subsets, n_proj)
    store_pieces(rows_ref, pieces, 0, rows_ref.shape[1] // len(pieces), slice(None))


def final_kernel(
    half, n_parts, bits, n_proj, length, subsets, select_ref, rows_ref, cos_ref, sin_ref, last_ref, *rest
):
    parts, (late_ref, give_ref) = rest[:n_parts], rest[n_parts:]
    shifts, wide = cos_ref.shape
    cross, turned, norm = None, None, None
    for span in spans_of(wide):
        terms, others, powers = [], [], []
        for real, imag in bank_pieces(last_ref, span, n_proj):
            real_rows, imag_rows = shifted_rows(real, imag, cos_ref, sin_ref, span)
            terms.append(multiply(rows_of(parts, span), real_rows))
            other = slice(wide + span.start, wide + span.stop)
            others.append(multiply(imag_rows, rows_of(parts, other)))
            powers.append(real * real + imag * imag)
        cross = added(cross, jnp.concatenate(terms, axis=1))
        turned = added(turned, jnp.concatenate(others, axis=0))
        power = split_terms(jnp.concatenate(powers, axis=0))
        norm = added(norm, multiply(select_ref[:, span], power))
    cross = cross + turned.T
    extra = rows_of(parts, slice(2 * wide, None)).astype(F32)
    pieces = pieces_of(cross, norm, extra, [last_ref], length, subsets, n_proj)
    slot = late_ref.shape[1] // len(pieces)
    zeros = jnp.zeros((extra.shape[0], slot - pieces[0].shape[1]), F32)
    late = [jnp.concatenate([piece, zeros], axis=1) for piece in pieces]
    late_ref[...] = jnp.concatenate(late, axis=1)
    dest, lanes = give_ref.shape
    width = pieces[0].shape[1]
    rows = [in_rows(values, 1, bits, dest)[:, :width] for values in slots_of(rows_ref, slot) + late]
    if lanes > half * width:
        rows.append(jnp.zeros((dest, lanes - half * width), F32))
    give_ref[...] = jnp.concatenate(rows, axis=1)


def slots_of(rows_ref, slot):
    return [rows_ref[:, at : at + slot] for at in range(0, rows_ref.shape[1], slot)]


def in_rows(values, d, bits, dest):
    ng = 1 << len(bits)
    n_part = dest // ng
    g = lax.axis_index("grp")
    row = lax.broadcasted_iota(jnp.int32, (dest, values.shape[1]), 0)
    found = []
    for away in range(ng):
        source = d
        for n, bit in enumerate(bits):
            source += (2 << n) if away & bit else 0
        found.append(values[source * n_part : (source + 1) * n_part])
    values = jnp.concatenate(found, axis=0)
    for bit in bits:
        step = bit * n_part
        other = jnp.where(
            (row & step) != 0, pltpu.roll(values, step, 0), pltpu.roll(values, dest - step, 0)
        )
        values = jnp.where((g & bit) != 0, other, values)
    return values


def by_shift(pieces, order, n_proj, shifts):
    blk = lax.axis_index("blk")
    half = len(order)
    found = [pieces[order.index(n)] for n in range(half)]
    bit = 1
    while bit < half:
        swapped = (blk & bit) != 0
        found = [jnp.where(swapped, found[n ^ bit], found[n]) for n in range(half)]
        bit *= 2

    def line(t):
        return jnp.concatenate([piece[:, t * n_proj : (t + 1) * n_proj] for piece in found], axis=1)

    offset = line(shifts)
    return [line(t) + offset for t in range(shifts)]


def keep_kernel(slot, n_proj, order, bits, rows_ref, late_ref, out_ref):
    shifts, dest, _ = out_ref.shape
    pieces = [in_rows(values, 0, bits, dest) for values in slots_of(rows_ref, slot) + slots_of(late_ref, slot)]
    for t, line in enumerate(by_shift(pieces, order, n_proj, shifts)):
        out_ref[t] = line


def place_kernel(half, n_proj, order, keep_ref, recv_ref, out_ref):
    own_first = lax.axis_index("blk") < half
    shifts = out_ref.shape[0]
    width = (shifts + 1) * n_proj
    recv = recv_ref[...]
    pieces = [recv[:, n * width : (n + 1) * width] for n in range(half)]
    for t, line in enumerate(by_shift(pieces, order, n_proj, shifts)):
        keep = keep_ref[t]
        low, high = jnp.where(own_first, keep, line), jnp.where(own_first, line, keep)
        out_ref[t] = jnp.concatenate([low, high], axis=1)


def per_device(
    particles,
    ctf_class,
    orient_prior,
    ctf_curves,
    noise_weight,
    shift_phase,
    trans_index,
    projections,
    orient_subset,
):
    nb, ng = lax.axis_size("blk"), lax.axis_size("grp")
    half = nb // 2
    n_part, n_proj = particles.shape[0], projections.shape[0]
    length = particles.shape[2]
    shifts = shift_phase.shape[0]
    classes_count = ctf_curves.shape[0]
    subsets = orient_prior.shape[1]
    wide = 128 * (length // 128 + 1)
    extra = 128 * (subsets // 128 + 1)
    noise = noise_weight.reshape(1, length)
    shape = jax.ShapeDtypeStruct

    def vmem_out(dims, dtype):
        return pltpu.VMEM(dims, dtype)

    operands = (
        ctf_class,
        orient_subset,
        particles,
        orient_prior,
        ctf_curves,
        noise,
        projections,
        shift_phase,
        trans_index,
    )
    bank, part, curves, noise, angle = pl.pallas_call(
        pack_kernel,
        out_shape=[
            vmem_out((2 * n_proj, wide), BF16),
            vmem_out((n_part, 2 * wide + extra), BF16),
            vmem_out(ctf_curves.shape, F32),
            vmem_out(noise.shape, F32),
            vmem_out(shift_phase.shape, F32),
        ],
        in_specs=[pl.BlockSpec(memory_space=pltpu.HBM)] * len(operands),
        out_specs=[_vmem()] * 5,
        scratch_shapes=[
            pltpu.SMEM(ctf_class.shape, jnp.int32),
            pltpu.SMEM(orient_subset.shape, jnp.int32),
            pltpu.SMEM(trans_index.shape, jnp.int32),
            pltpu.VMEM(particles.shape, BF16),
            pltpu.VMEM(orient_prior.shape, BF16),
            pltpu.VMEM(shift_phase.shape, F32),
            pltpu.VMEM(projections.shape, BF16),
            pltpu.SemaphoreType.DMA((len(operands) + 4,)),
        ],
        compiler_params=_params(16),
        name="pack",
    )(*[pltpu.with_memory_space_constraint(operand, pltpu.HBM) for operand in operands])

    def swap(value, axis, bit):
        size = lax.axis_size(axis)
        return lax.ppermute(value, axis, [(i, i ^ bit) for i in range(size)])

    def joined(pieces):
        return pieces[0] if len(pieces) == 1 else jnp.concatenate(pieces, axis=0)

    across = swap(part, "blk", half)
    near = swap(bank, "blk", 1)
    planes, order = [bank], [0]
    for n in range(half.bit_length() - 2, 0, -1):
        planes.append(swap(joined(planes), "blk", 1 << n))
        order += [offset ^ (1 << n) for offset in order]
    far, near = lax.optimization_barrier((joined(planes[1:]), near))
    last = swap(jnp.pad(far, ((0, 0), (0, 3 * 128))), "blk", 1)
    order = [0, 1] + order[1:] + [offset ^ 1 for offset in order[1:]]

    cos_part, sin_part, square = pl.pallas_call(
        table_kernel,
        out_shape=[
            vmem_out((shifts, wide), F32),
            vmem_out((shifts, wide), F32),
            vmem_out((2 * classes_count, wide), BF16),
        ],
        in_specs=[_vmem()] * 3,
        out_specs=[_vmem()] * 3,
        compiler_params=_params(8),
        cost_estimate=pl.CostEstimate(flops=4_000_000, bytes_accessed=2_000_000, transcendentals=0),
        name="tables",
    )(curves, noise, angle)

    def shifted_call(banks, name):
        total = sum(piece.shape[0] for piece in banks) // 2
        return pl.pallas_call(
            functools.partial(shift_kernel, n_proj),
            out_shape=[vmem_out((shifts * total, 2 * wide), BF16), vmem_out((2 * total, wide), BF16)],
            in_specs=[_vmem()] * (2 + len(banks)),
            out_specs=[_vmem()] * 2,
            compiler_params=_params(16),
            cost_estimate=pl.CostEstimate(
                flops=6 * total * shifts * wide, bytes_accessed=4_000_000, transcendentals=0
            ),
            name=name,
        )(cos_part, sin_part, *banks)

    own_rows, own_power = shifted_call([bank], "shift_own")

    across, own_power = lax.optimization_barrier((across, own_power))
    parts = [part, across]
    bits = [1 << n for n in range(ng.bit_length() - 2, -1, -1)]
    for bit in bits:
        rows = parts[0].shape[0]
        part = lax.dynamic_update_slice(jnp.pad(parts[0], ((0, rows), (0, 0))), parts[1], (rows, 0))
        parts = [part, swap(part, "grp", bit)]

    rest_rows, rest_power = shifted_call([near, far], "shift_rest")
    count = 2 * ng * n_part
    late = half // 2 - 1
    slot = 128 * -(-(shifts + 1) * n_proj // 128)
    lanes = 128 * -(-(shifts + 1) * n_proj * half // 128)
    select, rows = pl.pallas_call(
        functools.partial(early_kernel, len(parts), (1, 2), n_proj, length, subsets),
        out_shape=[
            vmem_out((2 * count, wide), BF16),
            vmem_out((count, (half - late) * slot), F32),
        ],
        in_specs=[_vmem()] * (8 + len(parts)),
        out_specs=[_vmem()] * 2,
        compiler_params=_params(16),
        cost_estimate=pl.CostEstimate(
            flops=4 * count * (half - late) * n_proj * shifts * wide,
            bytes_accessed=4_000_000,
            transcendentals=0,
        ),
        name="early",
    )(square, *parts, own_rows, own_power, bank, rest_rows, rest_power, near, far)
    late_rows, give = pl.pallas_call(
        functools.partial(final_kernel, half, len(parts), bits, n_proj, length, subsets),
        out_shape=[vmem_out((count, late * slot), F32), vmem_out((ng * n_part, lanes), F32)],
        in_specs=[_vmem()] * (5 + len(parts)),
        out_specs=[_vmem()] * 2,
        compiler_params=_params(16),
        cost_estimate=pl.CostEstimate(
            flops=4 * count * late * n_proj * shifts * wide, bytes_accessed=4_000_000, transcendentals=0
        ),
        name="final",
    )(select, rows, cos_part, sin_part, last, *parts)
    recv = swap(give, "blk", half)
    keep = pl.pallas_call(
        functools.partial(keep_kernel, slot, n_proj, order, bits),
        out_shape=vmem_out((shifts, ng * n_part, half * n_proj), F32),
        in_specs=[_vmem()] * 2,
        out_specs=_vmem(),
        compiler_params=_params(4),
        name="keep",
    )(rows, late_rows)
    scores = pl.pallas_call(
        functools.partial(place_kernel, half, n_proj, order),
        out_shape=shape((shifts, ng * n_part, nb * n_proj), F32),
        in_specs=[_vmem()] * 2,
        out_specs=_vmem(),
        compiler_params=_params(4),
        name="place",
    )(keep, recv)
    return scores.transpose(1, 0, 2)


def solution(mesh):
    placed = (
        P(("blk", "grp"), None, None),
        P(("blk", "grp")),
        P(("blk", "grp"), None),
        P(),
        P(),
        P(),
        P(),
        P(("grp", "blk"), None, None),
        P(("grp", "blk")),
    )
    return jax.shard_map(
        per_device, mesh=mesh, in_specs=placed, out_specs=P("blk", None, "grp"), check_vma=False
    )
```

```python
import functools

import jax
import jax.numpy as jnp
from jax import lax
from jax.experimental import pallas as pl
from jax.experimental.pallas import tpu as pltpu
from jax.sharding import PartitionSpec as P

F32 = jnp.float32
BF16 = jnp.bfloat16
HIGHEST = lax.Precision.HIGHEST
NT_DIMS = (((1,), (1,)), ((), ()))
MIB = 1 << 20


def _vmem():
    return pl.BlockSpec(memory_space=pltpu.VMEM)


def _params(mib):
    return pltpu.CompilerParams(vmem_limit_bytes=mib * MIB)


def pack_kernel(
    class_hbm,
    subset_hbm,
    particles_hbm,
    prior_hbm,
    curves_hbm,
    noise_hbm,
    proj_hbm,
    phase_hbm,
    trans_hbm,
    bank_ref,
    part_ref,
    curves_ref,
    noise_ref,
    angle_ref,
    class_ref,
    subset_ref,
    trans_ref,
    particles_ref,
    prior_ref,
    phase_ref,
    proj_ref,
    sems,
):
    n_proj, n_class = proj_hbm.shape[0], curves_hbm.shape[0]
    pairs = [
        (proj_hbm.at[: n_proj // 2], proj_ref.at[: n_proj // 2]),
        (proj_hbm.at[n_proj // 2 :], proj_ref.at[n_proj // 2 :]),
        (subset_hbm, subset_ref),
        (class_hbm, class_ref),
        (curves_hbm.at[: n_class // 4], curves_ref.at[: n_class // 4]),
        (curves_hbm.at[n_class // 4 : n_class // 2], curves_ref.at[n_class // 4 : n_class // 2]),
        (curves_hbm.at[n_class // 2 : 3 * n_class // 4], curves_ref.at[n_class // 2 : 3 * n_class // 4]),
        (curves_hbm.at[3 * n_class // 4 :], curves_ref.at[3 * n_class // 4 :]),
        (particles_hbm, particles_ref),
        (noise_hbm, noise_ref),
        (prior_hbm, prior_ref),
        (trans_hbm, trans_ref),
        (phase_hbm, phase_ref),
    ]
    copies = [pltpu.make_async_copy(a, b, sems.at[n]) for n, (a, b) in enumerate(pairs)]
    for copy in copies:
        copy.start()
    n_part = particles_ref.shape[0]
    length = proj_ref.shape[2]
    wide = bank_ref.shape[1]

    def padded(values, width):
        zeros = jnp.zeros((values.shape[0], width - values.shape[1]), values.dtype)
        return jnp.concatenate([values, zeros], axis=1)

    row = lax.broadcasted_iota(jnp.int32, (n_proj, wide), 0)
    lane = lax.broadcasted_iota(jnp.int32, (n_proj, wide), 1)
    for copy in copies[:3]:
        copy.wait()
    real = jnp.zeros((n_proj, wide), F32)
    imag = jnp.zeros((n_proj, wide), F32)
    for j in range(n_proj):
        both = padded(proj_ref[j].astype(F32), wide)
        real = jnp.where(row == j, both[0:1], real)
        imag = jnp.where(row == j, both[1:2], imag)
    last = slice(wide - 128, wide)
    ends = real[:, last]
    for j in range(n_proj):
        here = (row[:, last] == j) & (lane[:, last] == length)
        ends = jnp.where(here, subset_ref[j].astype(F32), ends)
    real = jnp.concatenate([real[:, : wide - 128], ends], axis=1)
    bank_ref[...] = jnp.concatenate([real, imag], axis=0).astype(BF16)

    for copy in copies[3:]:
        copy.wait()
    subsets = prior_ref.shape[1]
    extra = part_ref.shape[1] - 2 * wide
    row = lax.broadcasted_iota(jnp.int32, (n_part, wide), 0)
    row_extra = lax.broadcasted_iota(jnp.int32, (n_part, extra), 0)
    lane_extra = lax.broadcasted_iota(jnp.int32, (n_part, extra), 1)
    real = jnp.zeros((n_part, wide), F32)
    imag = jnp.zeros((n_part, wide), F32)
    small = padded(prior_ref[...].astype(F32), extra)
    for i in range(n_part):
        curve = curves_ref[pl.ds(class_ref[i], 1), :] * noise_ref[...]
        both = padded(particles_ref[i].astype(F32) * curve, wide)
        real = jnp.where(row == i, both[0:1], real)
        imag = jnp.where(row == i, both[1:2], imag)
        place = (row_extra == i) & (lane_extra == subsets)
        small = jnp.where(place, class_ref[i].astype(F32), small)
    part_ref[:, :wide] = real.astype(BF16)
    part_ref[:, wide : 2 * wide] = imag.astype(BF16)
    part_ref[:, 2 * wide :] = small.astype(BF16)
    for t in range(phase_ref.shape[0]):
        angle_ref[t : t + 1, :] = phase_ref[pl.ds(trans_ref[t], 1), :]


def sine_cosine(x):
    turns = jnp.floor(x * 0.6366197723675814 + 0.5)
    r = ((x - turns * 1.5703125) - turns * 4.837512969970703125e-4) - turns * 7.549789954891882e-8
    z = r * r
    sine = r + r * z * (-1.6666654611e-1 + z * (8.3321608736e-3 - z * 1.9515295891e-4))
    cosine = 1.0 - 0.5 * z + z * z * (
        4.166664568298827e-2 + z * (-1.388731625493765e-3 + z * 2.443315711809948e-5)
    )
    quarter = turns.astype(jnp.int32) & 3
    swapped = (quarter & 1) == 1
    first, second = jnp.where(swapped, cosine, sine), jnp.where(swapped, sine, cosine)
    first = jnp.where(quarter >= 2, -first, first)
    second = jnp.where((quarter == 1) | (quarter == 2), -second, second)
    return first, second


def split_terms(values):
    high = values.astype(BF16)
    low = (values - high.astype(F32)).astype(BF16)
    return jnp.concatenate([high, low], axis=0)


def table_kernel(curves_ref, noise_ref, angle_ref, cos_ref, sin_ref, square_ref):
    length = curves_ref.shape[1]
    wide = cos_ref.shape[1]
    zeros = jnp.zeros((cos_ref.shape[0], wide - length), F32)
    sine, cosine = sine_cosine(angle_ref[...])
    cos_ref[...] = jnp.concatenate([cosine, zeros], axis=1)
    sin_ref[...] = jnp.concatenate([sine, zeros], axis=1)
    curve = curves_ref[...]
    square = split_terms(curve * curve * noise_ref[...])
    square_ref[...] = jnp.concatenate(
        [square, jnp.zeros((square.shape[0], wide - length), BF16)], axis=1
    )


def added_rows(extra, norm, banks, n_proj, length, subsets):
    ids_at = length // 128 * 128
    ids = []
    for bank in banks:
        for first in range(0, bank.shape[0], 2 * n_proj):
            rows = bank[first : first + 2 * n_proj, ids_at : ids_at + 128].astype(F32)
            ids.append(rows[:n_proj])
    ids = jnp.concatenate(ids, axis=0)[:, length - ids_at : length - ids_at + 1]
    subset_col = lax.broadcasted_iota(jnp.int32, (ids.shape[0], subsets), 1).astype(F32)
    subset_hot = (subset_col == ids).astype(F32).astype(BF16)
    prior = lax.dot_general(
        extra[:, :subsets].astype(BF16), subset_hot, NT_DIMS, preferred_element_type=F32
    )
    return prior - 0.5 * norm


def bank_pieces(bank, span, n_proj):
    for first in range(0, bank.shape[0], 2 * n_proj):
        both = bank[first : first + 2 * n_proj, span].astype(F32)
        yield both[:n_proj], both[n_proj:]


def shifted_rows(real, imag, cos_ref, sin_ref, span):
    real_rows, imag_rows = [], []
    for t in range(cos_ref.shape[0]):
        cos_part, sin_part = cos_ref[t : t + 1, span], sin_ref[t : t + 1, span]
        real_rows.append(cos_part * real + sin_part * imag)
        imag_rows.append(cos_part * imag - sin_part * real)
    return (
        jnp.concatenate(real_rows, axis=0).astype(BF16),
        jnp.concatenate(imag_rows, axis=0).astype(BF16),
    )


def spans_of(wide):
    step = 256 if wide % 256 == 0 else 128
    return [slice(at, at + step) for at in range(0, wide, step)]


def shift_kernel(n_proj, cos_ref, sin_ref, *rest):
    *banks, shifted_ref, power_ref = rest
    shifts, wide = cos_ref.shape
    width = shifts * n_proj
    for span in spans_of(wide):
        powers, at = [], 0
        for bank in banks:
            for real, imag in bank_pieces(bank, span, n_proj):
                real_rows, imag_rows = shifted_rows(real, imag, cos_ref, sin_ref, span)
                shifted_ref[at : at + width, span] = real_rows
                shifted_ref[at : at + width, wide + span.start : wide + span.stop] = imag_rows
                powers.append(real * real + imag * imag)
                at += width
        power_ref[:, span] = split_terms(jnp.concatenate(powers, axis=0))


def multiply(left, right):
    return lax.dot_general(left, right, NT_DIMS, preferred_element_type=F32)


def added(total, terms):
    return terms if total is None else total + terms


def pieces_of(cross, norm, extra, banks, length, subsets, n_proj):
    count, total = cross.shape[0], norm.shape[1] // 2
    width = cross.shape[1] * n_proj // total
    norm = norm[:count, total:] + norm[count:, :total] + norm[:count, :total]
    offset = added_rows(extra, norm, banks, n_proj, length, subsets)
    pieces = []
    for n in range(total // n_proj):
        scores = cross[:, n * width : (n + 1) * width]
        pieces.append(jnp.concatenate([scores, offset[:, n * n_proj : (n + 1) * n_proj]], axis=1))
    return pieces


def store_pieces(out, pieces, first, slot, rows):
    for n, piece in enumerate(pieces):
        at = (first + n) * slot
        out[:, at : at + piece.shape[1]] = piece[rows]


def rows_of(parts, span):
    return jnp.concatenate([part[:, span] for part in parts], axis=0)


def early_kernel(n_parts, n_banks, n_proj, length, subsets, square_ref, *rest):
    parts, rest = rest[:n_parts], rest[n_parts:]
    groups, (select_ref, rows_ref) = [], rest[-2:]
    for n in n_banks:
        groups.append((rest[0], rest[1], rest[2 : 2 + n]))
        rest = rest[2 + n :]
    wide = select_ref.shape[1]
    classes_count = square_ref.shape[0] // 2
    extra = rows_of(parts, slice(2 * wide, None)).astype(F32)
    count = extra.shape[0]
    class_col = lax.broadcasted_iota(jnp.int32, (count, classes_count), 1).astype(F32)
    onehot = (class_col == extra[:, subsets : subsets + 1]).astype(F32).astype(BF16)
    for n in range(2):
        squares = square_ref[n * classes_count : (n + 1) * classes_count, :]
        chosen = jnp.dot(onehot, squares, preferred_element_type=F32)
        select_ref[n * count : (n + 1) * count, :] = chosen.astype(BF16)

    pieces = []
    for shifted_ref, power_ref, banks in groups:
        cross, turned = None, None
        for at in range(0, wide, 512):
            span = slice(at, min(at + 512, wide))
            other = slice(wide + span.start, wide + span.stop)
            cross = added(cross, multiply(rows_of(parts, span), shifted_ref[:, span]))
            turned = added(turned, multiply(shifted_ref[:, other], rows_of(parts, other)))
        norm = multiply(select_ref[...], power_ref[...])
        pieces += pieces_of(cross + turned.T, norm, extra, banks, length, subsets, n_proj)
    store_pieces(rows_ref, pieces, 0, rows_ref.shape[1] // len(pieces), slice(None))


def final_kernel(
    order, n_parts, bits, n_proj, length, subsets, select_ref, rows_ref, cos_ref, sin_ref, last_ref, *rest
):
    parts, (late_ref, give_ref) = rest[:n_parts], rest[n_parts:]
    shifts, wide = cos_ref.shape
    cross, norm = None, None
    for span in spans_of(wide):
        terms, powers = [], []
        for real, imag in bank_pieces(last_ref, span, n_proj):
            real_rows, imag_rows = shifted_rows(real, imag, cos_ref, sin_ref, span)
            other = slice(wide + span.start, wide + span.stop)
            terms.append(
                multiply(rows_of(parts, span), real_rows) + multiply(rows_of(parts, other), imag_rows)
            )
            powers.append(real * real + imag * imag)
        cross = added(cross, jnp.concatenate(terms, axis=1))
        power = split_terms(jnp.concatenate(powers, axis=0))
        norm = added(norm, multiply(select_ref[:, span], power))
    extra = rows_of(parts, slice(2 * wide, None)).astype(F32)
    pieces = pieces_of(cross, norm, extra, [last_ref], length, subsets, n_proj)
    slot = late_ref.shape[1] // len(pieces)
    zeros = jnp.zeros((extra.shape[0], slot - pieces[0].shape[1]), F32)
    late = [jnp.concatenate([piece, zeros], axis=1) for piece in pieces]
    late_ref[...] = jnp.concatenate(late, axis=1)
    dest, lanes = give_ref.shape
    width = pieces[0].shape[1]
    rows = [in_rows(values, 1, bits, dest) for values in slots_of(rows_ref, slot) + late]
    rows = [values[:, :width] for values in in_order(rows, order)]
    if lanes > len(rows) * width:
        rows.append(jnp.zeros((dest, lanes - len(rows) * width), F32))
    give_ref[...] = jnp.concatenate(rows, axis=1)


def slots_of(rows_ref, slot):
    return [rows_ref[:, at : at + slot] for at in range(0, rows_ref.shape[1], slot)]


def in_rows(values, d, bits, dest):
    ng = 1 << len(bits)
    n_part = dest // ng
    g = lax.axis_index("grp")
    row = lax.broadcasted_iota(jnp.int32, (dest, values.shape[1]), 0)
    found = []
    for away in range(ng):
        source = d
        for n, bit in enumerate(bits):
            source += (2 << n) if away & bit else 0
        found.append(values[source * n_part : (source + 1) * n_part])
    values = jnp.concatenate(found, axis=0)
    for bit in bits:
        step = bit * n_part
        other = jnp.where(
            (row & step) != 0, pltpu.roll(values, step, 0), pltpu.roll(values, dest - step, 0)
        )
        values = jnp.where((g & bit) != 0, other, values)
    return values


def in_order(pieces, order):
    blk = lax.axis_index("blk")
    found = [pieces[order.index(n)] for n in range(len(order))]
    bit = 1
    while bit < len(order):
        swapped = (blk & bit) != 0
        found = [jnp.where(swapped, found[n ^ bit], found[n]) for n in range(len(order))]
        bit *= 2
    return found


def by_shift(pieces, n_proj, shifts):
    def line(t):
        one = [piece[:, t * n_proj : (t + 1) * n_proj] for piece in pieces]
        return jnp.concatenate(one + one, axis=1)

    offset = line(shifts)
    return [line(t) + offset for t in range(shifts)]


def keep_kernel(slot, n_proj, order, bits, rows_ref, late_ref, out_ref):
    shifts, dest, _ = out_ref.shape
    pieces = [in_rows(values, 0, bits, dest) for values in slots_of(rows_ref, slot) + slots_of(late_ref, slot)]
    for t, line in enumerate(by_shift(in_order(pieces, order), n_proj, shifts)):
        out_ref[t] = line


def place_kernel(half, n_proj, keep_ref, recv_ref, out_ref):
    shifts, dest, total = out_ref.shape
    width = (shifts + 1) * n_proj
    lower = lax.broadcasted_iota(jnp.int32, (dest, total), 1) < total // 2
    own = lower == (lax.axis_index("blk") < half)
    pieces = [recv_ref[:, n * width : (n + 1) * width] for n in range(half)]
    for t, line in enumerate(by_shift(pieces, n_proj, shifts)):
        out_ref[t] = jnp.where(own, keep_ref[t], line)


def per_device(
    particles,
    ctf_class,
    orient_prior,
    ctf_curves,
    noise_weight,
    shift_phase,
    trans_index,
    projections,
    orient_subset,
):
    nb, ng = lax.axis_size("blk"), lax.axis_size("grp")
    half = nb // 2
    n_part, n_proj = particles.shape[0], projections.shape[0]
    length = particles.shape[2]
    shifts = shift_phase.shape[0]
    classes_count = ctf_curves.shape[0]
    subsets = orient_prior.shape[1]
    wide = 128 * (length // 128 + 1)
    extra = 128 * (subsets // 128 + 1)
    noise = noise_weight.reshape(1, length)
    shape = jax.ShapeDtypeStruct

    def vmem_out(dims, dtype):
        return pltpu.VMEM(dims, dtype)

    operands = (
        ctf_class,
        orient_subset,
        particles,
        orient_prior,
        ctf_curves,
        noise,
        projections,
        shift_phase,
        trans_index,
    )
    bank, part, curves, noise, angle = pl.pallas_call(
        pack_kernel,
        out_shape=[
            vmem_out((2 * n_proj, wide), BF16),
            vmem_out((n_part, 2 * wide + extra), BF16),
            vmem_out(ctf_curves.shape, F32),
            vmem_out(noise.shape, F32),
            vmem_out(shift_phase.shape, F32),
        ],
        in_specs=[pl.BlockSpec(memory_space=pltpu.HBM)] * len(operands),
        out_specs=[_vmem()] * 5,
        scratch_shapes=[
            pltpu.SMEM(ctf_class.shape, jnp.int32),
            pltpu.SMEM(orient_subset.shape, jnp.int32),
            pltpu.SMEM(trans_index.shape, jnp.int32),
            pltpu.VMEM(particles.shape, BF16),
            pltpu.VMEM(orient_prior.shape, BF16),
            pltpu.VMEM(shift_phase.shape, F32),
            pltpu.VMEM(projections.shape, BF16),
            pltpu.SemaphoreType.DMA((len(operands) + 4,)),
        ],
        compiler_params=_params(16),
        name="pack",
    )(*[pltpu.with_memory_space_constraint(operand, pltpu.HBM) for operand in operands])

    def swap(value, axis, bit):
        size = lax.axis_size(axis)
        return lax.ppermute(value, axis, [(i, i ^ bit) for i in range(size)])

    def joined(pieces):
        return pieces[0] if len(pieces) == 1 else jnp.concatenate(pieces, axis=0)

    across = swap(part, "blk", half)
    near = swap(bank, "blk", 1)
    planes, order = [bank], [0]
    for n in range(half.bit_length() - 2, 0, -1):
        planes.append(swap(joined(planes), "blk", 1 << n))
        order += [offset ^ (1 << n) for offset in order]
    far, near = lax.optimization_barrier((joined(planes[1:]), near))
    last = swap(jnp.pad(far, ((0, 0), (0, 3 * 128))), "blk", 1)
    order = [0, 1] + order[1:] + [offset ^ 1 for offset in order[1:]]

    cos_part, sin_part, square = pl.pallas_call(
        table_kernel,
        out_shape=[
            vmem_out((shifts, wide), F32),
            vmem_out((shifts, wide), F32),
            vmem_out((2 * classes_count, wide), BF16),
        ],
        in_specs=[_vmem()] * 3,
        out_specs=[_vmem()] * 3,
        compiler_params=_params(8),
        cost_estimate=pl.CostEstimate(flops=4_000_000, bytes_accessed=2_000_000, transcendentals=0),
        name="tables",
    )(curves, noise, angle)

    def shifted_call(banks, name):
        total = sum(piece.shape[0] for piece in banks) // 2
        return pl.pallas_call(
            functools.partial(shift_kernel, n_proj),
            out_shape=[vmem_out((shifts * total, 2 * wide), BF16), vmem_out((2 * total, wide), BF16)],
            in_specs=[_vmem()] * (2 + len(banks)),
            out_specs=[_vmem()] * 2,
            compiler_params=_params(16),
            cost_estimate=pl.CostEstimate(
                flops=6 * total * shifts * wide, bytes_accessed=4_000_000, transcendentals=0
            ),
            name=name,
        )(cos_part, sin_part, *banks)

    own_rows, own_power = shifted_call([bank], "shift_own")

    across, own_power = lax.optimization_barrier((across, own_power))
    parts = [part, across]
    bits = [1 << n for n in range(ng.bit_length() - 2, -1, -1)]
    for bit in bits:
        part = joined(parts)
        parts = [part, swap(part, "grp", bit)]

    rest_rows, rest_power = shifted_call([near, far], "shift_rest")
    count = 2 * ng * n_part
    late = half // 2 - 1
    slot = 128 * -(-(shifts + 1) * n_proj // 128)
    lanes = 128 * -(-(shifts + 1) * n_proj * half // 128)
    select, rows = pl.pallas_call(
        functools.partial(early_kernel, len(parts), (1, 2), n_proj, length, subsets),
        out_shape=[
            vmem_out((2 * count, wide), BF16),
            vmem_out((count, (half - late) * slot), F32),
        ],
        in_specs=[_vmem()] * (8 + len(parts)),
        out_specs=[_vmem()] * 2,
        compiler_params=_params(16),
        cost_estimate=pl.CostEstimate(
            flops=4 * count * (half - late) * n_proj * shifts * wide,
            bytes_accessed=4_000_000,
            transcendentals=0,
        ),
        name="early",
    )(square, *parts, own_rows, own_power, bank, rest_rows, rest_power, near, far)
    late_rows, give = pl.pallas_call(
        functools.partial(final_kernel, order, len(parts), bits, n_proj, length, subsets),
        out_shape=[vmem_out((count, late * slot), F32), vmem_out((ng * n_part, lanes), F32)],
        in_specs=[_vmem()] * (5 + len(parts)),
        out_specs=[_vmem()] * 2,
        compiler_params=_params(16),
        cost_estimate=pl.CostEstimate(
            flops=4 * count * late * n_proj * shifts * wide, bytes_accessed=4_000_000, transcendentals=0
        ),
        name="final",
    )(select, rows, cos_part, sin_part, last, *parts)
    recv = swap(give, "blk", half)
    keep = pl.pallas_call(
        functools.partial(keep_kernel, slot, n_proj, order, bits),
        out_shape=vmem_out((shifts, ng * n_part, nb * n_proj), F32),
        in_specs=[_vmem()] * 2,
        out_specs=_vmem(),
        compiler_params=_params(4),
        name="keep",
    )(rows, late_rows)
    scores = pl.pallas_call(
        functools.partial(place_kernel, half, n_proj),
        out_shape=shape((shifts, ng * n_part, nb * n_proj), F32),
        in_specs=[_vmem()] * 2,
        out_specs=_vmem(),
        compiler_params=_params(4),
        name="place",
    )(keep, recv)
    return scores.transpose(1, 0, 2)


def solution(mesh):
    placed = (
        P(("blk", "grp"), None, None),
        P(("blk", "grp")),
        P(("blk", "grp"), None),
        P(),
        P(),
        P(),
        P(),
        P(("grp", "blk"), None, None),
        P(("grp", "blk")),
    )
    return jax.shard_map(
        per_device, mesh=mesh, in_specs=placed, out_specs=P("blk", None, "grp"), check_vma=False
    )
```

```python
import functools

import jax
import jax.numpy as jnp
from jax import lax
from jax.experimental import pallas as pl
from jax.experimental.pallas import tpu as pltpu
from jax.sharding import PartitionSpec as P

F32 = jnp.float32
BF16 = jnp.bfloat16
HIGHEST = lax.Precision.HIGHEST
NT_DIMS = (((1,), (1,)), ((), ()))
MIB = 1 << 20


def _vmem():
    return pl.BlockSpec(memory_space=pltpu.VMEM)


def _params(mib):
    return pltpu.CompilerParams(vmem_limit_bytes=mib * MIB)


def pack_kernel(
    class_hbm,
    subset_hbm,
    particles_hbm,
    prior_hbm,
    curves_hbm,
    noise_hbm,
    proj_hbm,
    phase_hbm,
    trans_hbm,
    bank_ref,
    part_ref,
    curves_ref,
    noise_ref,
    angle_ref,
    class_ref,
    subset_ref,
    trans_ref,
    particles_ref,
    prior_ref,
    phase_ref,
    proj_ref,
    sems,
):
    n_proj = proj_hbm.shape[0]
    pairs = [
        (proj_hbm, proj_ref),
        (curves_hbm, curves_ref),
        (subset_hbm, subset_ref),
        (class_hbm, class_ref),
        (particles_hbm, particles_ref),
        (noise_hbm, noise_ref),
        (prior_hbm, prior_ref),
        (trans_hbm, trans_ref),
        (phase_hbm, phase_ref),
    ]
    copies = [pltpu.make_async_copy(a, b, sems.at[n]) for n, (a, b) in enumerate(pairs)]
    for copy in copies:
        copy.start()
    n_part = particles_ref.shape[0]
    length = proj_ref.shape[2]
    wide = bank_ref.shape[1]

    def padded(values, width):
        zeros = jnp.zeros((values.shape[0], width - values.shape[1]), values.dtype)
        return jnp.concatenate([values, zeros], axis=1)

    row = lax.broadcasted_iota(jnp.int32, (n_proj, wide), 0)
    lane = lax.broadcasted_iota(jnp.int32, (n_proj, wide), 1)
    copies[0].wait()
    copies[2].wait()
    real = jnp.zeros((n_proj, wide), F32)
    imag = jnp.zeros((n_proj, wide), F32)
    for j in range(n_proj):
        both = padded(proj_ref[j].astype(F32), wide)
        real = jnp.where(row == j, both[0:1], real)
        imag = jnp.where(row == j, both[1:2], imag)
    last = slice(wide - 128, wide)
    ends = real[:, last]
    for j in range(n_proj):
        here = (row[:, last] == j) & (lane[:, last] == length)
        ends = jnp.where(here, subset_ref[j].astype(F32), ends)
    real = jnp.concatenate([real[:, : wide - 128], ends], axis=1)
    bank_ref[...] = jnp.concatenate([real, imag], axis=0).astype(BF16)

    copies[1].wait()
    for copy in copies[3:]:
        copy.wait()
    subsets = prior_ref.shape[1]
    extra = part_ref.shape[1] - 2 * wide
    row = lax.broadcasted_iota(jnp.int32, (n_part, wide), 0)
    row_extra = lax.broadcasted_iota(jnp.int32, (n_part, extra), 0)
    lane_extra = lax.broadcasted_iota(jnp.int32, (n_part, extra), 1)
    real = jnp.zeros((n_part, wide), F32)
    imag = jnp.zeros((n_part, wide), F32)
    small = padded(prior_ref[...].astype(F32), extra)
    for i in range(n_part):
        curve = curves_ref[pl.ds(class_ref[i], 1), :] * noise_ref[...]
        both = padded(particles_ref[i].astype(F32) * curve, wide)
        real = jnp.where(row == i, both[0:1], real)
        imag = jnp.where(row == i, both[1:2], imag)
        place = (row_extra == i) & (lane_extra == subsets)
        small = jnp.where(place, class_ref[i].astype(F32), small)
    part_ref[:, :wide] = real.astype(BF16)
    part_ref[:, wide : 2 * wide] = imag.astype(BF16)
    part_ref[:, 2 * wide :] = small.astype(BF16)
    for t in range(phase_ref.shape[0]):
        angle_ref[t : t + 1, :] = phase_ref[pl.ds(trans_ref[t], 1), :]


def sine_cosine(x):
    turns = jnp.floor(x * 0.6366197723675814 + 0.5)
    r = ((x - turns * 1.5703125) - turns * 4.837512969970703125e-4) - turns * 7.549789954891882e-8
    z = r * r
    sine = r + r * z * (-1.6666654611e-1 + z * (8.3321608736e-3 - z * 1.9515295891e-4))
    cosine = 1.0 - 0.5 * z + z * z * (
        4.166664568298827e-2 + z * (-1.388731625493765e-3 + z * 2.443315711809948e-5)
    )
    quarter = turns.astype(jnp.int32) & 3
    swapped = (quarter & 1) == 1
    first, second = jnp.where(swapped, cosine, sine), jnp.where(swapped, sine, cosine)
    first = jnp.where(quarter >= 2, -first, first)
    second = jnp.where((quarter == 1) | (quarter == 2), -second, second)
    return first, second


def split_terms(values):
    high = values.astype(BF16)
    low = (values - high.astype(F32)).astype(BF16)
    return jnp.concatenate([high, low], axis=0)


def table_kernel(curves_ref, noise_ref, angle_ref, cos_ref, sin_ref, square_ref):
    length = curves_ref.shape[1]
    wide = cos_ref.shape[1]
    zeros = jnp.zeros((cos_ref.shape[0], wide - length), F32)
    sine, cosine = sine_cosine(angle_ref[...])
    cos_ref[...] = jnp.concatenate([cosine, zeros], axis=1)
    sin_ref[...] = jnp.concatenate([sine, zeros], axis=1)
    curve = curves_ref[...]
    square = split_terms(curve * curve * noise_ref[...])
    square_ref[...] = jnp.concatenate(
        [square, jnp.zeros((square.shape[0], wide - length), BF16)], axis=1
    )


def added_rows(extra, norm, banks, n_proj, length, subsets):
    ids_at = length // 128 * 128
    ids = []
    for bank in banks:
        for first in range(0, bank.shape[0], 2 * n_proj):
            rows = bank[first : first + 2 * n_proj, ids_at : ids_at + 128].astype(F32)
            ids.append(rows[:n_proj])
    ids = jnp.concatenate(ids, axis=0)[:, length - ids_at : length - ids_at + 1]
    subset_col = lax.broadcasted_iota(jnp.int32, (ids.shape[0], subsets), 1).astype(F32)
    subset_hot = (subset_col == ids).astype(F32).astype(BF16)
    prior = lax.dot_general(
        extra[:, :subsets].astype(BF16), subset_hot, NT_DIMS, preferred_element_type=F32
    )
    return prior - 0.5 * norm


def bank_pieces(bank, span, n_proj):
    for first in range(0, bank.shape[0], 2 * n_proj):
        both = bank[first : first + 2 * n_proj, span].astype(F32)
        yield both[:n_proj], both[n_proj:]


def shifted_rows(real, imag, cos_ref, sin_ref, span):
    real_rows, imag_rows = [], []
    for t in range(cos_ref.shape[0]):
        cos_part, sin_part = cos_ref[t : t + 1, span], sin_ref[t : t + 1, span]
        real_rows.append(cos_part * real + sin_part * imag)
        imag_rows.append(cos_part * imag - sin_part * real)
    return (
        jnp.concatenate(real_rows, axis=0).astype(BF16),
        jnp.concatenate(imag_rows, axis=0).astype(BF16),
    )


def spans_of(wide):
    step = 256 if wide % 256 == 0 else 128
    return [slice(at, at + step) for at in range(0, wide, step)]


def shift_kernel(n_proj, cos_ref, sin_ref, *rest):
    *banks, shifted_ref, power_ref = rest
    shifts, wide = cos_ref.shape
    width = shifts * n_proj
    for span in spans_of(wide):
        powers, at = [], 0
        for bank in banks:
            for real, imag in bank_pieces(bank, span, n_proj):
                real_rows, imag_rows = shifted_rows(real, imag, cos_ref, sin_ref, span)
                shifted_ref[at : at + width, span] = real_rows
                shifted_ref[at : at + width, wide + span.start : wide + span.stop] = imag_rows
                powers.append(real * real + imag * imag)
                at += width
        power_ref[:, span] = split_terms(jnp.concatenate(powers, axis=0))


def multiply(left, right):
    return lax.dot_general(left, right, NT_DIMS, preferred_element_type=F32)


def added(total, terms):
    return terms if total is None else total + terms


def pieces_of(cross, norm, extra, banks, length, subsets, n_proj):
    count, total = cross.shape[0], norm.shape[1] // 2
    width = cross.shape[1] * n_proj // total
    norm = norm[:count, total:] + norm[count:, :total] + norm[:count, :total]
    offset = added_rows(extra, norm, banks, n_proj, length, subsets)
    pieces = []
    for n in range(total // n_proj):
        scores = cross[:, n * width : (n + 1) * width]
        pieces.append(jnp.concatenate([scores, offset[:, n * n_proj : (n + 1) * n_proj]], axis=1))
    return pieces


def store_pieces(out, pieces, first, slot, rows):
    for n, piece in enumerate(pieces):
        at = (first + n) * slot
        out[:, at : at + piece.shape[1]] = piece[rows]


def rows_of(parts, span):
    return jnp.concatenate([part[:, span] for part in parts], axis=0)


def early_kernel(n_parts, n_banks, n_proj, length, subsets, square_ref, *rest):
    parts, rest = rest[:n_parts], rest[n_parts:]
    groups, (select_ref, rows_ref) = [], rest[-2:]
    for n in n_banks:
        groups.append((rest[0], rest[1], rest[2 : 2 + n]))
        rest = rest[2 + n :]
    wide = select_ref.shape[1]
    classes_count = square_ref.shape[0] // 2
    extra = rows_of(parts, slice(2 * wide, None)).astype(F32)
    count = extra.shape[0]
    class_col = lax.broadcasted_iota(jnp.int32, (count, classes_count), 1).astype(F32)
    onehot = (class_col == extra[:, subsets : subsets + 1]).astype(F32).astype(BF16)
    for n in range(2):
        squares = square_ref[n * classes_count : (n + 1) * classes_count, :]
        chosen = jnp.dot(onehot, squares, preferred_element_type=F32)
        select_ref[n * count : (n + 1) * count, :] = chosen.astype(BF16)

    pieces = []
    for shifted_ref, power_ref, banks in groups:
        cross, turned = None, None
        for at in range(0, wide, 512):
            span = slice(at, min(at + 512, wide))
            other = slice(wide + span.start, wide + span.stop)
            cross = added(cross, multiply(rows_of(parts, span), shifted_ref[:, span]))
            turned = added(turned, multiply(shifted_ref[:, other], rows_of(parts, other)))
        norm = multiply(select_ref[...], power_ref[...])
        pieces += pieces_of(cross + turned.T, norm, extra, banks, length, subsets, n_proj)
    store_pieces(rows_ref, pieces, 0, rows_ref.shape[1] // len(pieces), slice(None))


def final_kernel(
    order, n_parts, bits, n_proj, length, subsets, select_ref, rows_ref, cos_ref, sin_ref, last_ref, *rest
):
    parts, (late_ref, give_ref) = rest[:n_parts], rest[n_parts:]
    shifts, wide = cos_ref.shape
    cross, norm = None, None
    for span in spans_of(wide):
        terms, powers = [], []
        for real, imag in bank_pieces(last_ref, span, n_proj):
            real_rows, imag_rows = shifted_rows(real, imag, cos_ref, sin_ref, span)
            other = slice(wide + span.start, wide + span.stop)
            terms.append(
                multiply(rows_of(parts, span), real_rows) + multiply(rows_of(parts, other), imag_rows)
            )
            powers.append(real * real + imag * imag)
        cross = added(cross, jnp.concatenate(terms, axis=1))
        power = split_terms(jnp.concatenate(powers, axis=0))
        norm = added(norm, multiply(select_ref[:, span], power))
    extra = rows_of(parts, slice(2 * wide, None)).astype(F32)
    pieces = pieces_of(cross, norm, extra, [last_ref], length, subsets, n_proj)
    slot = late_ref.shape[1] // len(pieces)
    zeros = jnp.zeros((extra.shape[0], slot - pieces[0].shape[1]), F32)
    late = [jnp.concatenate([piece, zeros], axis=1) for piece in pieces]
    late_ref[...] = jnp.concatenate(late, axis=1)
    dest, lanes = give_ref.shape
    width = pieces[0].shape[1]
    rows = [in_rows(values, 1, bits, dest) for values in slots_of(rows_ref, slot) + late]
    rows = [values[:, :width] for values in in_order(rows, order)]
    if lanes > len(rows) * width:
        rows.append(jnp.zeros((dest, lanes - len(rows) * width), F32))
    give_ref[...] = jnp.concatenate(rows, axis=1)


def slots_of(rows_ref, slot):
    return [rows_ref[:, at : at + slot] for at in range(0, rows_ref.shape[1], slot)]


def in_rows(values, d, bits, dest):
    ng = 1 << len(bits)
    n_part = dest // ng
    g = lax.axis_index("grp")
    row = lax.broadcasted_iota(jnp.int32, (dest, values.shape[1]), 0)
    found = []
    for away in range(ng):
        source = d
        for n, bit in enumerate(bits):
            source += (2 << n) if away & bit else 0
        found.append(values[source * n_part : (source + 1) * n_part])
    values = jnp.concatenate(found, axis=0)
    for bit in bits:
        step = bit * n_part
        other = jnp.where(
            (row & step) != 0, pltpu.roll(values, step, 0), pltpu.roll(values, dest - step, 0)
        )
        values = jnp.where((g & bit) != 0, other, values)
    return values


def in_order(pieces, order):
    blk = lax.axis_index("blk")
    found = [pieces[order.index(n)] for n in range(len(order))]
    bit = 1
    while bit < len(order):
        swapped = (blk & bit) != 0
        found = [jnp.where(swapped, found[n ^ bit], found[n]) for n in range(len(order))]
        bit *= 2
    return found


def by_shift(pieces, n_proj, shifts):
    def line(t):
        one = [piece[:, t * n_proj : (t + 1) * n_proj] for piece in pieces]
        return jnp.concatenate(one + one, axis=1)

    offset = line(shifts)
    return [line(t) + offset for t in range(shifts)]


def keep_kernel(slot, n_proj, order, bits, rows_ref, late_ref, out_ref):
    shifts, dest, _ = out_ref.shape
    pieces = [in_rows(values, 0, bits, dest) for values in slots_of(rows_ref, slot) + slots_of(late_ref, slot)]
    for t, line in enumerate(by_shift(in_order(pieces, order), n_proj, shifts)):
        out_ref[t] = line


def place_kernel(half, n_proj, keep_ref, recv_ref, out_ref):
    shifts, dest, total = out_ref.shape
    width = (shifts + 1) * n_proj
    lower = lax.broadcasted_iota(jnp.int32, (dest, total), 1) < total // 2
    own = lower == (lax.axis_index("blk") < half)
    pieces = [recv_ref[:, n * width : (n + 1) * width] for n in range(half)]
    for t, line in enumerate(by_shift(pieces, n_proj, shifts)):
        out_ref[t] = jnp.where(own, keep_ref[t], line)


def per_device(
    particles,
    ctf_class,
    orient_prior,
    ctf_curves,
    noise_weight,
    shift_phase,
    trans_index,
    projections,
    orient_subset,
):
    nb, ng = lax.axis_size("blk"), lax.axis_size("grp")
    half = nb // 2
    n_part, n_proj = particles.shape[0], projections.shape[0]
    length = particles.shape[2]
    shifts = shift_phase.shape[0]
    classes_count = ctf_curves.shape[0]
    subsets = orient_prior.shape[1]
    wide = 128 * (length // 128 + 1)
    extra = 128 * (subsets // 128 + 1)
    noise = noise_weight.reshape(1, length)
    shape = jax.ShapeDtypeStruct

    def vmem_out(dims, dtype):
        return pltpu.VMEM(dims, dtype)

    operands = (
        ctf_class,
        orient_subset,
        particles,
        orient_prior,
        ctf_curves,
        noise,
        projections,
        shift_phase,
        trans_index,
    )
    bank, part, curves, noise, angle = pl.pallas_call(
        pack_kernel,
        out_shape=[
            vmem_out((2 * n_proj, wide), BF16),
            vmem_out((n_part, 2 * wide + extra), BF16),
            vmem_out(ctf_curves.shape, F32),
            vmem_out(noise.shape, F32),
            vmem_out(shift_phase.shape, F32),
        ],
        in_specs=[pl.BlockSpec(memory_space=pltpu.HBM)] * len(operands),
        out_specs=[_vmem()] * 5,
        scratch_shapes=[
            pltpu.SMEM(ctf_class.shape, jnp.int32),
            pltpu.SMEM(orient_subset.shape, jnp.int32),
            pltpu.SMEM(trans_index.shape, jnp.int32),
            pltpu.VMEM(particles.shape, BF16),
            pltpu.VMEM(orient_prior.shape, BF16),
            pltpu.VMEM(shift_phase.shape, F32),
            pltpu.VMEM(projections.shape, BF16),
            pltpu.SemaphoreType.DMA((len(operands),)),
        ],
        compiler_params=_params(16),
        name="pack",
    )(*[pltpu.with_memory_space_constraint(operand, pltpu.HBM) for operand in operands])

    def swap(value, axis, bit):
        size = lax.axis_size(axis)
        return lax.ppermute(value, axis, [(i, i ^ bit) for i in range(size)])

    def joined(pieces):
        return pieces[0] if len(pieces) == 1 else jnp.concatenate(pieces, axis=0)

    across = swap(part, "blk", half)
    near = swap(bank, "blk", 1)
    planes, order = [bank], [0]
    for n in range(half.bit_length() - 2, 0, -1):
        planes.append(swap(joined(planes), "blk", 1 << n))
        order += [offset ^ (1 << n) for offset in order]
    far, near = lax.optimization_barrier((joined(planes[1:]), near))
    last = swap(jnp.pad(far, ((0, 0), (0, 3 * 128))), "blk", 1)
    order = [0, 1] + order[1:] + [offset ^ 1 for offset in order[1:]]

    cos_part, sin_part, square = pl.pallas_call(
        table_kernel,
        out_shape=[
            vmem_out((shifts, wide), F32),
            vmem_out((shifts, wide), F32),
            vmem_out((2 * classes_count, wide), BF16),
        ],
        in_specs=[_vmem()] * 3,
        out_specs=[_vmem()] * 3,
        compiler_params=_params(8),
        cost_estimate=pl.CostEstimate(flops=4_000_000, bytes_accessed=2_000_000, transcendentals=0),
        name="tables",
    )(curves, noise, angle)

    def shifted_call(banks, name):
        total = sum(piece.shape[0] for piece in banks) // 2
        return pl.pallas_call(
            functools.partial(shift_kernel, n_proj),
            out_shape=[vmem_out((shifts * total, 2 * wide), BF16), vmem_out((2 * total, wide), BF16)],
            in_specs=[_vmem()] * (2 + len(banks)),
            out_specs=[_vmem()] * 2,
            compiler_params=_params(16),
            cost_estimate=pl.CostEstimate(
                flops=6 * total * shifts * wide, bytes_accessed=4_000_000, transcendentals=0
            ),
            name=name,
        )(cos_part, sin_part, *banks)

    own_rows, own_power = shifted_call([bank], "shift_own")

    across, own_power = lax.optimization_barrier((across, own_power))
    parts = [part, across]
    bits = [1 << n for n in range(ng.bit_length() - 2, -1, -1)]
    for bit in bits:
        part = lax.optimization_barrier(joined(parts))
        parts = [part, swap(part, "grp", bit)]

    rest_rows, rest_power = shifted_call([near, far], "shift_rest")
    count = 2 * ng * n_part
    late = half // 2 - 1
    slot = 128 * -(-(shifts + 1) * n_proj // 128)
    lanes = 128 * -(-(shifts + 1) * n_proj * half // 128)
    select, rows = pl.pallas_call(
        functools.partial(early_kernel, len(parts), (1, 2), n_proj, length, subsets),
        out_shape=[
            vmem_out((2 * count, wide), BF16),
            vmem_out((count, (half - late) * slot), F32),
        ],
        in_specs=[_vmem()] * (8 + len(parts)),
        out_specs=[_vmem()] * 2,
        compiler_params=_params(16),
        cost_estimate=pl.CostEstimate(
            flops=4 * count * (half - late) * n_proj * shifts * wide,
            bytes_accessed=4_000_000,
            transcendentals=0,
        ),
        name="early",
    )(square, *parts, own_rows, own_power, bank, rest_rows, rest_power, near, far)
    late_rows, give = pl.pallas_call(
        functools.partial(final_kernel, order, len(parts), bits, n_proj, length, subsets),
        out_shape=[vmem_out((count, late * slot), F32), vmem_out((ng * n_part, lanes), F32)],
        in_specs=[_vmem()] * (5 + len(parts)),
        out_specs=[_vmem()] * 2,
        compiler_params=_params(16),
        cost_estimate=pl.CostEstimate(
            flops=4 * count * late * n_proj * shifts * wide, bytes_accessed=4_000_000, transcendentals=0
        ),
        name="final",
    )(select, rows, cos_part, sin_part, last, *parts)
    recv = swap(give, "blk", half)
    keep = pl.pallas_call(
        functools.partial(keep_kernel, slot, n_proj, order, bits),
        out_shape=vmem_out((shifts, ng * n_part, nb * n_proj), F32),
        in_specs=[_vmem()] * 2,
        out_specs=_vmem(),
        compiler_params=_params(4),
        name="keep",
    )(rows, late_rows)
    scores = pl.pallas_call(
        functools.partial(place_kernel, half, n_proj),
        out_shape=shape((shifts, ng * n_part, nb * n_proj), F32),
        in_specs=[_vmem()] * 2,
        out_specs=_vmem(),
        compiler_params=_params(4),
        name="place",
    )(keep, recv)
    return scores.transpose(1, 0, 2)


def solution(mesh):
    placed = (
        P(("blk", "grp"), None, None),
        P(("blk", "grp")),
        P(("blk", "grp"), None),
        P(),
        P(),
        P(),
        P(),
        P(("grp", "blk"), None, None),
        P(("grp", "blk")),
    )
    return jax.shard_map(
        per_device, mesh=mesh, in_specs=placed, out_specs=P("blk", None, "grp"), check_vma=False
    )
```

```python
import functools

import jax
import jax.numpy as jnp
from jax import lax
from jax.experimental import pallas as pl
from jax.experimental.pallas import tpu as pltpu
from jax.sharding import PartitionSpec as P

F32 = jnp.float32
BF16 = jnp.bfloat16
HIGHEST = lax.Precision.HIGHEST
NT_DIMS = (((1,), (1,)), ((), ()))
MIB = 1 << 20


def _vmem():
    return pl.BlockSpec(memory_space=pltpu.VMEM)


def _params(mib):
    return pltpu.CompilerParams(vmem_limit_bytes=mib * MIB)


def pack_kernel(
    class_hbm,
    subset_hbm,
    particles_hbm,
    prior_hbm,
    curves_hbm,
    noise_hbm,
    proj_hbm,
    phase_hbm,
    trans_hbm,
    bank_ref,
    part_ref,
    curves_ref,
    noise_ref,
    angle_ref,
    class_ref,
    subset_ref,
    trans_ref,
    particles_ref,
    prior_ref,
    phase_ref,
    proj_ref,
    sems,
):
    n_proj = proj_hbm.shape[0]
    pairs = [
        (proj_hbm, proj_ref),
        (curves_hbm, curves_ref),
        (subset_hbm, subset_ref),
        (class_hbm, class_ref),
        (particles_hbm, particles_ref),
        (noise_hbm, noise_ref),
        (prior_hbm, prior_ref),
        (trans_hbm, trans_ref),
        (phase_hbm, phase_ref),
    ]
    copies = [pltpu.make_async_copy(a, b, sems.at[n]) for n, (a, b) in enumerate(pairs)]
    for copy in copies:
        copy.start()
    n_part = particles_ref.shape[0]
    length = proj_ref.shape[2]
    wide = bank_ref.shape[1]

    def padded(values, width):
        zeros = jnp.zeros((values.shape[0], width - values.shape[1]), values.dtype)
        return jnp.concatenate([values, zeros], axis=1)

    row = lax.broadcasted_iota(jnp.int32, (n_proj, wide), 0)
    lane = lax.broadcasted_iota(jnp.int32, (n_proj, wide), 1)
    copies[0].wait()
    copies[2].wait()
    real = jnp.zeros((n_proj, wide), F32)
    imag = jnp.zeros((n_proj, wide), F32)
    for j in range(n_proj):
        both = padded(proj_ref[j].astype(F32), wide)
        real = jnp.where(row == j, both[0:1], real)
        imag = jnp.where(row == j, both[1:2], imag)
    last = slice(wide - 128, wide)
    ends = real[:, last]
    for j in range(n_proj):
        here = (row[:, last] == j) & (lane[:, last] == length)
        ends = jnp.where(here, subset_ref[j].astype(F32), ends)
    real = jnp.concatenate([real[:, : wide - 128], ends], axis=1)
    bank_ref[...] = jnp.concatenate([real, imag], axis=0).astype(BF16)

    copies[1].wait()
    for copy in copies[3:]:
        copy.wait()
    subsets = prior_ref.shape[1]
    extra = part_ref.shape[1] - 2 * wide
    row = lax.broadcasted_iota(jnp.int32, (n_part, wide), 0)
    row_extra = lax.broadcasted_iota(jnp.int32, (n_part, extra), 0)
    lane_extra = lax.broadcasted_iota(jnp.int32, (n_part, extra), 1)
    real = jnp.zeros((n_part, wide), F32)
    imag = jnp.zeros((n_part, wide), F32)
    small = padded(prior_ref[...].astype(F32), extra)
    for i in range(n_part):
        curve = curves_ref[pl.ds(class_ref[i], 1), :] * noise_ref[...]
        both = padded(particles_ref[i].astype(F32) * curve, wide)
        real = jnp.where(row == i, both[0:1], real)
        imag = jnp.where(row == i, both[1:2], imag)
        place = (row_extra == i) & (lane_extra == subsets)
        small = jnp.where(place, class_ref[i].astype(F32), small)
    part_ref[:, :wide] = real.astype(BF16)
    part_ref[:, wide : 2 * wide] = imag.astype(BF16)
    part_ref[:, 2 * wide :] = small.astype(BF16)
    for t in range(phase_ref.shape[0]):
        angle_ref[t : t + 1, :] = phase_ref[pl.ds(trans_ref[t], 1), :]


def sine_cosine(x):
    turns = jnp.floor(x * 0.6366197723675814 + 0.5)
    r = ((x - turns * 1.5703125) - turns * 4.837512969970703125e-4) - turns * 7.549789954891882e-8
    z = r * r
    sine = r + r * z * (-1.6666654611e-1 + z * (8.3321608736e-3 - z * 1.9515295891e-4))
    cosine = 1.0 - 0.5 * z + z * z * (
        4.166664568298827e-2 + z * (-1.388731625493765e-3 + z * 2.443315711809948e-5)
    )
    quarter = turns.astype(jnp.int32) & 3
    swapped = (quarter & 1) == 1
    first, second = jnp.where(swapped, cosine, sine), jnp.where(swapped, sine, cosine)
    first = jnp.where(quarter >= 2, -first, first)
    second = jnp.where((quarter == 1) | (quarter == 2), -second, second)
    return first, second


def split_terms(values):
    high = values.astype(BF16)
    low = (values - high.astype(F32)).astype(BF16)
    return jnp.concatenate([high, low], axis=0)


def table_kernel(curves_ref, noise_ref, angle_ref, cos_ref, sin_ref, square_ref):
    length = curves_ref.shape[1]
    wide = cos_ref.shape[1]
    zeros = jnp.zeros((cos_ref.shape[0], wide - length), F32)
    sine, cosine = sine_cosine(angle_ref[...])
    cos_ref[...] = jnp.concatenate([cosine, zeros], axis=1)
    sin_ref[...] = jnp.concatenate([sine, zeros], axis=1)
    curve = curves_ref[...]
    square = split_terms(curve * curve * noise_ref[...])
    square_ref[...] = jnp.concatenate(
        [square, jnp.zeros((square.shape[0], wide - length), BF16)], axis=1
    )


def added_rows(extra, norm, banks, n_proj, length, subsets):
    ids_at = length // 128 * 128
    ids = []
    for bank in banks:
        for first in range(0, bank.shape[0], 2 * n_proj):
            rows = bank[first : first + 2 * n_proj, ids_at : ids_at + 128].astype(F32)
            ids.append(rows[:n_proj])
    ids = jnp.concatenate(ids, axis=0)[:, length - ids_at : length - ids_at + 1]
    subset_col = lax.broadcasted_iota(jnp.int32, (ids.shape[0], subsets), 1).astype(F32)
    subset_hot = (subset_col == ids).astype(F32).astype(BF16)
    prior = lax.dot_general(
        extra[:, :subsets].astype(BF16), subset_hot, NT_DIMS, preferred_element_type=F32
    )
    return prior - 0.5 * norm


def bank_pieces(bank, span, n_proj):
    for first in range(0, bank.shape[0], 2 * n_proj):
        both = bank[first : first + 2 * n_proj, span].astype(F32)
        yield both[:n_proj], both[n_proj:]


def shifted_rows(real, imag, cos_ref, sin_ref, span):
    real_rows, imag_rows = [], []
    for t in range(cos_ref.shape[0]):
        cos_part, sin_part = cos_ref[t : t + 1, span], sin_ref[t : t + 1, span]
        real_rows.append(cos_part * real + sin_part * imag)
        imag_rows.append(cos_part * imag - sin_part * real)
    return (
        jnp.concatenate(real_rows, axis=0).astype(BF16),
        jnp.concatenate(imag_rows, axis=0).astype(BF16),
    )


def spans_of(wide):
    step = 256 if wide % 256 == 0 else 128
    return [slice(at, at + step) for at in range(0, wide, step)]


def shift_kernel(n_proj, cos_ref, sin_ref, *rest):
    *banks, shifted_ref, power_ref = rest
    shifts, wide = cos_ref.shape
    width = shifts * n_proj
    for span in spans_of(wide):
        powers, at = [], 0
        for bank in banks:
            for real, imag in bank_pieces(bank, span, n_proj):
                real_rows, imag_rows = shifted_rows(real, imag, cos_ref, sin_ref, span)
                shifted_ref[at : at + width, span] = real_rows
                shifted_ref[at : at + width, wide + span.start : wide + span.stop] = imag_rows
                powers.append(real * real + imag * imag)
                at += width
        power_ref[:, span] = split_terms(jnp.concatenate(powers, axis=0))


def multiply(left, right):
    return lax.dot_general(left, right, NT_DIMS, preferred_element_type=F32)


def added(total, terms):
    return terms if total is None else total + terms


def pieces_of(cross, norm, extra, banks, length, subsets, n_proj):
    count, total = cross.shape[0], norm.shape[1] // 2
    width = cross.shape[1] * n_proj // total
    norm = norm[:count, total:] + norm[count:, :total] + norm[:count, :total]
    offset = added_rows(extra, norm, banks, n_proj, length, subsets)
    pieces = []
    for n in range(total // n_proj):
        scores = cross[:, n * width : (n + 1) * width]
        pieces.append(jnp.concatenate([scores, offset[:, n * n_proj : (n + 1) * n_proj]], axis=1))
    return pieces


def rows_of(parts, span):
    return jnp.concatenate([part[:, span] for part in parts], axis=0)


def rows_of(parts, span):
    return jnp.concatenate([part[:, span] for part in parts], axis=0)


def score_kernel(order, bits, n_parts, n_banks, n_proj, length, subsets, square_ref, *rest):
    parts, rest = rest[:n_parts], rest[n_parts:]
    groups, (rows_ref, give_ref, select_ref) = [], rest[-3:]
    for n in n_banks:
        groups.append((rest[0], rest[1], rest[2 : 2 + n]))
        rest = rest[2 + n :]
    wide = select_ref.shape[1]
    classes_count = square_ref.shape[0] // 2
    extra = rows_of(parts, slice(2 * wide, None)).astype(F32)
    count = extra.shape[0]
    class_col = lax.broadcasted_iota(jnp.int32, (count, classes_count), 1).astype(F32)
    onehot = (class_col == extra[:, subsets : subsets + 1]).astype(F32).astype(BF16)
    for n in range(2):
        squares = square_ref[n * classes_count : (n + 1) * classes_count, :]
        chosen = jnp.dot(onehot, squares, preferred_element_type=F32)
        select_ref[n * count : (n + 1) * count, :] = chosen.astype(BF16)

    pieces = []
    for shifted_ref, power_ref, banks in groups:
        cross, turned = None, None
        for at in range(0, wide, 512):
            span = slice(at, min(at + 512, wide))
            other = slice(wide + span.start, wide + span.stop)
            cross = added(cross, multiply(rows_of(parts, span), shifted_ref[:, span]))
            turned = added(turned, multiply(shifted_ref[:, other], rows_of(parts, other)))
        norm = multiply(select_ref[...], power_ref[...])
        pieces += pieces_of(cross + turned.T, norm, extra, banks, length, subsets, n_proj)

    slot = rows_ref.shape[1] // len(order)
    width = pieces[0].shape[1]
    zeros = jnp.zeros((count, slot - width), F32)
    pieces = [jnp.concatenate([piece, zeros], axis=1) for piece in pieces]
    rows_ref[...] = jnp.concatenate(pieces, axis=1)
    dest, lanes = give_ref.shape
    rows = [in_rows(values, 1, bits, dest) for values in pieces]
    rows = [values[:, :width] for values in in_order(rows, order)]
    if lanes > len(rows) * width:
        rows.append(jnp.zeros((dest, lanes - len(rows) * width), F32))
    give_ref[...] = jnp.concatenate(rows, axis=1)


def slots_of(rows_ref, slot):
    return [rows_ref[:, at : at + slot] for at in range(0, rows_ref.shape[1], slot)]


def in_rows(values, d, bits, dest):
    ng = 1 << len(bits)
    n_part = dest // ng
    g = lax.axis_index("grp")
    row = lax.broadcasted_iota(jnp.int32, (dest, values.shape[1]), 0)
    found = []
    for away in range(ng):
        source = d
        for n, bit in enumerate(bits):
            source += (2 << n) if away & bit else 0
        found.append(values[source * n_part : (source + 1) * n_part])
    values = jnp.concatenate(found, axis=0)
    for bit in bits:
        step = bit * n_part
        other = jnp.where(
            (row & step) != 0, pltpu.roll(values, step, 0), pltpu.roll(values, dest - step, 0)
        )
        values = jnp.where((g & bit) != 0, other, values)
    return values


def in_order(pieces, order):
    blk = lax.axis_index("blk")
    found = [pieces[order.index(n)] for n in range(len(order))]
    bit = 1
    while bit < len(order):
        swapped = (blk & bit) != 0
        found = [jnp.where(swapped, found[n ^ bit], found[n]) for n in range(len(order))]
        bit *= 2
    return found


def by_shift(pieces, n_proj, shifts):
    def line(t):
        one = [piece[:, t * n_proj : (t + 1) * n_proj] for piece in pieces]
        return jnp.concatenate(one + one, axis=1)

    offset = line(shifts)
    return [line(t) + offset for t in range(shifts)]


def keep_kernel(slot, n_proj, order, bits, rows_ref, out_ref):
    shifts, dest, _ = out_ref.shape
    pieces = [in_rows(values, 0, bits, dest) for values in slots_of(rows_ref, slot)]
    for t, line in enumerate(by_shift(in_order(pieces, order), n_proj, shifts)):
        out_ref[t] = line


def place_kernel(half, n_proj, keep_ref, recv_ref, out_ref):
    shifts, dest, total = out_ref.shape
    width = (shifts + 1) * n_proj
    lower = lax.broadcasted_iota(jnp.int32, (dest, total), 1) < total // 2
    own = lower == (lax.axis_index("blk") < half)
    pieces = [recv_ref[:, n * width : (n + 1) * width] for n in range(half)]
    for t, line in enumerate(by_shift(pieces, n_proj, shifts)):
        out_ref[t] = jnp.where(own, keep_ref[t], line)


def per_device(
    particles,
    ctf_class,
    orient_prior,
    ctf_curves,
    noise_weight,
    shift_phase,
    trans_index,
    projections,
    orient_subset,
):
    nb, ng = lax.axis_size("blk"), lax.axis_size("grp")
    half = nb // 2
    n_part, n_proj = particles.shape[0], projections.shape[0]
    length = particles.shape[2]
    shifts = shift_phase.shape[0]
    classes_count = ctf_curves.shape[0]
    subsets = orient_prior.shape[1]
    wide = 128 * (length // 128 + 1)
    extra = 128 * (subsets // 128 + 1)
    noise = noise_weight.reshape(1, length)
    shape = jax.ShapeDtypeStruct

    def vmem_out(dims, dtype):
        return pltpu.VMEM(dims, dtype)

    operands = (
        ctf_class,
        orient_subset,
        particles,
        orient_prior,
        ctf_curves,
        noise,
        projections,
        shift_phase,
        trans_index,
    )
    bank, part, curves, noise, angle = pl.pallas_call(
        pack_kernel,
        out_shape=[
            vmem_out((2 * n_proj, wide), BF16),
            vmem_out((n_part, 2 * wide + extra), BF16),
            vmem_out(ctf_curves.shape, F32),
            vmem_out(noise.shape, F32),
            vmem_out(shift_phase.shape, F32),
        ],
        in_specs=[pl.BlockSpec(memory_space=pltpu.HBM)] * len(operands),
        out_specs=[_vmem()] * 5,
        scratch_shapes=[
            pltpu.SMEM(ctf_class.shape, jnp.int32),
            pltpu.SMEM(orient_subset.shape, jnp.int32),
            pltpu.SMEM(trans_index.shape, jnp.int32),
            pltpu.VMEM(particles.shape, BF16),
            pltpu.VMEM(orient_prior.shape, BF16),
            pltpu.VMEM(shift_phase.shape, F32),
            pltpu.VMEM(projections.shape, BF16),
            pltpu.SemaphoreType.DMA((len(operands),)),
        ],
        compiler_params=_params(16),
        name="pack",
    )(*[pltpu.with_memory_space_constraint(operand, pltpu.HBM) for operand in operands])

    def swap(value, axis, bit):
        size = lax.axis_size(axis)
        return lax.ppermute(value, axis, [(i, i ^ bit) for i in range(size)])

    def joined(pieces):
        return pieces[0] if len(pieces) == 1 else jnp.concatenate(pieces, axis=0)

    across = swap(part, "blk", half)
    near = swap(bank, "blk", 1)
    planes, order = [bank], [0]
    for n in range(half.bit_length() - 2, 0, -1):
        planes.append(swap(joined(planes), "blk", 1 << n))
        order += [offset ^ (1 << n) for offset in order]
    far = joined(planes[1:])
    last = swap(bank, "blk", 3) if half == 4 else swap(far, "blk", 1)
    order = [0, 1] + order[1:] + [offset ^ 1 for offset in order[1:]]

    cos_part, sin_part, square = pl.pallas_call(
        table_kernel,
        out_shape=[
            vmem_out((shifts, wide), F32),
            vmem_out((shifts, wide), F32),
            vmem_out((2 * classes_count, wide), BF16),
        ],
        in_specs=[_vmem()] * 3,
        out_specs=[_vmem()] * 3,
        compiler_params=_params(8),
        cost_estimate=pl.CostEstimate(flops=4_000_000, bytes_accessed=2_000_000, transcendentals=0),
        name="tables",
    )(curves, noise, angle)

    def shifted_call(banks, name):
        total = sum(piece.shape[0] for piece in banks) // 2
        return pl.pallas_call(
            functools.partial(shift_kernel, n_proj),
            out_shape=[vmem_out((shifts * total, 2 * wide), BF16), vmem_out((2 * total, wide), BF16)],
            in_specs=[_vmem()] * (2 + len(banks)),
            out_specs=[_vmem()] * 2,
            compiler_params=_params(16),
            cost_estimate=pl.CostEstimate(
                flops=6 * total * shifts * wide, bytes_accessed=4_000_000, transcendentals=0
            ),
            name=name,
        )(cos_part, sin_part, *banks)

    early_rows, early_power = shifted_call([bank, near, far], "shift")

    parts = [part, across]
    bits = [1 << n for n in range(ng.bit_length() - 2, -1, -1)]
    for bit in bits:
        if bit == 1:
            parts[1], early_power, last = lax.optimization_barrier((parts[1], early_power, last))
        part = lax.optimization_barrier(joined(parts))
        parts = [part, swap(part, "grp", bit)]

    last_rows, last_power = shifted_call([last], "shift_last")

    count = 2 * ng * n_part
    slot = 128 * -(-(shifts + 1) * n_proj // 128)
    lanes = 128 * -(-(shifts + 1) * n_proj * half // 128)
    rows, give = pl.pallas_call(
        functools.partial(score_kernel, order, bits, len(parts), (3, 1), n_proj, length, subsets),
        out_shape=[vmem_out((count, half * slot), F32), vmem_out((ng * n_part, lanes), F32)],
        in_specs=[_vmem()] * (9 + len(parts)),
        out_specs=[_vmem()] * 2,
        scratch_shapes=[pltpu.VMEM((2 * count, wide), BF16)],
        compiler_params=_params(24),
        cost_estimate=pl.CostEstimate(
            flops=4 * count * half * n_proj * shifts * wide, bytes_accessed=4_000_000, transcendentals=0
        ),
        name="score",
    )(square, *parts, early_rows, early_power, bank, near, far, last_rows, last_power, last)
    recv = swap(give, "blk", half)
    keep = pl.pallas_call(
        functools.partial(keep_kernel, slot, n_proj, order, bits),
        out_shape=vmem_out((shifts, ng * n_part, nb * n_proj), F32),
        in_specs=[_vmem()],
        out_specs=_vmem(),
        compiler_params=_params(4),
        name="keep",
    )(rows)
    scores = pl.pallas_call(
        functools.partial(place_kernel, half, n_proj),
        out_shape=shape((shifts, ng * n_part, nb * n_proj), F32),
        in_specs=[_vmem()] * 2,
        out_specs=_vmem(),
        compiler_params=_params(4),
        name="place",
    )(keep, recv)
    return scores.transpose(1, 0, 2)


def solution(mesh):
    placed = (
        P(("blk", "grp"), None, None),
        P(("blk", "grp")),
        P(("blk", "grp"), None),
        P(),
        P(),
        P(),
        P(),
        P(("grp", "blk"), None, None),
        P(("grp", "blk")),
    )
    return jax.shard_map(
        per_device, mesh=mesh, in_specs=placed, out_specs=P("blk", None, "grp"), check_vma=False
    )
```

```python
import functools

import jax
import jax.numpy as jnp
from jax import lax
from jax.experimental import pallas as pl
from jax.experimental.pallas import tpu as pltpu
from jax.sharding import PartitionSpec as P

F32 = jnp.float32
BF16 = jnp.bfloat16
HIGHEST = lax.Precision.HIGHEST
NT_DIMS = (((1,), (1,)), ((), ()))
MIB = 1 << 20


def _vmem():
    return pl.BlockSpec(memory_space=pltpu.VMEM)


def _params(mib):
    return pltpu.CompilerParams(vmem_limit_bytes=mib * MIB)


def pack_kernel(
    class_hbm,
    subset_hbm,
    particles_hbm,
    prior_hbm,
    curves_hbm,
    noise_hbm,
    proj_hbm,
    phase_hbm,
    trans_hbm,
    bank_ref,
    part_ref,
    curves_ref,
    noise_ref,
    angle_ref,
    class_ref,
    subset_ref,
    trans_ref,
    particles_ref,
    prior_ref,
    phase_ref,
    proj_ref,
    sems,
):
    n_proj = proj_hbm.shape[0]
    pairs = [
        (proj_hbm, proj_ref),
        (curves_hbm, curves_ref),
        (subset_hbm, subset_ref),
        (class_hbm, class_ref),
        (particles_hbm, particles_ref),
        (noise_hbm, noise_ref),
        (prior_hbm, prior_ref),
        (trans_hbm, trans_ref),
        (phase_hbm, phase_ref),
    ]
    copies = [pltpu.make_async_copy(a, b, sems.at[n]) for n, (a, b) in enumerate(pairs)]
    for copy in copies:
        copy.start()
    n_part = particles_ref.shape[0]
    length = proj_ref.shape[2]
    wide = bank_ref.shape[1]

    def padded(values, width):
        zeros = jnp.zeros((values.shape[0], width - values.shape[1]), values.dtype)
        return jnp.concatenate([values, zeros], axis=1)

    row = lax.broadcasted_iota(jnp.int32, (n_proj, wide), 0)
    lane = lax.broadcasted_iota(jnp.int32, (n_proj, wide), 1)
    copies[0].wait()
    copies[2].wait()
    real = jnp.zeros((n_proj, wide), F32)
    imag = jnp.zeros((n_proj, wide), F32)
    for j in range(n_proj):
        both = padded(proj_ref[j].astype(F32), wide)
        real = jnp.where(row == j, both[0:1], real)
        imag = jnp.where(row == j, both[1:2], imag)
    last = slice(wide - 128, wide)
    ends = real[:, last]
    for j in range(n_proj):
        here = (row[:, last] == j) & (lane[:, last] == length)
        ends = jnp.where(here, subset_ref[j].astype(F32), ends)
    real = jnp.concatenate([real[:, : wide - 128], ends], axis=1)
    bank_ref[...] = jnp.concatenate([real, imag], axis=0).astype(BF16)

    copies[1].wait()
    for copy in copies[3:]:
        copy.wait()
    subsets = prior_ref.shape[1]
    extra = part_ref.shape[1] - 2 * wide
    row = lax.broadcasted_iota(jnp.int32, (n_part, wide), 0)
    row_extra = lax.broadcasted_iota(jnp.int32, (n_part, extra), 0)
    lane_extra = lax.broadcasted_iota(jnp.int32, (n_part, extra), 1)
    real = jnp.zeros((n_part, wide), F32)
    imag = jnp.zeros((n_part, wide), F32)
    small = padded(prior_ref[...].astype(F32), extra)
    for i in range(n_part):
        curve = curves_ref[pl.ds(class_ref[i], 1), :] * noise_ref[...]
        both = padded(particles_ref[i].astype(F32) * curve, wide)
        real = jnp.where(row == i, both[0:1], real)
        imag = jnp.where(row == i, both[1:2], imag)
        place = (row_extra == i) & (lane_extra == subsets)
        small = jnp.where(place, class_ref[i].astype(F32), small)
    part_ref[:, :wide] = real.astype(BF16)
    part_ref[:, wide : 2 * wide] = imag.astype(BF16)
    part_ref[:, 2 * wide :] = small.astype(BF16)
    for t in range(phase_ref.shape[0]):
        angle_ref[t : t + 1, :] = phase_ref[pl.ds(trans_ref[t], 1), :]


def sine_cosine(x):
    turns = jnp.floor(x * 0.6366197723675814 + 0.5)
    r = ((x - turns * 1.5703125) - turns * 4.837512969970703125e-4) - turns * 7.549789954891882e-8
    z = r * r
    sine = r + r * z * (-1.6666654611e-1 + z * (8.3321608736e-3 - z * 1.9515295891e-4))
    cosine = 1.0 - 0.5 * z + z * z * (
        4.166664568298827e-2 + z * (-1.388731625493765e-3 + z * 2.443315711809948e-5)
    )
    quarter = turns.astype(jnp.int32) & 3
    swapped = (quarter & 1) == 1
    first, second = jnp.where(swapped, cosine, sine), jnp.where(swapped, sine, cosine)
    first = jnp.where(quarter >= 2, -first, first)
    second = jnp.where((quarter == 1) | (quarter == 2), -second, second)
    return first, second


def split_terms(values):
    high = values.astype(BF16)
    low = (values - high.astype(F32)).astype(BF16)
    return jnp.concatenate([high, low], axis=0)


def table_kernel(curves_ref, noise_ref, angle_ref, cos_ref, sin_ref, square_ref):
    length = curves_ref.shape[1]
    wide = cos_ref.shape[1]
    zeros = jnp.zeros((cos_ref.shape[0], wide - length), F32)
    sine, cosine = sine_cosine(angle_ref[...])
    cos_ref[...] = jnp.concatenate([cosine, zeros], axis=1)
    sin_ref[...] = jnp.concatenate([sine, zeros], axis=1)
    curve = curves_ref[...]
    square = split_terms(curve * curve * noise_ref[...])
    square_ref[...] = jnp.concatenate(
        [square, jnp.zeros((square.shape[0], wide - length), BF16)], axis=1
    )


def added_rows(extra, norm, banks, n_proj, length, subsets):
    ids_at = length // 128 * 128
    ids = []
    for bank in banks:
        for first in range(0, bank.shape[0], 2 * n_proj):
            rows = bank[first : first + 2 * n_proj, ids_at : ids_at + 128].astype(F32)
            ids.append(rows[:n_proj])
    ids = jnp.concatenate(ids, axis=0)[:, length - ids_at : length - ids_at + 1]
    subset_col = lax.broadcasted_iota(jnp.int32, (ids.shape[0], subsets), 1).astype(F32)
    subset_hot = (subset_col == ids).astype(F32).astype(BF16)
    prior = lax.dot_general(
        extra[:, :subsets].astype(BF16), subset_hot, NT_DIMS, preferred_element_type=F32
    )
    return prior - 0.5 * norm


def bank_pieces(bank, span, n_proj):
    for first in range(0, bank.shape[0], 2 * n_proj):
        both = bank[first : first + 2 * n_proj, span].astype(F32)
        yield both[:n_proj], both[n_proj:]


def shifted_rows(real, imag, cos_ref, sin_ref, span):
    real_rows, imag_rows = [], []
    for t in range(cos_ref.shape[0]):
        cos_part, sin_part = cos_ref[t : t + 1, span], sin_ref[t : t + 1, span]
        real_rows.append(cos_part * real + sin_part * imag)
        imag_rows.append(cos_part * imag - sin_part * real)
    return (
        jnp.concatenate(real_rows, axis=0).astype(BF16),
        jnp.concatenate(imag_rows, axis=0).astype(BF16),
    )


def spans_of(wide):
    step = 256 if wide % 256 == 0 else 128
    return [slice(at, at + step) for at in range(0, wide, step)]


def shift_kernel(n_proj, cos_ref, sin_ref, *rest):
    *banks, shifted_ref, power_ref = rest
    shifts, wide = cos_ref.shape
    width = shifts * n_proj
    for span in spans_of(wide):
        powers, at = [], 0
        for bank in banks:
            for real, imag in bank_pieces(bank, span, n_proj):
                real_rows, imag_rows = shifted_rows(real, imag, cos_ref, sin_ref, span)
                shifted_ref[at : at + width, span] = real_rows
                shifted_ref[at : at + width, wide + span.start : wide + span.stop] = imag_rows
                powers.append(real * real + imag * imag)
                at += width
        power_ref[:, span] = split_terms(jnp.concatenate(powers, axis=0))


def multiply(left, right):
    return lax.dot_general(left, right, NT_DIMS, preferred_element_type=F32)


def added(total, terms):
    return terms if total is None else total + terms


def pieces_of(cross, norm, extra, banks, length, subsets, n_proj):
    count, total = cross.shape[0], norm.shape[1] // 2
    width = cross.shape[1] * n_proj // total
    norm = norm[:count, total:] + norm[count:, :total] + norm[:count, :total]
    offset = added_rows(extra, norm, banks, n_proj, length, subsets)
    pieces = []
    for n in range(total // n_proj):
        scores = cross[:, n * width : (n + 1) * width]
        pieces.append(jnp.concatenate([scores, offset[:, n * n_proj : (n + 1) * n_proj]], axis=1))
    return pieces


def rows_of(parts, span):
    return jnp.concatenate([part[:, span] for part in parts], axis=0)


def rows_of(parts, span):
    return jnp.concatenate([part[:, span] for part in parts], axis=0)


def score_kernel(order, bits, n_parts, n_banks, n_proj, length, subsets, square_ref, *rest):
    parts, rest = rest[:n_parts], rest[n_parts:]
    groups, (rows_ref, give_ref, select_ref) = [], rest[-3:]
    for n in n_banks:
        groups.append((rest[0], rest[1], rest[2 : 2 + n]))
        rest = rest[2 + n :]
    wide = select_ref.shape[1]
    classes_count = square_ref.shape[0] // 2
    extra = rows_of(parts, slice(2 * wide, None)).astype(F32)
    count = extra.shape[0]
    class_col = lax.broadcasted_iota(jnp.int32, (count, classes_count), 1).astype(F32)
    onehot = (class_col == extra[:, subsets : subsets + 1]).astype(F32).astype(BF16)
    for n in range(2):
        squares = square_ref[n * classes_count : (n + 1) * classes_count, :]
        chosen = jnp.dot(onehot, squares, preferred_element_type=F32)
        select_ref[n * count : (n + 1) * count, :] = chosen.astype(BF16)

    pieces = []
    for shifted_ref, power_ref, banks in groups:
        cross, turned = None, None
        for at in range(0, wide, 512):
            span = slice(at, min(at + 512, wide))
            other = slice(wide + span.start, wide + span.stop)
            cross = added(cross, multiply(rows_of(parts, span), shifted_ref[:, span]))
            turned = added(turned, multiply(shifted_ref[:, other], rows_of(parts, other)))
        norm = multiply(select_ref[...], power_ref[...])
        pieces += pieces_of(cross + turned.T, norm, extra, banks, length, subsets, n_proj)

    slot = rows_ref.shape[1] // len(order)
    width = pieces[0].shape[1]
    zeros = jnp.zeros((count, slot - width), F32)
    pieces = [jnp.concatenate([piece, zeros], axis=1) for piece in pieces]
    rows_ref[...] = jnp.concatenate(pieces, axis=1)
    dest, lanes = give_ref.shape
    rows = [in_rows(values, 1, bits, dest) for values in pieces]
    rows = [values[:, :width] for values in in_order(rows, order)]
    if lanes > len(rows) * width:
        rows.append(jnp.zeros((dest, lanes - len(rows) * width), F32))
    give_ref[...] = jnp.concatenate(rows, axis=1)


def slots_of(rows_ref, slot):
    return [rows_ref[:, at : at + slot] for at in range(0, rows_ref.shape[1], slot)]


def in_rows(values, d, bits, dest):
    ng = 1 << len(bits)
    n_part = dest // ng
    g = lax.axis_index("grp")
    row = lax.broadcasted_iota(jnp.int32, (dest, values.shape[1]), 0)
    found = []
    for away in range(ng):
        source = d
        for n, bit in enumerate(bits):
            source += (2 << n) if away & bit else 0
        found.append(values[source * n_part : (source + 1) * n_part])
    values = jnp.concatenate(found, axis=0)
    for bit in bits:
        step = bit * n_part
        other = jnp.where(
            (row & step) != 0, pltpu.roll(values, step, 0), pltpu.roll(values, dest - step, 0)
        )
        values = jnp.where((g & bit) != 0, other, values)
    return values


def in_order(pieces, order):
    blk = lax.axis_index("blk")
    found = [pieces[order.index(n)] for n in range(len(order))]
    bit = 1
    while bit < len(order):
        swapped = (blk & bit) != 0
        found = [jnp.where(swapped, found[n ^ bit], found[n]) for n in range(len(order))]
        bit *= 2
    return found


def by_shift(pieces, n_proj, shifts):
    def line(t):
        one = [piece[:, t * n_proj : (t + 1) * n_proj] for piece in pieces]
        return jnp.concatenate(one + one, axis=1)

    offset = line(shifts)
    return [line(t) + offset for t in range(shifts)]


def keep_kernel(slot, n_proj, order, bits, rows_ref, out_ref):
    shifts, dest, _ = out_ref.shape
    pieces = [in_rows(values, 0, bits, dest) for values in slots_of(rows_ref, slot)]
    for t, line in enumerate(by_shift(in_order(pieces, order), n_proj, shifts)):
        out_ref[t] = line


def place_kernel(half, n_proj, keep_ref, recv_ref, out_ref):
    shifts, dest, total = out_ref.shape
    width = (shifts + 1) * n_proj
    lower = lax.broadcasted_iota(jnp.int32, (dest, total), 1) < total // 2
    own = lower == (lax.axis_index("blk") < half)
    pieces = [recv_ref[:, n * width : (n + 1) * width] for n in range(half)]
    for t, line in enumerate(by_shift(pieces, n_proj, shifts)):
        out_ref[t] = jnp.where(own, keep_ref[t], line)


def per_device(
    particles,
    ctf_class,
    orient_prior,
    ctf_curves,
    noise_weight,
    shift_phase,
    trans_index,
    projections,
    orient_subset,
):
    nb, ng = lax.axis_size("blk"), lax.axis_size("grp")
    half = nb // 2
    n_part, n_proj = particles.shape[0], projections.shape[0]
    length = particles.shape[2]
    shifts = shift_phase.shape[0]
    classes_count = ctf_curves.shape[0]
    subsets = orient_prior.shape[1]
    wide = 128 * (length // 128 + 1)
    extra = 128 * (subsets // 128 + 1)
    noise = noise_weight.reshape(1, length)
    shape = jax.ShapeDtypeStruct

    def vmem_out(dims, dtype):
        return pltpu.VMEM(dims, dtype)

    operands = (
        ctf_class,
        orient_subset,
        particles,
        orient_prior,
        ctf_curves,
        noise,
        projections,
        shift_phase,
        trans_index,
    )
    bank, part, curves, noise, angle = pl.pallas_call(
        pack_kernel,
        out_shape=[
            vmem_out((2 * n_proj, wide), BF16),
            vmem_out((n_part, 2 * wide + extra), BF16),
            vmem_out(ctf_curves.shape, F32),
            vmem_out(noise.shape, F32),
            vmem_out(shift_phase.shape, F32),
        ],
        in_specs=[pl.BlockSpec(memory_space=pltpu.HBM)] * len(operands),
        out_specs=[_vmem()] * 5,
        scratch_shapes=[
            pltpu.SMEM(ctf_class.shape, jnp.int32),
            pltpu.SMEM(orient_subset.shape, jnp.int32),
            pltpu.SMEM(trans_index.shape, jnp.int32),
            pltpu.VMEM(particles.shape, BF16),
            pltpu.VMEM(orient_prior.shape, BF16),
            pltpu.VMEM(shift_phase.shape, F32),
            pltpu.VMEM(projections.shape, BF16),
            pltpu.SemaphoreType.DMA((len(operands),)),
        ],
        compiler_params=_params(16),
        name="pack",
    )(*[pltpu.with_memory_space_constraint(operand, pltpu.HBM) for operand in operands])

    def swap(value, axis, bit):
        size = lax.axis_size(axis)
        return lax.ppermute(value, axis, [(i, i ^ bit) for i in range(size)])

    def joined(pieces):
        return pieces[0] if len(pieces) == 1 else jnp.concatenate(pieces, axis=0)

    across = swap(part, "blk", half)
    near = swap(bank, "blk", 1)
    planes, order = [bank], [0]
    for n in range(half.bit_length() - 2, 0, -1):
        planes.append(swap(joined(planes), "blk", 1 << n))
        order += [offset ^ (1 << n) for offset in order]
    far = joined(planes[1:])
    last = swap(bank, "blk", 3) if half == 4 else swap(far, "blk", 1)
    order = order + [1] + [offset ^ 1 for offset in order[1:]]

    cos_part, sin_part, square = pl.pallas_call(
        table_kernel,
        out_shape=[
            vmem_out((shifts, wide), F32),
            vmem_out((shifts, wide), F32),
            vmem_out((2 * classes_count, wide), BF16),
        ],
        in_specs=[_vmem()] * 3,
        out_specs=[_vmem()] * 3,
        compiler_params=_params(8),
        cost_estimate=pl.CostEstimate(flops=4_000_000, bytes_accessed=2_000_000, transcendentals=0),
        name="tables",
    )(curves, noise, angle)

    def shifted_call(banks, name):
        total = sum(piece.shape[0] for piece in banks) // 2
        return pl.pallas_call(
            functools.partial(shift_kernel, n_proj),
            out_shape=[vmem_out((shifts * total, 2 * wide), BF16), vmem_out((2 * total, wide), BF16)],
            in_specs=[_vmem()] * (2 + len(banks)),
            out_specs=[_vmem()] * 2,
            compiler_params=_params(16),
            cost_estimate=pl.CostEstimate(
                flops=6 * total * shifts * wide, bytes_accessed=4_000_000, transcendentals=0
            ),
            name=name,
        )(cos_part, sin_part, *banks)

    early_rows, early_power = shifted_call([bank, far, near], "shift")

    parts = [part, across]
    bits = [1 << n for n in range(ng.bit_length() - 2, -1, -1)]
    for bit in bits:
        if bit == 1:
            parts[1], early_power, last = lax.optimization_barrier((parts[1], early_power, last))
        part = lax.optimization_barrier(joined(parts))
        parts = [part, swap(part, "grp", bit)]

    last_rows, last_power = shifted_call([last], "shift_last")

    count = 2 * ng * n_part
    slot = 128 * -(-(shifts + 1) * n_proj // 128)
    lanes = 128 * -(-(shifts + 1) * n_proj * half // 128)
    rows, give = pl.pallas_call(
        functools.partial(score_kernel, order, bits, len(parts), (3, 1), n_proj, length, subsets),
        out_shape=[vmem_out((count, half * slot), F32), vmem_out((ng * n_part, lanes), F32)],
        in_specs=[_vmem()] * (9 + len(parts)),
        out_specs=[_vmem()] * 2,
        scratch_shapes=[pltpu.VMEM((2 * count, wide), BF16)],
        compiler_params=_params(24),
        cost_estimate=pl.CostEstimate(
            flops=4 * count * half * n_proj * shifts * wide, bytes_accessed=4_000_000, transcendentals=0
        ),
        name="score",
    )(square, *parts, early_rows, early_power, bank, far, near, last_rows, last_power, last)
    recv = swap(give, "blk", half)
    keep = pl.pallas_call(
        functools.partial(keep_kernel, slot, n_proj, order, bits),
        out_shape=vmem_out((shifts, ng * n_part, nb * n_proj), F32),
        in_specs=[_vmem()],
        out_specs=_vmem(),
        compiler_params=_params(4),
        name="keep",
    )(rows)
    scores = pl.pallas_call(
        functools.partial(place_kernel, half, n_proj),
        out_shape=shape((shifts, ng * n_part, nb * n_proj), F32),
        in_specs=[_vmem()] * 2,
        out_specs=_vmem(),
        compiler_params=_params(4),
        name="place",
    )(keep, recv)
    return scores.transpose(1, 0, 2)


def solution(mesh):
    placed = (
        P(("blk", "grp"), None, None),
        P(("blk", "grp")),
        P(("blk", "grp"), None),
        P(),
        P(),
        P(),
        P(),
        P(("grp", "blk"), None, None),
        P(("grp", "blk")),
    )
    return jax.shard_map(
        per_device, mesh=mesh, in_specs=placed, out_specs=P("blk", None, "grp"), check_vma=False
    )
```

```python
import functools

import jax
import jax.numpy as jnp
from jax import lax
from jax.experimental import pallas as pl
from jax.experimental.pallas import tpu as pltpu
from jax.sharding import PartitionSpec as P

F32 = jnp.float32
BF16 = jnp.bfloat16
HIGHEST = lax.Precision.HIGHEST
NT_DIMS = (((1,), (1,)), ((), ()))
MIB = 1 << 20


def _vmem():
    return pl.BlockSpec(memory_space=pltpu.VMEM)


def _params(mib):
    return pltpu.CompilerParams(vmem_limit_bytes=mib * MIB)


def pack_kernel(
    class_hbm,
    subset_hbm,
    particles_hbm,
    prior_hbm,
    curves_hbm,
    noise_hbm,
    proj_hbm,
    phase_hbm,
    trans_hbm,
    bank_ref,
    part_ref,
    curves_ref,
    noise_ref,
    angle_ref,
    class_ref,
    subset_ref,
    trans_ref,
    particles_ref,
    prior_ref,
    phase_ref,
    proj_ref,
    sems,
):
    n_proj = proj_hbm.shape[0]
    pairs = [
        (proj_hbm, proj_ref),
        (curves_hbm, curves_ref),
        (subset_hbm, subset_ref),
        (class_hbm, class_ref),
        (particles_hbm, particles_ref),
        (noise_hbm, noise_ref),
        (prior_hbm, prior_ref),
        (trans_hbm, trans_ref),
        (phase_hbm, phase_ref),
    ]
    copies = [pltpu.make_async_copy(a, b, sems.at[n]) for n, (a, b) in enumerate(pairs)]
    for copy in copies:
        copy.start()
    n_part = particles_ref.shape[0]
    length = proj_ref.shape[2]
    wide = bank_ref.shape[1]

    def padded(values, width):
        zeros = jnp.zeros((values.shape[0], width - values.shape[1]), values.dtype)
        return jnp.concatenate([values, zeros], axis=1)

    row = lax.broadcasted_iota(jnp.int32, (n_proj, wide), 0)
    lane = lax.broadcasted_iota(jnp.int32, (n_proj, wide), 1)
    copies[0].wait()
    copies[2].wait()
    real = jnp.zeros((n_proj, wide), F32)
    imag = jnp.zeros((n_proj, wide), F32)
    for j in range(n_proj):
        both = padded(proj_ref[j].astype(F32), wide)
        real = jnp.where(row == j, both[0:1], real)
        imag = jnp.where(row == j, both[1:2], imag)
    last = slice(wide - 128, wide)
    ends = real[:, last]
    for j in range(n_proj):
        here = (row[:, last] == j) & (lane[:, last] == length)
        ends = jnp.where(here, subset_ref[j].astype(F32), ends)
    real = jnp.concatenate([real[:, : wide - 128], ends], axis=1)
    bank_ref[...] = jnp.concatenate([real, imag], axis=0).astype(BF16)

    copies[1].wait()
    for copy in copies[3:]:
        copy.wait()
    subsets = prior_ref.shape[1]
    extra = part_ref.shape[1] - 2 * wide
    row = lax.broadcasted_iota(jnp.int32, (n_part, wide), 0)
    row_extra = lax.broadcasted_iota(jnp.int32, (n_part, extra), 0)
    lane_extra = lax.broadcasted_iota(jnp.int32, (n_part, extra), 1)
    real = jnp.zeros((n_part, wide), F32)
    imag = jnp.zeros((n_part, wide), F32)
    small = padded(prior_ref[...].astype(F32), extra)
    for i in range(n_part):
        curve = curves_ref[pl.ds(class_ref[i], 1), :] * noise_ref[...]
        both = padded(particles_ref[i].astype(F32) * curve, wide)
        real = jnp.where(row == i, both[0:1], real)
        imag = jnp.where(row == i, both[1:2], imag)
        place = (row_extra == i) & (lane_extra == subsets)
        small = jnp.where(place, class_ref[i].astype(F32), small)
    part_ref[:, :wide] = real.astype(BF16)
    part_ref[:, wide : 2 * wide] = imag.astype(BF16)
    part_ref[:, 2 * wide :] = small.astype(BF16)
    for t in range(phase_ref.shape[0]):
        angle_ref[t : t + 1, :] = phase_ref[pl.ds(trans_ref[t], 1), :]


def sine_cosine(x):
    turns = jnp.floor(x * 0.6366197723675814 + 0.5)
    r = ((x - turns * 1.5703125) - turns * 4.837512969970703125e-4) - turns * 7.549789954891882e-8
    z = r * r
    sine = r + r * z * (-1.6666654611e-1 + z * (8.3321608736e-3 - z * 1.9515295891e-4))
    cosine = 1.0 - 0.5 * z + z * z * (
        4.166664568298827e-2 + z * (-1.388731625493765e-3 + z * 2.443315711809948e-5)
    )
    quarter = turns.astype(jnp.int32) & 3
    swapped = (quarter & 1) == 1
    first, second = jnp.where(swapped, cosine, sine), jnp.where(swapped, sine, cosine)
    first = jnp.where(quarter >= 2, -first, first)
    second = jnp.where((quarter == 1) | (quarter == 2), -second, second)
    return first, second


def split_terms(values):
    high = values.astype(BF16)
    low = (values - high.astype(F32)).astype(BF16)
    return jnp.concatenate([high, low], axis=0)


def table_kernel(curves_ref, noise_ref, angle_ref, cos_ref, sin_ref, square_ref):
    length = curves_ref.shape[1]
    wide = cos_ref.shape[1]
    zeros = jnp.zeros((cos_ref.shape[0], wide - length), F32)
    sine, cosine = sine_cosine(angle_ref[...])
    cos_ref[...] = jnp.concatenate([cosine, zeros], axis=1)
    sin_ref[...] = jnp.concatenate([sine, zeros], axis=1)
    curve = curves_ref[...]
    square = split_terms(curve * curve * noise_ref[...])
    square_ref[...] = jnp.concatenate(
        [square, jnp.zeros((square.shape[0], wide - length), BF16)], axis=1
    )


def added_rows(extra, norm, banks, n_proj, length, subsets):
    ids_at = length // 128 * 128
    ids = []
    for bank in banks:
        for first in range(0, bank.shape[0], 2 * n_proj):
            rows = bank[first : first + 2 * n_proj, ids_at : ids_at + 128].astype(F32)
            ids.append(rows[:n_proj])
    ids = jnp.concatenate(ids, axis=0)[:, length - ids_at : length - ids_at + 1]
    subset_col = lax.broadcasted_iota(jnp.int32, (ids.shape[0], subsets), 1).astype(F32)
    subset_hot = (subset_col == ids).astype(F32).astype(BF16)
    prior = lax.dot_general(
        extra[:, :subsets].astype(BF16), subset_hot, NT_DIMS, preferred_element_type=F32
    )
    return prior - 0.5 * norm


def bank_pieces(bank, span, n_proj):
    for first in range(0, bank.shape[0], 2 * n_proj):
        both = bank[first : first + 2 * n_proj, span].astype(F32)
        yield both[:n_proj], both[n_proj:]


def shifted_rows(real, imag, cos_ref, sin_ref, span):
    real_rows, imag_rows = [], []
    for t in range(cos_ref.shape[0]):
        cos_part, sin_part = cos_ref[t : t + 1, span], sin_ref[t : t + 1, span]
        real_rows.append(cos_part * real + sin_part * imag)
        imag_rows.append(cos_part * imag - sin_part * real)
    return (
        jnp.concatenate(real_rows, axis=0).astype(BF16),
        jnp.concatenate(imag_rows, axis=0).astype(BF16),
    )


def spans_of(wide, step=256):
    step = step if wide % step == 0 else 128
    return [slice(at, at + step) for at in range(0, wide, step)]


def shift_kernel(n_proj, cos_ref, sin_ref, *rest):
    *banks, shifted_ref, power_ref = rest
    shifts, wide = cos_ref.shape
    width = shifts * n_proj
    for span in spans_of(wide):
        powers, at = [], 0
        for bank in banks:
            for real, imag in bank_pieces(bank, span, n_proj):
                real_rows, imag_rows = shifted_rows(real, imag, cos_ref, sin_ref, span)
                shifted_ref[at : at + width, span] = real_rows
                shifted_ref[at : at + width, wide + span.start : wide + span.stop] = imag_rows
                powers.append(real * real + imag * imag)
                at += width
        power_ref[:, span] = split_terms(jnp.concatenate(powers, axis=0))


def multiply(left, right):
    return lax.dot_general(left, right, NT_DIMS, preferred_element_type=F32)


def added(total, terms):
    return terms if total is None else total + terms


def pieces_of(cross, norm, extra, banks, length, subsets, n_proj):
    count, total = cross.shape[0], norm.shape[1] // 2
    width = cross.shape[1] * n_proj // total
    norm = norm[:count, total:] + norm[count:, :total] + norm[:count, :total]
    offset = added_rows(extra, norm, banks, n_proj, length, subsets)
    pieces = []
    for n in range(total // n_proj):
        scores = cross[:, n * width : (n + 1) * width]
        pieces.append(jnp.concatenate([scores, offset[:, n * n_proj : (n + 1) * n_proj]], axis=1))
    return pieces


def store_pieces(out, pieces, first, slot, rows):
    for n, piece in enumerate(pieces):
        at = (first + n) * slot
        out[:, at : at + piece.shape[1]] = piece[rows]


def rows_of(parts, span):
    return jnp.concatenate([part[:, span] for part in parts], axis=0)


def early_kernel(n_parts, n_banks, n_proj, length, subsets, square_ref, *rest):
    parts, rest = rest[:n_parts], rest[n_parts:]
    groups, (select_ref, rows_ref) = [], rest[-2:]
    for n in n_banks:
        groups.append((rest[0], rest[1], rest[2 : 2 + n]))
        rest = rest[2 + n :]
    wide = select_ref.shape[1]
    classes_count = square_ref.shape[0] // 2
    extra = rows_of(parts, slice(2 * wide, None)).astype(F32)
    count = extra.shape[0]
    class_col = lax.broadcasted_iota(jnp.int32, (count, classes_count), 1).astype(F32)
    onehot = (class_col == extra[:, subsets : subsets + 1]).astype(F32).astype(BF16)
    for n in range(2):
        squares = square_ref[n * classes_count : (n + 1) * classes_count, :]
        chosen = jnp.dot(onehot, squares, preferred_element_type=F32)
        select_ref[n * count : (n + 1) * count, :] = chosen.astype(BF16)

    pieces = []
    for shifted_ref, power_ref, banks in groups:
        cross, turned = None, None
        for at in range(0, wide, 512):
            span = slice(at, min(at + 512, wide))
            other = slice(wide + span.start, wide + span.stop)
            cross = added(cross, multiply(rows_of(parts, span), shifted_ref[:, span]))
            turned = added(turned, multiply(shifted_ref[:, other], rows_of(parts, other)))
        norm = multiply(select_ref[...], power_ref[...])
        pieces += pieces_of(cross + turned.T, norm, extra, banks, length, subsets, n_proj)
    store_pieces(rows_ref, pieces, 0, rows_ref.shape[1] // len(pieces), slice(None))


def final_kernel(
    order, n_parts, bits, n_proj, length, subsets, select_ref, rows_ref, cos_ref, sin_ref, last_ref, *rest
):
    parts, (late_ref, give_ref) = rest[:n_parts], rest[n_parts:]
    shifts, wide = cos_ref.shape
    cross, norm = None, None
    for span in spans_of(wide, 512):
        terms, powers = [], []
        for real, imag in bank_pieces(last_ref, span, n_proj):
            real_rows, imag_rows = shifted_rows(real, imag, cos_ref, sin_ref, span)
            other = slice(wide + span.start, wide + span.stop)
            terms.append(
                multiply(rows_of(parts, span), real_rows) + multiply(rows_of(parts, other), imag_rows)
            )
            powers.append(real * real + imag * imag)
        cross = added(cross, jnp.concatenate(terms, axis=1))
        power = split_terms(jnp.concatenate(powers, axis=0))
        norm = added(norm, multiply(select_ref[:, span], power))
    extra = rows_of(parts, slice(2 * wide, None)).astype(F32)
    pieces = pieces_of(cross, norm, extra, [last_ref], length, subsets, n_proj)
    slot = late_ref.shape[1] // len(pieces)
    zeros = jnp.zeros((extra.shape[0], slot - pieces[0].shape[1]), F32)
    late = [jnp.concatenate([piece, zeros], axis=1) for piece in pieces]
    late_ref[...] = jnp.concatenate(late, axis=1)
    dest, lanes = give_ref.shape
    width = pieces[0].shape[1]
    rows = [in_rows(values, 1, bits, dest) for values in slots_of(rows_ref, slot) + late]
    rows = [values[:, :width] for values in in_order(rows, order)]
    if lanes > len(rows) * width:
        rows.append(jnp.zeros((dest, lanes - len(rows) * width), F32))
    give_ref[...] = jnp.concatenate(rows, axis=1)


def slots_of(rows_ref, slot):
    return [rows_ref[:, at : at + slot] for at in range(0, rows_ref.shape[1], slot)]


def in_rows(values, d, bits, dest):
    ng = 1 << len(bits)
    n_part = dest // ng
    g = lax.axis_index("grp")
    row = lax.broadcasted_iota(jnp.int32, (dest, values.shape[1]), 0)
    found = []
    for away in range(ng):
        source = d
        for n, bit in enumerate(bits):
            source += (2 << n) if away & bit else 0
        found.append(values[source * n_part : (source + 1) * n_part])
    values = jnp.concatenate(found, axis=0)
    for bit in bits:
        step = bit * n_part
        other = jnp.where(
            (row & step) != 0, pltpu.roll(values, step, 0), pltpu.roll(values, dest - step, 0)
        )
        values = jnp.where((g & bit) != 0, other, values)
    return values


def in_order(pieces, order):
    blk = lax.axis_index("blk")
    found = [pieces[order.index(n)] for n in range(len(order))]
    bit = 1
    while bit < len(order):
        swapped = (blk & bit) != 0
        found = [jnp.where(swapped, found[n ^ bit], found[n]) for n in range(len(order))]
        bit *= 2
    return found


def by_shift(pieces, n_proj, shifts):
    def line(t):
        one = [piece[:, t * n_proj : (t + 1) * n_proj] for piece in pieces]
        return jnp.concatenate(one + one, axis=1)

    offset = line(shifts)
    return [line(t) + offset for t in range(shifts)]


def keep_kernel(slot, n_proj, order, bits, rows_ref, late_ref, out_ref):
    shifts, dest, _ = out_ref.shape
    pieces = [in_rows(values, 0, bits, dest) for values in slots_of(rows_ref, slot) + slots_of(late_ref, slot)]
    for t, line in enumerate(by_shift(in_order(pieces, order), n_proj, shifts)):
        out_ref[t] = line


def place_kernel(half, n_proj, keep_ref, recv_ref, out_ref):
    shifts, dest, total = out_ref.shape
    width = (shifts + 1) * n_proj
    lower = lax.broadcasted_iota(jnp.int32, (dest, total), 1) < total // 2
    own = lower == (lax.axis_index("blk") < half)
    pieces = [recv_ref[:, n * width : (n + 1) * width] for n in range(half)]
    for t, line in enumerate(by_shift(pieces, n_proj, shifts)):
        out_ref[t] = jnp.where(own, keep_ref[t], line)


def per_device(
    particles,
    ctf_class,
    orient_prior,
    ctf_curves,
    noise_weight,
    shift_phase,
    trans_index,
    projections,
    orient_subset,
):
    nb, ng = lax.axis_size("blk"), lax.axis_size("grp")
    half = nb // 2
    n_part, n_proj = particles.shape[0], projections.shape[0]
    length = particles.shape[2]
    shifts = shift_phase.shape[0]
    classes_count = ctf_curves.shape[0]
    subsets = orient_prior.shape[1]
    wide = 128 * (length // 128 + 1)
    extra = 128 * (subsets // 128 + 1)
    noise = noise_weight.reshape(1, length)
    shape = jax.ShapeDtypeStruct

    def vmem_out(dims, dtype):
        return pltpu.VMEM(dims, dtype)

    operands = (
        ctf_class,
        orient_subset,
        particles,
        orient_prior,
        ctf_curves,
        noise,
        projections,
        shift_phase,
        trans_index,
    )
    bank, part, curves, noise, angle = pl.pallas_call(
        pack_kernel,
        out_shape=[
            vmem_out((2 * n_proj, wide), BF16),
            vmem_out((n_part, 2 * wide + extra), BF16),
            vmem_out(ctf_curves.shape, F32),
            vmem_out(noise.shape, F32),
            vmem_out(shift_phase.shape, F32),
        ],
        in_specs=[pl.BlockSpec(memory_space=pltpu.HBM)] * len(operands),
        out_specs=[_vmem()] * 5,
        scratch_shapes=[
            pltpu.SMEM(ctf_class.shape, jnp.int32),
            pltpu.SMEM(orient_subset.shape, jnp.int32),
            pltpu.SMEM(trans_index.shape, jnp.int32),
            pltpu.VMEM(particles.shape, BF16),
            pltpu.VMEM(orient_prior.shape, BF16),
            pltpu.VMEM(shift_phase.shape, F32),
            pltpu.VMEM(projections.shape, BF16),
            pltpu.SemaphoreType.DMA((len(operands),)),
        ],
        compiler_params=_params(16),
        name="pack",
    )(*[pltpu.with_memory_space_constraint(operand, pltpu.HBM) for operand in operands])

    def swap(value, axis, bit):
        size = lax.axis_size(axis)
        return lax.ppermute(value, axis, [(i, i ^ bit) for i in range(size)])

    def joined(pieces):
        return pieces[0] if len(pieces) == 1 else jnp.concatenate(pieces, axis=0)

    across = swap(part, "blk", half)
    near = swap(bank, "blk", 1)
    planes, order = [bank], [0]
    for n in range(half.bit_length() - 2, 0, -1):
        planes.append(swap(joined(planes), "blk", 1 << n))
        order += [offset ^ (1 << n) for offset in order]
    far, near = lax.optimization_barrier((joined(planes[1:]), near))
    last = swap(jnp.pad(far, ((0, 0), (0, 3 * 128))), "blk", 1)
    order = [0, 1] + order[1:] + [offset ^ 1 for offset in order[1:]]

    cos_part, sin_part, square = pl.pallas_call(
        table_kernel,
        out_shape=[
            vmem_out((shifts, wide), F32),
            vmem_out((shifts, wide), F32),
            vmem_out((2 * classes_count, wide), BF16),
        ],
        in_specs=[_vmem()] * 3,
        out_specs=[_vmem()] * 3,
        compiler_params=_params(8),
        cost_estimate=pl.CostEstimate(flops=4_000_000, bytes_accessed=2_000_000, transcendentals=0),
        name="tables",
    )(curves, noise, angle)

    def shifted_call(banks, name):
        total = sum(piece.shape[0] for piece in banks) // 2
        return pl.pallas_call(
            functools.partial(shift_kernel, n_proj),
            out_shape=[vmem_out((shifts * total, 2 * wide), BF16), vmem_out((2 * total, wide), BF16)],
            in_specs=[_vmem()] * (2 + len(banks)),
            out_specs=[_vmem()] * 2,
            compiler_params=_params(16),
            cost_estimate=pl.CostEstimate(
                flops=6 * total * shifts * wide, bytes_accessed=4_000_000, transcendentals=0
            ),
            name=name,
        )(cos_part, sin_part, *banks)

    own_rows, own_power = shifted_call([bank], "shift_own")

    across, own_power = lax.optimization_barrier((across, own_power))
    parts = [part, across]
    bits = [1 << n for n in range(ng.bit_length() - 2, -1, -1)]
    for bit in bits:
        part = lax.optimization_barrier(joined(parts))
        parts = [part, swap(part, "grp", bit)]

    rest_rows, rest_power = shifted_call([near, far], "shift_rest")
    count = 2 * ng * n_part
    late = half // 2 - 1
    slot = 128 * -(-(shifts + 1) * n_proj // 128)
    lanes = 128 * -(-(shifts + 1) * n_proj * half // 128)
    select, rows = pl.pallas_call(
        functools.partial(early_kernel, len(parts), (1, 2), n_proj, length, subsets),
        out_shape=[
            vmem_out((2 * count, wide), BF16),
            vmem_out((count, (half - late) * slot), F32),
        ],
        in_specs=[_vmem()] * (8 + len(parts)),
        out_specs=[_vmem()] * 2,
        compiler_params=_params(16),
        cost_estimate=pl.CostEstimate(
            flops=4 * count * (half - late) * n_proj * shifts * wide,
            bytes_accessed=4_000_000,
            transcendentals=0,
        ),
        name="early",
    )(square, *parts, own_rows, own_power, bank, rest_rows, rest_power, near, far)
    late_rows, give = pl.pallas_call(
        functools.partial(final_kernel, order, len(parts), bits, n_proj, length, subsets),
        out_shape=[vmem_out((count, late * slot), F32), vmem_out((ng * n_part, lanes), F32)],
        in_specs=[_vmem()] * (5 + len(parts)),
        out_specs=[_vmem()] * 2,
        compiler_params=_params(16),
        cost_estimate=pl.CostEstimate(
            flops=4 * count * late * n_proj * shifts * wide, bytes_accessed=4_000_000, transcendentals=0
        ),
        name="final",
    )(select, rows, cos_part, sin_part, last, *parts)
    recv = swap(give, "blk", half)
    keep = pl.pallas_call(
        functools.partial(keep_kernel, slot, n_proj, order, bits),
        out_shape=vmem_out((shifts, ng * n_part, nb * n_proj), F32),
        in_specs=[_vmem()] * 2,
        out_specs=_vmem(),
        compiler_params=_params(4),
        name="keep",
    )(rows, late_rows)
    scores = pl.pallas_call(
        functools.partial(place_kernel, half, n_proj),
        out_shape=shape((shifts, ng * n_part, nb * n_proj), F32),
        in_specs=[_vmem()] * 2,
        out_specs=_vmem(),
        compiler_params=_params(4),
        name="place",
    )(keep, recv)
    return scores.transpose(1, 0, 2)


def solution(mesh):
    placed = (
        P(("blk", "grp"), None, None),
        P(("blk", "grp")),
        P(("blk", "grp"), None),
        P(),
        P(),
        P(),
        P(),
        P(("grp", "blk"), None, None),
        P(("grp", "blk")),
    )
    return jax.shard_map(
        per_device, mesh=mesh, in_specs=placed, out_specs=P("blk", None, "grp"), check_vma=False
    )
```

```python
import functools

import jax
import jax.numpy as jnp
from jax import lax
from jax.experimental import pallas as pl
from jax.experimental.pallas import tpu as pltpu
from jax.sharding import PartitionSpec as P

F32 = jnp.float32
BF16 = jnp.bfloat16
HIGHEST = lax.Precision.HIGHEST
NT_DIMS = (((1,), (1,)), ((), ()))
MIB = 1 << 20


def _vmem():
    return pl.BlockSpec(memory_space=pltpu.VMEM)


def _params(mib):
    return pltpu.CompilerParams(vmem_limit_bytes=mib * MIB)


def pack_kernel(
    class_hbm,
    subset_hbm,
    particles_hbm,
    prior_hbm,
    curves_hbm,
    noise_hbm,
    proj_hbm,
    phase_hbm,
    trans_hbm,
    bank_ref,
    part_ref,
    curves_ref,
    noise_ref,
    angle_ref,
    class_ref,
    subset_ref,
    trans_ref,
    particles_ref,
    prior_ref,
    phase_ref,
    proj_ref,
    sems,
):
    n_proj = proj_hbm.shape[0]
    pairs = [
        (proj_hbm, proj_ref),
        (curves_hbm, curves_ref),
        (subset_hbm, subset_ref),
        (class_hbm, class_ref),
        (particles_hbm, particles_ref),
        (noise_hbm, noise_ref),
        (prior_hbm, prior_ref),
        (trans_hbm, trans_ref),
        (phase_hbm, phase_ref),
    ]
    copies = [pltpu.make_async_copy(a, b, sems.at[n]) for n, (a, b) in enumerate(pairs)]
    for copy in copies:
        copy.start()
    n_part = particles_ref.shape[0]
    length = proj_ref.shape[2]
    wide = bank_ref.shape[1]

    def padded(values, width):
        if values.shape[1] == width:
            return values
        zeros = jnp.zeros((values.shape[0], width - values.shape[1]), values.dtype)
        return jnp.concatenate([values, zeros], axis=1)

    row = lax.broadcasted_iota(jnp.int32, (n_proj, wide), 0)
    lane = lax.broadcasted_iota(jnp.int32, (n_proj, wide), 1)
    copies[0].wait()
    copies[2].wait()
    real = jnp.zeros((n_proj, wide), F32)
    imag = jnp.zeros((n_proj, wide), F32)
    for j in range(n_proj):
        both = padded(proj_ref[j].astype(F32), wide)
        real = jnp.where(row == j, both[0:1], real)
        imag = jnp.where(row == j, both[1:2], imag)
    start = length // 128 * 128
    last = slice(start, start + 128)
    ends = real[:, last]
    for j in range(n_proj):
        here = (row[:, last] == j) & (lane[:, last] == length)
        ends = jnp.where(here, subset_ref[j].astype(F32), ends)
    real = jnp.concatenate([real[:, :start], ends, real[:, start + 128 :]][: 3 if start + 128 < wide else 2], axis=1)
    bank_ref[...] = jnp.concatenate([real, imag], axis=0).astype(BF16)

    copies[1].wait()
    for copy in copies[3:]:
        copy.wait()
    subsets = prior_ref.shape[1]
    extra = part_ref.shape[1] - 2 * wide
    row = lax.broadcasted_iota(jnp.int32, (n_part, wide), 0)
    row_extra = lax.broadcasted_iota(jnp.int32, (n_part, extra), 0)
    real = jnp.zeros((n_part, wide), F32)
    imag = jnp.zeros((n_part, wide), F32)
    small = jnp.zeros((n_part, extra), F32)
    prior = prior_ref[...].astype(F32)
    middle = (subsets + 1) // 2
    for i in range(n_part):
        curve = curves_ref[pl.ds(class_ref[i], 1), :] * noise_ref[...]
        both = particles_ref[i].astype(F32) * curve
        first = padded(jnp.concatenate([both[0:1], prior[i : i + 1, :middle]], axis=1), wide)
        second = padded(jnp.concatenate([both[1:2], prior[i : i + 1, middle:]], axis=1), wide)
        real = jnp.where(row == i, first, real)
        imag = jnp.where(row == i, second, imag)
        small = jnp.where(row_extra == i, class_ref[i].astype(F32), small)
    part_ref[:, :wide] = real.astype(BF16)
    part_ref[:, wide : 2 * wide] = imag.astype(BF16)
    part_ref[:, 2 * wide :] = small.astype(BF16)
    for t in range(phase_ref.shape[0]):
        angle_ref[t : t + 1, :] = phase_ref[pl.ds(trans_ref[t], 1), :]


def sine_cosine(x):
    turns = jnp.floor(x * 0.6366197723675814 + 0.5)
    r = ((x - turns * 1.5703125) - turns * 4.837512969970703125e-4) - turns * 7.549789954891882e-8
    z = r * r
    sine = r + r * z * (-1.6666654611e-1 + z * (8.3321608736e-3 - z * 1.9515295891e-4))
    cosine = 1.0 - 0.5 * z + z * z * (
        4.166664568298827e-2 + z * (-1.388731625493765e-3 + z * 2.443315711809948e-5)
    )
    quarter = turns.astype(jnp.int32) & 3
    swapped = (quarter & 1) == 1
    first, second = jnp.where(swapped, cosine, sine), jnp.where(swapped, sine, cosine)
    first = jnp.where(quarter >= 2, -first, first)
    second = jnp.where((quarter == 1) | (quarter == 2), -second, second)
    return first, second


def split_terms(values):
    high = values.astype(BF16)
    low = (values - high.astype(F32)).astype(BF16)
    return jnp.concatenate([high, low], axis=0)


def table_kernel(curves_ref, noise_ref, angle_ref, cos_ref, sin_ref, square_ref):
    length = curves_ref.shape[1]
    wide = cos_ref.shape[1]
    zeros = jnp.zeros((cos_ref.shape[0], wide - length), F32)
    sine, cosine = sine_cosine(angle_ref[...])
    cos_ref[...] = jnp.concatenate([cosine, zeros], axis=1)
    sin_ref[...] = jnp.concatenate([sine, zeros], axis=1)
    curve = curves_ref[...]
    square = split_terms(curve * curve * noise_ref[...])
    square_ref[...] = jnp.concatenate(
        [square, jnp.zeros((square.shape[0], wide - length), BF16)], axis=1
    )


def added_rows(extra, norm, banks, n_proj, length, subsets):
    ids_at = length // 128 * 128
    ids = []
    for bank in banks:
        for first in range(0, bank.shape[0], 2 * n_proj):
            rows = bank[first : first + 2 * n_proj, ids_at : ids_at + 128].astype(F32)
            ids.append(rows[:n_proj])
    ids = jnp.concatenate(ids, axis=0)[:, length - ids_at : length - ids_at + 1]
    subset_col = lax.broadcasted_iota(jnp.int32, (ids.shape[0], subsets), 1).astype(F32)
    subset_hot = (subset_col == ids).astype(F32).astype(BF16)
    prior = lax.dot_general(
        extra[:, :subsets].astype(BF16), subset_hot, NT_DIMS, preferred_element_type=F32
    )
    return prior - 0.5 * norm


def bank_pieces(bank, span, n_proj):
    for first in range(0, bank.shape[0], 2 * n_proj):
        both = bank[first : first + 2 * n_proj, span].astype(F32)
        yield both[:n_proj], both[n_proj:]


def shifted_rows(real, imag, cos_ref, sin_ref, span):
    real_rows, imag_rows = [], []
    for t in range(cos_ref.shape[0]):
        cos_part, sin_part = cos_ref[t : t + 1, span], sin_ref[t : t + 1, span]
        real_rows.append(cos_part * real + sin_part * imag)
        imag_rows.append(cos_part * imag - sin_part * real)
    return (
        jnp.concatenate(real_rows, axis=0).astype(BF16),
        jnp.concatenate(imag_rows, axis=0).astype(BF16),
    )


def spans_of(wide):
    step = 256 if wide % 256 == 0 else 128
    return [slice(at, at + step) for at in range(0, wide, step)]


def shift_kernel(n_proj, cos_ref, sin_ref, *rest):
    *banks, shifted_ref, power_ref = rest
    shifts, wide = cos_ref.shape
    width = shifts * n_proj
    for span in spans_of(wide):
        powers, at = [], 0
        for bank in banks:
            for real, imag in bank_pieces(bank, span, n_proj):
                real_rows, imag_rows = shifted_rows(real, imag, cos_ref, sin_ref, span)
                shifted_ref[at : at + width, span] = real_rows
                shifted_ref[at : at + width, wide + span.start : wide + span.stop] = imag_rows
                powers.append(real * real + imag * imag)
                at += width
        power_ref[:, span] = split_terms(jnp.concatenate(powers, axis=0))


def multiply(left, right):
    return lax.dot_general(left, right, NT_DIMS, preferred_element_type=F32)


def added(total, terms):
    return terms if total is None else total + terms


def pieces_of(cross, norm, extra, banks, length, subsets, n_proj):
    count, total = cross.shape[0], norm.shape[1] // 2
    width = cross.shape[1] * n_proj // total
    norm = norm[:count, total:] + norm[count:, :total] + norm[:count, :total]
    offset = added_rows(extra, norm, banks, n_proj, length, subsets)
    pieces = []
    for n in range(total // n_proj):
        scores = cross[:, n * width : (n + 1) * width]
        pieces.append(jnp.concatenate([scores, offset[:, n * n_proj : (n + 1) * n_proj]], axis=1))
    return pieces


def store_pieces(out, pieces, first, slot, rows):
    for n, piece in enumerate(pieces):
        at = (first + n) * slot
        out[:, at : at + piece.shape[1]] = piece[rows]


def rows_of(parts, span):
    return jnp.concatenate([part[:, span] for part in parts], axis=0)


def extra_of(parts, wide, length, subsets):
    start, middle = length // 128 * 128, (subsets + 1) // 2
    at = length - start
    first = rows_of(parts, slice(start, wide)).astype(F32)[:, at : at + middle]
    second = rows_of(parts, slice(wide + start, 2 * wide)).astype(F32)[:, at : at + subsets - middle]
    return jnp.concatenate([first, second, rows_of(parts, slice(2 * wide, None)).astype(F32)], axis=1)


def early_kernel(n_parts, n_banks, n_proj, length, subsets, square_ref, *rest):
    parts, rest = rest[:n_parts], rest[n_parts:]
    groups, (select_ref, rows_ref) = [], rest[-2:]
    for n in n_banks:
        groups.append((rest[0], rest[1], rest[2 : 2 + n]))
        rest = rest[2 + n :]
    wide = select_ref.shape[1]
    classes_count = square_ref.shape[0] // 2
    extra = extra_of(parts, wide, length, subsets)
    count = extra.shape[0]
    class_col = lax.broadcasted_iota(jnp.int32, (count, classes_count), 1).astype(F32)
    onehot = (class_col == extra[:, subsets : subsets + 1]).astype(F32).astype(BF16)
    for n in range(2):
        squares = square_ref[n * classes_count : (n + 1) * classes_count, :]
        chosen = jnp.dot(onehot, squares, preferred_element_type=F32)
        select_ref[n * count : (n + 1) * count, :] = chosen.astype(BF16)

    pieces = []
    for shifted_ref, power_ref, banks in groups:
        cross, turned = None, None
        for at in range(0, wide, 512):
            span = slice(at, min(at + 512, wide))
            other = slice(wide + span.start, wide + span.stop)
            cross = added(cross, multiply(rows_of(parts, span), shifted_ref[:, span]))
            turned = added(turned, multiply(shifted_ref[:, other], rows_of(parts, other)))
        norm = multiply(select_ref[...], power_ref[...])
        pieces += pieces_of(cross + turned.T, norm, extra, banks, length, subsets, n_proj)
    store_pieces(rows_ref, pieces, 0, rows_ref.shape[1] // len(pieces), slice(None))


def final_kernel(
    order, n_parts, bits, n_proj, length, subsets, select_ref, rows_ref, cos_ref, sin_ref, last_ref, *rest
):
    parts, (late_ref, give_ref) = rest[:n_parts], rest[n_parts:]
    shifts, wide = cos_ref.shape
    cross, norm = None, None
    for span in spans_of(wide):
        terms, powers = [], []
        for real, imag in bank_pieces(last_ref, span, n_proj):
            real_rows, imag_rows = shifted_rows(real, imag, cos_ref, sin_ref, span)
            other = slice(wide + span.start, wide + span.stop)
            terms.append(
                multiply(rows_of(parts, span), real_rows) + multiply(rows_of(parts, other), imag_rows)
            )
            powers.append(real * real + imag * imag)
        cross = added(cross, jnp.concatenate(terms, axis=1))
        power = split_terms(jnp.concatenate(powers, axis=0))
        norm = added(norm, multiply(select_ref[:, span], power))
    extra = extra_of(parts, wide, length, subsets)
    pieces = pieces_of(cross, norm, extra, [last_ref], length, subsets, n_proj)
    slot = late_ref.shape[1] // len(pieces)
    zeros = jnp.zeros((extra.shape[0], slot - pieces[0].shape[1]), F32)
    late = [jnp.concatenate([piece, zeros], axis=1) for piece in pieces]
    late_ref[...] = jnp.concatenate(late, axis=1)
    dest, lanes = give_ref.shape
    width = pieces[0].shape[1]
    rows = [in_rows(values, 1, bits, dest) for values in slots_of(rows_ref, slot) + late]
    rows = [values[:, :width] for values in in_order(rows, order)]
    if lanes > len(rows) * width:
        rows.append(jnp.zeros((dest, lanes - len(rows) * width), F32))
    give_ref[...] = jnp.concatenate(rows, axis=1)


def slots_of(rows_ref, slot):
    return [rows_ref[:, at : at + slot] for at in range(0, rows_ref.shape[1], slot)]


def in_rows(values, d, bits, dest):
    ng = 1 << len(bits)
    n_part = dest // ng
    g = lax.axis_index("grp")
    row = lax.broadcasted_iota(jnp.int32, (dest, values.shape[1]), 0)
    found = []
    for away in range(ng):
        source = d
        for n, bit in enumerate(bits):
            source += (2 << n) if away & bit else 0
        found.append(values[source * n_part : (source + 1) * n_part])
    values = jnp.concatenate(found, axis=0)
    for bit in bits:
        step = bit * n_part
        other = jnp.where(
            (row & step) != 0, pltpu.roll(values, step, 0), pltpu.roll(values, dest - step, 0)
        )
        values = jnp.where((g & bit) != 0, other, values)
    return values


def in_order(pieces, order):
    blk = lax.axis_index("blk")
    found = [pieces[order.index(n)] for n in range(len(order))]
    bit = 1
    while bit < len(order):
        swapped = (blk & bit) != 0
        found = [jnp.where(swapped, found[n ^ bit], found[n]) for n in range(len(order))]
        bit *= 2
    return found


def by_shift(pieces, n_proj, shifts):
    def line(t):
        one = [piece[:, t * n_proj : (t + 1) * n_proj] for piece in pieces]
        return jnp.concatenate(one + one, axis=1)

    offset = line(shifts)
    return [line(t) + offset for t in range(shifts)]


def keep_kernel(slot, n_proj, order, bits, rows_ref, late_ref, out_ref):
    shifts, dest, _ = out_ref.shape
    pieces = [in_rows(values, 0, bits, dest) for values in slots_of(rows_ref, slot) + slots_of(late_ref, slot)]
    for t, line in enumerate(by_shift(in_order(pieces, order), n_proj, shifts)):
        out_ref[t] = line


def place_kernel(half, n_proj, keep_ref, recv_ref, out_ref):
    shifts, dest, total = out_ref.shape
    width = (shifts + 1) * n_proj
    lower = lax.broadcasted_iota(jnp.int32, (dest, total), 1) < total // 2
    own = lower == (lax.axis_index("blk") < half)
    pieces = [recv_ref[:, n * width : (n + 1) * width] for n in range(half)]
    for t, line in enumerate(by_shift(pieces, n_proj, shifts)):
        out_ref[t] = jnp.where(own, keep_ref[t], line)


def per_device(
    particles,
    ctf_class,
    orient_prior,
    ctf_curves,
    noise_weight,
    shift_phase,
    trans_index,
    projections,
    orient_subset,
):
    nb, ng = lax.axis_size("blk"), lax.axis_size("grp")
    half = nb // 2
    n_part, n_proj = particles.shape[0], projections.shape[0]
    length = particles.shape[2]
    shifts = shift_phase.shape[0]
    classes_count = ctf_curves.shape[0]
    subsets = orient_prior.shape[1]
    wide = 128 * -(-(length + (subsets + 1) // 2) // 128)
    extra = 128
    noise = noise_weight.reshape(1, length)
    shape = jax.ShapeDtypeStruct

    def vmem_out(dims, dtype):
        return pltpu.VMEM(dims, dtype)

    operands = (
        ctf_class,
        orient_subset,
        particles,
        orient_prior,
        ctf_curves,
        noise,
        projections,
        shift_phase,
        trans_index,
    )
    bank, part, curves, noise, angle = pl.pallas_call(
        pack_kernel,
        out_shape=[
            vmem_out((2 * n_proj, wide), BF16),
            vmem_out((n_part, 2 * wide + extra), BF16),
            vmem_out(ctf_curves.shape, F32),
            vmem_out(noise.shape, F32),
            vmem_out(shift_phase.shape, F32),
        ],
        in_specs=[pl.BlockSpec(memory_space=pltpu.HBM)] * len(operands),
        out_specs=[_vmem()] * 5,
        scratch_shapes=[
            pltpu.SMEM(ctf_class.shape, jnp.int32),
            pltpu.SMEM(orient_subset.shape, jnp.int32),
            pltpu.SMEM(trans_index.shape, jnp.int32),
            pltpu.VMEM(particles.shape, BF16),
            pltpu.VMEM(orient_prior.shape, BF16),
            pltpu.VMEM(shift_phase.shape, F32),
            pltpu.VMEM(projections.shape, BF16),
            pltpu.SemaphoreType.DMA((len(operands),)),
        ],
        compiler_params=_params(16),
        name="pack",
    )(*[pltpu.with_memory_space_constraint(operand, pltpu.HBM) for operand in operands])

    def swap(value, axis, bit):
        size = lax.axis_size(axis)
        return lax.ppermute(value, axis, [(i, i ^ bit) for i in range(size)])

    def joined(pieces):
        return pieces[0] if len(pieces) == 1 else jnp.concatenate(pieces, axis=0)

    across = swap(part, "blk", half)
    near = swap(bank, "blk", 1)
    planes, order = [bank], [0]
    for n in range(half.bit_length() - 2, 0, -1):
        planes.append(swap(joined(planes), "blk", 1 << n))
        order += [offset ^ (1 << n) for offset in order]
    far, near = lax.optimization_barrier((joined(planes[1:]), near))
    last = swap(jnp.pad(far, ((0, 0), (0, 2 * 128))), "blk", 1)
    order = [0, 1] + order[1:] + [offset ^ 1 for offset in order[1:]]

    cos_part, sin_part, square = pl.pallas_call(
        table_kernel,
        out_shape=[
            vmem_out((shifts, wide), F32),
            vmem_out((shifts, wide), F32),
            vmem_out((2 * classes_count, wide), BF16),
        ],
        in_specs=[_vmem()] * 3,
        out_specs=[_vmem()] * 3,
        compiler_params=_params(8),
        cost_estimate=pl.CostEstimate(flops=4_000_000, bytes_accessed=2_000_000, transcendentals=0),
        name="tables",
    )(curves, noise, angle)

    def shifted_call(banks, name):
        total = sum(piece.shape[0] for piece in banks) // 2
        return pl.pallas_call(
            functools.partial(shift_kernel, n_proj),
            out_shape=[vmem_out((shifts * total, 2 * wide), BF16), vmem_out((2 * total, wide), BF16)],
            in_specs=[_vmem()] * (2 + len(banks)),
            out_specs=[_vmem()] * 2,
            compiler_params=_params(16),
            cost_estimate=pl.CostEstimate(
                flops=6 * total * shifts * wide, bytes_accessed=4_000_000, transcendentals=0
            ),
            name=name,
        )(cos_part, sin_part, *banks)

    own_rows, own_power = shifted_call([bank], "shift_own")

    across, own_power = lax.optimization_barrier((across, own_power))
    parts = [part, across]
    bits = [1 << n for n in range(ng.bit_length() - 2, -1, -1)]
    for bit in bits:
        part = lax.optimization_barrier(joined(parts))
        parts = [part, swap(part, "grp", bit)]

    rest_rows, rest_power = shifted_call([near, far], "shift_rest")
    count = 2 * ng * n_part
    late = half // 2 - 1
    slot = 128 * -(-(shifts + 1) * n_proj // 128)
    lanes = 128 * -(-(shifts + 1) * n_proj * half // 128)
    select, rows = pl.pallas_call(
        functools.partial(early_kernel, len(parts), (1, 2), n_proj, length, subsets),
        out_shape=[
            vmem_out((2 * count, wide), BF16),
            vmem_out((count, (half - late) * slot), F32),
        ],
        in_specs=[_vmem()] * (8 + len(parts)),
        out_specs=[_vmem()] * 2,
        compiler_params=_params(16),
        cost_estimate=pl.CostEstimate(
            flops=4 * count * (half - late) * n_proj * shifts * wide,
            bytes_accessed=4_000_000,
            transcendentals=0,
        ),
        name="early",
    )(square, *parts, own_rows, own_power, bank, rest_rows, rest_power, near, far)
    late_rows, give = pl.pallas_call(
        functools.partial(final_kernel, order, len(parts), bits, n_proj, length, subsets),
        out_shape=[vmem_out((count, late * slot), F32), vmem_out((ng * n_part, lanes), F32)],
        in_specs=[_vmem()] * (5 + len(parts)),
        out_specs=[_vmem()] * 2,
        compiler_params=_params(16),
        cost_estimate=pl.CostEstimate(
            flops=4 * count * late * n_proj * shifts * wide, bytes_accessed=4_000_000, transcendentals=0
        ),
        name="final",
    )(select, rows, cos_part, sin_part, last, *parts)
    recv = swap(give, "blk", half)
    keep = pl.pallas_call(
        functools.partial(keep_kernel, slot, n_proj, order, bits),
        out_shape=vmem_out((shifts, ng * n_part, nb * n_proj), F32),
        in_specs=[_vmem()] * 2,
        out_specs=_vmem(),
        compiler_params=_params(4),
        name="keep",
    )(rows, late_rows)
    scores = pl.pallas_call(
        functools.partial(place_kernel, half, n_proj),
        out_shape=shape((shifts, ng * n_part, nb * n_proj), F32),
        in_specs=[_vmem()] * 2,
        out_specs=_vmem(),
        compiler_params=_params(4),
        name="place",
    )(keep, recv)
    return scores.transpose(1, 0, 2)


def solution(mesh):
    placed = (
        P(("blk", "grp"), None, None),
        P(("blk", "grp")),
        P(("blk", "grp"), None),
        P(),
        P(),
        P(),
        P(),
        P(("grp", "blk"), None, None),
        P(("grp", "blk")),
    )
    return jax.shard_map(
        per_device, mesh=mesh, in_specs=placed, out_specs=P("blk", None, "grp"), check_vma=False
    )
```

```python
import functools

import jax
import jax.numpy as jnp
from jax import lax
from jax.experimental import pallas as pl
from jax.experimental.pallas import tpu as pltpu
from jax.sharding import PartitionSpec as P

F32 = jnp.float32
BF16 = jnp.bfloat16
HIGHEST = lax.Precision.HIGHEST
NT_DIMS = (((1,), (1,)), ((), ()))
MIB = 1 << 20


def _vmem():
    return pl.BlockSpec(memory_space=pltpu.VMEM)


def _params(mib):
    return pltpu.CompilerParams(vmem_limit_bytes=mib * MIB)


def pack_kernel(
    class_hbm,
    subset_hbm,
    particles_hbm,
    prior_hbm,
    curves_hbm,
    noise_hbm,
    proj_hbm,
    phase_hbm,
    trans_hbm,
    bank_ref,
    part_ref,
    curves_ref,
    noise_ref,
    angle_ref,
    class_ref,
    subset_ref,
    trans_ref,
    particles_ref,
    prior_ref,
    phase_ref,
    proj_ref,
    sems,
):
    n_proj = proj_hbm.shape[0]
    pairs = [
        (proj_hbm, proj_ref),
        (curves_hbm, curves_ref),
        (subset_hbm, subset_ref),
        (class_hbm, class_ref),
        (particles_hbm, particles_ref),
        (noise_hbm, noise_ref),
        (prior_hbm, prior_ref),
        (trans_hbm, trans_ref),
        (phase_hbm, phase_ref),
    ]
    copies = [pltpu.make_async_copy(a, b, sems.at[n]) for n, (a, b) in enumerate(pairs)]
    for copy in copies:
        copy.start()
    n_part = particles_ref.shape[0]
    length = proj_ref.shape[2]
    wide = bank_ref.shape[1]

    def padded(values, width):
        if values.shape[1] == width:
            return values
        zeros = jnp.zeros((values.shape[0], width - values.shape[1]), values.dtype)
        return jnp.concatenate([values, zeros], axis=1)

    row = lax.broadcasted_iota(jnp.int32, (n_proj, wide), 0)
    lane = lax.broadcasted_iota(jnp.int32, (n_proj, wide), 1)
    copies[0].wait()
    copies[2].wait()
    real = jnp.zeros((n_proj, wide), F32)
    imag = jnp.zeros((n_proj, wide), F32)
    for j in range(n_proj):
        both = padded(proj_ref[j].astype(F32), wide)
        real = jnp.where(row == j, both[0:1], real)
        imag = jnp.where(row == j, both[1:2], imag)
    start = length // 128 * 128
    last = slice(start, start + 128)
    ends = real[:, last]
    for j in range(n_proj):
        here = (row[:, last] == j) & (lane[:, last] == length)
        ends = jnp.where(here, subset_ref[j].astype(F32), ends)
    real = jnp.concatenate([real[:, :start], ends, real[:, start + 128 :]][: 3 if start + 128 < wide else 2], axis=1)
    bank_ref[...] = jnp.concatenate([real, imag], axis=0).astype(BF16)

    copies[1].wait()
    for copy in copies[3:]:
        copy.wait()
    subsets = prior_ref.shape[1]
    extra = part_ref.shape[1] - 2 * wide
    row = lax.broadcasted_iota(jnp.int32, (n_part, wide), 0)
    row_extra = lax.broadcasted_iota(jnp.int32, (n_part, extra), 0)
    real = jnp.zeros((n_part, wide), F32)
    imag = jnp.zeros((n_part, wide), F32)
    small = jnp.zeros((n_part, extra), F32)
    prior = prior_ref[...].astype(F32)
    middle = (subsets + 1) // 2
    for i in range(n_part):
        curve = curves_ref[pl.ds(class_ref[i], 1), :] * noise_ref[...]
        both = particles_ref[i].astype(F32) * curve
        first = padded(jnp.concatenate([both[0:1], prior[i : i + 1, :middle]], axis=1), wide)
        second = padded(jnp.concatenate([both[1:2], prior[i : i + 1, middle:]], axis=1), wide)
        real = jnp.where(row == i, first, real)
        imag = jnp.where(row == i, second, imag)
        small = jnp.where(row_extra == i, class_ref[i].astype(F32), small)
    part_ref[:, :wide] = real.astype(BF16)
    part_ref[:, wide : 2 * wide] = imag.astype(BF16)
    part_ref[:, 2 * wide :] = small.astype(BF16)
    for t in range(phase_ref.shape[0]):
        angle_ref[t : t + 1, :] = phase_ref[pl.ds(trans_ref[t], 1), :]


def sine_cosine(x):
    turns = jnp.floor(x * 0.6366197723675814 + 0.5)
    r = ((x - turns * 1.5703125) - turns * 4.837512969970703125e-4) - turns * 7.549789954891882e-8
    z = r * r
    sine = r + r * z * (-1.6666654611e-1 + z * (8.3321608736e-3 - z * 1.9515295891e-4))
    cosine = 1.0 - 0.5 * z + z * z * (
        4.166664568298827e-2 + z * (-1.388731625493765e-3 + z * 2.443315711809948e-5)
    )
    quarter = turns.astype(jnp.int32) & 3
    swapped = (quarter & 1) == 1
    first, second = jnp.where(swapped, cosine, sine), jnp.where(swapped, sine, cosine)
    first = jnp.where(quarter >= 2, -first, first)
    second = jnp.where((quarter == 1) | (quarter == 2), -second, second)
    return first, second


def split_terms(values):
    high = values.astype(BF16)
    low = (values - high.astype(F32)).astype(BF16)
    return jnp.concatenate([high, low], axis=0)


def table_kernel(curves_ref, noise_ref, angle_ref, cos_ref, sin_ref, square_ref):
    length = curves_ref.shape[1]
    wide = cos_ref.shape[1]
    zeros = jnp.zeros((cos_ref.shape[0], wide - length), F32)
    sine, cosine = sine_cosine(angle_ref[...])
    cos_ref[...] = jnp.concatenate([cosine, zeros], axis=1)
    sin_ref[...] = jnp.concatenate([sine, zeros], axis=1)
    curve = curves_ref[...]
    square = split_terms(curve * curve * noise_ref[...])
    square_ref[...] = jnp.concatenate(
        [square, jnp.zeros((square.shape[0], wide - length), BF16)], axis=1
    )


def added_rows(extra, norm, banks, n_proj, length, subsets):
    ids_at = length // 128 * 128
    ids = []
    for bank in banks:
        for first in range(0, bank.shape[0], 2 * n_proj):
            rows = bank[first : first + 2 * n_proj, ids_at : ids_at + 128].astype(F32)
            ids.append(rows[:n_proj])
    ids = jnp.concatenate(ids, axis=0)[:, length - ids_at : length - ids_at + 1]
    subset_col = lax.broadcasted_iota(jnp.int32, (ids.shape[0], subsets), 1).astype(F32)
    subset_hot = (subset_col == ids).astype(F32).astype(BF16)
    prior = lax.dot_general(
        extra[:, :subsets].astype(BF16), subset_hot, NT_DIMS, preferred_element_type=F32
    )
    return prior - 0.5 * norm


def bank_pieces(bank, span, n_proj):
    for first in range(0, bank.shape[0], 2 * n_proj):
        both = bank[first : first + 2 * n_proj, span].astype(F32)
        yield both[:n_proj], both[n_proj:]


def shifted_rows(real, imag, cos_ref, sin_ref, span):
    real_rows, imag_rows = [], []
    for t in range(cos_ref.shape[0]):
        cos_part, sin_part = cos_ref[t : t + 1, span], sin_ref[t : t + 1, span]
        real_rows.append(cos_part * real + sin_part * imag)
        imag_rows.append(cos_part * imag - sin_part * real)
    return (
        jnp.concatenate(real_rows, axis=0).astype(BF16),
        jnp.concatenate(imag_rows, axis=0).astype(BF16),
    )


def spans_of(wide):
    step = 256 if wide % 256 == 0 else 128
    return [slice(at, at + step) for at in range(0, wide, step)]


def shift_kernel(n_proj, cos_ref, sin_ref, *rest):
    *banks, shifted_ref, power_ref = rest
    shifts, wide = cos_ref.shape
    width = shifts * n_proj
    for span in spans_of(wide):
        powers, at = [], 0
        for bank in banks:
            for real, imag in bank_pieces(bank, span, n_proj):
                real_rows, imag_rows = shifted_rows(real, imag, cos_ref, sin_ref, span)
                shifted_ref[at : at + width, span] = real_rows
                shifted_ref[at : at + width, wide + span.start : wide + span.stop] = imag_rows
                powers.append(real * real + imag * imag)
                at += width
        power_ref[:, span] = split_terms(jnp.concatenate(powers, axis=0))


def multiply(left, right):
    return lax.dot_general(left, right, NT_DIMS, preferred_element_type=F32)


def added(total, terms):
    return terms if total is None else total + terms


def pieces_of(cross, norm, extra, banks, length, subsets, n_proj):
    count, total = cross.shape[0], norm.shape[1] // 2
    width = cross.shape[1] * n_proj // total
    norm = norm[:count, total:] + norm[count:, :total] + norm[:count, :total]
    offset = added_rows(extra, norm, banks, n_proj, length, subsets)
    pieces = []
    for n in range(total // n_proj):
        scores = cross[:, n * width : (n + 1) * width]
        pieces.append(jnp.concatenate([scores, offset[:, n * n_proj : (n + 1) * n_proj]], axis=1))
    return pieces


def store_pieces(out, pieces, first, slot, rows):
    for n, piece in enumerate(pieces):
        at = (first + n) * slot
        out[:, at : at + piece.shape[1]] = piece[rows]


def rows_of(parts, span):
    return jnp.concatenate([part[:, span] for part in parts], axis=0)


def extra_of(parts, wide, length, subsets):
    start, middle = length // 128 * 128, (subsets + 1) // 2
    at = length - start
    first = rows_of(parts, slice(start, wide)).astype(F32)[:, at : at + middle]
    second = rows_of(parts, slice(wide + start, 2 * wide)).astype(F32)[:, at : at + subsets - middle]
    return jnp.concatenate([first, second, rows_of(parts, slice(2 * wide, None)).astype(F32)], axis=1)


def early_kernel(n_parts, n_banks, n_proj, length, subsets, square_ref, *rest):
    parts, rest = rest[:n_parts], rest[n_parts:]
    groups, (select_ref, rows_ref) = [], rest[-2:]
    for n in n_banks:
        groups.append((rest[0], rest[1], rest[2 : 2 + n]))
        rest = rest[2 + n :]
    wide = select_ref.shape[1]
    classes_count = square_ref.shape[0] // 2
    extra = extra_of(parts, wide, length, subsets)
    count = extra.shape[0]
    class_col = lax.broadcasted_iota(jnp.int32, (count, classes_count), 1).astype(F32)
    onehot = (class_col == extra[:, subsets : subsets + 1]).astype(F32).astype(BF16)
    for n in range(2):
        squares = square_ref[n * classes_count : (n + 1) * classes_count, :]
        chosen = jnp.dot(onehot, squares, preferred_element_type=F32)
        select_ref[n * count : (n + 1) * count, :] = chosen.astype(BF16)

    pieces = []
    for shifted_ref, power_ref, banks in groups:
        cross, turned = None, None
        for at in range(0, wide, 1024):
            span = slice(at, min(at + 1024, wide))
            other = slice(wide + span.start, wide + span.stop)
            cross = added(cross, multiply(rows_of(parts, span), shifted_ref[:, span]))
            turned = added(turned, multiply(shifted_ref[:, other], rows_of(parts, other)))
        norm = multiply(select_ref[...], power_ref[...])
        pieces += pieces_of(cross + turned.T, norm, extra, banks, length, subsets, n_proj)
    store_pieces(rows_ref, pieces, 0, rows_ref.shape[1] // len(pieces), slice(None))


def final_kernel(
    order, n_parts, bits, n_proj, length, subsets, select_ref, rows_ref, cos_ref, sin_ref, last_ref, *rest
):
    parts, (late_ref, give_ref) = rest[:n_parts], rest[n_parts:]
    shifts, wide = cos_ref.shape
    cross, norm = None, None
    for span in spans_of(wide):
        terms, powers = [], []
        for real, imag in bank_pieces(last_ref, span, n_proj):
            real_rows, imag_rows = shifted_rows(real, imag, cos_ref, sin_ref, span)
            other = slice(wide + span.start, wide + span.stop)
            terms.append(
                multiply(rows_of(parts, span), real_rows) + multiply(rows_of(parts, other), imag_rows)
            )
            powers.append(real * real + imag * imag)
        cross = added(cross, jnp.concatenate(terms, axis=1))
        power = split_terms(jnp.concatenate(powers, axis=0))
        norm = added(norm, multiply(select_ref[:, span], power))
    extra = extra_of(parts, wide, length, subsets)
    pieces = pieces_of(cross, norm, extra, [last_ref], length, subsets, n_proj)
    slot = late_ref.shape[1] // len(pieces)
    zeros = jnp.zeros((extra.shape[0], slot - pieces[0].shape[1]), F32)
    late = [jnp.concatenate([piece, zeros], axis=1) for piece in pieces]
    late_ref[...] = jnp.concatenate(late, axis=1)
    dest, lanes = give_ref.shape
    width = pieces[0].shape[1]
    rows = [in_rows(values, 1, bits, dest) for values in slots_of(rows_ref, slot) + late]
    rows = [values[:, :width] for values in in_order(rows, order)]
    if lanes > len(rows) * width:
        rows.append(jnp.zeros((dest, lanes - len(rows) * width), F32))
    give_ref[...] = jnp.concatenate(rows, axis=1)


def slots_of(rows_ref, slot):
    return [rows_ref[:, at : at + slot] for at in range(0, rows_ref.shape[1], slot)]


def in_rows(values, d, bits, dest):
    ng = 1 << len(bits)
    n_part = dest // ng
    g = lax.axis_index("grp")
    row = lax.broadcasted_iota(jnp.int32, (dest, values.shape[1]), 0)
    found = []
    for away in range(ng):
        source = d
        for n, bit in enumerate(bits):
            source += (2 << n) if away & bit else 0
        found.append(values[source * n_part : (source + 1) * n_part])
    values = jnp.concatenate(found, axis=0)
    for bit in bits:
        step = bit * n_part
        other = jnp.where(
            (row & step) != 0, pltpu.roll(values, step, 0), pltpu.roll(values, dest - step, 0)
        )
        values = jnp.where((g & bit) != 0, other, values)
    return values


def in_order(pieces, order):
    blk = lax.axis_index("blk")
    found = [pieces[order.index(n)] for n in range(len(order))]
    bit = 1
    while bit < len(order):
        swapped = (blk & bit) != 0
        found = [jnp.where(swapped, found[n ^ bit], found[n]) for n in range(len(order))]
        bit *= 2
    return found


def by_shift(pieces, n_proj, shifts):
    def line(t):
        one = [piece[:, t * n_proj : (t + 1) * n_proj] for piece in pieces]
        return jnp.concatenate(one + one, axis=1)

    offset = line(shifts)
    return [line(t) + offset for t in range(shifts)]


def keep_kernel(slot, n_proj, order, bits, rows_ref, late_ref, out_ref):
    shifts, dest, _ = out_ref.shape
    pieces = [in_rows(values, 0, bits, dest) for values in slots_of(rows_ref, slot) + slots_of(late_ref, slot)]
    for t, line in enumerate(by_shift(in_order(pieces, order), n_proj, shifts)):
        out_ref[t] = line


def place_kernel(half, n_proj, keep_ref, recv_ref, out_ref):
    shifts, dest, total = out_ref.shape
    width = (shifts + 1) * n_proj
    lower = lax.broadcasted_iota(jnp.int32, (dest, total), 1) < total // 2
    own = lower == (lax.axis_index("blk") < half)
    pieces = [recv_ref[:, n * width : (n + 1) * width] for n in range(half)]
    for t, line in enumerate(by_shift(pieces, n_proj, shifts)):
        out_ref[t] = jnp.where(own, keep_ref[t], line)


def per_device(
    particles,
    ctf_class,
    orient_prior,
    ctf_curves,
    noise_weight,
    shift_phase,
    trans_index,
    projections,
    orient_subset,
):
    nb, ng = lax.axis_size("blk"), lax.axis_size("grp")
    half = nb // 2
    n_part, n_proj = particles.shape[0], projections.shape[0]
    length = particles.shape[2]
    shifts = shift_phase.shape[0]
    classes_count = ctf_curves.shape[0]
    subsets = orient_prior.shape[1]
    wide = 128 * -(-(length + (subsets + 1) // 2) // 128)
    extra = 128
    noise = noise_weight.reshape(1, length)
    shape = jax.ShapeDtypeStruct

    def vmem_out(dims, dtype):
        return pltpu.VMEM(dims, dtype)

    operands = (
        ctf_class,
        orient_subset,
        particles,
        orient_prior,
        ctf_curves,
        noise,
        projections,
        shift_phase,
        trans_index,
    )
    bank, part, curves, noise, angle = pl.pallas_call(
        pack_kernel,
        out_shape=[
            vmem_out((2 * n_proj, wide), BF16),
            vmem_out((n_part, 2 * wide + extra), BF16),
            vmem_out(ctf_curves.shape, F32),
            vmem_out(noise.shape, F32),
            vmem_out(shift_phase.shape, F32),
        ],
        in_specs=[pl.BlockSpec(memory_space=pltpu.HBM)] * len(operands),
        out_specs=[_vmem()] * 5,
        scratch_shapes=[
            pltpu.SMEM(ctf_class.shape, jnp.int32),
            pltpu.SMEM(orient_subset.shape, jnp.int32),
            pltpu.SMEM(trans_index.shape, jnp.int32),
            pltpu.VMEM(particles.shape, BF16),
            pltpu.VMEM(orient_prior.shape, BF16),
            pltpu.VMEM(shift_phase.shape, F32),
            pltpu.VMEM(projections.shape, BF16),
            pltpu.SemaphoreType.DMA((len(operands),)),
        ],
        compiler_params=_params(16),
        name="pack",
    )(*[pltpu.with_memory_space_constraint(operand, pltpu.HBM) for operand in operands])

    def swap(value, axis, bit):
        size = lax.axis_size(axis)
        return lax.ppermute(value, axis, [(i, i ^ bit) for i in range(size)])

    def joined(pieces):
        return pieces[0] if len(pieces) == 1 else jnp.concatenate(pieces, axis=0)

    across = swap(part, "blk", half)
    near = swap(bank, "blk", 1)
    planes, order = [bank], [0]
    for n in range(half.bit_length() - 2, 0, -1):
        planes.append(swap(joined(planes), "blk", 1 << n))
        order += [offset ^ (1 << n) for offset in order]
    far, near = lax.optimization_barrier((joined(planes[1:]), near))
    last = swap(jnp.pad(far, ((0, 0), (0, 2 * 128))), "blk", 1)
    order = [0, 1] + order[1:] + [offset ^ 1 for offset in order[1:]]

    cos_part, sin_part, square = pl.pallas_call(
        table_kernel,
        out_shape=[
            vmem_out((shifts, wide), F32),
            vmem_out((shifts, wide), F32),
            vmem_out((2 * classes_count, wide), BF16),
        ],
        in_specs=[_vmem()] * 3,
        out_specs=[_vmem()] * 3,
        compiler_params=_params(8),
        cost_estimate=pl.CostEstimate(flops=4_000_000, bytes_accessed=2_000_000, transcendentals=0),
        name="tables",
    )(curves, noise, angle)

    def shifted_call(banks, name):
        total = sum(piece.shape[0] for piece in banks) // 2
        return pl.pallas_call(
            functools.partial(shift_kernel, n_proj),
            out_shape=[vmem_out((shifts * total, 2 * wide), BF16), vmem_out((2 * total, wide), BF16)],
            in_specs=[_vmem()] * (2 + len(banks)),
            out_specs=[_vmem()] * 2,
            compiler_params=_params(16),
            cost_estimate=pl.CostEstimate(
                flops=6 * total * shifts * wide, bytes_accessed=4_000_000, transcendentals=0
            ),
            name=name,
        )(cos_part, sin_part, *banks)

    own_rows, own_power = shifted_call([bank], "shift_own")

    across, own_power = lax.optimization_barrier((across, own_power))
    parts = [part, across]
    bits = [1 << n for n in range(ng.bit_length() - 2, -1, -1)]
    for bit in bits:
        part = lax.optimization_barrier(joined(parts))
        parts = [part, swap(part, "grp", bit)]

    rest_rows, rest_power = shifted_call([near, far], "shift_rest")
    count = 2 * ng * n_part
    late = half // 2 - 1
    slot = 128 * -(-(shifts + 1) * n_proj // 128)
    lanes = 128 * -(-(shifts + 1) * n_proj * half // 128)
    select, rows = pl.pallas_call(
        functools.partial(early_kernel, len(parts), (1, 2), n_proj, length, subsets),
        out_shape=[
            vmem_out((2 * count, wide), BF16),
            vmem_out((count, (half - late) * slot), F32),
        ],
        in_specs=[_vmem()] * (8 + len(parts)),
        out_specs=[_vmem()] * 2,
        compiler_params=_params(16),
        cost_estimate=pl.CostEstimate(
            flops=4 * count * (half - late) * n_proj * shifts * wide,
            bytes_accessed=4_000_000,
            transcendentals=0,
        ),
        name="early",
    )(square, *parts, own_rows, own_power, bank, rest_rows, rest_power, near, far)
    late_rows, give = pl.pallas_call(
        functools.partial(final_kernel, order, len(parts), bits, n_proj, length, subsets),
        out_shape=[vmem_out((count, late * slot), F32), vmem_out((ng * n_part, lanes), F32)],
        in_specs=[_vmem()] * (5 + len(parts)),
        out_specs=[_vmem()] * 2,
        compiler_params=_params(16),
        cost_estimate=pl.CostEstimate(
            flops=4 * count * late * n_proj * shifts * wide, bytes_accessed=4_000_000, transcendentals=0
        ),
        name="final",
    )(select, rows, cos_part, sin_part, last, *parts)
    recv = swap(give, "blk", half)
    keep = pl.pallas_call(
        functools.partial(keep_kernel, slot, n_proj, order, bits),
        out_shape=vmem_out((shifts, ng * n_part, nb * n_proj), F32),
        in_specs=[_vmem()] * 2,
        out_specs=_vmem(),
        compiler_params=_params(4),
        name="keep",
    )(rows, late_rows)
    scores = pl.pallas_call(
        functools.partial(place_kernel, half, n_proj),
        out_shape=shape((shifts, ng * n_part, nb * n_proj), F32),
        in_specs=[_vmem()] * 2,
        out_specs=_vmem(),
        compiler_params=_params(4),
        name="place",
    )(keep, recv)
    return scores.transpose(1, 0, 2)


def solution(mesh):
    placed = (
        P(("blk", "grp"), None, None),
        P(("blk", "grp")),
        P(("blk", "grp"), None),
        P(),
        P(),
        P(),
        P(),
        P(("grp", "blk"), None, None),
        P(("grp", "blk")),
    )
    return jax.shard_map(
        per_device, mesh=mesh, in_specs=placed, out_specs=P("blk", None, "grp"), check_vma=False
    )
```
